32 devices in a mesh: depth: 16 (over z, y, core), shot: 2 (over x).
Axes of the slice: x: 2, y: 2, z: 4, core: 2. Of those that a mesh axis runs over, the one named last changes fastest.
Arguments:
- down_state: bfloat16 [32, 4, 2, 256, 256], P('depth', 'shot'), may hold values from -6 to 6
- up_state: bfloat16 [32, 4, 2, 256, 256], P('depth', 'shot'), may hold values from -6 to 6
- source: bfloat16 [4, 2, 256, 256], P('shot'), may hold values from -6 to 6
- reflect: float32 [32, 256, 256], P('depth'), may hold values from -0.3 to 0.3
- screen_class: int32 [32, 256, 256], P('depth'), may hold values from 0 to 15
- screen_values: float32 [16], replicated, may hold values from -1 to 1
- freq_index: int32 [4], P('shot'), may hold values from 0 to 127
Outputs:
- down_out: bfloat16 [32, 4, 2, 256, 256], P('depth', 'shot')
- up_out: bfloat16 [32, 4, 2, 256, 256], P('depth', 'shot')
- gradient: float32 [32, 256, 256], P('depth', 'shot')
The draws below stay inside these ranges and needn't reach their ends.
All inputs are finite; a program needn't handle non-finite values.
Results may differ from the reference program's by a relative error of at most 0.034.
Values may be sent and summed in bfloat16 or wider, within the bound.
No kernel may reach another device: no remote copies, remote signals or barrier semaphores. Data moves between devices by JAX's collectives and lax.ppermute only.
A program may use at most 64 MiB of HBM per device.

```python
import math
import jax
import jax.numpy as jnp
from jax import lax

NX = 256
NY = 256
HOPS = 3
NCLASS = 16
NFREQ = 128
NZ = 32
FRONTS = 4


def with_ends(entries, rng, low, high):
    spot = [jax.random.randint(jax.random.fold_in(rng, axis), (), 0, length) for axis, length in enumerate(entries.shape)]
    main_axis = entries.shape.index(max(entries.shape))
    beside = spot[:main_axis] + [(spot[main_axis] + 1) % entries.shape[main_axis]] + spot[main_axis + 1:]
    return entries.at[tuple(spot)].set(low).at[tuple(beside)].set(high)


def shard_levels(rng, dims, split, least, high):
    def one(position, blocks):
        draws = jax.random.uniform(jax.random.fold_in(jax.random.fold_in(rng, 6), position), (blocks,), jnp.float32, least / len(split), high / len(split))
        return jnp.repeat(jnp.exp(draws), dims[position] // blocks).reshape((-1,) + (1,) * (len(dims) - position - 1))

    loudness = one(*split[0])
    for cut in split[1:]:
        loudness = loudness * one(*cut)
    return loudness


def normal_values(key, dims, spread, reach, split=(), kind=jnp.bfloat16):
    array = spread * jax.random.normal(key, dims, jnp.float32)
    if split:
        array = array * shard_levels(key, dims, split, -0.22, 0.18)
    return jnp.clip(array, -reach, reach).astype(kind)


def setup_inputs(seed: int = 0) -> dict:
    splits = jax.random.split(jax.random.key(seed), 8)
    return {
        "down_state": normal_values(splits[0], (NZ, FRONTS, 2, NX, NY), 1.0, 6.0, ((0, 16), (1, 2))),
        "up_state": normal_values(splits[1], (NZ, FRONTS, 2, NX, NY), 1.0, 6.0, ((0, 16), (1, 2))),
        "source": normal_values(splits[2], (FRONTS, 2, NX, NY), 1.0, 6.0, ((0, 2),)),
        "reflect": jnp.clip(jax.random.uniform(splits[3], (NZ, NX, NY), jnp.float32, -0.3, 0.3) * shard_levels(splits[3], (NZ, NX, NY), ((0, 16),), -0.4, 0.0), -0.3, 0.3),
        "screen_class": with_ends(jax.random.randint(splits[4], (NZ, NX, NY), 0, NCLASS), jax.random.fold_in(splits[4], 1), 0, NCLASS - 1).astype(jnp.int32),
        "screen_values": jnp.clip(jax.random.uniform(splits[5], (NCLASS,), jnp.float32, -1.0, 1.0), -1.0, 1.0),
        "freq_index": with_ends(jax.random.randint(splits[6], (FRONTS,), 0, NFREQ), jax.random.fold_in(splits[6], 1), 0, NFREQ - 1).astype(jnp.int32),
    }


def dft_tables(length):
    counter = jnp.arange(length, dtype=jnp.int32)
    product = counter[:, None] * counter[None, :] % length
    angles = 2.0 * math.pi / length * product.astype(jnp.float32)
    return (jnp.cos(angles).astype(jnp.bfloat16), jnp.sin(angles).astype(jnp.bfloat16))

def wavenumbers(length):
    counter = jnp.arange(length, dtype=jnp.int32)
    wrapped = jnp.where(counter >= length // 2, counter - length, counter)
    return 2.0 * math.pi / length * wrapped.astype(jnp.float32)

def left_mul(matrix, planes):
    return jnp.einsum('jk,...kl->...jl', matrix.astype(jnp.float32), planes.astype(jnp.float32))

def right_mul(planes, matrix):
    return jnp.einsum('...jk,kl->...jl', planes.astype(jnp.float32), matrix.astype(jnp.float32))

def propagate(planes, phase_re, phase_im, cos_x, sin_x, cos_y, sin_y):
    real_in = planes[:, 0]
    imag_in = planes[:, 1]
    first_re = (left_mul(cos_x, real_in) + left_mul(sin_x, imag_in)).astype(jnp.bfloat16)
    first_im = (left_mul(cos_x, imag_in) - left_mul(sin_x, real_in)).astype(jnp.bfloat16)
    second_re = right_mul(first_re, cos_y) + right_mul(first_im, sin_y)
    second_im = right_mul(first_im, cos_y) - right_mul(first_re, sin_y)
    turned_re = (second_re * phase_re - second_im * phase_im).astype(jnp.bfloat16)
    turned_im = (second_re * phase_im + second_im * phase_re).astype(jnp.bfloat16)
    third_re = (left_mul(cos_x, turned_re) - left_mul(sin_x, turned_im)).astype(jnp.bfloat16)
    third_im = (left_mul(sin_x, turned_re) + left_mul(cos_x, turned_im)).astype(jnp.bfloat16)
    final_re = (right_mul(third_re, cos_y) - right_mul(third_im, sin_y)).astype(jnp.bfloat16)
    final_im = (right_mul(third_re, sin_y) + right_mul(third_im, cos_y)).astype(jnp.bfloat16)
    return (final_re.astype(jnp.float32), final_im.astype(jnp.float32))

def reference(down_state, up_state, source, reflect, screen_class, screen_values, freq_index):
    cos_x, sin_x = dft_tables(NX)
    cos_y, sin_y = dft_tables(NY)
    kwave = 0.95 * math.pi * (freq_index.astype(jnp.float32) + 1.0) / NFREQ
    kx_wave = wavenumbers(NX)
    ky_wave = wavenumbers(NY)
    vertical = kwave[:, None, None] ** 2 - kx_wave[None, :, None] ** 2 - ky_wave[None, None, :] ** 2
    propag = jnp.sqrt(jnp.maximum(vertical, 0.0))
    damping = jnp.exp(-jnp.sqrt(jnp.maximum(-vertical, 0.0))) / (NX * NY)
    phase_re = damping * jnp.cos(propag)
    phase_im = damping * jnp.sin(propag)
    slowness = screen_values[screen_class]
    scale = 1.0 / math.sqrt(FRONTS)

    def level(items):
        above, below, refl, slow = items
        angle = kwave[:, None, None] * slow[None]
        screen_re = jnp.cos(angle)
        screen_im = jnp.sin(angle)
        qa_re, qa_im = propagate(above, phase_re, phase_im, cos_x, sin_x, cos_y, sin_y)
        qb_re, qb_im = propagate(below, phase_re, phase_im, cos_x, sin_x, cos_y, sin_y)
        a_re = screen_re * qa_re - screen_im * qa_im
        a_im = screen_re * qa_im + screen_im * qa_re
        b_re = screen_re * qb_re - screen_im * qb_im
        b_im = screen_re * qb_im + screen_im * qb_re
        new_down = jnp.stack([(1.0 + refl) * a_re - refl * b_re, (1.0 + refl) * a_im - refl * b_im], axis=1).astype(jnp.bfloat16)
        new_up = jnp.stack([(1.0 - refl) * b_re + refl * a_re, (1.0 - refl) * b_im + refl * a_im], axis=1).astype(jnp.bfloat16)
        grad = scale * lax.optimization_barrier(jnp.sum(a_re * b_re + a_im * b_im, axis=0))
        return (new_down, new_up, grad)
    down = down_state
    up = up_state
    grad = jnp.zeros((NZ, NX, NY), jnp.float32)
    for repeat in range(HOPS):
        from_above = jnp.concatenate([source[None], down[:-1]], axis=0)
        from_below = jnp.concatenate([up[1:], jnp.zeros_like(up[:1])], axis=0)
        down, up, grad = lax.map(level, (from_above, from_below, reflect, slowness))
    return (down, up, grad)
```

```python
import functools
import math

import jax
import jax.numpy as jnp
import numpy as np
from jax import lax
from jax.experimental import pallas as pl
from jax.experimental.pallas import tpu as pltpu
from jax.sharding import PartitionSpec as P

HOPS = 3
NCLASS = 16
NFREQ = 128
F32 = jnp.float32
BF16 = jnp.bfloat16
VMEM = pl.BlockSpec(memory_space=pltpu.VMEM)
HBM = pl.BlockSpec(memory_space=pltpu.HBM)
SMEM = pl.BlockSpec(memory_space=pltpu.SMEM)
PARAMS = pltpu.CompilerParams(vmem_limit_bytes=28 * 2**20)


def passed_along(block, axis, distance):
    devices = range(lax.axis_size(axis))
    route = [(i - distance, i) for i in devices if i - distance in devices]
    return lax.ppermute(block, axis, route)


def dft_tables(length):
    counter = jnp.arange(length, dtype=jnp.int32)
    product = counter[:, None] * counter[None, :] % length
    angles = 2.0 * math.pi / length * product.astype(jnp.float32)
    return (jnp.cos(angles).astype(jnp.bfloat16), jnp.sin(angles).astype(jnp.bfloat16))


def wavenumbers(length):
    counter = jnp.arange(length, dtype=jnp.int32)
    wrapped = jnp.where(counter >= length // 2, counter - length, counter)
    return 2.0 * math.pi / length * wrapped.astype(jnp.float32)


def propagate(planes, phase_re, phase_im, tables):
    fwd_left, fwd_right, inv_left, inv_right = tables
    first = jnp.einsum(
        "cdjk,...dkl->...cjl", fwd_left, planes, preferred_element_type=jnp.float32
    ).astype(jnp.bfloat16)
    second = jnp.einsum("...djl,dclm->...cjm", first, fwd_right, preferred_element_type=jnp.float32)
    real_part = second[..., 0, :, :]
    imag_part = second[..., 1, :, :]
    turned = jnp.stack(
        [real_part * phase_re - imag_part * phase_im, real_part * phase_im + imag_part * phase_re],
        axis=-3,
    ).astype(jnp.bfloat16)
    third = jnp.einsum(
        "cdjk,...dkl->...cjl", inv_left, turned, preferred_element_type=jnp.float32
    ).astype(jnp.bfloat16)
    return jnp.einsum(
        "...djl,dclm->...cjm", third, inv_right, preferred_element_type=jnp.float32
    ).astype(jnp.bfloat16)


def trade(down_edge, up_edge):
    got_down = passed_along(down_edge, "depth", 1)
    got_up = passed_along(up_edge, "depth", -1)
    return (got_down, got_up)


def per_device_plain(down_state, up_state, source, reflect, screen_class, screen_values, freq_index):
    levels = down_state.shape[0]
    rows_x = down_state.shape[3]
    rows_y = down_state.shape[4]
    front_count = down_state.shape[1]
    depth_rank = lax.axis_index("depth")
    scale = 1.0 / math.sqrt(front_count * lax.axis_size("shot"))
    cos_x, sin_x = dft_tables(rows_x)
    cos_y, sin_y = dft_tables(rows_y)
    tables = (
        jnp.stack([jnp.stack([cos_x, sin_x]), jnp.stack([-sin_x, cos_x])]),
        jnp.stack([jnp.stack([cos_y, -sin_y]), jnp.stack([sin_y, cos_y])]),
        jnp.stack([jnp.stack([cos_x, -sin_x]), jnp.stack([sin_x, cos_x])]),
        jnp.stack([jnp.stack([cos_y, sin_y]), jnp.stack([-sin_y, cos_y])]),
    )
    kwave = 0.95 * math.pi * (freq_index.astype(jnp.float32) + 1.0) / NFREQ
    kx_wave = wavenumbers(rows_x)
    ky_wave = wavenumbers(rows_y)
    vertical = kwave[:, None, None] ** 2 - kx_wave[None, :, None] ** 2 - ky_wave[None, None, :] ** 2
    propag = jnp.sqrt(jnp.maximum(vertical, 0.0))
    damping = jnp.exp(-jnp.sqrt(jnp.maximum(-vertical, 0.0))) / (rows_x * rows_y)
    phase_re = damping * jnp.cos(propag)
    phase_im = damping * jnp.sin(propag)
    classes = jnp.arange(NCLASS, dtype=jnp.int32)
    onehot = (screen_class[None] == classes[:, None, None, None]).astype(jnp.float32)
    slowness = jnp.einsum("c,clxy->lxy", screen_values, onehot, precision=lax.Precision.HIGHEST)
    angle = kwave[None, :, None, None] * slowness[:, None]
    screen_re = jnp.cos(angle)
    screen_im = jnp.sin(angle)
    refl = reflect[:, None]
    top_slab = depth_rank == 0
    down = down_state
    up = up_state
    a_re = a_im = b_re = b_im = None
    for repeat in range(HOPS):
        down_edge = down[levels - 1]
        up_edge = up[0]
        got_down, got_up = trade(down_edge, up_edge)
        got_down = jnp.where(top_slab, source, got_down)
        moved = propagate(
            jnp.concatenate([got_down[None], down[: levels - 1], up[1:], got_up[None]], axis=0),
            phase_re,
            phase_im,
            tables,
        )
        from_above = moved[:levels]
        from_below = moved[levels:]
        qa_re = from_above[:, :, 0].astype(jnp.float32)
        qa_im = from_above[:, :, 1].astype(jnp.float32)
        qb_re = from_below[:, :, 0].astype(jnp.float32)
        qb_im = from_below[:, :, 1].astype(jnp.float32)
        a_re = screen_re * qa_re - screen_im * qa_im
        a_im = screen_re * qa_im + screen_im * qa_re
        b_re = screen_re * qb_re - screen_im * qb_im
        b_im = screen_re * qb_im + screen_im * qb_re
        down = jnp.stack(
            [(1.0 + refl) * a_re - refl * b_re, (1.0 + refl) * a_im - refl * b_im], axis=2
        ).astype(jnp.bfloat16)
        up = jnp.stack(
            [(1.0 - refl) * b_re + refl * a_re, (1.0 - refl) * b_im + refl * a_im], axis=2
        ).astype(jnp.bfloat16)
    terms = scale * jnp.sum(a_re * b_re + a_im * b_im, axis=1)
    gradient = lax.psum_scatter(
        terms.astype(jnp.bfloat16), "shot", scatter_dimension=1, tiled=True
    ).astype(jnp.float32)
    return (down, up, gradient)


def hartley(length):
    counter = np.arange(length)
    angles = 2.0 * np.pi / length * (counter[:, None] * counter[None, :] % length)
    cosine = np.cos(angles).astype(BF16).astype(np.float32)
    sine = np.sin(angles).astype(BF16).astype(np.float32)
    return (cosine + sine).astype(BF16)


def odd_place():
    return lax.rem(lax.axis_index("depth"), 2)


def mm(left, right):
    return jnp.dot(left, right, preferred_element_type=F32)


def spread(real_part, imag_part, hx, hy, phase, front):
    rows = real_part.shape[0]
    first = mm(jnp.concatenate([real_part, imag_part], axis=0), hy).astype(BF16)
    second_re = mm(hx, first[:rows])
    second_im = mm(hx, first[rows:])
    turn_re = phase[front, 0]
    turn_im = phase[front, 1]
    turned_re = (second_re * turn_re - second_im * turn_im).astype(BF16)
    turned_im = (second_re * turn_im + second_im * turn_re).astype(BF16)
    third_re = mm(hx, turned_re).astype(BF16)
    third_im = mm(hx, turned_im).astype(BF16)
    last = mm(jnp.concatenate([third_re, third_im], axis=0), hy).astype(BF16)
    return last[:rows], last[rows:]


def screened(real_part, imag_part, screen_re, screen_im):
    return (
        screen_re * real_part - screen_im * imag_part,
        screen_re * imag_part + screen_im * real_part,
    )


def mixed(a_re, a_im, b_re, b_im, refl, screen_re, screen_im):
    a_re, a_im, b_re, b_im = (part.astype(F32) for part in (a_re, a_im, b_re, b_im))
    step_re = refl * (a_re - b_re)
    step_im = refl * (a_im - b_im)
    inward = screened(a_re + step_re, a_im + step_im, screen_re, screen_im)
    outward = screened(b_re + step_re, b_im + step_im, screen_re, screen_im)
    return tuple(part.astype(BF16) for part in inward + outward)


def edges_kernel(down, up, outward_outer, inward_inner, sems):
    levels = down.shape[0]

    def fetch(first, second):
        copies = [
            pltpu.make_async_copy(first, outward_outer, sems.at[0]),
            pltpu.make_async_copy(second, inward_inner, sems.at[1]),
        ]
        for copy in copies:
            copy.start()
        for copy in copies:
            copy.wait()

    odd = odd_place()

    @pl.when(odd == 0)
    def _():
        fetch(up.at[0], down.at[levels - 1])

    @pl.when(odd == 1)
    def _():
        fetch(down.at[levels - 1], up.at[0])


def class_rows(slowness, kwave, shape):
    lanes = lax.broadcasted_iota(jnp.int32, shape, 1)
    table = jnp.zeros(shape, F32)
    for entry in range(NCLASS):
        table = jnp.where(lanes == entry, slowness[entry], table)
    angle = kwave * table
    return jnp.cos(angle), jnp.sin(angle)


def look_up(table, classes):
    width = 128
    rows = classes.shape[0]
    wide = jnp.broadcast_to(table[:1], (rows, width))
    pieces = [
        jnp.take_along_axis(wide, classes[:, start : start + width], axis=1, mode="promise_in_bounds")
        for start in range(0, classes.shape[1], width)
    ]
    return jnp.concatenate(pieces, axis=1)


def front_wave(freq, front):
    return 0.95 * math.pi * (freq[front].astype(F32) + 1.0) / NFREQ


def setup_kernel(
    down, up, reflect, classes_in, slowness, freq, outward_outer, hx, hy,
    q_out_inner, q_in_outer, q_out_outer, screen, phase, refl, message,
    fields, klass, sems,
):
    fronts = q_out_inner.shape[0]
    rows_x, rows_y = refl.shape[1:]
    odd = odd_place()
    fixed = [
        pltpu.make_async_copy(reflect.at[odd], refl.at[0], sems.at[2]),
        pltpu.make_async_copy(reflect.at[1 - odd], refl.at[1], sems.at[3]),
        pltpu.make_async_copy(classes_in.at[odd], klass.at[0], sems.at[4]),
        pltpu.make_async_copy(classes_in.at[1 - odd], klass.at[1], sems.at[5]),
    ]
    for copy in fixed:
        copy.start()

    @pl.when(odd == 0)
    def _():
        pltpu.make_async_copy(down.at[0], fields.at[0], sems.at[0]).start()
        pltpu.make_async_copy(up.at[1], fields.at[1], sems.at[1]).start()

    @pl.when(odd == 1)
    def _():
        pltpu.make_async_copy(up.at[1], fields.at[0], sems.at[0]).start()
        pltpu.make_async_copy(down.at[0], fields.at[1], sems.at[1]).start()

    def squares(length, axis):
        counter = lax.broadcasted_iota(jnp.int32, (rows_x, rows_y), axis)
        wrapped = jnp.where(counter >= length // 2, counter - length, counter)
        wave = 2.0 * math.pi / length * wrapped.astype(F32)
        return wave * wave

    lateral = squares(rows_x, 0) + squares(rows_y, 1)
    for front in range(fronts):
        kwave = front_wave(freq, front)
        vertical = kwave * kwave - lateral
        propag = jnp.sqrt(jnp.maximum(vertical, 0.0))
        damping = jnp.exp(-jnp.sqrt(jnp.maximum(-vertical, 0.0))) / (rows_x * rows_y)
        phase[front, 0] = damping * jnp.cos(propag)
        phase[front, 1] = damping * jnp.sin(propag)
    for copy in fixed:
        copy.wait()
    sign = jnp.where(odd == 0, 1.0, -1.0).astype(F32)
    for level in range(2):
        refl[level] = sign * refl[level]
    for front in range(fronts):
        cos_row, sin_row = class_rows(slowness, front_wave(freq, front), (8, 128))
        for level in range(2):
            screen[level, front, 0] = look_up(cos_row, klass[level])
            screen[level, front, 1] = look_up(sin_row, klass[level])
    message[fronts, 0] = refl[0].astype(BF16)
    message[fronts, 1] = klass[0].astype(BF16)
    pltpu.make_async_copy(down.at[0], fields.at[0], sems.at[0]).wait()
    pltpu.make_async_copy(down.at[0], fields.at[1], sems.at[1]).wait()
    hx = hx[...]
    hy = hy[...]
    for front in range(fronts):
        q_re, q_im = spread(fields[1, front, 0], fields[1, front, 1], hx, hy, phase, front)
        q_out_inner[front, 0] = q_re
        q_out_inner[front, 1] = q_im
        b_re, b_im = screened(q_re.astype(F32), q_im.astype(F32), screen[0, front, 0], screen[0, front, 1])
        kept = 1.0 - refl[0]
        message[front, 0] = (kept * b_re).astype(BF16)
        message[front, 1] = (kept * b_im).astype(BF16)
        q_re, q_im = spread(outward_outer[front, 0], outward_outer[front, 1], hx, hy, phase, front)
        q_out_outer[front, 0] = q_re
        q_out_outer[front, 1] = q_im
        q_re, q_im = spread(fields[0, front, 0], fields[0, front, 1], hx, hy, phase, front)
        q_in_outer[front, 0] = q_re
        q_in_outer[front, 1] = q_im


def ahead_kernel(
    partner, q_in_outer, screen, refl, phase, hx, hy,
    inward_inner, q_out_inner, last_far, last_near,
):
    fronts = partner.shape[0]
    half = partner.shape[2] // 2
    far_first = lax.axis_index("shot") % 2
    hx = hx[...]
    hy = hy[...]
    for front in range(fronts):
        q_re, q_im = spread(partner[front, 0], partner[front, 1], hx, hy, phase, front)
        in_re, in_im, out_re, out_im = mixed(
            q_in_outer[front, 0], q_in_outer[front, 1], q_re, q_im,
            refl[1], screen[1, front, 0], screen[1, front, 1],
        )
        inward_inner[front, 0] = in_re
        inward_inner[front, 1] = in_im
        q_re, q_im = spread(out_re, out_im, hx, hy, phase, front)
        q_out_inner[front, 0] = q_re
        q_out_inner[front, 1] = q_im
        b_re, b_im = screened(q_re.astype(F32), q_im.astype(F32), screen[0, front, 0], screen[0, front, 1])
        kept = 1.0 - refl[0]
        parts = spread((kept * b_re).astype(BF16), (kept * b_im).astype(BF16), hx, hy, phase, front)
        for index, part in enumerate(parts):
            top, bottom = part[:half], part[half:]
            flip = far_first == 0
            last_far[front, index] = jnp.where(flip, bottom, top)
            last_near[front, index] = jnp.where(flip, top, bottom)


def edge_kernel(
    arrived, source, partner, q_out_inner, screen, refl, phase, hx, hy,
    inward_inner, q_arrived, q_out_outer, q_out_inner_next,
):
    fronts = partner.shape[0]
    first = lax.axis_index("depth") == 0
    hx = hx[...]
    hy = hy[...]
    for front in range(fronts):
        entering = [jnp.where(first, source[front, part], arrived[front, part]) for part in range(2)]
        q_re, q_im = spread(entering[0], entering[1], hx, hy, phase, front)
        q_arrived[front, 0] = q_re
        q_arrived[front, 1] = q_im
        in_re, in_im, out_re, out_im = mixed(
            q_re, q_im, q_out_inner[front, 0], q_out_inner[front, 1],
            refl[0], screen[0, front, 0], screen[0, front, 1],
        )
        a_re, a_im = spread(in_re, in_im, hx, hy, phase, front)
        b_re, b_im = spread(partner[front, 0], partner[front, 1], hx, hy, phase, front)
        q_re, q_im = spread(out_re, out_im, hx, hy, phase, front)
        q_out_outer[front, 0] = q_re
        q_out_outer[front, 1] = q_im
        in_re, in_im, out_re, out_im = mixed(
            a_re, a_im, b_re, b_im, refl[1], screen[1, front, 0], screen[1, front, 1]
        )
        inward_inner[front, 0] = in_re
        inward_inner[front, 1] = in_im
        q_re, q_im = spread(out_re, out_im, hx, hy, phase, front)
        q_out_inner_next[front, 0] = q_re
        q_out_inner_next[front, 1] = q_im


def beyond_kernel(
    message, source, q_out_outer_0, q_out_outer_1, q_out_inner, slowness, freq, screen, refl, phase, hx, hy,
    q_in_outer, rest,
):
    fronts = source.shape[0]
    first = lax.axis_index("depth") == 0
    hx = hx[...]
    hy = hy[...]
    refl_beyond = message[fronts, 0].astype(F32)
    klass = message[fronts, 1].astype(F32).astype(jnp.int32)
    for front in range(fronts):
        cos_row, sin_row = class_rows(slowness, front_wave(freq, front), (8, 128))
        back_re = refl_beyond * look_up(cos_row, klass)
        back_im = refl_beyond * look_up(sin_row, klass)
        part_re, part_im = screened(
            q_out_outer_0[front, 0].astype(F32), q_out_outer_0[front, 1].astype(F32), back_re, back_im
        )
        entering = [
            jnp.where(first, source[front, index], (message[front, index].astype(F32) + part).astype(BF16))
            for index, part in enumerate((part_re, part_im))
        ]
        q_re, q_im = spread(entering[0], entering[1], hx, hy, phase, front)
        in_re, in_im, _, _ = mixed(
            q_re, q_im, q_out_inner[front, 0], q_out_inner[front, 1],
            refl[0], screen[0, front, 0], screen[0, front, 1],
        )
        q_re, q_im = spread(in_re, in_im, hx, hy, phase, front)
        q_in_outer[front, 0] = q_re
        q_in_outer[front, 1] = q_im
        part_re, part_im = screened(
            q_out_outer_1[front, 0].astype(F32), q_out_outer_1[front, 1].astype(F32), back_re, back_im
        )
        q_re, q_im = spread(part_re.astype(BF16), part_im.astype(BF16), hx, hy, phase, front)
        rest[front, 0] = q_re
        rest[front, 1] = q_im


def inner_kernel(
    partner, q_in_outer, screen, refl, phase, hx, hy,
    down_out, up_out, terms,
    inward, outward, sems,
):
    fronts = partner.shape[0]
    odd = odd_place()
    hx = hx[...]
    hy = hy[...]
    total = None
    for front in range(fronts):
        q_re, q_im = spread(partner[front, 0], partner[front, 1], hx, hy, phase, front)
        a_re, a_im = q_in_outer[front, 0], q_in_outer[front, 1]
        in_re, in_im, out_re, out_im = mixed(
            a_re, a_im, q_re, q_im, refl[1], screen[1, front, 0], screen[1, front, 1]
        )
        inward[front, 0] = in_re
        inward[front, 1] = in_im
        outward[front, 0] = out_re
        outward[front, 1] = out_im
        term = a_re.astype(F32) * q_re.astype(F32) + a_im.astype(F32) * q_im.astype(F32)
        total = term if total is None else total + term

    @pl.when(odd == 0)
    def _():
        pltpu.make_async_copy(inward, down_out.at[1], sems.at[0]).start()
        pltpu.make_async_copy(outward, up_out.at[1], sems.at[1]).start()

    @pl.when(odd == 1)
    def _():
        pltpu.make_async_copy(inward, up_out.at[0], sems.at[0]).start()
        pltpu.make_async_copy(outward, down_out.at[0], sems.at[1]).start()

    terms[...] = total
    pltpu.make_async_copy(inward, down_out.at[0], sems.at[0]).wait()
    pltpu.make_async_copy(outward, up_out.at[0], sems.at[1]).wait()


def outer_rows(
    near, last, q_arrived, rest, q_out_inner, screen, refl, down_in, up_in, down_out, up_out, inward, outward, sems
):
    del down_in, up_in
    fronts, _, half, _ = last.shape
    first = lax.axis_index("depth") == 0
    odd = odd_place()
    shot = lax.axis_index("shot") % 2
    start = pl.multiple_of((shot if near else 1 - shot) * half, half)
    rows = pl.ds(start, half)
    total = None
    kept = refl[0, rows, :]
    for front in range(fronts):
        a_re, a_im = (
            jnp.where(
                first,
                q_arrived[front, part, rows, :].astype(F32),
                last[front, part].astype(F32) + rest[front, part, rows, :].astype(F32),
            )
            for part in range(2)
        )
        b_re, b_im = (q_out_inner[front, part, rows, :].astype(F32) for part in range(2))
        in_re, in_im, out_re, out_im = mixed(
            a_re, a_im, b_re, b_im, kept, screen[0, front, 0, rows, :], screen[0, front, 1, rows, :]
        )
        inward[front, 0] = in_re
        inward[front, 1] = in_im
        outward[front, 0] = out_re
        outward[front, 1] = out_im
        term = a_re * b_re + a_im * b_im
        total = term if total is None else total + term

    def copies(level, inward_out, outward_out):
        return [
            pltpu.make_async_copy(inward, inward_out.at[level, :, :, rows, :], sems.at[0]),
            pltpu.make_async_copy(outward, outward_out.at[level, :, :, rows, :], sems.at[1]),
        ]

    @pl.when(odd == 0)
    def _():
        for copy in copies(0, down_out, up_out):
            copy.start()

    @pl.when(odd == 1)
    def _():
        for copy in copies(1, up_out, down_out):
            copy.start()

    def finish():
        for copy in copies(0, down_out, up_out):
            copy.wait()

    return rows, total, finish


def far_rows_kernel(
    last, q_arrived, rest, q_out_inner, screen, refl, inner_terms, down_in, up_in,
    down_out, up_out, terms,
    inward, outward, sems,
):
    rows, total, finish = outer_rows(
        False, last, q_arrived, rest, q_out_inner, screen, refl, down_in, up_in, down_out, up_out, inward, outward, sems
    )
    terms[0] = total.astype(BF16)
    terms[1] = inner_terms[rows, :].astype(BF16)
    finish()


def near_rows_kernel(
    scale, last, q_arrived, rest, q_out_inner, screen, refl, inner_terms, other, down_in, up_in,
    down_out, up_out, gradient,
    inward, outward, sems,
):
    rows, total, finish = outer_rows(
        True, last, q_arrived, rest, q_out_inner, screen, refl, down_in, up_in, down_out, up_out, inward, outward, sems
    )
    odd = odd_place()
    gradient[odd] = scale * (total + other[0].astype(F32))
    gradient[1 - odd] = scale * (inner_terms[rows, :] + other[1].astype(F32))
    finish()


def per_device(down_state, up_state, source, reflect, screen_class, screen_values, freq_index):
    depth = lax.axis_size("depth")
    shots = lax.axis_size("shot")
    levels, fronts, parts, rows_x, rows_y = down_state.shape
    if levels != 2 or depth % 2 or shots != 2 or HOPS != 3:
        return per_device_plain(down_state, up_state, source, reflect, screen_class, screen_values, freq_index)
    scale = 1.0 / math.sqrt(fronts * shots)
    half = rows_x // 2
    hx = jnp.asarray(hartley(rows_x))
    hy = jnp.asarray(hartley(rows_y))
    partners = [(i, i ^ 1) for i in range(depth)]
    beyond = [(i, i + 1) for i in range(1, depth - 1, 2)] + [(i + 1, i) for i in range(1, depth - 1, 2)]
    to_partner = functools.partial(lax.ppermute, axis_name="depth", perm=partners)
    to_beyond = functools.partial(lax.ppermute, axis_name="depth", perm=beyond)
    across = functools.partial(lax.ppermute, axis_name="shot", perm=[(0, 1), (1, 0)])
    plane = jax.ShapeDtypeStruct((fronts, parts, rows_x, rows_y), BF16)
    half_plane = jax.ShapeDtypeStruct((fronts, parts, half, rows_y), BF16)
    pair = jax.ShapeDtypeStruct((2, rows_x, rows_y), F32)
    turns = jax.ShapeDtypeStruct((fronts, parts, rows_x, rows_y), F32)
    screens = jax.ShapeDtypeStruct((2, fronts, parts, rows_x, rows_y), F32)
    parcel = jax.ShapeDtypeStruct((fronts + 1, parts, rows_x, rows_y), BF16)
    state = jax.ShapeDtypeStruct(down_state.shape, BF16)
    dma = pltpu.SemaphoreType.DMA

    def call(kernel, in_specs, out_specs, out_shape, scratch=(), **more):
        return pl.pallas_call(
            kernel,
            in_specs=in_specs,
            out_specs=out_specs,
            out_shape=out_shape,
            scratch_shapes=list(scratch),
            compiler_params=PARAMS,
            **more,
        )

    out_outer, in_inner = call(edges_kernel, [HBM] * 2, [VMEM] * 2, [plane] * 2, [dma((2,))])(down_state, up_state)
    arrived = to_beyond(out_outer)
    partner_0 = to_partner(in_inner)
    q_out_inner_0, q_in_outer_0, q_out_outer_0, screen, phase, refl, message = call(
        setup_kernel,
        [HBM] * 4 + [SMEM] * 2 + [VMEM] * 3,
        [VMEM] * 7,
        [plane] * 3 + [screens, turns, pair, parcel],
        [
            pltpu.VMEM((2, fronts, parts, rows_x, rows_y), BF16),
            pltpu.VMEM((2, rows_x, rows_y), jnp.int32),
            dma((6,)),
        ],
    )(down_state, up_state, reflect, screen_class, screen_values, freq_index, out_outer, hx, hy)
    message = to_beyond(message)
    in_inner_1, q_out_inner_1, last_far, last_near = call(
        ahead_kernel, [VMEM] * 7, [VMEM] * 4, [plane] * 2 + [half_plane] * 2
    )(partner_0, q_in_outer_0, screen, refl, phase, hx, hy)
    partner_1 = to_partner(in_inner_1)
    last_far = to_beyond(last_far)
    last_near = to_beyond(last_near)
    in_inner_2, q_arrived, q_out_outer_1, q_out_inner_2 = call(edge_kernel, [VMEM] * 9, [VMEM] * 4, [plane] * 4)(
        arrived, source, partner_1, q_out_inner_0, screen, refl, phase, hx, hy
    )
    partner_2 = to_partner(in_inner_2)
    q_in_outer_2, rest = call(
        beyond_kernel, [VMEM] * 5 + [SMEM] * 2 + [VMEM] * 5, [VMEM] * 2, [plane] * 2
    )(
        message, source, q_out_outer_0, q_out_outer_1, q_out_inner_1, screen_values, freq_index,
        screen, refl, phase, hx, hy,
    )
    down, up, inner_terms = call(
        inner_kernel,
        [VMEM] * 7,
        [HBM] * 2 + [VMEM],
        [state, state, jax.ShapeDtypeStruct((rows_x, rows_y), F32)],
        [pltpu.VMEM(plane.shape, BF16)] * 2 + [dma((2,))],
    )(partner_2, q_in_outer_2, screen, refl, phase, hx, hy)
    halves = [pltpu.VMEM(half_plane.shape, BF16)] * 2 + [dma((2,))]
    down, up, terms = call(
        far_rows_kernel,
        [VMEM] * 7 + [HBM] * 2,
        [HBM] * 2 + [VMEM],
        [state, state, jax.ShapeDtypeStruct((2, half, rows_y), BF16)],
        halves,
        input_output_aliases={7: 0, 8: 1},
    )(last_far, q_arrived, rest, q_out_inner_2, screen, refl, inner_terms, down, up)
    other = across(terms)
    down, up, gradient = call(
        functools.partial(near_rows_kernel, scale),
        [VMEM] * 8 + [HBM] * 2,
        [HBM] * 2 + [VMEM],
        [state, state, jax.ShapeDtypeStruct((2, half, rows_y), F32)],
        halves,
        input_output_aliases={8: 0, 9: 1},
    )(last_near, q_arrived, rest, q_out_inner_2, screen, refl, inner_terms, other, down, up)
    return (down, up, gradient)


def solution(mesh):
    return jax.shard_map(
        per_device,
        mesh=mesh,
        in_specs=(
            P("depth", "shot", None, None, None),
            P("depth", "shot", None, None, None),
            P("shot", None, None, None),
            P("depth", None, None),
            P("depth", None, None),
            P(),
            P("shot"),
        ),
        out_specs=(
            P("depth", "shot", None, None, None),
            P("depth", "shot", None, None, None),
            P("depth", "shot", None),
        ),
        check_vma=False,
    )
```

```python
import functools
import math

import jax
import jax.numpy as jnp
import numpy as np
from jax import lax
from jax.experimental import pallas as pl
from jax.experimental.pallas import tpu as pltpu
from jax.sharding import PartitionSpec as P

HOPS = 3
NCLASS = 16
NFREQ = 128
F32 = jnp.float32
BF16 = jnp.bfloat16
VMEM = pl.BlockSpec(memory_space=pltpu.VMEM)
HBM = pl.BlockSpec(memory_space=pltpu.HBM)
SMEM = pl.BlockSpec(memory_space=pltpu.SMEM)
PARAMS = pltpu.CompilerParams(vmem_limit_bytes=28 * 2**20)


def passed_along(block, axis, distance):
    devices = range(lax.axis_size(axis))
    route = [(i - distance, i) for i in devices if i - distance in devices]
    return lax.ppermute(block, axis, route)


def dft_tables(length):
    counter = jnp.arange(length, dtype=jnp.int32)
    product = counter[:, None] * counter[None, :] % length
    angles = 2.0 * math.pi / length * product.astype(jnp.float32)
    return (jnp.cos(angles).astype(jnp.bfloat16), jnp.sin(angles).astype(jnp.bfloat16))


def wavenumbers(length):
    counter = jnp.arange(length, dtype=jnp.int32)
    wrapped = jnp.where(counter >= length // 2, counter - length, counter)
    return 2.0 * math.pi / length * wrapped.astype(jnp.float32)


def propagate(planes, phase_re, phase_im, tables):
    fwd_left, fwd_right, inv_left, inv_right = tables
    first = jnp.einsum(
        "cdjk,...dkl->...cjl", fwd_left, planes, preferred_element_type=jnp.float32
    ).astype(jnp.bfloat16)
    second = jnp.einsum("...djl,dclm->...cjm", first, fwd_right, preferred_element_type=jnp.float32)
    real_part = second[..., 0, :, :]
    imag_part = second[..., 1, :, :]
    turned = jnp.stack(
        [real_part * phase_re - imag_part * phase_im, real_part * phase_im + imag_part * phase_re],
        axis=-3,
    ).astype(jnp.bfloat16)
    third = jnp.einsum(
        "cdjk,...dkl->...cjl", inv_left, turned, preferred_element_type=jnp.float32
    ).astype(jnp.bfloat16)
    return jnp.einsum(
        "...djl,dclm->...cjm", third, inv_right, preferred_element_type=jnp.float32
    ).astype(jnp.bfloat16)


def trade(down_edge, up_edge):
    got_down = passed_along(down_edge, "depth", 1)
    got_up = passed_along(up_edge, "depth", -1)
    return (got_down, got_up)


def per_device_plain(down_state, up_state, source, reflect, screen_class, screen_values, freq_index):
    levels = down_state.shape[0]
    rows_x = down_state.shape[3]
    rows_y = down_state.shape[4]
    front_count = down_state.shape[1]
    depth_rank = lax.axis_index("depth")
    scale = 1.0 / math.sqrt(front_count * lax.axis_size("shot"))
    cos_x, sin_x = dft_tables(rows_x)
    cos_y, sin_y = dft_tables(rows_y)
    tables = (
        jnp.stack([jnp.stack([cos_x, sin_x]), jnp.stack([-sin_x, cos_x])]),
        jnp.stack([jnp.stack([cos_y, -sin_y]), jnp.stack([sin_y, cos_y])]),
        jnp.stack([jnp.stack([cos_x, -sin_x]), jnp.stack([sin_x, cos_x])]),
        jnp.stack([jnp.stack([cos_y, sin_y]), jnp.stack([-sin_y, cos_y])]),
    )
    kwave = 0.95 * math.pi * (freq_index.astype(jnp.float32) + 1.0) / NFREQ
    kx_wave = wavenumbers(rows_x)
    ky_wave = wavenumbers(rows_y)
    vertical = kwave[:, None, None] ** 2 - kx_wave[None, :, None] ** 2 - ky_wave[None, None, :] ** 2
    propag = jnp.sqrt(jnp.maximum(vertical, 0.0))
    damping = jnp.exp(-jnp.sqrt(jnp.maximum(-vertical, 0.0))) / (rows_x * rows_y)
    phase_re = damping * jnp.cos(propag)
    phase_im = damping * jnp.sin(propag)
    classes = jnp.arange(NCLASS, dtype=jnp.int32)
    onehot = (screen_class[None] == classes[:, None, None, None]).astype(jnp.float32)
    slowness = jnp.einsum("c,clxy->lxy", screen_values, onehot, precision=lax.Precision.HIGHEST)
    angle = kwave[None, :, None, None] * slowness[:, None]
    screen_re = jnp.cos(angle)
    screen_im = jnp.sin(angle)
    refl = reflect[:, None]
    top_slab = depth_rank == 0
    down = down_state
    up = up_state
    a_re = a_im = b_re = b_im = None
    for repeat in range(HOPS):
        down_edge = down[levels - 1]
        up_edge = up[0]
        got_down, got_up = trade(down_edge, up_edge)
        got_down = jnp.where(top_slab, source, got_down)
        moved = propagate(
            jnp.concatenate([got_down[None], down[: levels - 1], up[1:], got_up[None]], axis=0),
            phase_re,
            phase_im,
            tables,
        )
        from_above = moved[:levels]
        from_below = moved[levels:]
        qa_re = from_above[:, :, 0].astype(jnp.float32)
        qa_im = from_above[:, :, 1].astype(jnp.float32)
        qb_re = from_below[:, :, 0].astype(jnp.float32)
        qb_im = from_below[:, :, 1].astype(jnp.float32)
        a_re = screen_re * qa_re - screen_im * qa_im
        a_im = screen_re * qa_im + screen_im * qa_re
        b_re = screen_re * qb_re - screen_im * qb_im
        b_im = screen_re * qb_im + screen_im * qb_re
        down = jnp.stack(
            [(1.0 + refl) * a_re - refl * b_re, (1.0 + refl) * a_im - refl * b_im], axis=2
        ).astype(jnp.bfloat16)
        up = jnp.stack(
            [(1.0 - refl) * b_re + refl * a_re, (1.0 - refl) * b_im + refl * a_im], axis=2
        ).astype(jnp.bfloat16)
    terms = scale * jnp.sum(a_re * b_re + a_im * b_im, axis=1)
    gradient = lax.psum_scatter(
        terms.astype(jnp.bfloat16), "shot", scatter_dimension=1, tiled=True
    ).astype(jnp.float32)
    return (down, up, gradient)


def hartley(length):
    counter = np.arange(length)
    angles = 2.0 * np.pi / length * (counter[:, None] * counter[None, :] % length)
    cosine = np.cos(angles).astype(BF16).astype(np.float32)
    sine = np.sin(angles).astype(BF16).astype(np.float32)
    return (cosine + sine).astype(BF16)


def odd_place():
    return lax.rem(lax.axis_index("depth"), 2)


def mm(left, right):
    return jnp.dot(left, right, preferred_element_type=F32)


def spread(jobs, work, hx, hy, phase):
    jobs = list(enumerate(jobs))
    for slot, (plane, _, _) in jobs:
        for part in range(2):
            work[slot, part] = mm(plane[part], hy[...]).astype(BF16)
    for slot, (_, front, _) in jobs:
        turn_re, turn_im = phase[front, 0], phase[front, 1]
        part_re = mm(hx[...], work[slot, 0])
        part_im = mm(hx[...], work[slot, 1])
        work[slot, 0] = (part_re * turn_re - part_im * turn_im).astype(BF16)
        work[slot, 1] = (part_re * turn_im + part_im * turn_re).astype(BF16)
    for slot, _ in jobs:
        for part in range(2):
            work[slot, part] = mm(hx[...], work[slot, part]).astype(BF16)
    for slot, (_, _, target) in jobs:
        for part in range(2):
            target[part] = mm(work[slot, part], hy[...]).astype(BF16)


def screened(real_part, imag_part, screen_re, screen_im):
    return (
        screen_re * real_part - screen_im * imag_part,
        screen_re * imag_part + screen_im * real_part,
    )


def mixed(a_re, a_im, b_re, b_im, refl, screen_re, screen_im):
    a_re, a_im, b_re, b_im = (part.astype(F32) for part in (a_re, a_im, b_re, b_im))
    step_re = refl * (a_re - b_re)
    step_im = refl * (a_im - b_im)
    inward = screened(a_re + step_re, a_im + step_im, screen_re, screen_im)
    outward = screened(b_re + step_re, b_im + step_im, screen_re, screen_im)
    return tuple(part.astype(BF16) for part in inward + outward)


def put(target, real_part, imag_part):
    target[0] = real_part.astype(BF16)
    target[1] = imag_part.astype(BF16)


def edges_kernel(down, up, reflect, classes_in, parcel, inward_inner, refl, klass, sems):
    levels = down.shape[0]
    fronts = inward_inner.shape[0]
    odd = odd_place()
    outward_outer = parcel.at[pl.ds(0, fronts)]

    def fetch(first, second):
        pltpu.make_async_copy(first, outward_outer, sems.at[0]).start()
        pltpu.make_async_copy(second, inward_inner, sems.at[1]).start()

    fixed = [
        pltpu.make_async_copy(reflect.at[odd], refl, sems.at[2]),
        pltpu.make_async_copy(classes_in.at[odd], klass, sems.at[3]),
    ]
    for copy in fixed:
        copy.start()

    @pl.when(odd == 0)
    def _():
        fetch(up.at[0], down.at[levels - 1])

    @pl.when(odd == 1)
    def _():
        fetch(down.at[levels - 1], up.at[0])

    for copy in fixed:
        copy.wait()
    put(parcel.at[fronts], jnp.where(odd == 0, 1.0, -1.0).astype(F32) * refl[...], klass[...])
    pltpu.make_async_copy(up.at[0], outward_outer, sems.at[0]).wait()
    pltpu.make_async_copy(up.at[0], inward_inner, sems.at[1]).wait()


def class_rows(slowness, kwave, shape):
    lanes = lax.broadcasted_iota(jnp.int32, shape, 1)
    table = jnp.zeros(shape, F32)
    for entry in range(NCLASS):
        table = jnp.where(lanes == entry, slowness[entry], table)
    angle = kwave * table
    return jnp.cos(angle), jnp.sin(angle)


def look_up(table, classes):
    width = 128
    rows = classes.shape[0]
    wide = jnp.broadcast_to(table[:1], (rows, width))
    pieces = [
        jnp.take_along_axis(wide, classes[:, start : start + width], axis=1, mode="promise_in_bounds")
        for start in range(0, classes.shape[1], width)
    ]
    return jnp.concatenate(pieces, axis=1)


def front_wave(freq, front):
    return 0.95 * math.pi * (freq[front].astype(F32) + 1.0) / NFREQ


def series(square, shift):
    total = jnp.full_like(square, 1.0 / math.factorial(18 + shift))
    for order in range(16, -1, -2):
        total = 1.0 / math.factorial(order + shift) - square * total
    return total


def setup_kernel(
    down, up, reflect, classes_in, slowness, freq, parcel, hx, hy,
    q_out_inner, q_in_outer, q_out_outer, screen, phase, refl, second,
    fields, klass, work, sems,
):
    fronts = q_out_inner.shape[0]
    rows_x, rows_y = refl.shape[1:]
    odd = odd_place()
    fixed = [
        pltpu.make_async_copy(reflect.at[odd], refl.at[0], sems.at[2]),
        pltpu.make_async_copy(reflect.at[1 - odd], refl.at[1], sems.at[3]),
        pltpu.make_async_copy(classes_in.at[odd], klass.at[0], sems.at[4]),
        pltpu.make_async_copy(classes_in.at[1 - odd], klass.at[1], sems.at[5]),
    ]
    for copy in fixed:
        copy.start()

    @pl.when(odd == 0)
    def _():
        pltpu.make_async_copy(down.at[0], fields.at[0], sems.at[0]).start()
        pltpu.make_async_copy(up.at[1], fields.at[1], sems.at[1]).start()

    @pl.when(odd == 1)
    def _():
        pltpu.make_async_copy(up.at[1], fields.at[0], sems.at[0]).start()
        pltpu.make_async_copy(down.at[0], fields.at[1], sems.at[1]).start()

    def squares(length, axis):
        counter = lax.broadcasted_iota(jnp.int32, (rows_x, rows_y), axis)
        wrapped = jnp.where(counter >= length // 2, counter - length, counter)
        wave = 2.0 * math.pi / length * wrapped.astype(F32)
        return wave * wave

    lateral = squares(rows_x, 0) + squares(rows_y, 1)
    level_out = 1.0 / (rows_x * rows_y)
    for front in range(fronts):
        kwave = front_wave(freq, front)
        vertical = kwave * kwave - lateral
        travels = vertical > 0.0
        square = jnp.maximum(vertical, 0.0)
        root = jnp.sqrt(jnp.abs(vertical))
        phase[front, 0] = jnp.where(travels, series(square, 0), jnp.exp(-root)) * level_out
        phase[front, 1] = jnp.where(travels, root * series(square, 1), 0.0) * level_out
    for copy in fixed:
        copy.wait()
    sign = jnp.where(odd == 0, 1.0, -1.0).astype(F32)
    for level in range(2):
        refl[level] = sign * refl[level]
    for front in range(fronts):
        cos_row, sin_row = class_rows(slowness, front_wave(freq, front), (8, 128))
        for level in range(2):
            screen[level, front, 0] = look_up(cos_row, klass[level])
            screen[level, front, 1] = look_up(sin_row, klass[level])
    pltpu.make_async_copy(down.at[0], fields.at[0], sems.at[0]).wait()
    pltpu.make_async_copy(down.at[0], fields.at[1], sems.at[1]).wait()
    jobs = [(fields.at[1, front], front, q_out_inner.at[front]) for front in range(fronts)]
    jobs += [(fields.at[0, front], front, q_in_outer.at[front]) for front in range(fronts)]
    spread(jobs, work, hx, hy, phase)
    jobs = leaving(q_out_inner, refl, screen, fields.at[0], second)
    jobs += [(parcel.at[front], front, q_out_outer.at[front]) for front in range(fronts)]
    spread(jobs, work, hx, hy, phase)


def leaving(q_out_inner, refl, screen, field, target):
    fronts = q_out_inner.shape[0]
    kept = 1.0 - refl[0]
    for front in range(fronts):
        b_re, b_im = (q_out_inner[front, part].astype(F32) for part in range(2))
        b_re, b_im = screened(b_re, b_im, screen[0, front, 0], screen[0, front, 1])
        put(field.at[front], kept * b_re, kept * b_im)
    return [(field.at[front], front, target.at[front]) for front in range(fronts)]


def ahead_kernel(
    partner, q_in_outer, screen, refl, phase, hx, hy,
    inward_inner, q_out_inner, last_far, last_near,
    field, third, work,
):
    fronts = partner.shape[0]
    half = partner.shape[2] // 2
    far_bottom = lax.axis_index("shot") % 2 == 0
    spread([(partner.at[front], front, third.at[front]) for front in range(fronts)], work, hx, hy, phase)
    for front in range(fronts):
        in_re, in_im, out_re, out_im = mixed(
            q_in_outer[front, 0], q_in_outer[front, 1], third[front, 0], third[front, 1],
            refl[1], screen[1, front, 0], screen[1, front, 1],
        )
        put(inward_inner.at[front], in_re, in_im)
        put(field.at[front], out_re, out_im)
    spread([(field.at[front], front, q_out_inner.at[front]) for front in range(fronts)], work, hx, hy, phase)
    spread(leaving(q_out_inner, refl, screen, field, third), work, hx, hy, phase)
    for front in range(fronts):
        for part in range(2):
            top, bottom = third[front, part, :half], third[front, part, half:]
            last_far[front, part] = jnp.where(far_bottom, bottom, top)
            last_near[front, part] = jnp.where(far_bottom, top, bottom)


def edge_kernel(
    arrived, source, partner, q_out_inner, q_out_outer, slowness, freq, screen, refl, phase, hx, hy,
    inward_inner, q_arrived, q_out_inner_next, rest_2, rest_3,
    inward, outward, q_partner, q_inward, q_outward, work,
):
    fronts = partner.shape[0]
    everyone = range(fronts)
    first = lax.axis_index("depth") == 0
    for front in everyone:
        put(inward.at[front], *(jnp.where(first, source[front, part], arrived[front, part]) for part in range(2)))
    jobs = [(inward.at[front], front, q_arrived.at[front]) for front in everyone]
    jobs += [(partner.at[front], front, q_partner.at[front]) for front in everyone]
    spread(jobs, work, hx, hy, phase)
    for front in everyone:
        in_re, in_im, out_re, out_im = mixed(
            q_arrived[front, 0], q_arrived[front, 1], q_out_inner[front, 0], q_out_inner[front, 1],
            refl[0], screen[0, front, 0], screen[0, front, 1],
        )
        put(inward.at[front], in_re, in_im)
        put(outward.at[front], out_re, out_im)
    jobs = [(inward.at[front], front, q_inward.at[front]) for front in everyone]
    jobs += [(outward.at[front], front, q_outward.at[front]) for front in everyone]
    spread(jobs, work, hx, hy, phase)
    refl_beyond = arrived[fronts, 0].astype(F32)
    klass = arrived[fronts, 1].astype(F32).astype(jnp.int32)
    for front in everyone:
        in_re, in_im, out_re, out_im = mixed(
            q_inward[front, 0], q_inward[front, 1], q_partner[front, 0], q_partner[front, 1],
            refl[1], screen[1, front, 0], screen[1, front, 1],
        )
        put(inward_inner.at[front], in_re, in_im)
        put(inward.at[front], out_re, out_im)
        cos_row, sin_row = class_rows(slowness, front_wave(freq, front), (8, 128))
        back_re = refl_beyond * look_up(cos_row, klass)
        back_im = refl_beyond * look_up(sin_row, klass)
        for known, target in ((q_out_outer, q_inward), (q_outward, q_partner)):
            known_re, known_im = (known[front, part].astype(F32) for part in range(2))
            put(target.at[front], *screened(known_re, known_im, back_re, back_im))
    jobs = [(inward.at[front], front, q_out_inner_next.at[front]) for front in everyone]
    jobs += [(q_inward.at[front], front, rest_2.at[front]) for front in everyone]
    jobs += [(q_partner.at[front], front, rest_3.at[front]) for front in everyone]
    spread(jobs, work, hx, hy, phase)


def inner_kernel(
    second, rest_2, q_arrived, q_out_inner, partner, screen, refl, phase, hx, hy,
    inward, outward, terms,
    field, q_partner, q_inward, work,
):
    fronts = partner.shape[0]
    everyone = range(fronts)
    first = lax.axis_index("depth") == 0
    for front in everyone:
        a_re, a_im = (
            jnp.where(
                first,
                q_arrived[front, part].astype(F32),
                second[front, part].astype(F32) + rest_2[front, part].astype(F32),
            )
            for part in range(2)
        )
        in_re, in_im, _, _ = mixed(
            a_re, a_im, q_out_inner[front, 0], q_out_inner[front, 1],
            refl[0], screen[0, front, 0], screen[0, front, 1],
        )
        put(field.at[front], in_re, in_im)
    jobs = [(field.at[front], front, q_inward.at[front]) for front in everyone]
    jobs += [(partner.at[front], front, q_partner.at[front]) for front in everyone]
    spread(jobs, work, hx, hy, phase)
    total = None
    for front in everyone:
        a_re, a_im = (q_inward[front, part].astype(F32) for part in range(2))
        b_re, b_im = (q_partner[front, part].astype(F32) for part in range(2))
        in_re, in_im, out_re, out_im = mixed(
            a_re, a_im, b_re, b_im, refl[1], screen[1, front, 0], screen[1, front, 1]
        )
        put(inward.at[front], in_re, in_im)
        put(outward.at[front], out_re, out_im)
        term = a_re * b_re + a_im * b_im
        total = term if total is None else total + term
    terms[...] = total


def outer_rows(near, last, q_arrived, rest, q_out_inner, screen, refl, inward, outward):
    fronts, _, half, _ = last.shape
    first = lax.axis_index("depth") == 0
    shot = lax.axis_index("shot") % 2
    rows = pl.ds(pl.multiple_of((shot if near else 1 - shot) * half, half), half)
    total = None
    for front in range(fronts):
        a_re, a_im = (
            jnp.where(
                first,
                q_arrived[front, part, rows, :].astype(F32),
                last[front, part].astype(F32) + rest[front, part, rows, :].astype(F32),
            )
            for part in range(2)
        )
        b_re, b_im = (q_out_inner[front, part, rows, :].astype(F32) for part in range(2))
        in_re, in_im, out_re, out_im = mixed(
            a_re, a_im, b_re, b_im, refl[0, rows, :], screen[0, front, 0, rows, :], screen[0, front, 1, rows, :]
        )
        put(inward.at[front], in_re, in_im)
        put(outward.at[front], out_re, out_im)
        term = a_re * b_re + a_im * b_im
        total = term if total is None else total + term
    return rows, total


def send_home(level, rows, inward, outward, down_out, up_out, sems):
    odd = odd_place()

    def copies(place, inward_out, outward_out):
        return [
            pltpu.make_async_copy(inward, inward_out.at[place, :, :, rows, :], sems.at[0]),
            pltpu.make_async_copy(outward, outward_out.at[place, :, :, rows, :], sems.at[1]),
        ]

    @pl.when(odd == 0)
    def _():
        for copy in copies(level, down_out, up_out):
            copy.start()

    @pl.when(odd == 1)
    def _():
        for copy in copies(1 - level, up_out, down_out):
            copy.start()

    return copies(0, down_out, up_out)


def far_rows_kernel(
    last, q_arrived, rest, q_out_inner, screen, refl, inner_terms, inner_in, inner_out,
    down_out, up_out, terms,
    inward, outward, sems,
):
    every_row = pl.ds(0, inner_in.shape[2])
    waits = send_home(1, every_row, inner_in, inner_out, down_out, up_out, sems.at[1])
    rows, total = outer_rows(False, last, q_arrived, rest, q_out_inner, screen, refl, inward, outward)
    waits += send_home(0, rows, inward, outward, down_out, up_out, sems.at[0])
    terms[0] = total.astype(BF16)
    terms[1] = inner_terms[rows, :].astype(BF16)
    for copy in waits:
        copy.wait()


def near_rows_kernel(
    scale, last, q_arrived, rest, q_out_inner, screen, refl, inner_terms, other, down_in, up_in,
    down_out, up_out, gradient,
    inward, outward, sums, sems,
):
    del down_in, up_in
    rows, total = outer_rows(True, last, q_arrived, rest, q_out_inner, screen, refl, inward, outward)
    waits = send_home(0, rows, inward, outward, down_out, up_out, sems.at[0])
    odd = odd_place()
    sums[odd] = scale * (total + other[0].astype(F32))
    sums[1 - odd] = scale * (inner_terms[rows, :] + other[1].astype(F32))
    done = pltpu.make_async_copy(sums, gradient, sems.at[1, 0])
    done.start()
    for copy in waits + [done]:
        copy.wait()


def per_device(down_state, up_state, source, reflect, screen_class, screen_values, freq_index):
    depth = lax.axis_size("depth")
    shots = lax.axis_size("shot")
    levels, fronts, parts, rows_x, rows_y = down_state.shape
    if levels != 2 or depth % 2 or shots != 2 or HOPS != 3:
        return per_device_plain(down_state, up_state, source, reflect, screen_class, screen_values, freq_index)
    scale = 1.0 / math.sqrt(fronts * shots)
    half = rows_x // 2
    hx = jnp.asarray(hartley(rows_x))
    hy = jnp.asarray(hartley(rows_y))
    partners = [(i, i ^ 1) for i in range(depth)]
    beyond = [(i, i + 1) for i in range(1, depth - 1, 2)] + [(i + 1, i) for i in range(1, depth - 1, 2)]
    to_partner = functools.partial(lax.ppermute, axis_name="depth", perm=partners)
    to_beyond = functools.partial(lax.ppermute, axis_name="depth", perm=beyond)
    across = functools.partial(lax.ppermute, axis_name="shot", perm=[(0, 1), (1, 0)])
    plane = jax.ShapeDtypeStruct((fronts, parts, rows_x, rows_y), BF16)
    half_plane = jax.ShapeDtypeStruct((fronts, parts, half, rows_y), BF16)
    pair = jax.ShapeDtypeStruct((2, rows_x, rows_y), F32)
    turns = jax.ShapeDtypeStruct((fronts, parts, rows_x, rows_y), F32)
    screens = jax.ShapeDtypeStruct((2, fronts, parts, rows_x, rows_y), F32)
    state = jax.ShapeDtypeStruct(down_state.shape, BF16)
    dma = pltpu.SemaphoreType.DMA

    def call(kernel, in_specs, out_specs, out_shape, scratch=(), **more):
        return pl.pallas_call(
            kernel,
            in_specs=in_specs,
            out_specs=out_specs,
            out_shape=out_shape,
            scratch_shapes=list(scratch),
            compiler_params=PARAMS,
            **more,
        )

    def kept_in_hbm(*arrays):
        return [pltpu.with_memory_space_constraint(array, pltpu.HBM) for array in arrays]

    def buffers(count, shape=plane):
        return [pltpu.VMEM(shape.shape, shape.dtype)] * count

    def work(slots):
        return pltpu.VMEM((slots, *plane.shape[1:]), BF16)

    parcel, in_inner = call(
        edges_kernel,
        [HBM] * 4,
        [VMEM] * 2,
        [jax.ShapeDtypeStruct((fronts + 1, parts, rows_x, rows_y), BF16), plane],
        [pltpu.VMEM((rows_x, rows_y), F32), pltpu.VMEM((rows_x, rows_y), jnp.int32), dma((4,))],
    )(*kept_in_hbm(down_state, up_state, reflect, screen_class))
    arrived = to_beyond(parcel)
    partner_0 = to_partner(in_inner)
    q_out_inner_0, q_in_outer_0, q_out_outer_0, screen, phase, refl, second = call(
        setup_kernel,
        [HBM] * 4 + [SMEM] * 2 + [VMEM] * 3,
        [VMEM] * 7,
        [plane] * 3 + [screens, turns, pair, plane],
        [
            pltpu.VMEM((2, *plane.shape), BF16),
            pltpu.VMEM((2, rows_x, rows_y), jnp.int32),
            work(2 * fronts),
            dma((6,)),
        ],
    )(*kept_in_hbm(down_state, up_state, reflect, screen_class), screen_values, freq_index, parcel, hx, hy)
    second = to_beyond(second)
    in_inner_1, q_out_inner_1, last_far, last_near = call(
        ahead_kernel, [VMEM] * 7, [VMEM] * 4, [plane] * 2 + [half_plane] * 2, buffers(2) + [work(fronts)]
    )(partner_0, q_in_outer_0, screen, refl, phase, hx, hy)
    partner_1 = to_partner(in_inner_1)
    last_far = to_beyond(last_far)
    last_near = to_beyond(last_near)
    in_inner_2, q_arrived, q_out_inner_2, rest_2, rest_3 = call(
        edge_kernel,
        [VMEM] * 5 + [SMEM] * 2 + [VMEM] * 5,
        [VMEM] * 5,
        [plane] * 5,
        buffers(5) + [work(3 * fronts)],
    )(
        arrived, source, partner_1, q_out_inner_0, q_out_outer_0, screen_values, freq_index,
        screen, refl, phase, hx, hy,
    )
    partner_2 = to_partner(in_inner_2)
    inner_in, inner_out, inner_terms = call(
        inner_kernel,
        [VMEM] * 10,
        [VMEM] * 3,
        [plane, plane, jax.ShapeDtypeStruct((rows_x, rows_y), F32)],
        buffers(3) + [work(2 * fronts)],
    )(second, rest_2, q_arrived, q_out_inner_1, partner_2, screen, refl, phase, hx, hy)
    down, up, terms = call(
        far_rows_kernel,
        [VMEM] * 9,
        [HBM] * 2 + [VMEM],
        [state, state, jax.ShapeDtypeStruct((2, half, rows_y), BF16)],
        buffers(2, half_plane) + [dma((2, 2))],
    )(last_far, q_arrived, rest_3, q_out_inner_2, screen, refl, inner_terms, inner_in, inner_out)
    other = across(terms)
    down, up, gradient = call(
        functools.partial(near_rows_kernel, scale),
        [VMEM] * 8 + [HBM] * 2,
        [HBM] * 3,
        [state, state, jax.ShapeDtypeStruct((2, half, rows_y), F32)],
        buffers(2, half_plane) + [pltpu.VMEM((2, half, rows_y), F32), dma((2, 2))],
        input_output_aliases={8: 0, 9: 1},
    )(last_near, q_arrived, rest_3, q_out_inner_2, screen, refl, inner_terms, other, down, up)
    return (down, up, gradient)


def solution(mesh):
    return jax.shard_map(
        per_device,
        mesh=mesh,
        in_specs=(
            P("depth", "shot", None, None, None),
            P("depth", "shot", None, None, None),
            P("shot", None, None, None),
            P("depth", None, None),
            P("depth", None, None),
            P(),
            P("shot"),
        ),
        out_specs=(
            P("depth", "shot", None, None, None),
            P("depth", "shot", None, None, None),
            P("depth", "shot", None),
        ),
        check_vma=False,
    )
```

```python
import functools
import math

import jax
import jax.numpy as jnp
import numpy as np
from jax import lax
from jax.experimental import pallas as pl
from jax.experimental.pallas import tpu as pltpu
from jax.sharding import PartitionSpec as P

HOPS = 3
NCLASS = 16
NFREQ = 128
F32 = jnp.float32
BF16 = jnp.bfloat16
VMEM = pl.BlockSpec(memory_space=pltpu.VMEM)
HBM = pl.BlockSpec(memory_space=pltpu.HBM)
SMEM = pl.BlockSpec(memory_space=pltpu.SMEM)
PARAMS = pltpu.CompilerParams(vmem_limit_bytes=28 * 2**20)


def passed_along(block, axis, distance):
    devices = range(lax.axis_size(axis))
    route = [(i - distance, i) for i in devices if i - distance in devices]
    return lax.ppermute(block, axis, route)


def dft_tables(length):
    counter = jnp.arange(length, dtype=jnp.int32)
    product = counter[:, None] * counter[None, :] % length
    angles = 2.0 * math.pi / length * product.astype(jnp.float32)
    return (jnp.cos(angles).astype(jnp.bfloat16), jnp.sin(angles).astype(jnp.bfloat16))


def wavenumbers(length):
    counter = jnp.arange(length, dtype=jnp.int32)
    wrapped = jnp.where(counter >= length // 2, counter - length, counter)
    return 2.0 * math.pi / length * wrapped.astype(jnp.float32)


def propagate(planes, phase_re, phase_im, tables):
    fwd_left, fwd_right, inv_left, inv_right = tables
    first = jnp.einsum(
        "cdjk,...dkl->...cjl", fwd_left, planes, preferred_element_type=jnp.float32
    ).astype(jnp.bfloat16)
    second = jnp.einsum("...djl,dclm->...cjm", first, fwd_right, preferred_element_type=jnp.float32)
    real_part = second[..., 0, :, :]
    imag_part = second[..., 1, :, :]
    turned = jnp.stack(
        [real_part * phase_re - imag_part * phase_im, real_part * phase_im + imag_part * phase_re],
        axis=-3,
    ).astype(jnp.bfloat16)
    third = jnp.einsum(
        "cdjk,...dkl->...cjl", inv_left, turned, preferred_element_type=jnp.float32
    ).astype(jnp.bfloat16)
    return jnp.einsum(
        "...djl,dclm->...cjm", third, inv_right, preferred_element_type=jnp.float32
    ).astype(jnp.bfloat16)


def trade(down_edge, up_edge):
    got_down = passed_along(down_edge, "depth", 1)
    got_up = passed_along(up_edge, "depth", -1)
    return (got_down, got_up)


def per_device_plain(down_state, up_state, source, reflect, screen_class, screen_values, freq_index):
    levels = down_state.shape[0]
    rows_x = down_state.shape[3]
    rows_y = down_state.shape[4]
    front_count = down_state.shape[1]
    depth_rank = lax.axis_index("depth")
    scale = 1.0 / math.sqrt(front_count * lax.axis_size("shot"))
    cos_x, sin_x = dft_tables(rows_x)
    cos_y, sin_y = dft_tables(rows_y)
    tables = (
        jnp.stack([jnp.stack([cos_x, sin_x]), jnp.stack([-sin_x, cos_x])]),
        jnp.stack([jnp.stack([cos_y, -sin_y]), jnp.stack([sin_y, cos_y])]),
        jnp.stack([jnp.stack([cos_x, -sin_x]), jnp.stack([sin_x, cos_x])]),
        jnp.stack([jnp.stack([cos_y, sin_y]), jnp.stack([-sin_y, cos_y])]),
    )
    kwave = 0.95 * math.pi * (freq_index.astype(jnp.float32) + 1.0) / NFREQ
    kx_wave = wavenumbers(rows_x)
    ky_wave = wavenumbers(rows_y)
    vertical = kwave[:, None, None] ** 2 - kx_wave[None, :, None] ** 2 - ky_wave[None, None, :] ** 2
    propag = jnp.sqrt(jnp.maximum(vertical, 0.0))
    damping = jnp.exp(-jnp.sqrt(jnp.maximum(-vertical, 0.0))) / (rows_x * rows_y)
    phase_re = damping * jnp.cos(propag)
    phase_im = damping * jnp.sin(propag)
    classes = jnp.arange(NCLASS, dtype=jnp.int32)
    onehot = (screen_class[None] == classes[:, None, None, None]).astype(jnp.float32)
    slowness = jnp.einsum("c,clxy->lxy", screen_values, onehot, precision=lax.Precision.HIGHEST)
    angle = kwave[None, :, None, None] * slowness[:, None]
    screen_re = jnp.cos(angle)
    screen_im = jnp.sin(angle)
    refl = reflect[:, None]
    top_slab = depth_rank == 0
    down = down_state
    up = up_state
    a_re = a_im = b_re = b_im = None
    for repeat in range(HOPS):
        down_edge = down[levels - 1]
        up_edge = up[0]
        got_down, got_up = trade(down_edge, up_edge)
        got_down = jnp.where(top_slab, source, got_down)
        moved = propagate(
            jnp.concatenate([got_down[None], down[: levels - 1], up[1:], got_up[None]], axis=0),
            phase_re,
            phase_im,
            tables,
        )
        from_above = moved[:levels]
        from_below = moved[levels:]
        qa_re = from_above[:, :, 0].astype(jnp.float32)
        qa_im = from_above[:, :, 1].astype(jnp.float32)
        qb_re = from_below[:, :, 0].astype(jnp.float32)
        qb_im = from_below[:, :, 1].astype(jnp.float32)
        a_re = screen_re * qa_re - screen_im * qa_im
        a_im = screen_re * qa_im + screen_im * qa_re
        b_re = screen_re * qb_re - screen_im * qb_im
        b_im = screen_re * qb_im + screen_im * qb_re
        down = jnp.stack(
            [(1.0 + refl) * a_re - refl * b_re, (1.0 + refl) * a_im - refl * b_im], axis=2
        ).astype(jnp.bfloat16)
        up = jnp.stack(
            [(1.0 - refl) * b_re + refl * a_re, (1.0 - refl) * b_im + refl * a_im], axis=2
        ).astype(jnp.bfloat16)
    terms = scale * jnp.sum(a_re * b_re + a_im * b_im, axis=1)
    gradient = lax.psum_scatter(
        terms.astype(jnp.bfloat16), "shot", scatter_dimension=1, tiled=True
    ).astype(jnp.float32)
    return (down, up, gradient)


def hartley(length):
    counter = np.arange(length)
    angles = 2.0 * np.pi / length * (counter[:, None] * counter[None, :] % length)
    cosine = np.cos(angles).astype(BF16).astype(np.float32)
    sine = np.sin(angles).astype(BF16).astype(np.float32)
    return (cosine + sine).astype(BF16)


def odd_place():
    return lax.rem(lax.axis_index("depth"), 2)


def mm(left, right):
    return jnp.dot(left, right, preferred_element_type=F32)


def spread(jobs, work, hx, hy, phase):
    jobs = list(enumerate(jobs))
    for slot, (plane, _, _) in jobs:
        for part in range(2):
            work[slot, part] = mm(plane[part], hy[...]).astype(BF16)
    for slot, (_, front, _) in jobs:
        turn_re, turn_im = phase[front, 0], phase[front, 1]
        part_re = mm(hx[...], work[slot, 0])
        part_im = mm(hx[...], work[slot, 1])
        work[slot, 0] = (part_re * turn_re - part_im * turn_im).astype(BF16)
        work[slot, 1] = (part_re * turn_im + part_im * turn_re).astype(BF16)
    for slot, _ in jobs:
        for part in range(2):
            work[slot, part] = mm(hx[...], work[slot, part]).astype(BF16)
    for slot, (_, _, target) in jobs:
        for part in range(2):
            target[part] = mm(work[slot, part], hy[...]).astype(BF16)


def screened(real_part, imag_part, screen_re, screen_im):
    return (
        screen_re * real_part - screen_im * imag_part,
        screen_re * imag_part + screen_im * real_part,
    )


def mixed(a_re, a_im, b_re, b_im, refl, screen_re, screen_im):
    a_re, a_im, b_re, b_im = (part.astype(F32) for part in (a_re, a_im, b_re, b_im))
    step_re = refl * (a_re - b_re)
    step_im = refl * (a_im - b_im)
    inward = screened(a_re + step_re, a_im + step_im, screen_re, screen_im)
    outward = screened(b_re + step_re, b_im + step_im, screen_re, screen_im)
    return tuple(part.astype(BF16) for part in inward + outward)


def put(target, real_part, imag_part):
    target[0] = real_part.astype(BF16)
    target[1] = imag_part.astype(BF16)


def half_rows(of, half):
    shot = lax.rem(lax.axis_index("shot"), 2)
    return pl.ds(pl.multiple_of((shot if of == 0 else 1 - shot) * half, half), half)


def joined(mine, other):
    shot = lax.rem(lax.axis_index("shot"), 2)
    return jnp.concatenate([jnp.where(shot == 0, mine, other), jnp.where(shot == 0, other, mine)], axis=0)


def edges_kernel(down, up, reflect, classes_in, parcel, inward_inner, refl, klass, sems):
    levels = down.shape[0]
    fronts = inward_inner.shape[0]
    half = refl.shape[0]
    odd = odd_place()
    rows = half_rows(0, half)

    def fetch(first, second):
        for front in range(fronts):
            pltpu.make_async_copy(first.at[front], parcel.at[pl.ds(2 * front, 2)], sems.at[0]).start()
        pltpu.make_async_copy(second, inward_inner, sems.at[1]).start()

    fixed = [
        pltpu.make_async_copy(reflect.at[odd, rows], refl, sems.at[2]),
        pltpu.make_async_copy(classes_in.at[odd, rows], klass, sems.at[3]),
    ]
    for copy in fixed:
        copy.start()

    @pl.when(odd == 0)
    def _():
        fetch(up.at[0], down.at[levels - 1])

    @pl.when(odd == 1)
    def _():
        fetch(down.at[levels - 1], up.at[0])

    for copy in fixed:
        copy.wait()
    parcel[2 * fronts, :half] = (jnp.where(odd == 0, 1.0, -1.0).astype(F32) * refl[...]).astype(BF16)
    parcel[2 * fronts, half:] = klass[...].astype(BF16)
    for front in range(fronts):
        pltpu.make_async_copy(up.at[0, front], parcel.at[pl.ds(2 * front, 2)], sems.at[0]).wait()
    pltpu.make_async_copy(up.at[0], inward_inner, sems.at[1]).wait()


def class_rows(slowness, kwave, shape):
    lanes = lax.broadcasted_iota(jnp.int32, shape, 1)
    table = jnp.zeros(shape, F32)
    for entry in range(NCLASS):
        table = jnp.where(lanes == entry, slowness[entry], table)
    angle = kwave * table
    return jnp.cos(angle), jnp.sin(angle)


def look_up(table, classes):
    width = 128
    rows = classes.shape[0]
    wide = jnp.broadcast_to(table[:1], (rows, width))
    pieces = [
        jnp.take_along_axis(wide, classes[:, start : start + width], axis=1, mode="promise_in_bounds")
        for start in range(0, classes.shape[1], width)
    ]
    return jnp.concatenate(pieces, axis=1)


def front_wave(freq, front):
    return 0.95 * math.pi * (freq[front].astype(F32) + 1.0) / NFREQ


def series(square, shift):
    total = jnp.full_like(square, 1.0 / math.factorial(18 + shift))
    for order in range(16, -1, -2):
        total = 1.0 / math.factorial(order + shift) - square * total
    return total


def setup_kernel(
    down, up, reflect, classes_in, slowness, freq, hx, hy,
    q_out_inner, q_in_outer, screen, phase, refl,
    fields, klass, work, sems,
):
    fronts = q_out_inner.shape[0]
    rows_x, rows_y = refl.shape[1:]
    odd = odd_place()
    fixed = [
        pltpu.make_async_copy(reflect.at[odd], refl.at[0], sems.at[2]),
        pltpu.make_async_copy(reflect.at[1 - odd], refl.at[1], sems.at[3]),
        pltpu.make_async_copy(classes_in.at[odd], klass.at[0], sems.at[4]),
        pltpu.make_async_copy(classes_in.at[1 - odd], klass.at[1], sems.at[5]),
    ]
    for copy in fixed:
        copy.start()

    @pl.when(odd == 0)
    def _():
        pltpu.make_async_copy(down.at[0], fields.at[0], sems.at[0]).start()
        pltpu.make_async_copy(up.at[1], fields.at[1], sems.at[1]).start()

    @pl.when(odd == 1)
    def _():
        pltpu.make_async_copy(up.at[1], fields.at[0], sems.at[0]).start()
        pltpu.make_async_copy(down.at[0], fields.at[1], sems.at[1]).start()

    def squares(length, axis):
        counter = lax.broadcasted_iota(jnp.int32, (rows_x, rows_y), axis)
        wrapped = jnp.where(counter >= length // 2, counter - length, counter)
        wave = 2.0 * math.pi / length * wrapped.astype(F32)
        return wave * wave

    lateral = squares(rows_x, 0) + squares(rows_y, 1)
    level_out = 1.0 / (rows_x * rows_y)
    for front in range(fronts):
        kwave = front_wave(freq, front)
        vertical = kwave * kwave - lateral
        travels = vertical > 0.0
        square = jnp.maximum(vertical, 0.0)
        root = jnp.sqrt(jnp.abs(vertical))
        phase[front, 0] = jnp.where(travels, series(square, 0), jnp.exp(-root)) * level_out
        phase[front, 1] = jnp.where(travels, root * series(square, 1), 0.0) * level_out
    for copy in fixed:
        copy.wait()
    sign = jnp.where(odd == 0, 1.0, -1.0).astype(F32)
    for level in range(2):
        refl[level] = sign * refl[level]
    for front in range(fronts):
        cos_row, sin_row = class_rows(slowness, front_wave(freq, front), (8, 128))
        for level in range(2):
            screen[level, front, 0] = look_up(cos_row, klass[level])
            screen[level, front, 1] = look_up(sin_row, klass[level])
    pltpu.make_async_copy(down.at[0], fields.at[0], sems.at[0]).wait()
    pltpu.make_async_copy(down.at[0], fields.at[1], sems.at[1]).wait()
    jobs = [(fields.at[1, front], front, q_out_inner.at[front]) for front in range(fronts)]
    jobs += [(fields.at[0, front], front, q_in_outer.at[front]) for front in range(fronts)]
    spread(jobs, work, hx, hy, phase)


def leaving(q_out_inner, refl, screen, field, target):
    fronts = q_out_inner.shape[0]
    kept = 1.0 - refl[0]
    for front in range(fronts):
        b_re, b_im = (q_out_inner[front, part].astype(F32) for part in range(2))
        b_re, b_im = screened(b_re, b_im, screen[0, front, 0], screen[0, front, 1])
        put(field.at[front], kept * b_re, kept * b_im)
    return [(field.at[front], front, target.at[front]) for front in range(fronts)]


def ahead_kernel(
    partner, parcel, q_in_outer, q_out_inner, screen, refl, phase, hx, hy,
    inward_inner, q_out_inner_next, q_out_outer, second, last,
    field, other_field, q_field, work,
):
    fronts, _, rows_x, _ = partner.shape
    everyone = range(fronts)
    half = rows_x // 2
    far_bottom = lax.rem(lax.axis_index("shot"), 2) == 0
    jobs = leaving(q_out_inner, refl, screen, field, second.at[:, :, pl.ds(0, rows_x)])
    jobs += [(partner.at[front], front, q_field.at[front]) for front in everyone]
    spread(jobs, work, hx, hy, phase)
    for front in everyone:
        in_re, in_im, out_re, out_im = mixed(
            q_in_outer[front, 0], q_in_outer[front, 1], q_field[front, 0], q_field[front, 1],
            refl[1], screen[1, front, 0], screen[1, front, 1],
        )
        put(inward_inner.at[front], in_re, in_im)
        put(other_field.at[front], out_re, out_im)
    jobs = [(other_field.at[front], front, q_out_inner_next.at[front]) for front in everyone]
    jobs += [(parcel.at[pl.ds(2 * front, 2)], front, q_out_outer.at[front]) for front in everyone]
    spread(jobs, work, hx, hy, phase)
    spread(leaving(q_out_inner_next, refl, screen, field, q_field), work, hx, hy, phase)
    for front in everyone:
        for part in range(2):
            top, bottom = q_field[front, part, :half], q_field[front, part, half:]
            second[front, part, rows_x:] = jnp.where(far_bottom, bottom, top)
            last[front, part] = jnp.where(far_bottom, top, bottom)


def edge_kernel(
    arrived, source, partner, q_out_inner, screen, refl, phase, hx, hy,
    inward_inner, out_inner, q_arrived, q_out_outer,
    inward, outward, q_partner, q_inward, work,
):
    fronts = partner.shape[0]
    everyone = range(fronts)
    first = lax.axis_index("depth") == 0
    for front in everyone:
        put(inward.at[front], *(jnp.where(first, source[front, part], arrived[2 * front + part]) for part in range(2)))
    jobs = [(inward.at[front], front, q_arrived.at[front]) for front in everyone]
    jobs += [(partner.at[front], front, q_partner.at[front]) for front in everyone]
    spread(jobs, work, hx, hy, phase)
    for front in everyone:
        in_re, in_im, out_re, out_im = mixed(
            q_arrived[front, 0], q_arrived[front, 1], q_out_inner[front, 0], q_out_inner[front, 1],
            refl[0], screen[0, front, 0], screen[0, front, 1],
        )
        put(inward.at[front], in_re, in_im)
        put(outward.at[front], out_re, out_im)
    jobs = [(inward.at[front], front, q_inward.at[front]) for front in everyone]
    jobs += [(outward.at[front], front, q_out_outer.at[front]) for front in everyone]
    spread(jobs, work, hx, hy, phase)
    for front in everyone:
        in_re, in_im, out_re, out_im = mixed(
            q_inward[front, 0], q_inward[front, 1], q_partner[front, 0], q_partner[front, 1],
            refl[1], screen[1, front, 0], screen[1, front, 1],
        )
        put(inward_inner.at[front], in_re, in_im)
        put(out_inner.at[front], out_re, out_im)


def beyond_kernel(
    mine, other, out_inner, q_out_outer_0, q_out_outer_1, slowness, freq, phase, hx, hy,
    q_out_inner, rest_2, rest_3,
    field_2, field_3, work,
):
    fronts = out_inner.shape[0]
    everyone = range(fronts)
    half = mine.shape[0] // 2
    refl_beyond = joined(mine[:half], other[:half]).astype(F32)
    klass = joined(mine[half:], other[half:]).astype(F32).astype(jnp.int32)
    for front in everyone:
        cos_row, sin_row = class_rows(slowness, front_wave(freq, front), (8, 128))
        back_re = refl_beyond * look_up(cos_row, klass)
        back_im = refl_beyond * look_up(sin_row, klass)
        for known, target in ((q_out_outer_0, field_2), (q_out_outer_1, field_3)):
            known_re, known_im = (known[front, part].astype(F32) for part in range(2))
            put(target.at[front], *screened(known_re, known_im, back_re, back_im))
    jobs = [(out_inner.at[front], front, q_out_inner.at[front]) for front in everyone]
    jobs += [(field_2.at[front], front, rest_2.at[front]) for front in everyone]
    jobs += [(field_3.at[front], front, rest_3.at[front]) for front in everyone]
    spread(jobs, work, hx, hy, phase)


def partner_kernel(partner, phase, hx, hy, q_partner, work):
    fronts = partner.shape[0]
    spread([(partner.at[front], front, q_partner.at[front]) for front in range(fronts)], work, hx, hy, phase)


def inner_kernel(
    second, rest_2, rest_3, q_arrived, q_out_inner_1, q_out_inner_2, q_partner, screen, refl, phase, hx, hy,
    inward, outward, far_inward, far_outward, terms, inner_terms,
    field, q_inward, work,
):
    fronts, _, rows_x, _ = q_partner.shape
    everyone = range(fronts)
    first = lax.axis_index("depth") == 0
    for front in everyone:
        a_re, a_im = (
            jnp.where(
                first,
                q_arrived[front, part].astype(F32),
                second[front, part, :rows_x].astype(F32) + rest_2[front, part].astype(F32),
            )
            for part in range(2)
        )
        in_re, in_im, _, _ = mixed(
            a_re, a_im, q_out_inner_1[front, 0], q_out_inner_1[front, 1],
            refl[0], screen[0, front, 0], screen[0, front, 1],
        )
        put(field.at[front], in_re, in_im)
    spread([(field.at[front], front, q_inward.at[front]) for front in everyone], work, hx, hy, phase)
    rows, total = outer_rows(
        1, second.at[:, :, pl.ds(rows_x, rows_x // 2)], q_arrived, rest_3, q_out_inner_2, screen, refl,
        far_inward, far_outward,
    )
    terms[0] = total.astype(BF16)
    total = None
    for front in everyone:
        a_re, a_im = (q_inward[front, part].astype(F32) for part in range(2))
        b_re, b_im = (q_partner[front, part].astype(F32) for part in range(2))
        in_re, in_im, out_re, out_im = mixed(
            a_re, a_im, b_re, b_im, refl[1], screen[1, front, 0], screen[1, front, 1]
        )
        put(inward.at[front], in_re, in_im)
        put(outward.at[front], out_re, out_im)
        term = a_re * b_re + a_im * b_im
        total = term if total is None else total + term
    inner_terms[...] = total
    terms[1] = inner_terms[rows, :].astype(BF16)


def outer_rows(of, last, q_arrived, rest, q_out_inner, screen, refl, inward, outward, ready=None):
    fronts, _, half, _ = last.shape
    first = lax.axis_index("depth") == 0
    rows = half_rows(of, half)
    total = None
    for front in range(fronts):
        a_re, a_im = (
            jnp.where(
                first,
                q_arrived[front, part, rows, :].astype(F32),
                last[front, part].astype(F32) + rest[front, part, rows, :].astype(F32),
            )
            for part in range(2)
        )
        b_re, b_im = (q_out_inner[front, part, rows, :].astype(F32) for part in range(2))
        in_re, in_im, out_re, out_im = mixed(
            a_re, a_im, b_re, b_im, refl[0, rows, :], screen[0, front, 0, rows, :], screen[0, front, 1, rows, :]
        )
        put(inward.at[front], in_re, in_im)
        put(outward.at[front], out_re, out_im)
        term = a_re * b_re + a_im * b_im
        total = term if total is None else total + term
    return rows, total


def send_home(level, rows, inward, outward, down_out, up_out, sems):
    odd = odd_place()

    def copies(place, inward_out, outward_out):
        return [
            pltpu.make_async_copy(inward, inward_out.at[place, :, :, rows, :], sems.at[0]),
            pltpu.make_async_copy(outward, outward_out.at[place, :, :, rows, :], sems.at[1]),
        ]

    @pl.when(odd == 0)
    def _():
        for copy in copies(level, down_out, up_out):
            copy.start()

    @pl.when(odd == 1)
    def _():
        for copy in copies(1 - level, up_out, down_out):
            copy.start()

    return copies(0, down_out, up_out)


def home_kernel(inward, outward, far_inward, far_outward, down_out, up_out, sems):
    rows_x, half = inward.shape[2], far_inward.shape[2]
    waits = send_home(1, pl.ds(0, rows_x), inward, outward, down_out, up_out, sems.at[0])
    waits += send_home(0, half_rows(1, half), far_inward, far_outward, down_out, up_out, sems.at[1])
    for copy in waits:
        copy.wait()


def near_rows_kernel(
    scale, last, q_arrived, rest, q_out_inner, screen, refl, inner_terms, other, down_in, up_in,
    down_out, up_out, gradient,
    inward, outward, sums, sems,
):
    del down_in, up_in
    rows, total = outer_rows(0, last, q_arrived, rest, q_out_inner, screen, refl, inward, outward)
    waits = send_home(0, rows, inward, outward, down_out, up_out, sems.at[0])
    odd = odd_place()
    sums[odd] = scale * (total + other[0].astype(F32))
    sums[1 - odd] = scale * (inner_terms[rows, :] + other[1].astype(F32))
    done = pltpu.make_async_copy(sums, gradient, sems.at[1, 0])
    done.start()
    for copy in waits + [done]:
        copy.wait()


def per_device(down_state, up_state, source, reflect, screen_class, screen_values, freq_index):
    depth = lax.axis_size("depth")
    shots = lax.axis_size("shot")
    levels, fronts, parts, rows_x, rows_y = down_state.shape
    if levels != 2 or depth % 2 or shots % 2 or HOPS != 3:
        return per_device_plain(down_state, up_state, source, reflect, screen_class, screen_values, freq_index)
    scale = 1.0 / math.sqrt(fronts * shots)
    half = rows_x // 2
    hx = jnp.asarray(hartley(rows_x))
    hy = jnp.asarray(hartley(rows_y))
    partners = [(i, i ^ 1) for i in range(depth)]
    beyond = [(i, i + 1) for i in range(1, depth - 1, 2)] + [(i + 1, i) for i in range(1, depth - 1, 2)]
    to_partner = functools.partial(lax.ppermute, axis_name="depth", perm=partners)
    to_beyond = functools.partial(lax.ppermute, axis_name="depth", perm=beyond)
    across = functools.partial(lax.ppermute, axis_name="shot", perm=[(i, i ^ 1) for i in range(shots)])
    plane = jax.ShapeDtypeStruct((fronts, parts, rows_x, rows_y), BF16)
    half_plane = jax.ShapeDtypeStruct((fronts, parts, half, rows_y), BF16)
    pair = jax.ShapeDtypeStruct((2, rows_x, rows_y), F32)
    turns = jax.ShapeDtypeStruct((fronts, parts, rows_x, rows_y), F32)
    screens = jax.ShapeDtypeStruct((2, fronts, parts, rows_x, rows_y), F32)
    state = jax.ShapeDtypeStruct(down_state.shape, BF16)
    dma = pltpu.SemaphoreType.DMA

    def call(kernel, in_specs, out_specs, out_shape, scratch=(), **more):
        return pl.pallas_call(
            kernel,
            in_specs=in_specs,
            out_specs=out_specs,
            out_shape=out_shape,
            scratch_shapes=list(scratch),
            compiler_params=PARAMS,
            **more,
        )

    def kept_in_hbm(*arrays):
        return [pltpu.with_memory_space_constraint(array, pltpu.HBM) for array in arrays]

    def buffers(count, shape=plane):
        return [pltpu.VMEM(shape.shape, shape.dtype)] * count

    def work(slots):
        return pltpu.VMEM((slots, *plane.shape[1:]), BF16)

    parcel, in_inner = call(
        edges_kernel,
        [HBM] * 4,
        [VMEM] * 2,
        [jax.ShapeDtypeStruct((fronts * parts + 1, rows_x, rows_y), BF16), plane],
        [pltpu.VMEM((half, rows_y), F32), pltpu.VMEM((half, rows_y), jnp.int32), dma((4,))],
    )(*kept_in_hbm(down_state, up_state, reflect, screen_class))
    arrived = to_beyond(parcel)
    partner_0 = to_partner(in_inner)
    q_out_inner_0, q_in_outer_0, screen, phase, refl = call(
        setup_kernel,
        [HBM] * 4 + [SMEM] * 2 + [VMEM] * 2,
        [VMEM] * 5,
        [plane] * 2 + [screens, turns, pair],
        [
            pltpu.VMEM((2, *plane.shape), BF16),
            pltpu.VMEM((2, rows_x, rows_y), jnp.int32),
            work(2 * fronts),
            dma((6,)),
        ],
    )(*kept_in_hbm(down_state, up_state, reflect, screen_class), screen_values, freq_index, hx, hy)
    in_inner_1, q_out_inner_1, q_out_outer_0, second, last = call(
        ahead_kernel,
        [VMEM] * 9,
        [VMEM] * 5,
        [plane] * 3 + [jax.ShapeDtypeStruct((fronts, parts, rows_x + half, rows_y), BF16), half_plane],
        buffers(3) + [work(2 * fronts)],
    )(partner_0, parcel, q_in_outer_0, q_out_inner_0, screen, refl, phase, hx, hy)
    partner_1 = to_partner(in_inner_1)
    second = to_beyond(second)
    last = to_beyond(last)
    mine = arrived[fronts * parts]
    swapped = across(mine)
    in_inner_2, out_inner_2, q_arrived, q_out_outer_1 = call(
        edge_kernel, [VMEM] * 9, [VMEM] * 4, [plane] * 4, buffers(4) + [work(2 * fronts)]
    )(arrived, source, partner_1, q_out_inner_0, screen, refl, phase, hx, hy)
    partner_2 = to_partner(in_inner_2)
    q_out_inner_2, rest_2, rest_3 = call(
        beyond_kernel,
        [VMEM] * 5 + [SMEM] * 2 + [VMEM] * 3,
        [VMEM] * 3,
        [plane] * 3,
        buffers(2) + [work(3 * fronts)],
    )(mine, swapped, out_inner_2, q_out_outer_0, q_out_outer_1, screen_values, freq_index, phase, hx, hy)
    q_partner = call(partner_kernel, [VMEM] * 4, VMEM, plane, [work(fronts)])(partner_2, phase, hx, hy)
    inner_in, inner_out, far_in, far_out, terms, inner_terms = call(
        inner_kernel,
        [VMEM] * 12,
        [VMEM] * 6,
        [plane] * 2
        + [half_plane] * 2
        + [jax.ShapeDtypeStruct((2, half, rows_y), BF16), jax.ShapeDtypeStruct((rows_x, rows_y), F32)],
        buffers(2) + [work(fronts)],
    )(
        second, rest_2, rest_3, q_arrived, q_out_inner_1, q_out_inner_2, q_partner, screen, refl, phase, hx, hy
    )
    other = across(terms) if shots == 2 else jnp.zeros_like(terms)
    down, up = call(home_kernel, [VMEM] * 4, [HBM] * 2, [state] * 2, [dma((2, 2))])(
        inner_in, inner_out, far_in, far_out
    )
    down, up, gradient = call(
        functools.partial(near_rows_kernel, scale),
        [VMEM] * 8 + [HBM] * 2,
        [HBM] * 3,
        [state, state, jax.ShapeDtypeStruct((2, half, rows_y), F32)],
        buffers(2, half_plane) + [pltpu.VMEM((2, half, rows_y), F32), dma((2, 2))],
        input_output_aliases={8: 0, 9: 1},
    )(last, q_arrived, rest_3, q_out_inner_2, screen, refl, inner_terms, other, down, up)
    if shots != 2:
        terms = scale * terms.astype(F32)
        far = jnp.where(odd_place() == 0, terms, terms[::-1])
        top = lax.rem(lax.axis_index("shot"), 2) == 0
        whole = jnp.concatenate([jnp.where(top, gradient, far), jnp.where(top, far, gradient)], axis=1)
        gradient = lax.psum_scatter(whole.astype(BF16), "shot", scatter_dimension=1, tiled=True).astype(F32)
    return (down, up, gradient)


def solution(mesh):
    return jax.shard_map(
        per_device,
        mesh=mesh,
        in_specs=(
            P("depth", "shot", None, None, None),
            P("depth", "shot", None, None, None),
            P("shot", None, None, None),
            P("depth", None, None),
            P("depth", None, None),
            P(),
            P("shot"),
        ),
        out_specs=(
            P("depth", "shot", None, None, None),
            P("depth", "shot", None, None, None),
            P("depth", "shot", None),
        ),
        check_vma=False,
    )
```

```python
import functools
import math

import jax
import jax.numpy as jnp
import numpy as np
from jax import lax
from jax.experimental import pallas as pl
from jax.experimental.pallas import tpu as pltpu
from jax.sharding import PartitionSpec as P

HOPS = 3
NCLASS = 16
NFREQ = 128
F32 = jnp.float32
BF16 = jnp.bfloat16
VMEM = pl.BlockSpec(memory_space=pltpu.VMEM)
HBM = pl.BlockSpec(memory_space=pltpu.HBM)
SMEM = pl.BlockSpec(memory_space=pltpu.SMEM)
PARAMS = pltpu.CompilerParams(vmem_limit_bytes=28 * 2**20)


def passed_along(block, axis, distance):
    devices = range(lax.axis_size(axis))
    route = [(i - distance, i) for i in devices if i - distance in devices]
    return lax.ppermute(block, axis, route)


def dft_tables(length):
    counter = jnp.arange(length, dtype=jnp.int32)
    product = counter[:, None] * counter[None, :] % length
    angles = 2.0 * math.pi / length * product.astype(jnp.float32)
    return (jnp.cos(angles).astype(jnp.bfloat16), jnp.sin(angles).astype(jnp.bfloat16))


def wavenumbers(length):
    counter = jnp.arange(length, dtype=jnp.int32)
    wrapped = jnp.where(counter >= length // 2, counter - length, counter)
    return 2.0 * math.pi / length * wrapped.astype(jnp.float32)


def propagate(planes, phase_re, phase_im, tables):
    fwd_left, fwd_right, inv_left, inv_right = tables
    first = jnp.einsum(
        "cdjk,...dkl->...cjl", fwd_left, planes, preferred_element_type=jnp.float32
    ).astype(jnp.bfloat16)
    second = jnp.einsum("...djl,dclm->...cjm", first, fwd_right, preferred_element_type=jnp.float32)
    real_part = second[..., 0, :, :]
    imag_part = second[..., 1, :, :]
    turned = jnp.stack(
        [real_part * phase_re - imag_part * phase_im, real_part * phase_im + imag_part * phase_re],
        axis=-3,
    ).astype(jnp.bfloat16)
    third = jnp.einsum(
        "cdjk,...dkl->...cjl", inv_left, turned, preferred_element_type=jnp.float32
    ).astype(jnp.bfloat16)
    return jnp.einsum(
        "...djl,dclm->...cjm", third, inv_right, preferred_element_type=jnp.float32
    ).astype(jnp.bfloat16)


def trade(down_edge, up_edge):
    got_down = passed_along(down_edge, "depth", 1)
    got_up = passed_along(up_edge, "depth", -1)
    return (got_down, got_up)


def per_device_plain(down_state, up_state, source, reflect, screen_class, screen_values, freq_index):
    levels = down_state.shape[0]
    rows_x = down_state.shape[3]
    rows_y = down_state.shape[4]
    front_count = down_state.shape[1]
    depth_rank = lax.axis_index("depth")
    scale = 1.0 / math.sqrt(front_count * lax.axis_size("shot"))
    cos_x, sin_x = dft_tables(rows_x)
    cos_y, sin_y = dft_tables(rows_y)
    tables = (
        jnp.stack([jnp.stack([cos_x, sin_x]), jnp.stack([-sin_x, cos_x])]),
        jnp.stack([jnp.stack([cos_y, -sin_y]), jnp.stack([sin_y, cos_y])]),
        jnp.stack([jnp.stack([cos_x, -sin_x]), jnp.stack([sin_x, cos_x])]),
        jnp.stack([jnp.stack([cos_y, sin_y]), jnp.stack([-sin_y, cos_y])]),
    )
    kwave = 0.95 * math.pi * (freq_index.astype(jnp.float32) + 1.0) / NFREQ
    kx_wave = wavenumbers(rows_x)
    ky_wave = wavenumbers(rows_y)
    vertical = kwave[:, None, None] ** 2 - kx_wave[None, :, None] ** 2 - ky_wave[None, None, :] ** 2
    propag = jnp.sqrt(jnp.maximum(vertical, 0.0))
    damping = jnp.exp(-jnp.sqrt(jnp.maximum(-vertical, 0.0))) / (rows_x * rows_y)
    phase_re = damping * jnp.cos(propag)
    phase_im = damping * jnp.sin(propag)
    classes = jnp.arange(NCLASS, dtype=jnp.int32)
    onehot = (screen_class[None] == classes[:, None, None, None]).astype(jnp.float32)
    slowness = jnp.einsum("c,clxy->lxy", screen_values, onehot, precision=lax.Precision.HIGHEST)
    angle = kwave[None, :, None, None] * slowness[:, None]
    screen_re = jnp.cos(angle)
    screen_im = jnp.sin(angle)
    refl = reflect[:, None]
    top_slab = depth_rank == 0
    down = down_state
    up = up_state
    a_re = a_im = b_re = b_im = None
    for repeat in range(HOPS):
        down_edge = down[levels - 1]
        up_edge = up[0]
        got_down, got_up = trade(down_edge, up_edge)
        got_down = jnp.where(top_slab, source, got_down)
        moved = propagate(
            jnp.concatenate([got_down[None], down[: levels - 1], up[1:], got_up[None]], axis=0),
            phase_re,
            phase_im,
            tables,
        )
        from_above = moved[:levels]
        from_below = moved[levels:]
        qa_re = from_above[:, :, 0].astype(jnp.float32)
        qa_im = from_above[:, :, 1].astype(jnp.float32)
        qb_re = from_below[:, :, 0].astype(jnp.float32)
        qb_im = from_below[:, :, 1].astype(jnp.float32)
        a_re = screen_re * qa_re - screen_im * qa_im
        a_im = screen_re * qa_im + screen_im * qa_re
        b_re = screen_re * qb_re - screen_im * qb_im
        b_im = screen_re * qb_im + screen_im * qb_re
        down = jnp.stack(
            [(1.0 + refl) * a_re - refl * b_re, (1.0 + refl) * a_im - refl * b_im], axis=2
        ).astype(jnp.bfloat16)
        up = jnp.stack(
            [(1.0 - refl) * b_re + refl * a_re, (1.0 - refl) * b_im + refl * a_im], axis=2
        ).astype(jnp.bfloat16)
    terms = scale * jnp.sum(a_re * b_re + a_im * b_im, axis=1)
    gradient = lax.psum_scatter(
        terms.astype(jnp.bfloat16), "shot", scatter_dimension=1, tiled=True
    ).astype(jnp.float32)
    return (down, up, gradient)


def hartley(length):
    counter = np.arange(length)
    angles = 2.0 * np.pi / length * (counter[:, None] * counter[None, :] % length)
    cosine = np.cos(angles).astype(BF16).astype(np.float32)
    sine = np.sin(angles).astype(BF16).astype(np.float32)
    return (cosine + sine).astype(BF16)


def odd_place():
    return lax.rem(lax.axis_index("depth"), 2)


def mm(left, right):
    return jnp.dot(left, right, preferred_element_type=F32)


def spread(jobs, work, hx, hy, phase):
    jobs = list(enumerate(jobs))
    for slot, (plane, _, _) in jobs:
        for part in range(2):
            work[slot, part] = mm(plane[part], hy[...]).astype(BF16)
    for slot, (_, front, _) in jobs:
        turn_re, turn_im = phase[front, 0], phase[front, 1]
        part_re = mm(hx[...], work[slot, 0])
        part_im = mm(hx[...], work[slot, 1])
        work[slot, 0] = (part_re * turn_re - part_im * turn_im).astype(BF16)
        work[slot, 1] = (part_re * turn_im + part_im * turn_re).astype(BF16)
    for slot, _ in jobs:
        for part in range(2):
            work[slot, part] = mm(hx[...], work[slot, part]).astype(BF16)
    for slot, (_, _, target) in jobs:
        for part in range(2):
            target[part] = mm(work[slot, part], hy[...]).astype(BF16)


def screened(real_part, imag_part, screen_re, screen_im):
    return (
        screen_re * real_part - screen_im * imag_part,
        screen_re * imag_part + screen_im * real_part,
    )


def mixed(a_re, a_im, b_re, b_im, refl, screen_re, screen_im):
    a_re, a_im, b_re, b_im = (part.astype(F32) for part in (a_re, a_im, b_re, b_im))
    step_re = refl * (a_re - b_re)
    step_im = refl * (a_im - b_im)
    inward = screened(a_re + step_re, a_im + step_im, screen_re, screen_im)
    outward = screened(b_re + step_re, b_im + step_im, screen_re, screen_im)
    return tuple(part.astype(BF16) for part in inward + outward)


def put(target, real_part, imag_part):
    target[0] = real_part.astype(BF16)
    target[1] = imag_part.astype(BF16)


def half_rows(of, half):
    shot = lax.rem(lax.axis_index("shot"), 2)
    return pl.ds(pl.multiple_of((shot if of == 0 else 1 - shot) * half, half), half)


def joined(mine, other):
    shot = lax.rem(lax.axis_index("shot"), 2)
    return jnp.concatenate([jnp.where(shot == 0, mine, other), jnp.where(shot == 0, other, mine)], axis=0)


def edges_kernel(down, up, reflect, classes_in, parcel, inward_inner, refl, klass, sems):
    levels = down.shape[0]
    fronts = inward_inner.shape[0]
    half = refl.shape[0]
    odd = odd_place()
    rows = half_rows(0, half)

    def fetch(first, second):
        for front in range(fronts):
            pltpu.make_async_copy(first.at[front], parcel.at[pl.ds(2 * front, 2)], sems.at[0]).start()
        pltpu.make_async_copy(second, inward_inner, sems.at[1]).start()

    fixed = [
        pltpu.make_async_copy(reflect.at[odd, rows], refl, sems.at[2]),
        pltpu.make_async_copy(classes_in.at[odd, rows], klass, sems.at[3]),
    ]
    for copy in fixed:
        copy.start()

    @pl.when(odd == 0)
    def _():
        fetch(up.at[0], down.at[levels - 1])

    @pl.when(odd == 1)
    def _():
        fetch(down.at[levels - 1], up.at[0])

    for copy in fixed:
        copy.wait()
    parcel[2 * fronts, :half] = (jnp.where(odd == 0, 1.0, -1.0).astype(F32) * refl[...]).astype(BF16)
    parcel[2 * fronts, half:] = klass[...].astype(BF16)
    for front in range(fronts):
        pltpu.make_async_copy(up.at[0, front], parcel.at[pl.ds(2 * front, 2)], sems.at[0]).wait()
    pltpu.make_async_copy(up.at[0], inward_inner, sems.at[1]).wait()


def class_rows(slowness, kwave, shape):
    lanes = lax.broadcasted_iota(jnp.int32, shape, 1)
    table = jnp.zeros(shape, F32)
    for entry in range(NCLASS):
        table = jnp.where(lanes == entry, slowness[entry], table)
    angle = kwave * table
    return jnp.cos(angle), jnp.sin(angle)


def look_up(table, classes):
    width = 128
    rows = classes.shape[0]
    wide = jnp.broadcast_to(table[:1], (rows, width))
    pieces = [
        jnp.take_along_axis(wide, classes[:, start : start + width], axis=1, mode="promise_in_bounds")
        for start in range(0, classes.shape[1], width)
    ]
    return jnp.concatenate(pieces, axis=1)


def front_wave(freq, front):
    return 0.95 * math.pi * (freq[front].astype(F32) + 1.0) / NFREQ


def series(square, shift):
    total = jnp.full_like(square, 1.0 / math.factorial(18 + shift))
    for order in range(16, -1, -2):
        total = 1.0 / math.factorial(order + shift) - square * total
    return total


def setup_kernel(
    down, up, reflect, classes_in, slowness, freq, hx, hy,
    q_out_inner, q_in_outer, screen, phase, refl,
    fields, klass, work, sems,
):
    fronts = q_out_inner.shape[0]
    rows_x, rows_y = refl.shape[1:]
    odd = odd_place()
    fixed = [
        pltpu.make_async_copy(reflect.at[odd], refl.at[0], sems.at[2]),
        pltpu.make_async_copy(reflect.at[1 - odd], refl.at[1], sems.at[3]),
        pltpu.make_async_copy(classes_in.at[odd], klass.at[0], sems.at[4]),
        pltpu.make_async_copy(classes_in.at[1 - odd], klass.at[1], sems.at[5]),
    ]
    for copy in fixed:
        copy.start()

    @pl.when(odd == 0)
    def _():
        pltpu.make_async_copy(down.at[0], fields.at[0], sems.at[0]).start()
        pltpu.make_async_copy(up.at[1], fields.at[1], sems.at[1]).start()

    @pl.when(odd == 1)
    def _():
        pltpu.make_async_copy(up.at[1], fields.at[0], sems.at[0]).start()
        pltpu.make_async_copy(down.at[0], fields.at[1], sems.at[1]).start()

    def squares(length, axis):
        counter = lax.broadcasted_iota(jnp.int32, (rows_x, rows_y), axis)
        wrapped = jnp.where(counter >= length // 2, counter - length, counter)
        wave = 2.0 * math.pi / length * wrapped.astype(F32)
        return wave * wave

    lateral = squares(rows_x, 0) + squares(rows_y, 1)
    level_out = 1.0 / (rows_x * rows_y)
    for front in range(fronts):
        kwave = front_wave(freq, front)
        vertical = kwave * kwave - lateral
        travels = vertical > 0.0
        square = jnp.maximum(vertical, 0.0)
        root = jnp.sqrt(jnp.abs(vertical))
        phase[front, 0] = jnp.where(travels, series(square, 0), jnp.exp(-root)) * level_out
        phase[front, 1] = jnp.where(travels, root * series(square, 1), 0.0) * level_out
    for copy in fixed:
        copy.wait()
    sign = jnp.where(odd == 0, 1.0, -1.0).astype(F32)
    for level in range(2):
        refl[level] = sign * refl[level]
    for front in range(fronts):
        cos_row, sin_row = class_rows(slowness, front_wave(freq, front), (8, 128))
        for level in range(2):
            screen[level, front, 0] = look_up(cos_row, klass[level])
            screen[level, front, 1] = look_up(sin_row, klass[level])
    pltpu.make_async_copy(down.at[0], fields.at[0], sems.at[0]).wait()
    pltpu.make_async_copy(down.at[0], fields.at[1], sems.at[1]).wait()
    jobs = [(fields.at[1, front], front, q_out_inner.at[front]) for front in range(fronts)]
    jobs += [(fields.at[0, front], front, q_in_outer.at[front]) for front in range(fronts)]
    spread(jobs, work, hx, hy, phase)


def leaving(q_out_inner, refl, screen, field, target):
    fronts = q_out_inner.shape[0]
    kept = 1.0 - refl[0]
    for front in range(fronts):
        b_re, b_im = (q_out_inner[front, part].astype(F32) for part in range(2))
        b_re, b_im = screened(b_re, b_im, screen[0, front, 0], screen[0, front, 1])
        put(field.at[front], kept * b_re, kept * b_im)
    return [(field.at[front], front, target.at[front]) for front in range(fronts)]


def ahead_kernel(
    partner, parcel, q_in_outer, q_out_inner, screen, refl, phase, hx, hy,
    inward_inner, q_out_inner_next, q_out_outer, second, last,
    field, other_field, q_field, work,
):
    fronts, _, rows_x, _ = partner.shape
    everyone = range(fronts)
    half = rows_x // 2
    far_bottom = lax.rem(lax.axis_index("shot"), 2) == 0
    jobs = leaving(q_out_inner, refl, screen, field, second.at[:, :, pl.ds(0, rows_x)])
    jobs += [(partner.at[front], front, q_field.at[front]) for front in everyone]
    spread(jobs, work, hx, hy, phase)
    for front in everyone:
        in_re, in_im, out_re, out_im = mixed(
            q_in_outer[front, 0], q_in_outer[front, 1], q_field[front, 0], q_field[front, 1],
            refl[1], screen[1, front, 0], screen[1, front, 1],
        )
        put(inward_inner.at[front], in_re, in_im)
        put(other_field.at[front], out_re, out_im)
    jobs = [(other_field.at[front], front, q_out_inner_next.at[front]) for front in everyone]
    jobs += [(parcel.at[pl.ds(2 * front, 2)], front, q_out_outer.at[front]) for front in everyone]
    spread(jobs, work, hx, hy, phase)
    spread(leaving(q_out_inner_next, refl, screen, field, q_field), work, hx, hy, phase)
    for front in everyone:
        for part in range(2):
            top, bottom = q_field[front, part, :half], q_field[front, part, half:]
            second[front, part, rows_x:] = jnp.where(far_bottom, bottom, top)
            last[front, part] = jnp.where(far_bottom, top, bottom)


def edge_kernel(
    arrived, source, partner, q_out_inner, screen, refl, phase, hx, hy, held_in,
    inward_inner, out_inner, q_arrived, q_out_outer, held_out,
    inward, outward, q_partner, q_inward, work,
):
    del held_in, held_out
    fronts = partner.shape[0]
    everyone = range(fronts)
    first = lax.axis_index("depth") == 0
    for front in everyone:
        put(inward.at[front], *(jnp.where(first, source[front, part], arrived[2 * front + part]) for part in range(2)))
    jobs = [(inward.at[front], front, q_arrived.at[front]) for front in everyone]
    jobs += [(partner.at[front], front, q_partner.at[front]) for front in everyone]
    spread(jobs, work, hx, hy, phase)
    for front in everyone:
        in_re, in_im, out_re, out_im = mixed(
            q_arrived[front, 0], q_arrived[front, 1], q_out_inner[front, 0], q_out_inner[front, 1],
            refl[0], screen[0, front, 0], screen[0, front, 1],
        )
        put(inward.at[front], in_re, in_im)
        put(outward.at[front], out_re, out_im)
    jobs = [(inward.at[front], front, q_inward.at[front]) for front in everyone]
    jobs += [(outward.at[front], front, q_out_outer.at[front]) for front in everyone]
    spread(jobs, work, hx, hy, phase)
    for front in everyone:
        in_re, in_im, out_re, out_im = mixed(
            q_inward[front, 0], q_inward[front, 1], q_partner[front, 0], q_partner[front, 1],
            refl[1], screen[1, front, 0], screen[1, front, 1],
        )
        put(inward_inner.at[front], in_re, in_im)
        put(out_inner.at[front], out_re, out_im)


def beyond_kernel(
    mine, other, out_inner, q_out_outer_0, q_out_outer_1, slowness, freq, phase, hx, hy, last_in, inner_in,
    q_out_inner, rest_2, rest_3, last_out, inner_out,
    field_2, field_3, work,
):
    del last_in, inner_in, last_out, inner_out
    fronts = out_inner.shape[0]
    everyone = range(fronts)
    half = mine.shape[0] // 2
    refl_beyond = joined(mine[:half], other[:half]).astype(F32)
    klass = joined(mine[half:], other[half:]).astype(F32).astype(jnp.int32)
    for front in everyone:
        cos_row, sin_row = class_rows(slowness, front_wave(freq, front), (8, 128))
        back_re = refl_beyond * look_up(cos_row, klass)
        back_im = refl_beyond * look_up(sin_row, klass)
        for known, target in ((q_out_outer_0, field_2), (q_out_outer_1, field_3)):
            known_re, known_im = (known[front, part].astype(F32) for part in range(2))
            put(target.at[front], *screened(known_re, known_im, back_re, back_im))
    jobs = [(out_inner.at[front], front, q_out_inner.at[front]) for front in everyone]
    jobs += [(field_2.at[front], front, rest_2.at[front]) for front in everyone]
    jobs += [(field_3.at[front], front, rest_3.at[front]) for front in everyone]
    spread(jobs, work, hx, hy, phase)


def partner_kernel(partner, phase, hx, hy, q_partner, work):
    fronts = partner.shape[0]
    spread([(partner.at[front], front, q_partner.at[front]) for front in range(fronts)], work, hx, hy, phase)


def inner_kernel(
    second, rest_2, rest_3, q_arrived, q_out_inner_1, q_out_inner_2, q_partner, screen, refl, phase, hx, hy,
    inward, outward, far_inward, far_outward, terms, inner_terms,
    field, q_inward, work,
):
    fronts, _, rows_x, _ = q_partner.shape
    everyone = range(fronts)
    first = lax.axis_index("depth") == 0
    for front in everyone:
        a_re, a_im = (
            jnp.where(
                first,
                q_arrived[front, part].astype(F32),
                second[front, part, :rows_x].astype(F32) + rest_2[front, part].astype(F32),
            )
            for part in range(2)
        )
        in_re, in_im, _, _ = mixed(
            a_re, a_im, q_out_inner_1[front, 0], q_out_inner_1[front, 1],
            refl[0], screen[0, front, 0], screen[0, front, 1],
        )
        put(field.at[front], in_re, in_im)
    spread([(field.at[front], front, q_inward.at[front]) for front in everyone], work, hx, hy, phase)
    rows, total = outer_rows(
        1, second.at[:, :, pl.ds(rows_x, rows_x // 2)], q_arrived, rest_3, q_out_inner_2, screen, refl,
        far_inward, far_outward,
    )
    terms[0] = total.astype(BF16)
    total = None
    for front in everyone:
        a_re, a_im = (q_inward[front, part].astype(F32) for part in range(2))
        b_re, b_im = (q_partner[front, part].astype(F32) for part in range(2))
        in_re, in_im, out_re, out_im = mixed(
            a_re, a_im, b_re, b_im, refl[1], screen[1, front, 0], screen[1, front, 1]
        )
        put(inward.at[front], in_re, in_im)
        put(outward.at[front], out_re, out_im)
        term = a_re * b_re + a_im * b_im
        total = term if total is None else total + term
    inner_terms[...] = total
    terms[1] = inner_terms[rows, :].astype(BF16)


def outer_rows(of, last, q_arrived, rest, q_out_inner, screen, refl, inward, outward, ready=None):
    fronts, _, half, _ = last.shape
    first = lax.axis_index("depth") == 0
    rows = half_rows(of, half)
    total = None
    for front in range(fronts):
        a_re, a_im = (
            jnp.where(
                first,
                q_arrived[front, part, rows, :].astype(F32),
                last[front, part].astype(F32) + rest[front, part, rows, :].astype(F32),
            )
            for part in range(2)
        )
        b_re, b_im = (q_out_inner[front, part, rows, :].astype(F32) for part in range(2))
        in_re, in_im, out_re, out_im = mixed(
            a_re, a_im, b_re, b_im, refl[0, rows, :], screen[0, front, 0, rows, :], screen[0, front, 1, rows, :]
        )
        put(inward.at[front], in_re, in_im)
        put(outward.at[front], out_re, out_im)
        term = a_re * b_re + a_im * b_im
        total = term if total is None else total + term
    return rows, total


def send_home(level, rows, inward, outward, down_out, up_out, sems):
    odd = odd_place()

    def copies(place, inward_out, outward_out):
        return [
            pltpu.make_async_copy(inward, inward_out.at[place, :, :, rows, :], sems.at[0]),
            pltpu.make_async_copy(outward, outward_out.at[place, :, :, rows, :], sems.at[1]),
        ]

    @pl.when(odd == 0)
    def _():
        for copy in copies(level, down_out, up_out):
            copy.start()

    @pl.when(odd == 1)
    def _():
        for copy in copies(1 - level, up_out, down_out):
            copy.start()

    return copies(0, down_out, up_out)


def home_kernel(inward, outward, far_inward, far_outward, down_out, up_out, sems):
    rows_x, half = inward.shape[2], far_inward.shape[2]
    waits = send_home(1, pl.ds(0, rows_x), inward, outward, down_out, up_out, sems.at[0])
    waits += send_home(0, half_rows(1, half), far_inward, far_outward, down_out, up_out, sems.at[1])
    for copy in waits:
        copy.wait()


def near_rows_kernel(
    scale, last, q_arrived, rest, q_out_inner, screen, refl, inner_terms, other, down_in, up_in,
    down_out, up_out, gradient,
    inward, outward, sums, sems,
):
    del down_in, up_in
    rows, total = outer_rows(0, last, q_arrived, rest, q_out_inner, screen, refl, inward, outward)
    waits = send_home(0, rows, inward, outward, down_out, up_out, sems.at[0])
    odd = odd_place()
    sums[odd] = scale * (total + other[0].astype(F32))
    sums[1 - odd] = scale * (inner_terms[rows, :] + other[1].astype(F32))
    done = pltpu.make_async_copy(sums, gradient, sems.at[1, 0])
    done.start()
    for copy in waits + [done]:
        copy.wait()


def per_device(down_state, up_state, source, reflect, screen_class, screen_values, freq_index):
    depth = lax.axis_size("depth")
    shots = lax.axis_size("shot")
    levels, fronts, parts, rows_x, rows_y = down_state.shape
    if levels != 2 or depth % 2 or shots % 2 or HOPS != 3:
        return per_device_plain(down_state, up_state, source, reflect, screen_class, screen_values, freq_index)
    scale = 1.0 / math.sqrt(fronts * shots)
    half = rows_x // 2
    hx = jnp.asarray(hartley(rows_x))
    hy = jnp.asarray(hartley(rows_y))
    partners = [(i, i ^ 1) for i in range(depth)]
    beyond = [(i, i + 1) for i in range(1, depth - 1, 2)] + [(i + 1, i) for i in range(1, depth - 1, 2)]
    to_partner = functools.partial(lax.ppermute, axis_name="depth", perm=partners)
    to_beyond = functools.partial(lax.ppermute, axis_name="depth", perm=beyond)
    across = functools.partial(lax.ppermute, axis_name="shot", perm=[(i, i ^ 1) for i in range(shots)])
    plane = jax.ShapeDtypeStruct((fronts, parts, rows_x, rows_y), BF16)
    half_plane = jax.ShapeDtypeStruct((fronts, parts, half, rows_y), BF16)
    pair = jax.ShapeDtypeStruct((2, rows_x, rows_y), F32)
    turns = jax.ShapeDtypeStruct((fronts, parts, rows_x, rows_y), F32)
    screens = jax.ShapeDtypeStruct((2, fronts, parts, rows_x, rows_y), F32)
    state = jax.ShapeDtypeStruct(down_state.shape, BF16)
    dma = pltpu.SemaphoreType.DMA

    def call(kernel, in_specs, out_specs, out_shape, scratch=(), **more):
        return pl.pallas_call(
            kernel,
            in_specs=in_specs,
            out_specs=out_specs,
            out_shape=out_shape,
            scratch_shapes=list(scratch),
            compiler_params=PARAMS,
            **more,
        )

    def kept_in_hbm(*arrays):
        return [pltpu.with_memory_space_constraint(array, pltpu.HBM) for array in arrays]

    def buffers(count, shape=plane):
        return [pltpu.VMEM(shape.shape, shape.dtype)] * count

    def work(slots):
        return pltpu.VMEM((slots, *plane.shape[1:]), BF16)

    parcel, in_inner = call(
        edges_kernel,
        [HBM] * 4,
        [VMEM] * 2,
        [jax.ShapeDtypeStruct((fronts * parts + 1, rows_x, rows_y), BF16), plane],
        [pltpu.VMEM((half, rows_y), F32), pltpu.VMEM((half, rows_y), jnp.int32), dma((4,))],
    )(*kept_in_hbm(down_state, up_state, reflect, screen_class))
    arrived = to_beyond(parcel)
    partner_0 = to_partner(in_inner)
    q_out_inner_0, q_in_outer_0, screen, phase, refl = call(
        setup_kernel,
        [HBM] * 4 + [SMEM] * 2 + [VMEM] * 2,
        [VMEM] * 5,
        [plane] * 2 + [screens, turns, pair],
        [
            pltpu.VMEM((2, *plane.shape), BF16),
            pltpu.VMEM((2, rows_x, rows_y), jnp.int32),
            work(2 * fronts),
            dma((6,)),
        ],
    )(*kept_in_hbm(down_state, up_state, reflect, screen_class), screen_values, freq_index, hx, hy)
    in_inner_1, q_out_inner_1, q_out_outer_0, second, last = call(
        ahead_kernel,
        [VMEM] * 9,
        [VMEM] * 5,
        [plane] * 3 + [jax.ShapeDtypeStruct((fronts, parts, rows_x + half, rows_y), BF16), half_plane],
        buffers(3) + [work(2 * fronts)],
    )(partner_0, parcel, q_in_outer_0, q_out_inner_0, screen, refl, phase, hx, hy)
    partner_1 = to_partner(in_inner_1)
    mine = arrived[fronts * parts]
    swapped = across(mine)
    in_inner_2, out_inner_2, q_arrived, q_out_outer_1, second = call(
        edge_kernel,
        [VMEM] * 10,
        [VMEM] * 5,
        [plane] * 4 + [jax.ShapeDtypeStruct(second.shape, BF16)],
        buffers(4) + [work(2 * fronts)],
        input_output_aliases={9: 4},
    )(arrived, source, partner_1, q_out_inner_0, screen, refl, phase, hx, hy, second)
    second = to_beyond(second)
    q_out_inner_2, rest_2, rest_3, last, in_inner_2 = call(
        beyond_kernel,
        [VMEM] * 5 + [SMEM] * 2 + [VMEM] * 5,
        [VMEM] * 5,
        [plane] * 3 + [half_plane, plane],
        buffers(2) + [work(3 * fronts)],
        input_output_aliases={10: 3, 11: 4},
    )(
        mine, swapped, out_inner_2, q_out_outer_0, q_out_outer_1, screen_values, freq_index,
        phase, hx, hy, last, in_inner_2,
    )
    last = to_beyond(last)
    partner_2 = to_partner(in_inner_2)
    q_partner = call(partner_kernel, [VMEM] * 4, VMEM, plane, [work(fronts)])(partner_2, phase, hx, hy)
    inner_in, inner_out, far_in, far_out, terms, inner_terms = call(
        inner_kernel,
        [VMEM] * 12,
        [VMEM] * 6,
        [plane] * 2
        + [half_plane] * 2
        + [jax.ShapeDtypeStruct((2, half, rows_y), BF16), jax.ShapeDtypeStruct((rows_x, rows_y), F32)],
        buffers(2) + [work(fronts)],
    )(
        second, rest_2, rest_3, q_arrived, q_out_inner_1, q_out_inner_2, q_partner, screen, refl, phase, hx, hy
    )
    other = across(terms) if shots == 2 else jnp.zeros_like(terms)
    down, up = call(home_kernel, [VMEM] * 4, [HBM] * 2, [state] * 2, [dma((2, 2))])(
        inner_in, inner_out, far_in, far_out
    )
    down, up, gradient = call(
        functools.partial(near_rows_kernel, scale),
        [VMEM] * 8 + [HBM] * 2,
        [HBM] * 3,
        [state, state, jax.ShapeDtypeStruct((2, half, rows_y), F32)],
        buffers(2, half_plane) + [pltpu.VMEM((2, half, rows_y), F32), dma((2, 2))],
        input_output_aliases={8: 0, 9: 1},
    )(last, q_arrived, rest_3, q_out_inner_2, screen, refl, inner_terms, other, down, up)
    if shots != 2:
        terms = scale * terms.astype(F32)
        far = jnp.where(odd_place() == 0, terms, terms[::-1])
        top = lax.rem(lax.axis_index("shot"), 2) == 0
        whole = jnp.concatenate([jnp.where(top, gradient, far), jnp.where(top, far, gradient)], axis=1)
        gradient = lax.psum_scatter(whole.astype(BF16), "shot", scatter_dimension=1, tiled=True).astype(F32)
    return (down, up, gradient)


def solution(mesh):
    return jax.shard_map(
        per_device,
        mesh=mesh,
        in_specs=(
            P("depth", "shot", None, None, None),
            P("depth", "shot", None, None, None),
            P("shot", None, None, None),
            P("depth", None, None),
            P("depth", None, None),
            P(),
            P("shot"),
        ),
        out_specs=(
            P("depth", "shot", None, None, None),
            P("depth", "shot", None, None, None),
            P("depth", "shot", None),
        ),
        check_vma=False,
    )
```

```python
import functools
import math

import jax
import jax.numpy as jnp
import numpy as np
from jax import lax
from jax.experimental import pallas as pl
from jax.experimental.pallas import tpu as pltpu
from jax.sharding import PartitionSpec as P

HOPS = 3
NCLASS = 16
NFREQ = 128
F32 = jnp.float32
BF16 = jnp.bfloat16
VMEM = pl.BlockSpec(memory_space=pltpu.VMEM)
HBM = pl.BlockSpec(memory_space=pltpu.HBM)
SMEM = pl.BlockSpec(memory_space=pltpu.SMEM)
PARAMS = pltpu.CompilerParams(vmem_limit_bytes=28 * 2**20)


def passed_along(block, axis, distance):
    devices = range(lax.axis_size(axis))
    route = [(i - distance, i) for i in devices if i - distance in devices]
    return lax.ppermute(block, axis, route)


def dft_tables(length):
    counter = jnp.arange(length, dtype=jnp.int32)
    product = counter[:, None] * counter[None, :] % length
    angles = 2.0 * math.pi / length * product.astype(jnp.float32)
    return (jnp.cos(angles).astype(jnp.bfloat16), jnp.sin(angles).astype(jnp.bfloat16))


def wavenumbers(length):
    counter = jnp.arange(length, dtype=jnp.int32)
    wrapped = jnp.where(counter >= length // 2, counter - length, counter)
    return 2.0 * math.pi / length * wrapped.astype(jnp.float32)


def propagate(planes, phase_re, phase_im, tables):
    fwd_left, fwd_right, inv_left, inv_right = tables
    first = jnp.einsum(
        "cdjk,...dkl->...cjl", fwd_left, planes, preferred_element_type=jnp.float32
    ).astype(jnp.bfloat16)
    second = jnp.einsum("...djl,dclm->...cjm", first, fwd_right, preferred_element_type=jnp.float32)
    real_part = second[..., 0, :, :]
    imag_part = second[..., 1, :, :]
    turned = jnp.stack(
        [real_part * phase_re - imag_part * phase_im, real_part * phase_im + imag_part * phase_re],
        axis=-3,
    ).astype(jnp.bfloat16)
    third = jnp.einsum(
        "cdjk,...dkl->...cjl", inv_left, turned, preferred_element_type=jnp.float32
    ).astype(jnp.bfloat16)
    return jnp.einsum(
        "...djl,dclm->...cjm", third, inv_right, preferred_element_type=jnp.float32
    ).astype(jnp.bfloat16)


def trade(down_edge, up_edge):
    got_down = passed_along(down_edge, "depth", 1)
    got_up = passed_along(up_edge, "depth", -1)
    return (got_down, got_up)


def per_device_plain(down_state, up_state, source, reflect, screen_class, screen_values, freq_index):
    levels = down_state.shape[0]
    rows_x = down_state.shape[3]
    rows_y = down_state.shape[4]
    front_count = down_state.shape[1]
    depth_rank = lax.axis_index("depth")
    scale = 1.0 / math.sqrt(front_count * lax.axis_size("shot"))
    cos_x, sin_x = dft_tables(rows_x)
    cos_y, sin_y = dft_tables(rows_y)
    tables = (
        jnp.stack([jnp.stack([cos_x, sin_x]), jnp.stack([-sin_x, cos_x])]),
        jnp.stack([jnp.stack([cos_y, -sin_y]), jnp.stack([sin_y, cos_y])]),
        jnp.stack([jnp.stack([cos_x, -sin_x]), jnp.stack([sin_x, cos_x])]),
        jnp.stack([jnp.stack([cos_y, sin_y]), jnp.stack([-sin_y, cos_y])]),
    )
    kwave = 0.95 * math.pi * (freq_index.astype(jnp.float32) + 1.0) / NFREQ
    kx_wave = wavenumbers(rows_x)
    ky_wave = wavenumbers(rows_y)
    vertical = kwave[:, None, None] ** 2 - kx_wave[None, :, None] ** 2 - ky_wave[None, None, :] ** 2
    propag = jnp.sqrt(jnp.maximum(vertical, 0.0))
    damping = jnp.exp(-jnp.sqrt(jnp.maximum(-vertical, 0.0))) / (rows_x * rows_y)
    phase_re = damping * jnp.cos(propag)
    phase_im = damping * jnp.sin(propag)
    classes = jnp.arange(NCLASS, dtype=jnp.int32)
    onehot = (screen_class[None] == classes[:, None, None, None]).astype(jnp.float32)
    slowness = jnp.einsum("c,clxy->lxy", screen_values, onehot, precision=lax.Precision.HIGHEST)
    angle = kwave[None, :, None, None] * slowness[:, None]
    screen_re = jnp.cos(angle)
    screen_im = jnp.sin(angle)
    refl = reflect[:, None]
    top_slab = depth_rank == 0
    down = down_state
    up = up_state
    a_re = a_im = b_re = b_im = None
    for repeat in range(HOPS):
        down_edge = down[levels - 1]
        up_edge = up[0]
        got_down, got_up = trade(down_edge, up_edge)
        got_down = jnp.where(top_slab, source, got_down)
        moved = propagate(
            jnp.concatenate([got_down[None], down[: levels - 1], up[1:], got_up[None]], axis=0),
            phase_re,
            phase_im,
            tables,
        )
        from_above = moved[:levels]
        from_below = moved[levels:]
        qa_re = from_above[:, :, 0].astype(jnp.float32)
        qa_im = from_above[:, :, 1].astype(jnp.float32)
        qb_re = from_below[:, :, 0].astype(jnp.float32)
        qb_im = from_below[:, :, 1].astype(jnp.float32)
        a_re = screen_re * qa_re - screen_im * qa_im
        a_im = screen_re * qa_im + screen_im * qa_re
        b_re = screen_re * qb_re - screen_im * qb_im
        b_im = screen_re * qb_im + screen_im * qb_re
        down = jnp.stack(
            [(1.0 + refl) * a_re - refl * b_re, (1.0 + refl) * a_im - refl * b_im], axis=2
        ).astype(jnp.bfloat16)
        up = jnp.stack(
            [(1.0 - refl) * b_re + refl * a_re, (1.0 - refl) * b_im + refl * a_im], axis=2
        ).astype(jnp.bfloat16)
    terms = scale * jnp.sum(a_re * b_re + a_im * b_im, axis=1)
    gradient = lax.psum_scatter(
        terms.astype(jnp.bfloat16), "shot", scatter_dimension=1, tiled=True
    ).astype(jnp.float32)
    return (down, up, gradient)


def hartley(length):
    counter = np.arange(length)
    angles = 2.0 * np.pi / length * (counter[:, None] * counter[None, :] % length)
    cosine = np.cos(angles).astype(BF16).astype(np.float32)
    sine = np.sin(angles).astype(BF16).astype(np.float32)
    return (cosine + sine).astype(BF16)


def odd_place():
    return lax.rem(lax.axis_index("depth"), 2)


def mm(left, right):
    return jnp.dot(left, right, preferred_element_type=F32)


def spread(jobs, work, hx, hy, phase):
    jobs = list(enumerate(jobs))
    for slot, (plane, _, _) in jobs:
        for part in range(2):
            work[slot, part] = mm(plane[part], hy[...]).astype(BF16)
    for slot, (_, front, _) in jobs:
        turn_re, turn_im = phase[front, 0], phase[front, 1]
        part_re = mm(hx[...], work[slot, 0])
        part_im = mm(hx[...], work[slot, 1])
        work[slot, 0] = (part_re * turn_re - part_im * turn_im).astype(BF16)
        work[slot, 1] = (part_re * turn_im + part_im * turn_re).astype(BF16)
    for slot, _ in jobs:
        for part in range(2):
            work[slot, part] = mm(hx[...], work[slot, part]).astype(BF16)
    for slot, (_, _, target) in jobs:
        for part in range(2):
            target[part] = mm(work[slot, part], hy[...]).astype(BF16)


def screened(real_part, imag_part, screen_re, screen_im):
    return (
        screen_re * real_part - screen_im * imag_part,
        screen_re * imag_part + screen_im * real_part,
    )


def mixed(a_re, a_im, b_re, b_im, refl, screen_re, screen_im):
    a_re, a_im, b_re, b_im = (part.astype(F32) for part in (a_re, a_im, b_re, b_im))
    step_re = refl * (a_re - b_re)
    step_im = refl * (a_im - b_im)
    inward = screened(a_re + step_re, a_im + step_im, screen_re, screen_im)
    outward = screened(b_re + step_re, b_im + step_im, screen_re, screen_im)
    return tuple(part.astype(BF16) for part in inward + outward)


def put(target, real_part, imag_part):
    target[0] = real_part.astype(BF16)
    target[1] = imag_part.astype(BF16)


def half_rows(of, half):
    shot = lax.rem(lax.axis_index("shot"), 2)
    return pl.ds(pl.multiple_of((shot if of == 0 else 1 - shot) * half, half), half)


def edges_kernel(down, up, outward_outer, inward_inner, sems):
    levels = down.shape[0]
    odd = odd_place()

    def fetch(first, second):
        pltpu.make_async_copy(first, outward_outer, sems.at[0]).start()
        pltpu.make_async_copy(second, inward_inner, sems.at[1]).start()

    @pl.when(odd == 0)
    def _():
        fetch(up.at[0], down.at[levels - 1])

    @pl.when(odd == 1)
    def _():
        fetch(down.at[levels - 1], up.at[0])

    pltpu.make_async_copy(up.at[0], outward_outer, sems.at[0]).wait()
    pltpu.make_async_copy(up.at[0], inward_inner, sems.at[1]).wait()


def class_rows(slowness, kwave, shape):
    lanes = lax.broadcasted_iota(jnp.int32, shape, 1)
    table = jnp.zeros(shape, F32)
    for entry in range(NCLASS):
        table = jnp.where(lanes == entry, slowness[entry], table)
    angle = kwave * table
    return jnp.cos(angle), jnp.sin(angle)


def look_up(table, classes):
    width = 128
    rows = classes.shape[0]
    wide = jnp.broadcast_to(table[:1], (rows, width))
    pieces = [
        jnp.take_along_axis(wide, classes[:, start : start + width], axis=1, mode="promise_in_bounds")
        for start in range(0, classes.shape[1], width)
    ]
    return jnp.concatenate(pieces, axis=1)


def front_wave(freq, front):
    return 0.95 * math.pi * (freq[front].astype(F32) + 1.0) / NFREQ


def series(square, shift):
    total = jnp.full_like(square, 1.0 / math.factorial(18 + shift))
    for order in range(16, -1, -2):
        total = 1.0 / math.factorial(order + shift) - square * total
    return total


def setup_kernel(
    down, up, reflect, classes_in, slowness, freq, hx, hy,
    q_out_inner, q_in_outer, screen, phase, refl,
    fields, klass, work, sems,
):
    fronts = q_out_inner.shape[0]
    rows_x, rows_y = refl.shape[1:]
    odd = odd_place()
    fixed = [
        pltpu.make_async_copy(reflect.at[odd], refl.at[0], sems.at[2]),
        pltpu.make_async_copy(reflect.at[1 - odd], refl.at[1], sems.at[3]),
        pltpu.make_async_copy(classes_in.at[odd], klass.at[0], sems.at[4]),
        pltpu.make_async_copy(classes_in.at[1 - odd], klass.at[1], sems.at[5]),
    ]
    for copy in fixed:
        copy.start()

    @pl.when(odd == 0)
    def _():
        pltpu.make_async_copy(down.at[0], fields.at[0], sems.at[0]).start()
        pltpu.make_async_copy(up.at[1], fields.at[1], sems.at[1]).start()

    @pl.when(odd == 1)
    def _():
        pltpu.make_async_copy(up.at[1], fields.at[0], sems.at[0]).start()
        pltpu.make_async_copy(down.at[0], fields.at[1], sems.at[1]).start()

    def squares(length, axis):
        counter = lax.broadcasted_iota(jnp.int32, (rows_x, rows_y), axis)
        wrapped = jnp.where(counter >= length // 2, counter - length, counter)
        wave = 2.0 * math.pi / length * wrapped.astype(F32)
        return wave * wave

    lateral = squares(rows_x, 0) + squares(rows_y, 1)
    level_out = 1.0 / (rows_x * rows_y)
    for front in range(fronts):
        kwave = front_wave(freq, front)
        vertical = kwave * kwave - lateral
        travels = vertical > 0.0
        square = jnp.maximum(vertical, 0.0)
        root = jnp.sqrt(jnp.abs(vertical))
        phase[front, 0] = jnp.where(travels, series(square, 0), jnp.exp(-root)) * level_out
        phase[front, 1] = jnp.where(travels, root * series(square, 1), 0.0) * level_out
    for copy in fixed:
        copy.wait()
    sign = jnp.where(odd == 0, 1.0, -1.0).astype(F32)
    for level in range(2):
        refl[level] = sign * refl[level]
    for front in range(fronts):
        cos_row, sin_row = class_rows(slowness, front_wave(freq, front), (8, 128))
        for level in range(2):
            screen[level, front, 0] = look_up(cos_row, klass[level])
            screen[level, front, 1] = look_up(sin_row, klass[level])
    pltpu.make_async_copy(down.at[0], fields.at[0], sems.at[0]).wait()
    pltpu.make_async_copy(down.at[0], fields.at[1], sems.at[1]).wait()
    jobs = [(fields.at[1, front], front, q_out_inner.at[front]) for front in range(fronts)]
    jobs += [(fields.at[0, front], front, q_in_outer.at[front]) for front in range(fronts)]
    spread(jobs, work, hx, hy, phase)


def ahead_kernel(
    partner, q_in_outer, screen, refl, phase, hx, hy,
    inward_inner, q_out_inner,
    q_field, field, work,
):
    everyone = range(partner.shape[0])
    spread([(partner.at[front], front, q_field.at[front]) for front in everyone], work, hx, hy, phase)
    for front in everyone:
        in_re, in_im, out_re, out_im = mixed(
            q_in_outer[front, 0], q_in_outer[front, 1], q_field[front, 0], q_field[front, 1],
            refl[1], screen[1, front, 0], screen[1, front, 1],
        )
        put(inward_inner.at[front], in_re, in_im)
        put(field.at[front], out_re, out_im)
    spread([(field.at[front], front, q_out_inner.at[front]) for front in everyone], work, hx, hy, phase)


def outer_step(arrived, source, q_out_inner, screen, refl, phase, hx, hy, inward, outward, q_arrived, work):
    everyone = range(arrived.shape[0])
    first = lax.axis_index("depth") == 0
    for front in everyone:
        put(inward.at[front], *(jnp.where(first, source[front, part], arrived[front, part]) for part in range(2)))
    spread([(inward.at[front], front, q_arrived.at[front]) for front in everyone], work, hx, hy, phase)
    for front in everyone:
        in_re, in_im, out_re, out_im = mixed(
            q_arrived[front, 0], q_arrived[front, 1], q_out_inner[front, 0], q_out_inner[front, 1],
            refl[0], screen[0, front, 0], screen[0, front, 1],
        )
        put(inward.at[front], in_re, in_im)
        put(outward.at[front], out_re, out_im)


def edge_kernel(
    arrived, source, q_out_inner, screen, refl, phase, hx, hy,
    inward, outward, q_arrived,
    work,
):
    outer_step(arrived, source, q_out_inner, screen, refl, phase, hx, hy, inward, outward, q_arrived, work)


def last_edge_kernel(
    arrived, source, q_out_inner, screen, refl, phase, hx, hy,
    inward, last_far, last_near,
    outward, q_field, work,
):
    everyone = range(arrived.shape[0])
    half = arrived.shape[2] // 2
    far_bottom = lax.rem(lax.axis_index("shot"), 2) == 0
    outer_step(arrived, source, q_out_inner, screen, refl, phase, hx, hy, inward, outward, q_field, work)
    spread([(outward.at[front], front, q_field.at[front]) for front in everyone], work, hx, hy, phase)
    for front in everyone:
        for part in range(2):
            top, bottom = q_field[front, part, :half], q_field[front, part, half:]
            last_far[front, part] = jnp.where(far_bottom, bottom, top)
            last_near[front, part] = jnp.where(far_bottom, top, bottom)


def inner_kernel(
    inward_outer, partner, screen, refl, phase, hx, hy,
    inward, outward,
    q_inward, q_partner, work,
):
    everyone = range(partner.shape[0])
    jobs = [(inward_outer.at[front], front, q_inward.at[front]) for front in everyone]
    jobs += [(partner.at[front], front, q_partner.at[front]) for front in everyone]
    spread(jobs, work, hx, hy, phase)
    for front in everyone:
        in_re, in_im, out_re, out_im = mixed(
            q_inward[front, 0], q_inward[front, 1], q_partner[front, 0], q_partner[front, 1],
            refl[1], screen[1, front, 0], screen[1, front, 1],
        )
        put(inward.at[front], in_re, in_im)
        put(outward.at[front], out_re, out_im)


def last_inner_kernel(
    inward_outer, partner, out_inner, screen, refl, phase, hx, hy,
    inward, outward, terms, q_out_inner,
    q_inward, q_partner, work,
):
    everyone = range(partner.shape[0])
    jobs = [(inward_outer.at[front], front, q_inward.at[front]) for front in everyone]
    jobs += [(partner.at[front], front, q_partner.at[front]) for front in everyone]
    jobs += [(out_inner.at[front], front, q_out_inner.at[front]) for front in everyone]
    spread(jobs, work, hx, hy, phase)
    total = None
    for front in everyone:
        a_re, a_im = (q_inward[front, part].astype(F32) for part in range(2))
        b_re, b_im = (q_partner[front, part].astype(F32) for part in range(2))
        in_re, in_im, out_re, out_im = mixed(
            a_re, a_im, b_re, b_im, refl[1], screen[1, front, 0], screen[1, front, 1]
        )
        put(inward.at[front], in_re, in_im)
        put(outward.at[front], out_re, out_im)
        term = a_re * b_re + a_im * b_im
        total = term if total is None else total + term
    terms[...] = total


def far_rows_kernel(
    last, q_arrived, q_out_inner, screen, refl, inner_terms,
    inward, outward, terms,
):
    rows, total = outer_rows(1, last, q_arrived, q_out_inner, screen, refl, inward, outward)
    terms[0] = total.astype(BF16)
    terms[1] = inner_terms[rows, :].astype(BF16)


def outer_rows(of, last, q_arrived, q_out_inner, screen, refl, inward, outward):
    fronts, _, half, _ = last.shape
    first = lax.axis_index("depth") == 0
    rows = half_rows(of, half)
    total = None
    for front in range(fronts):
        a_re, a_im = (
            jnp.where(first, q_arrived[front, part, rows, :], last[front, part]).astype(F32)
            for part in range(2)
        )
        b_re, b_im = (q_out_inner[front, part, rows, :].astype(F32) for part in range(2))
        in_re, in_im, out_re, out_im = mixed(
            a_re, a_im, b_re, b_im, refl[0, rows, :], screen[0, front, 0, rows, :], screen[0, front, 1, rows, :]
        )
        put(inward.at[front], in_re, in_im)
        put(outward.at[front], out_re, out_im)
        term = a_re * b_re + a_im * b_im
        total = term if total is None else total + term
    return rows, total


def send_home(level, rows, inward, outward, down_out, up_out, sems):
    odd = odd_place()

    def copies(place, inward_out, outward_out):
        return [
            pltpu.make_async_copy(inward, inward_out.at[place, :, :, rows, :], sems.at[0]),
            pltpu.make_async_copy(outward, outward_out.at[place, :, :, rows, :], sems.at[1]),
        ]

    @pl.when(odd == 0)
    def _():
        for copy in copies(level, down_out, up_out):
            copy.start()

    @pl.when(odd == 1)
    def _():
        for copy in copies(1 - level, up_out, down_out):
            copy.start()

    return copies(0, down_out, up_out)


def home_kernel(inward, outward, far_inward, far_outward, down_out, up_out, sems):
    rows_x, half = inward.shape[2], far_inward.shape[2]
    waits = send_home(1, pl.ds(0, rows_x), inward, outward, down_out, up_out, sems.at[0])
    waits += send_home(0, half_rows(1, half), far_inward, far_outward, down_out, up_out, sems.at[1])
    for copy in waits:
        copy.wait()


def near_rows_kernel(
    scale, last, q_arrived, q_out_inner, screen, refl, inner_terms, other, down_in, up_in,
    down_out, up_out, gradient,
    inward, outward, sums, sems,
):
    del down_in, up_in
    rows, total = outer_rows(0, last, q_arrived, q_out_inner, screen, refl, inward, outward)
    waits = send_home(0, rows, inward, outward, down_out, up_out, sems.at[0])
    odd = odd_place()
    sums[odd] = scale * (total + other[0].astype(F32))
    sums[1 - odd] = scale * (inner_terms[rows, :] + other[1].astype(F32))
    done = pltpu.make_async_copy(sums, gradient, sems.at[1, 0])
    done.start()
    for copy in waits + [done]:
        copy.wait()


def per_device(down_state, up_state, source, reflect, screen_class, screen_values, freq_index):
    depth = lax.axis_size("depth")
    shots = lax.axis_size("shot")
    levels, fronts, parts, rows_x, rows_y = down_state.shape
    if levels != 2 or depth % 2 or shots % 2 or HOPS != 3:
        return per_device_plain(down_state, up_state, source, reflect, screen_class, screen_values, freq_index)
    scale = 1.0 / math.sqrt(fronts * shots)
    half = rows_x // 2
    hx = jnp.asarray(hartley(rows_x))
    hy = jnp.asarray(hartley(rows_y))
    partners = [(i, i ^ 1) for i in range(depth)]
    beyond = [(i, i + 1) for i in range(1, depth - 1, 2)] + [(i + 1, i) for i in range(1, depth - 1, 2)]
    to_partner = functools.partial(lax.ppermute, axis_name="depth", perm=partners)
    to_beyond = functools.partial(lax.ppermute, axis_name="depth", perm=beyond)
    across = functools.partial(lax.ppermute, axis_name="shot", perm=[(i, i ^ 1) for i in range(shots)])
    plane = jax.ShapeDtypeStruct((fronts, parts, rows_x, rows_y), BF16)
    half_plane = jax.ShapeDtypeStruct((fronts, parts, half, rows_y), BF16)
    pair = jax.ShapeDtypeStruct((2, rows_x, rows_y), F32)
    turns = jax.ShapeDtypeStruct((fronts, parts, rows_x, rows_y), F32)
    screens = jax.ShapeDtypeStruct((2, fronts, parts, rows_x, rows_y), F32)
    state = jax.ShapeDtypeStruct(down_state.shape, BF16)
    dma = pltpu.SemaphoreType.DMA

    def call(kernel, in_specs, out_specs, out_shape, scratch=(), **more):
        return pl.pallas_call(
            kernel,
            in_specs=in_specs,
            out_specs=out_specs,
            out_shape=out_shape,
            scratch_shapes=list(scratch),
            compiler_params=PARAMS,
            **more,
        )

    def kept_in_hbm(*arrays):
        return [pltpu.with_memory_space_constraint(array, pltpu.HBM) for array in arrays]

    def buffers(count, shape=plane):
        return [pltpu.VMEM(shape.shape, shape.dtype)] * count

    def work(slots):
        return pltpu.VMEM((slots, *plane.shape[1:]), BF16)

    out_outer, in_inner = call(edges_kernel, [HBM] * 2, [VMEM] * 2, [plane] * 2, [dma((2,))])(
        *kept_in_hbm(down_state, up_state)
    )
    arrived_0 = to_beyond(out_outer)
    partner_0 = to_partner(in_inner)
    q_out_inner_0, q_in_outer_0, screen, phase, refl = call(
        setup_kernel,
        [HBM] * 4 + [SMEM] * 2 + [VMEM] * 2,
        [VMEM] * 5,
        [plane] * 2 + [screens, turns, pair],
        [
            pltpu.VMEM((2, *plane.shape), BF16),
            pltpu.VMEM((2, rows_x, rows_y), jnp.int32),
            work(2 * fronts),
            dma((6,)),
        ],
    )(*kept_in_hbm(down_state, up_state, reflect, screen_class), screen_values, freq_index, hx, hy)
    fixed = (screen, refl, phase, hx, hy)
    in_inner_1, q_out_inner_1 = call(ahead_kernel, [VMEM] * 7, [VMEM] * 2, [plane] * 2, buffers(2) + [work(fronts)])(
        partner_0, q_in_outer_0, *fixed
    )
    partner_1 = to_partner(in_inner_1)
    in_outer_1, out_outer_1, q_arrived = call(edge_kernel, [VMEM] * 8, [VMEM] * 3, [plane] * 3, [work(fronts)])(
        arrived_0, source, q_out_inner_0, *fixed
    )
    arrived_1 = to_beyond(out_outer_1)
    in_inner_2, out_inner_2 = call(
        inner_kernel, [VMEM] * 7, [VMEM] * 2, [plane] * 2, buffers(2) + [work(2 * fronts)]
    )(in_outer_1, partner_1, *fixed)
    partner_2 = to_partner(in_inner_2)
    in_outer_2, last_far, last_near = call(
        last_edge_kernel, [VMEM] * 8, [VMEM] * 3, [plane] + [half_plane] * 2, buffers(2) + [work(fronts)]
    )(arrived_1, source, q_out_inner_1, *fixed)
    last_far = to_beyond(last_far)
    last_near = to_beyond(last_near)
    inner_in, inner_out, inner_terms, q_out_inner_2 = call(
        last_inner_kernel,
        [VMEM] * 8,
        [VMEM] * 4,
        [plane] * 2 + [jax.ShapeDtypeStruct((rows_x, rows_y), F32), plane],
        buffers(2) + [work(3 * fronts)],
    )(in_outer_2, partner_2, out_inner_2, *fixed)
    far_in, far_out, terms = call(
        far_rows_kernel,
        [VMEM] * 6,
        [VMEM] * 3,
        [half_plane] * 2 + [jax.ShapeDtypeStruct((2, half, rows_y), BF16)],
    )(last_far, q_arrived, q_out_inner_2, screen, refl, inner_terms)
    other = across(terms) if shots == 2 else jnp.zeros_like(terms)
    down, up = call(home_kernel, [VMEM] * 4, [HBM] * 2, [state] * 2, [dma((2, 2))])(
        inner_in, inner_out, far_in, far_out
    )
    down, up, gradient = call(
        functools.partial(near_rows_kernel, scale),
        [VMEM] * 7 + [HBM] * 2,
        [HBM] * 3,
        [state, state, jax.ShapeDtypeStruct((2, half, rows_y), F32)],
        buffers(2, half_plane) + [pltpu.VMEM((2, half, rows_y), F32), dma((2, 2))],
        input_output_aliases={7: 0, 8: 1},
    )(last_near, q_arrived, q_out_inner_2, screen, refl, inner_terms, other, down, up)
    if shots != 2:
        terms = scale * terms.astype(F32)
        far = jnp.where(odd_place() == 0, terms, terms[::-1])
        top = lax.rem(lax.axis_index("shot"), 2) == 0
        whole = jnp.concatenate([jnp.where(top, gradient, far), jnp.where(top, far, gradient)], axis=1)
        gradient = lax.psum_scatter(whole.astype(BF16), "shot", scatter_dimension=1, tiled=True).astype(F32)
    return (down, up, gradient)


def solution(mesh):
    return jax.shard_map(
        per_device,
        mesh=mesh,
        in_specs=(
            P("depth", "shot", None, None, None),
            P("depth", "shot", None, None, None),
            P("shot", None, None, None),
            P("depth", None, None),
            P("depth", None, None),
            P(),
            P("shot"),
        ),
        out_specs=(
            P("depth", "shot", None, None, None),
            P("depth", "shot", None, None, None),
            P("depth", "shot", None),
        ),
        check_vma=False,
    )
```

```python
import functools
import math

import jax
import jax.numpy as jnp
import numpy as np
from jax import lax
from jax.experimental import pallas as pl
from jax.experimental.pallas import tpu as pltpu
from jax.sharding import PartitionSpec as P

HOPS = 3
NCLASS = 16
NFREQ = 128
F32 = jnp.float32
BF16 = jnp.bfloat16
VMEM = pl.BlockSpec(memory_space=pltpu.VMEM)
HBM = pl.BlockSpec(memory_space=pltpu.HBM)
SMEM = pl.BlockSpec(memory_space=pltpu.SMEM)
PARAMS = pltpu.CompilerParams(vmem_limit_bytes=28 * 2**20)


def passed_along(block, axis, distance):
    devices = range(lax.axis_size(axis))
    route = [(i - distance, i) for i in devices if i - distance in devices]
    return lax.ppermute(block, axis, route)


def dft_tables(length):
    counter = jnp.arange(length, dtype=jnp.int32)
    product = counter[:, None] * counter[None, :] % length
    angles = 2.0 * math.pi / length * product.astype(jnp.float32)
    return (jnp.cos(angles).astype(jnp.bfloat16), jnp.sin(angles).astype(jnp.bfloat16))


def wavenumbers(length):
    counter = jnp.arange(length, dtype=jnp.int32)
    wrapped = jnp.where(counter >= length // 2, counter - length, counter)
    return 2.0 * math.pi / length * wrapped.astype(jnp.float32)


def propagate(planes, phase_re, phase_im, tables):
    fwd_left, fwd_right, inv_left, inv_right = tables
    first = jnp.einsum(
        "cdjk,...dkl->...cjl", fwd_left, planes, preferred_element_type=jnp.float32
    ).astype(jnp.bfloat16)
    second = jnp.einsum("...djl,dclm->...cjm", first, fwd_right, preferred_element_type=jnp.float32)
    real_part = second[..., 0, :, :]
    imag_part = second[..., 1, :, :]
    turned = jnp.stack(
        [real_part * phase_re - imag_part * phase_im, real_part * phase_im + imag_part * phase_re],
        axis=-3,
    ).astype(jnp.bfloat16)
    third = jnp.einsum(
        "cdjk,...dkl->...cjl", inv_left, turned, preferred_element_type=jnp.float32
    ).astype(jnp.bfloat16)
    return jnp.einsum(
        "...djl,dclm->...cjm", third, inv_right, preferred_element_type=jnp.float32
    ).astype(jnp.bfloat16)


def trade(down_edge, up_edge):
    got_down = passed_along(down_edge, "depth", 1)
    got_up = passed_along(up_edge, "depth", -1)
    return (got_down, got_up)


def per_device_plain(down_state, up_state, source, reflect, screen_class, screen_values, freq_index):
    levels = down_state.shape[0]
    rows_x = down_state.shape[3]
    rows_y = down_state.shape[4]
    front_count = down_state.shape[1]
    depth_rank = lax.axis_index("depth")
    scale = 1.0 / math.sqrt(front_count * lax.axis_size("shot"))
    cos_x, sin_x = dft_tables(rows_x)
    cos_y, sin_y = dft_tables(rows_y)
    tables = (
        jnp.stack([jnp.stack([cos_x, sin_x]), jnp.stack([-sin_x, cos_x])]),
        jnp.stack([jnp.stack([cos_y, -sin_y]), jnp.stack([sin_y, cos_y])]),
        jnp.stack([jnp.stack([cos_x, -sin_x]), jnp.stack([sin_x, cos_x])]),
        jnp.stack([jnp.stack([cos_y, sin_y]), jnp.stack([-sin_y, cos_y])]),
    )
    kwave = 0.95 * math.pi * (freq_index.astype(jnp.float32) + 1.0) / NFREQ
    kx_wave = wavenumbers(rows_x)
    ky_wave = wavenumbers(rows_y)
    vertical = kwave[:, None, None] ** 2 - kx_wave[None, :, None] ** 2 - ky_wave[None, None, :] ** 2
    propag = jnp.sqrt(jnp.maximum(vertical, 0.0))
    damping = jnp.exp(-jnp.sqrt(jnp.maximum(-vertical, 0.0))) / (rows_x * rows_y)
    phase_re = damping * jnp.cos(propag)
    phase_im = damping * jnp.sin(propag)
    classes = jnp.arange(NCLASS, dtype=jnp.int32)
    onehot = (screen_class[None] == classes[:, None, None, None]).astype(jnp.float32)
    slowness = jnp.einsum("c,clxy->lxy", screen_values, onehot, precision=lax.Precision.HIGHEST)
    angle = kwave[None, :, None, None] * slowness[:, None]
    screen_re = jnp.cos(angle)
    screen_im = jnp.sin(angle)
    refl = reflect[:, None]
    top_slab = depth_rank == 0
    down = down_state
    up = up_state
    a_re = a_im = b_re = b_im = None
    for repeat in range(HOPS):
        down_edge = down[levels - 1]
        up_edge = up[0]
        got_down, got_up = trade(down_edge, up_edge)
        got_down = jnp.where(top_slab, source, got_down)
        moved = propagate(
            jnp.concatenate([got_down[None], down[: levels - 1], up[1:], got_up[None]], axis=0),
            phase_re,
            phase_im,
            tables,
        )
        from_above = moved[:levels]
        from_below = moved[levels:]
        qa_re = from_above[:, :, 0].astype(jnp.float32)
        qa_im = from_above[:, :, 1].astype(jnp.float32)
        qb_re = from_below[:, :, 0].astype(jnp.float32)
        qb_im = from_below[:, :, 1].astype(jnp.float32)
        a_re = screen_re * qa_re - screen_im * qa_im
        a_im = screen_re * qa_im + screen_im * qa_re
        b_re = screen_re * qb_re - screen_im * qb_im
        b_im = screen_re * qb_im + screen_im * qb_re
        down = jnp.stack(
            [(1.0 + refl) * a_re - refl * b_re, (1.0 + refl) * a_im - refl * b_im], axis=2
        ).astype(jnp.bfloat16)
        up = jnp.stack(
            [(1.0 - refl) * b_re + refl * a_re, (1.0 - refl) * b_im + refl * a_im], axis=2
        ).astype(jnp.bfloat16)
    terms = scale * jnp.sum(a_re * b_re + a_im * b_im, axis=1)
    gradient = lax.psum_scatter(
        terms.astype(jnp.bfloat16), "shot", scatter_dimension=1, tiled=True
    ).astype(jnp.float32)
    return (down, up, gradient)


def hartley(length):
    counter = np.arange(length)
    angles = 2.0 * np.pi / length * (counter[:, None] * counter[None, :] % length)
    cosine = np.cos(angles).astype(BF16).astype(np.float32)
    sine = np.sin(angles).astype(BF16).astype(np.float32)
    return (cosine + sine).astype(BF16)


def odd_place():
    return lax.rem(lax.axis_index("depth"), 2)


def mm(left, right):
    return jnp.dot(left, right, preferred_element_type=F32)


def spread(jobs, work, hx, hy, phase):
    jobs = list(enumerate(jobs))
    for slot, (plane, _, _) in jobs:
        for part in range(2):
            work[slot, part] = mm(plane[part], hy[...]).astype(BF16)
    for slot, (_, front, _) in jobs:
        turn_re, turn_im = phase[front, 0], phase[front, 1]
        part_re = mm(hx[...], work[slot, 0])
        part_im = mm(hx[...], work[slot, 1])
        work[slot, 0] = (part_re * turn_re - part_im * turn_im).astype(BF16)
        work[slot, 1] = (part_re * turn_im + part_im * turn_re).astype(BF16)
    for slot, _ in jobs:
        for part in range(2):
            work[slot, part] = mm(hx[...], work[slot, part]).astype(BF16)
    for slot, (_, _, target) in jobs:
        for part in range(2):
            target[part] = mm(work[slot, part], hy[...]).astype(BF16)


def screened(real_part, imag_part, screen_re, screen_im):
    return (
        screen_re * real_part - screen_im * imag_part,
        screen_re * imag_part + screen_im * real_part,
    )


def mixed(a_re, a_im, b_re, b_im, refl, screen_re, screen_im):
    a_re, a_im, b_re, b_im = (part.astype(F32) for part in (a_re, a_im, b_re, b_im))
    step_re = refl * (a_re - b_re)
    step_im = refl * (a_im - b_im)
    inward = screened(a_re + step_re, a_im + step_im, screen_re, screen_im)
    outward = screened(b_re + step_re, b_im + step_im, screen_re, screen_im)
    return tuple(part.astype(BF16) for part in inward + outward)


def put(target, real_part, imag_part):
    target[0] = real_part.astype(BF16)
    target[1] = imag_part.astype(BF16)


def half_rows(of, half):
    shot = lax.rem(lax.axis_index("shot"), 2)
    return pl.ds(pl.multiple_of((shot if of == 0 else 1 - shot) * half, half), half)


def edges_kernel(down, up, outward_outer, inward_inner, sems):
    levels = down.shape[0]
    odd = odd_place()

    def fetch(first, second):
        pltpu.make_async_copy(first, outward_outer, sems.at[0]).start()
        pltpu.make_async_copy(second, inward_inner, sems.at[1]).start()

    @pl.when(odd == 0)
    def _():
        fetch(up.at[0], down.at[levels - 1])

    @pl.when(odd == 1)
    def _():
        fetch(down.at[levels - 1], up.at[0])

    pltpu.make_async_copy(up.at[0], outward_outer, sems.at[0]).wait()
    pltpu.make_async_copy(up.at[0], inward_inner, sems.at[1]).wait()


def class_rows(slowness, kwave, shape):
    lanes = lax.broadcasted_iota(jnp.int32, shape, 1)
    table = jnp.zeros(shape, F32)
    for entry in range(NCLASS):
        table = jnp.where(lanes == entry, slowness[entry], table)
    angle = kwave * table
    return jnp.cos(angle), jnp.sin(angle)


def look_up(table, classes):
    width = 128
    rows = classes.shape[0]
    wide = jnp.broadcast_to(table[:1], (rows, width))
    pieces = [
        jnp.take_along_axis(wide, classes[:, start : start + width], axis=1, mode="promise_in_bounds")
        for start in range(0, classes.shape[1], width)
    ]
    return jnp.concatenate(pieces, axis=1)


def front_wave(freq, front):
    return 0.95 * math.pi * (freq[front].astype(F32) + 1.0) / NFREQ


def series(square, shift):
    total = jnp.full_like(square, 1.0 / math.factorial(18 + shift))
    for order in range(16, -1, -2):
        total = 1.0 / math.factorial(order + shift) - square * total
    return total


def setup_kernel(
    down, up, reflect, classes_in, slowness, freq, hx, hy,
    q_out_inner, q_in_outer, screen, phase, refl,
    fields, klass, work, sems,
):
    fronts = q_out_inner.shape[0]
    rows_x, rows_y = refl.shape[1:]
    odd = odd_place()
    fixed = [
        pltpu.make_async_copy(reflect.at[odd], refl.at[0], sems.at[2]),
        pltpu.make_async_copy(reflect.at[1 - odd], refl.at[1], sems.at[3]),
        pltpu.make_async_copy(classes_in.at[odd], klass.at[0], sems.at[4]),
        pltpu.make_async_copy(classes_in.at[1 - odd], klass.at[1], sems.at[5]),
    ]
    for copy in fixed:
        copy.start()

    @pl.when(odd == 0)
    def _():
        pltpu.make_async_copy(down.at[0], fields.at[0], sems.at[0]).start()
        pltpu.make_async_copy(up.at[1], fields.at[1], sems.at[1]).start()

    @pl.when(odd == 1)
    def _():
        pltpu.make_async_copy(up.at[1], fields.at[0], sems.at[0]).start()
        pltpu.make_async_copy(down.at[0], fields.at[1], sems.at[1]).start()

    def squares(length, axis):
        counter = lax.broadcasted_iota(jnp.int32, (rows_x, rows_y), axis)
        wrapped = jnp.where(counter >= length // 2, counter - length, counter)
        wave = 2.0 * math.pi / length * wrapped.astype(F32)
        return wave * wave

    lateral = squares(rows_x, 0) + squares(rows_y, 1)
    level_out = 1.0 / (rows_x * rows_y)
    for front in range(fronts):
        kwave = front_wave(freq, front)
        vertical = kwave * kwave - lateral
        travels = vertical > 0.0
        square = jnp.maximum(vertical, 0.0)
        root = jnp.sqrt(jnp.abs(vertical))
        phase[front, 0] = jnp.where(travels, series(square, 0), jnp.exp(-root)) * level_out
        phase[front, 1] = jnp.where(travels, root * series(square, 1), 0.0) * level_out
    for copy in fixed:
        copy.wait()
    sign = jnp.where(odd == 0, 1.0, -1.0).astype(F32)
    for level in range(2):
        refl[level] = sign * refl[level]
    for front in range(fronts):
        cos_row, sin_row = class_rows(slowness, front_wave(freq, front), (8, 128))
        for level in range(2):
            screen[level, front, 0] = look_up(cos_row, klass[level])
            screen[level, front, 1] = look_up(sin_row, klass[level])
    pltpu.make_async_copy(down.at[0], fields.at[0], sems.at[0]).wait()
    pltpu.make_async_copy(down.at[0], fields.at[1], sems.at[1]).wait()
    jobs = [(fields.at[1, front], front, q_out_inner.at[front]) for front in range(fronts)]
    jobs += [(fields.at[0, front], front, q_in_outer.at[front]) for front in range(fronts)]
    spread(jobs, work, hx, hy, phase)


def ahead_kernel(
    partner, q_in_outer, screen, refl, phase, hx, hy,
    inward_inner, q_out_inner,
    q_field, field, work,
):
    everyone = range(partner.shape[0])
    spread([(partner.at[front], front, q_field.at[front]) for front in everyone], work, hx, hy, phase)
    for front in everyone:
        in_re, in_im, out_re, out_im = mixed(
            q_in_outer[front, 0], q_in_outer[front, 1], q_field[front, 0], q_field[front, 1],
            refl[1], screen[1, front, 0], screen[1, front, 1],
        )
        put(inward_inner.at[front], in_re, in_im)
        put(field.at[front], out_re, out_im)
    spread([(field.at[front], front, q_out_inner.at[front]) for front in everyone], work, hx, hy, phase)


def outer_step(arrived, source, q_out_inner, screen, refl, phase, hx, hy, inward, outward, q_arrived, work):
    everyone = range(arrived.shape[0])
    first = lax.axis_index("depth") == 0
    for front in everyone:
        put(inward.at[front], *(jnp.where(first, source[front, part], arrived[front, part]) for part in range(2)))
    spread([(inward.at[front], front, q_arrived.at[front]) for front in everyone], work, hx, hy, phase)
    for front in everyone:
        in_re, in_im, out_re, out_im = mixed(
            q_arrived[front, 0], q_arrived[front, 1], q_out_inner[front, 0], q_out_inner[front, 1],
            refl[0], screen[0, front, 0], screen[0, front, 1],
        )
        put(inward.at[front], in_re, in_im)
        put(outward.at[front], out_re, out_im)


def edge_kernel(
    arrived, source, q_out_inner, screen, refl, phase, hx, hy,
    inward, outward, q_arrived,
    work,
):
    outer_step(arrived, source, q_out_inner, screen, refl, phase, hx, hy, inward, outward, q_arrived, work)


def last_edge_kernel(
    arrived, source, q_out_inner, screen, refl, phase, hx, hy, after,
    inward, last_far, last_near,
    outward, q_field, work,
):
    del after
    everyone = range(arrived.shape[0])
    half = arrived.shape[2] // 2
    far_bottom = lax.rem(lax.axis_index("shot"), 2) == 0
    outer_step(arrived, source, q_out_inner, screen, refl, phase, hx, hy, inward, outward, q_field, work)
    spread([(outward.at[front], front, q_field.at[front]) for front in everyone], work, hx, hy, phase)
    for front in everyone:
        for part in range(2):
            top, bottom = q_field[front, part, :half], q_field[front, part, half:]
            last_far[front, part] = jnp.where(far_bottom, bottom, top)
            last_near[front, part] = jnp.where(far_bottom, top, bottom)


def inner_kernel(
    inward_outer, partner, screen, refl, phase, hx, hy,
    inward, outward,
    q_inward, q_partner, work,
):
    everyone = range(partner.shape[0])
    jobs = [(inward_outer.at[front], front, q_inward.at[front]) for front in everyone]
    jobs += [(partner.at[front], front, q_partner.at[front]) for front in everyone]
    spread(jobs, work, hx, hy, phase)
    for front in everyone:
        in_re, in_im, out_re, out_im = mixed(
            q_inward[front, 0], q_inward[front, 1], q_partner[front, 0], q_partner[front, 1],
            refl[1], screen[1, front, 0], screen[1, front, 1],
        )
        put(inward.at[front], in_re, in_im)
        put(outward.at[front], out_re, out_im)


def spread_kernel(fields, phase, hx, hy, q_fields, work):
    everyone = range(fields.shape[0])
    spread([(fields.at[front], front, q_fields.at[front]) for front in everyone], work, hx, hy, phase)


def last_inner_kernel(
    inward_outer, partner, screen, refl, phase, hx, hy,
    inward, outward, terms, far_terms,
    q_inward, q_partner, work,
):
    everyone = range(inward_outer.shape[0])
    jobs = [(inward_outer.at[front], front, q_inward.at[front]) for front in everyone]
    jobs += [(partner.at[front], front, q_partner.at[front]) for front in everyone]
    spread(jobs, work, hx, hy, phase)
    total = None
    for front in everyone:
        a_re, a_im = (q_inward[front, part].astype(F32) for part in range(2))
        b_re, b_im = (q_partner[front, part].astype(F32) for part in range(2))
        in_re, in_im, out_re, out_im = mixed(
            a_re, a_im, b_re, b_im, refl[1], screen[1, front, 0], screen[1, front, 1]
        )
        put(inward.at[front], in_re, in_im)
        put(outward.at[front], out_re, out_im)
        term = a_re * b_re + a_im * b_im
        total = term if total is None else total + term
    terms[...] = total
    far_terms[...] = terms[half_rows(1, far_terms.shape[0]), :].astype(BF16)


def far_rows_kernel(last, q_arrived, q_out_inner, screen, refl, after, inward, outward, terms):
    del after
    _, total = outer_rows(1, last, q_arrived, q_out_inner, screen, refl, inward, outward)
    terms[...] = total.astype(BF16)


def outer_rows(of, last, q_arrived, q_out_inner, screen, refl, inward, outward):
    fronts, _, half, _ = last.shape
    first = lax.axis_index("depth") == 0
    rows = half_rows(of, half)
    total = None
    for front in range(fronts):
        a_re, a_im = (
            jnp.where(first, q_arrived[front, part, rows, :], last[front, part]).astype(F32)
            for part in range(2)
        )
        b_re, b_im = (q_out_inner[front, part, rows, :].astype(F32) for part in range(2))
        in_re, in_im, out_re, out_im = mixed(
            a_re, a_im, b_re, b_im, refl[0, rows, :], screen[0, front, 0, rows, :], screen[0, front, 1, rows, :]
        )
        put(inward.at[front], in_re, in_im)
        put(outward.at[front], out_re, out_im)
        term = a_re * b_re + a_im * b_im
        total = term if total is None else total + term
    return rows, total


def send_home(level, rows, inward, outward, down_out, up_out, sems):
    odd = odd_place()

    def copies(place, inward_out, outward_out):
        return [
            pltpu.make_async_copy(inward, inward_out.at[place, :, :, rows, :], sems.at[0]),
            pltpu.make_async_copy(outward, outward_out.at[place, :, :, rows, :], sems.at[1]),
        ]

    @pl.when(odd == 0)
    def _():
        for copy in copies(level, down_out, up_out):
            copy.start()

    @pl.when(odd == 1)
    def _():
        for copy in copies(1 - level, up_out, down_out):
            copy.start()

    return copies(0, down_out, up_out)


def near_rows_kernel(
    last, q_arrived, q_out_inner, screen, refl, inner_in, inner_out, far_in, far_out,
    down_out, up_out, terms,
    inward, outward, sems,
):
    rows_x, half = inner_in.shape[2], far_in.shape[2]
    waits = send_home(1, pl.ds(0, rows_x), inner_in, inner_out, down_out, up_out, sems.at[0])
    waits += send_home(0, half_rows(1, half), far_in, far_out, down_out, up_out, sems.at[1])
    rows, total = outer_rows(0, last, q_arrived, q_out_inner, screen, refl, inward, outward)
    waits += send_home(0, rows, inward, outward, down_out, up_out, sems.at[2])
    terms[...] = total
    for copy in waits:
        copy.wait()


def gradient_kernel(scale, outer_terms, inner_terms, outer_other, inner_other, gradient, sums, sems):
    odd = odd_place()
    sums[odd] = scale * (outer_terms[...] + outer_other[...].astype(F32))
    sums[1 - odd] = scale * (inner_terms[half_rows(0, sums.shape[1]), :] + inner_other[...].astype(F32))
    done = pltpu.make_async_copy(sums, gradient, sems.at[0])
    done.start()
    done.wait()


def per_device(down_state, up_state, source, reflect, screen_class, screen_values, freq_index):
    depth = lax.axis_size("depth")
    shots = lax.axis_size("shot")
    levels, fronts, parts, rows_x, rows_y = down_state.shape
    if levels != 2 or depth % 2 or shots % 2 or HOPS != 3:
        return per_device_plain(down_state, up_state, source, reflect, screen_class, screen_values, freq_index)
    scale = 1.0 / math.sqrt(fronts * shots)
    half = rows_x // 2
    hx = jnp.asarray(hartley(rows_x))
    hy = jnp.asarray(hartley(rows_y))
    partners = [(i, i ^ 1) for i in range(depth)]
    beyond = [(i, i + 1) for i in range(1, depth - 1, 2)] + [(i + 1, i) for i in range(1, depth - 1, 2)]
    to_partner = functools.partial(lax.ppermute, axis_name="depth", perm=partners)
    to_beyond = functools.partial(lax.ppermute, axis_name="depth", perm=beyond)
    across = functools.partial(lax.ppermute, axis_name="shot", perm=[(i, i ^ 1) for i in range(shots)])
    plane = jax.ShapeDtypeStruct((fronts, parts, rows_x, rows_y), BF16)
    half_plane = jax.ShapeDtypeStruct((fronts, parts, half, rows_y), BF16)
    pair = jax.ShapeDtypeStruct((2, rows_x, rows_y), F32)
    turns = jax.ShapeDtypeStruct((fronts, parts, rows_x, rows_y), F32)
    screens = jax.ShapeDtypeStruct((2, fronts, parts, rows_x, rows_y), F32)
    state = jax.ShapeDtypeStruct(down_state.shape, BF16)
    dma = pltpu.SemaphoreType.DMA

    def call(kernel, in_specs, out_specs, out_shape, scratch=(), **more):
        return pl.pallas_call(
            kernel,
            in_specs=in_specs,
            out_specs=out_specs,
            out_shape=out_shape,
            scratch_shapes=list(scratch),
            compiler_params=PARAMS,
            **more,
        )

    def kept_in_hbm(*arrays):
        return [pltpu.with_memory_space_constraint(array, pltpu.HBM) for array in arrays]

    def buffers(count, shape=plane):
        return [pltpu.VMEM(shape.shape, shape.dtype)] * count

    def work(slots):
        return pltpu.VMEM((slots, *plane.shape[1:]), BF16)

    out_outer, in_inner = call(edges_kernel, [HBM] * 2, [VMEM] * 2, [plane] * 2, [dma((2,))])(
        *kept_in_hbm(down_state, up_state)
    )
    arrived_0 = to_beyond(out_outer)
    partner_0 = to_partner(in_inner)
    q_out_inner_0, q_in_outer_0, screen, phase, refl = call(
        setup_kernel,
        [HBM] * 4 + [SMEM] * 2 + [VMEM] * 2,
        [VMEM] * 5,
        [plane] * 2 + [screens, turns, pair],
        [
            pltpu.VMEM((2, *plane.shape), BF16),
            pltpu.VMEM((2, rows_x, rows_y), jnp.int32),
            work(2 * fronts),
            dma((6,)),
        ],
    )(*kept_in_hbm(down_state, up_state, reflect, screen_class), screen_values, freq_index, hx, hy)
    fixed = (screen, refl, phase, hx, hy)
    in_inner_1, q_out_inner_1 = call(ahead_kernel, [VMEM] * 7, [VMEM] * 2, [plane] * 2, buffers(2) + [work(fronts)])(
        partner_0, q_in_outer_0, *fixed
    )
    partner_1 = to_partner(in_inner_1)
    in_outer_1, out_outer_1, q_arrived = call(edge_kernel, [VMEM] * 8, [VMEM] * 3, [plane] * 3, [work(fronts)])(
        arrived_0, source, q_out_inner_0, *fixed
    )
    arrived_1 = to_beyond(out_outer_1)
    in_inner_2, out_inner_2 = call(
        inner_kernel, [VMEM] * 7, [VMEM] * 2, [plane] * 2, buffers(2) + [work(2 * fronts)]
    )(in_outer_1, partner_1, *fixed)
    partner_2 = to_partner(in_inner_2)
    q_out_inner_2 = call(spread_kernel, [VMEM] * 4, VMEM, plane, [work(fronts)])(out_inner_2, phase, hx, hy)
    in_outer_2, last_far, last_near = call(
        last_edge_kernel,
        [VMEM] * 8 + [pl.BlockSpec(memory_space=pl.ANY)],
        [VMEM] * 3,
        [plane] + [half_plane] * 2,
        buffers(2) + [work(fronts)],
    )(arrived_1, source, q_out_inner_1, *fixed, q_out_inner_2)
    last_far = to_beyond(last_far)
    last_near = to_beyond(last_near)
    half_sum = jax.ShapeDtypeStruct((half, rows_y), BF16)
    inner_in, inner_out, inner_terms, inner_far = call(
        last_inner_kernel,
        [VMEM] * 7,
        [VMEM] * 4,
        [plane] * 2 + [jax.ShapeDtypeStruct((rows_x, rows_y), F32), half_sum],
        buffers(2) + [work(2 * fronts)],
    )(in_outer_2, partner_2, *fixed)
    inner_other = across(inner_far) if shots == 2 else jnp.zeros_like(inner_far)
    far_in, far_out, outer_far = call(
        far_rows_kernel,
        [VMEM] * 5 + [pl.BlockSpec(memory_space=pl.ANY)],
        [VMEM] * 3,
        [half_plane] * 2 + [half_sum],
    )(last_far, q_arrived, q_out_inner_2, screen, refl, inner_terms)
    outer_other = across(outer_far) if shots == 2 else jnp.zeros_like(outer_far)
    down, up, outer_near = call(
        near_rows_kernel,
        [VMEM] * 9,
        [HBM] * 2 + [VMEM],
        [state, state, jax.ShapeDtypeStruct((half, rows_y), F32)],
        buffers(2, half_plane) + [dma((3, 2))],
    )(last_near, q_arrived, q_out_inner_2, screen, refl, inner_in, inner_out, far_in, far_out)
    gradient = call(
        functools.partial(gradient_kernel, scale),
        [VMEM] * 4,
        HBM,
        jax.ShapeDtypeStruct((2, half, rows_y), F32),
        [pltpu.VMEM((2, half, rows_y), F32), dma((1,))],
    )(outer_near, inner_terms, outer_other, inner_other)
    if shots != 2:
        terms = scale * jnp.stack([outer_far, inner_far]).astype(F32)
        far = jnp.where(odd_place() == 0, terms, terms[::-1])
        top = lax.rem(lax.axis_index("shot"), 2) == 0
        whole = jnp.concatenate([jnp.where(top, gradient, far), jnp.where(top, far, gradient)], axis=1)
        gradient = lax.psum_scatter(whole.astype(BF16), "shot", scatter_dimension=1, tiled=True).astype(F32)
    return (down, up, gradient)


def solution(mesh):
    return jax.shard_map(
        per_device,
        mesh=mesh,
        in_specs=(
            P("depth", "shot", None, None, None),
            P("depth", "shot", None, None, None),
            P("shot", None, None, None),
            P("depth", None, None),
            P("depth", None, None),
            P(),
            P("shot"),
        ),
        out_specs=(
            P("depth", "shot", None, None, None),
            P("depth", "shot", None, None, None),
            P("depth", "shot", None),
        ),
        check_vma=False,
    )
```

```python
import functools
import math

import jax
import jax.numpy as jnp
import numpy as np
from jax import lax
from jax.experimental import pallas as pl
from jax.experimental.pallas import tpu as pltpu
from jax.sharding import PartitionSpec as P

HOPS = 3
NCLASS = 16
NFREQ = 128
F32 = jnp.float32
BF16 = jnp.bfloat16
VMEM = pl.BlockSpec(memory_space=pltpu.VMEM)
HBM = pl.BlockSpec(memory_space=pltpu.HBM)
SMEM = pl.BlockSpec(memory_space=pltpu.SMEM)
PARAMS = pltpu.CompilerParams(vmem_limit_bytes=28 * 2**20)


def passed_along(block, axis, distance):
    devices = range(lax.axis_size(axis))
    route = [(i - distance, i) for i in devices if i - distance in devices]
    return lax.ppermute(block, axis, route)


def dft_tables(length):
    counter = jnp.arange(length, dtype=jnp.int32)
    product = counter[:, None] * counter[None, :] % length
    angles = 2.0 * math.pi / length * product.astype(jnp.float32)
    return (jnp.cos(angles).astype(jnp.bfloat16), jnp.sin(angles).astype(jnp.bfloat16))


def wavenumbers(length):
    counter = jnp.arange(length, dtype=jnp.int32)
    wrapped = jnp.where(counter >= length // 2, counter - length, counter)
    return 2.0 * math.pi / length * wrapped.astype(jnp.float32)


def propagate(planes, phase_re, phase_im, tables):
    fwd_left, fwd_right, inv_left, inv_right = tables
    first = jnp.einsum(
        "cdjk,...dkl->...cjl", fwd_left, planes, preferred_element_type=jnp.float32
    ).astype(jnp.bfloat16)
    second = jnp.einsum("...djl,dclm->...cjm", first, fwd_right, preferred_element_type=jnp.float32)
    real_part = second[..., 0, :, :]
    imag_part = second[..., 1, :, :]
    turned = jnp.stack(
        [real_part * phase_re - imag_part * phase_im, real_part * phase_im + imag_part * phase_re],
        axis=-3,
    ).astype(jnp.bfloat16)
    third = jnp.einsum(
        "cdjk,...dkl->...cjl", inv_left, turned, preferred_element_type=jnp.float32
    ).astype(jnp.bfloat16)
    return jnp.einsum(
        "...djl,dclm->...cjm", third, inv_right, preferred_element_type=jnp.float32
    ).astype(jnp.bfloat16)


def trade(down_edge, up_edge):
    got_down = passed_along(down_edge, "depth", 1)
    got_up = passed_along(up_edge, "depth", -1)
    return (got_down, got_up)


def per_device_plain(down_state, up_state, source, reflect, screen_class, screen_values, freq_index):
    levels = down_state.shape[0]
    rows_x = down_state.shape[3]
    rows_y = down_state.shape[4]
    front_count = down_state.shape[1]
    depth_rank = lax.axis_index("depth")
    scale = 1.0 / math.sqrt(front_count * lax.axis_size("shot"))
    cos_x, sin_x = dft_tables(rows_x)
    cos_y, sin_y = dft_tables(rows_y)
    tables = (
        jnp.stack([jnp.stack([cos_x, sin_x]), jnp.stack([-sin_x, cos_x])]),
        jnp.stack([jnp.stack([cos_y, -sin_y]), jnp.stack([sin_y, cos_y])]),
        jnp.stack([jnp.stack([cos_x, -sin_x]), jnp.stack([sin_x, cos_x])]),
        jnp.stack([jnp.stack([cos_y, sin_y]), jnp.stack([-sin_y, cos_y])]),
    )
    kwave = 0.95 * math.pi * (freq_index.astype(jnp.float32) + 1.0) / NFREQ
    kx_wave = wavenumbers(rows_x)
    ky_wave = wavenumbers(rows_y)
    vertical = kwave[:, None, None] ** 2 - kx_wave[None, :, None] ** 2 - ky_wave[None, None, :] ** 2
    propag = jnp.sqrt(jnp.maximum(vertical, 0.0))
    damping = jnp.exp(-jnp.sqrt(jnp.maximum(-vertical, 0.0))) / (rows_x * rows_y)
    phase_re = damping * jnp.cos(propag)
    phase_im = damping * jnp.sin(propag)
    classes = jnp.arange(NCLASS, dtype=jnp.int32)
    onehot = (screen_class[None] == classes[:, None, None, None]).astype(jnp.float32)
    slowness = jnp.einsum("c,clxy->lxy", screen_values, onehot, precision=lax.Precision.HIGHEST)
    angle = kwave[None, :, None, None] * slowness[:, None]
    screen_re = jnp.cos(angle)
    screen_im = jnp.sin(angle)
    refl = reflect[:, None]
    top_slab = depth_rank == 0
    down = down_state
    up = up_state
    a_re = a_im = b_re = b_im = None
    for repeat in range(HOPS):
        down_edge = down[levels - 1]
        up_edge = up[0]
        got_down, got_up = trade(down_edge, up_edge)
        got_down = jnp.where(top_slab, source, got_down)
        moved = propagate(
            jnp.concatenate([got_down[None], down[: levels - 1], up[1:], got_up[None]], axis=0),
            phase_re,
            phase_im,
            tables,
        )
        from_above = moved[:levels]
        from_below = moved[levels:]
        qa_re = from_above[:, :, 0].astype(jnp.float32)
        qa_im = from_above[:, :, 1].astype(jnp.float32)
        qb_re = from_below[:, :, 0].astype(jnp.float32)
        qb_im = from_below[:, :, 1].astype(jnp.float32)
        a_re = screen_re * qa_re - screen_im * qa_im
        a_im = screen_re * qa_im + screen_im * qa_re
        b_re = screen_re * qb_re - screen_im * qb_im
        b_im = screen_re * qb_im + screen_im * qb_re
        down = jnp.stack(
            [(1.0 + refl) * a_re - refl * b_re, (1.0 + refl) * a_im - refl * b_im], axis=2
        ).astype(jnp.bfloat16)
        up = jnp.stack(
            [(1.0 - refl) * b_re + refl * a_re, (1.0 - refl) * b_im + refl * a_im], axis=2
        ).astype(jnp.bfloat16)
    terms = scale * jnp.sum(a_re * b_re + a_im * b_im, axis=1)
    gradient = lax.psum_scatter(
        terms.astype(jnp.bfloat16), "shot", scatter_dimension=1, tiled=True
    ).astype(jnp.float32)
    return (down, up, gradient)


def hartley(length):
    counter = np.arange(length)
    angles = 2.0 * np.pi / length * (counter[:, None] * counter[None, :] % length)
    cosine = np.cos(angles).astype(BF16).astype(np.float32)
    sine = np.sin(angles).astype(BF16).astype(np.float32)
    return (cosine + sine).astype(BF16)


def odd_place():
    return lax.rem(lax.axis_index("depth"), 2)


def mm(left, right):
    return jnp.dot(left, right, preferred_element_type=F32)


def spread(jobs, work, hx, hy, phase):
    jobs = list(enumerate(jobs))
    for slot, (plane, _, _) in jobs:
        for part in range(2):
            work[slot, part] = mm(plane(part) if callable(plane) else plane[part], hy[...]).astype(BF16)
    for slot, (_, front, _) in jobs:
        turn_re, turn_im = phase[front, 0], phase[front, 1]
        part_re = mm(hx[...], work[slot, 0])
        part_im = mm(hx[...], work[slot, 1])
        work[slot, 0] = (part_re * turn_re - part_im * turn_im).astype(BF16)
        work[slot, 1] = (part_re * turn_im + part_im * turn_re).astype(BF16)
    for slot, _ in jobs:
        for part in range(2):
            work[slot, part] = mm(hx[...], work[slot, part]).astype(BF16)
    for slot, (_, _, target) in jobs:
        for part in range(2):
            if isinstance(target, list):
                for rows, piece in target:
                    piece[part] = mm(work[slot, part, rows, :], hy[...]).astype(BF16)
            else:
                target[part] = mm(work[slot, part], hy[...]).astype(BF16)


def screened(real_part, imag_part, screen_re, screen_im):
    return (
        screen_re * real_part - screen_im * imag_part,
        screen_re * imag_part + screen_im * real_part,
    )


def mixed(a_re, a_im, b_re, b_im, refl, screen_re, screen_im, waves="both"):
    a_re, a_im, b_re, b_im = (part.astype(F32) for part in (a_re, a_im, b_re, b_im))
    step_re = refl * (a_re - b_re)
    step_im = refl * (a_im - b_im)
    fields = ()
    if waves != "outward":
        fields += screened(a_re + step_re, a_im + step_im, screen_re, screen_im)
    if waves != "inward":
        fields += screened(b_re + step_re, b_im + step_im, screen_re, screen_im)
    return fields


def put(target, real_part, imag_part):
    target[0] = real_part.astype(BF16)
    target[1] = imag_part.astype(BF16)


def half_rows(of, half):
    shot = lax.rem(lax.axis_index("shot"), 2)
    return pl.ds(pl.multiple_of((shot if of == 0 else 1 - shot) * half, half), half)


def edges_kernel(down, up, outward_outer, inward_inner, sems):
    levels = down.shape[0]
    odd = odd_place()

    def fetch(first, second):
        pltpu.make_async_copy(first, outward_outer, sems.at[0]).start()
        pltpu.make_async_copy(second, inward_inner, sems.at[1]).start()

    @pl.when(odd == 0)
    def _():
        fetch(up.at[0], down.at[levels - 1])

    @pl.when(odd == 1)
    def _():
        fetch(down.at[levels - 1], up.at[0])

    pltpu.make_async_copy(up.at[0], outward_outer, sems.at[0]).wait()
    pltpu.make_async_copy(up.at[0], inward_inner, sems.at[1]).wait()


def class_rows(slowness, kwave, shape):
    lanes = lax.broadcasted_iota(jnp.int32, shape, 1)
    table = jnp.zeros(shape, F32)
    for entry in range(NCLASS):
        table = jnp.where(lanes == entry, slowness[entry], table)
    angle = kwave * table
    return jnp.cos(angle), jnp.sin(angle)


def look_up(table, classes):
    width = 128
    rows = classes.shape[0]
    wide = jnp.broadcast_to(table[:1], (rows, width))
    pieces = [
        jnp.take_along_axis(wide, classes[:, start : start + width], axis=1, mode="promise_in_bounds")
        for start in range(0, classes.shape[1], width)
    ]
    return jnp.concatenate(pieces, axis=1)


def front_wave(freq, front):
    return 0.95 * math.pi * (freq[front].astype(F32) + 1.0) / NFREQ


def series(square, shift):
    total = jnp.full_like(square, 1.0 / math.factorial(18 + shift))
    for order in range(16, -1, -2):
        total = 1.0 / math.factorial(order + shift) - square * total
    return total


def setup_kernel(
    down, up, reflect, classes_in, slowness, freq, hx, hy,
    q_out_inner, q_in_outer, screen, phase, refl,
    fields, klass, work, sems,
):
    fronts = q_out_inner.shape[0]
    rows_x, rows_y = refl.shape[1:]
    odd = odd_place()
    fixed = [
        pltpu.make_async_copy(reflect.at[odd], refl.at[0], sems.at[2]),
        pltpu.make_async_copy(reflect.at[1 - odd], refl.at[1], sems.at[3]),
        pltpu.make_async_copy(classes_in.at[odd], klass.at[0], sems.at[4]),
        pltpu.make_async_copy(classes_in.at[1 - odd], klass.at[1], sems.at[5]),
    ]
    for copy in fixed:
        copy.start()

    @pl.when(odd == 0)
    def _():
        pltpu.make_async_copy(down.at[0], fields.at[0], sems.at[0]).start()
        pltpu.make_async_copy(up.at[1], fields.at[1], sems.at[1]).start()

    @pl.when(odd == 1)
    def _():
        pltpu.make_async_copy(up.at[1], fields.at[0], sems.at[0]).start()
        pltpu.make_async_copy(down.at[0], fields.at[1], sems.at[1]).start()

    def squares(length, axis):
        counter = lax.broadcasted_iota(jnp.int32, (rows_x, rows_y), axis)
        wrapped = jnp.where(counter >= length // 2, counter - length, counter)
        wave = 2.0 * math.pi / length * wrapped.astype(F32)
        return wave * wave

    lateral = squares(rows_x, 0) + squares(rows_y, 1)
    level_out = 1.0 / (rows_x * rows_y)
    for front in range(fronts):
        kwave = front_wave(freq, front)
        vertical = kwave * kwave - lateral
        travels = vertical > 0.0
        square = jnp.maximum(vertical, 0.0)
        root = jnp.sqrt(jnp.abs(vertical))
        phase[front, 0] = jnp.where(travels, series(square, 0), jnp.exp(-root)) * level_out
        phase[front, 1] = jnp.where(travels, root * series(square, 1), 0.0) * level_out
    for copy in fixed:
        copy.wait()
    sign = jnp.where(odd == 0, 1.0, -1.0).astype(F32)
    for level in range(2):
        refl[level] = sign * refl[level]
    for front in range(fronts):
        cos_row, sin_row = class_rows(slowness, front_wave(freq, front), (8, 128))
        for level in range(2):
            screen[level, front, 0] = look_up(cos_row, klass[level])
            screen[level, front, 1] = look_up(sin_row, klass[level])
    pltpu.make_async_copy(down.at[0], fields.at[0], sems.at[0]).wait()
    pltpu.make_async_copy(down.at[0], fields.at[1], sems.at[1]).wait()
    jobs = [(fields.at[1, front], front, q_out_inner.at[front]) for front in range(fronts)]
    jobs += [(fields.at[0, front], front, q_in_outer.at[front]) for front in range(fronts)]
    spread(jobs, work, hx, hy, phase)


def ahead_kernel(
    partner, q_in_outer, screen, refl, phase, hx, hy,
    inward_inner, q_out_inner,
    q_field, field, work,
):
    everyone = range(partner.shape[0])
    spread([(partner.at[front], front, q_field.at[front]) for front in everyone], work, hx, hy, phase)
    for front in everyone:
        in_re, in_im, out_re, out_im = mixed(
            q_in_outer[front, 0], q_in_outer[front, 1], q_field[front, 0], q_field[front, 1],
            refl[1], screen[1, front, 0], screen[1, front, 1],
        )
        put(inward_inner.at[front], in_re, in_im)
        put(field.at[front], out_re, out_im)
    spread([(field.at[front], front, q_out_inner.at[front]) for front in everyone], work, hx, hy, phase)


def entering(arrived, source, front):
    first = lax.axis_index("depth") == 0
    return lambda part: jnp.where(first, source[front, part], arrived[front, part])


def outer_step(q_arrived, q_out_inner, screen, refl, waves, field):
    for front in range(field.shape[0]):
        put(
            field.at[front],
            *mixed(
                q_arrived[front, 0], q_arrived[front, 1], q_out_inner[front, 0], q_out_inner[front, 1],
                refl[0], screen[0, front, 0], screen[0, front, 1], waves,
            ),
        )


def edge_kernel(arrived, source, q_out_inner, screen, refl, phase, hx, hy, outward, q_arrived, work):
    everyone = range(arrived.shape[0])
    spread([(entering(arrived, source, front), front, q_arrived.at[front]) for front in everyone], work, hx, hy, phase)
    outer_step(q_arrived, q_out_inner, screen, refl, "outward", outward)


def last_edge_kernel(
    arrived, source, q_out_inner, screen, refl, phase, hx, hy, after,
    q_arrived, last_far, last_near,
    outward, work,
):
    del after
    everyone = range(arrived.shape[0])
    half = arrived.shape[2] // 2
    spread([(entering(arrived, source, front), front, q_arrived.at[front]) for front in everyone], work, hx, hy, phase)
    outer_step(q_arrived, q_out_inner, screen, refl, "outward", outward)
    jobs = [
        (outward.at[front], front, [(half_rows(1, half), last_far.at[front]), (half_rows(0, half), last_near.at[front])])
        for front in everyone
    ]
    spread(jobs, work, hx, hy, phase)


def inner_kernel(
    q_arrived, q_out_inner, partner, screen, refl, phase, hx, hy,
    inward, outward,
    field, q_inward, q_partner, work,
):
    everyone = range(partner.shape[0])
    outer_step(q_arrived, q_out_inner, screen, refl, "inward", field)
    jobs = [(partner.at[front], front, q_partner.at[front]) for front in everyone]
    jobs += [(field.at[front], front, q_inward.at[front]) for front in everyone]
    spread(jobs, work, hx, hy, phase)
    for front in everyone:
        in_re, in_im, out_re, out_im = mixed(
            q_inward[front, 0], q_inward[front, 1], q_partner[front, 0], q_partner[front, 1],
            refl[1], screen[1, front, 0], screen[1, front, 1],
        )
        put(inward.at[front], in_re, in_im)
        put(outward.at[front], out_re, out_im)


def spread_kernel(fields, phase, hx, hy, q_fields, work):
    everyone = range(fields.shape[0])
    spread([(fields.at[front], front, q_fields.at[front]) for front in everyone], work, hx, hy, phase)


def last_inner_kernel(
    q_arrived, q_out_inner, partner, screen, refl, phase, hx, hy,
    inward, outward, terms,
    field, q_inward, q_partner, work,
):
    everyone = range(partner.shape[0])
    outer_step(q_arrived, q_out_inner, screen, refl, "inward", field)
    jobs = [(partner.at[front], front, q_partner.at[front]) for front in everyone]
    jobs += [(field.at[front], front, q_inward.at[front]) for front in everyone]
    spread(jobs, work, hx, hy, phase)
    total = None
    for front in everyone:
        a_re, a_im = (q_inward[front, part].astype(F32) for part in range(2))
        b_re, b_im = (q_partner[front, part].astype(F32) for part in range(2))
        in_re, in_im, out_re, out_im = mixed(
            a_re, a_im, b_re, b_im, refl[1], screen[1, front, 0], screen[1, front, 1]
        )
        put(inward.at[front], in_re, in_im)
        put(outward.at[front], out_re, out_im)
        term = a_re * b_re + a_im * b_im
        total = term if total is None else total + term
    terms[...] = total


def far_rows_kernel(last, q_arrived, q_out_inner, screen, refl, inner_terms, inward, outward, terms):
    rows, total = outer_rows(1, last, q_arrived, q_out_inner, screen, refl, inward, outward)
    terms[0] = total.astype(BF16)
    terms[1] = inner_terms[rows, :].astype(BF16)


def outer_rows(of, last, q_arrived, q_out_inner, screen, refl, inward, outward):
    fronts, _, half, _ = last.shape
    first = lax.axis_index("depth") == 0
    rows = half_rows(of, half)
    total = None
    for front in range(fronts):
        a_re, a_im = (
            jnp.where(first, q_arrived[front, part, rows, :], last[front, part]).astype(F32)
            for part in range(2)
        )
        b_re, b_im = (q_out_inner[front, part, rows, :].astype(F32) for part in range(2))
        in_re, in_im, out_re, out_im = mixed(
            a_re, a_im, b_re, b_im, refl[0, rows, :], screen[0, front, 0, rows, :], screen[0, front, 1, rows, :]
        )
        put(inward.at[front], in_re, in_im)
        put(outward.at[front], out_re, out_im)
        term = a_re * b_re + a_im * b_im
        total = term if total is None else total + term
    return rows, total


def send_home(level, rows, inward, outward, down_out, up_out, sems):
    odd = odd_place()

    def copies(place, inward_out, outward_out):
        return [
            pltpu.make_async_copy(inward, inward_out.at[place, :, :, rows, :], sems.at[0]),
            pltpu.make_async_copy(outward, outward_out.at[place, :, :, rows, :], sems.at[1]),
        ]

    @pl.when(odd == 0)
    def _():
        for copy in copies(level, down_out, up_out):
            copy.start()

    @pl.when(odd == 1)
    def _():
        for copy in copies(1 - level, up_out, down_out):
            copy.start()

    return copies(0, down_out, up_out)


def near_rows_kernel(
    scale, last, q_arrived, q_out_inner, screen, refl, inner_in, inner_out, far_in, far_out, inner_terms, other,
    down_out, up_out, gradient,
    inward, outward, sums, sems,
):
    rows_x, half = inner_in.shape[2], far_in.shape[2]
    waits = send_home(1, pl.ds(0, rows_x), inner_in, inner_out, down_out, up_out, sems.at[0])
    waits += send_home(0, half_rows(1, half), far_in, far_out, down_out, up_out, sems.at[1])
    rows, total = outer_rows(0, last, q_arrived, q_out_inner, screen, refl, inward, outward)
    waits += send_home(0, rows, inward, outward, down_out, up_out, sems.at[2])
    odd = odd_place()
    sums[odd] = scale * (total + other[0].astype(F32))
    sums[1 - odd] = scale * (inner_terms[rows, :] + other[1].astype(F32))
    done = pltpu.make_async_copy(sums, gradient, sems.at[3, 0])
    done.start()
    for copy in waits + [done]:
        copy.wait()


def per_device(down_state, up_state, source, reflect, screen_class, screen_values, freq_index):
    depth = lax.axis_size("depth")
    shots = lax.axis_size("shot")
    levels, fronts, parts, rows_x, rows_y = down_state.shape
    if levels != 2 or depth % 2 or shots % 2 or HOPS != 3:
        return per_device_plain(down_state, up_state, source, reflect, screen_class, screen_values, freq_index)
    scale = 1.0 / math.sqrt(fronts * shots)
    half = rows_x // 2
    hx = jnp.asarray(hartley(rows_x))
    hy = jnp.asarray(hartley(rows_y))
    partners = [(i, i ^ 1) for i in range(depth)]
    beyond = [(i, i + 1) for i in range(1, depth - 1, 2)] + [(i + 1, i) for i in range(1, depth - 1, 2)]
    to_partner = functools.partial(lax.ppermute, axis_name="depth", perm=partners)
    to_beyond = functools.partial(lax.ppermute, axis_name="depth", perm=beyond)
    across = functools.partial(lax.ppermute, axis_name="shot", perm=[(i, i ^ 1) for i in range(shots)])
    plane = jax.ShapeDtypeStruct((fronts, parts, rows_x, rows_y), BF16)
    half_plane = jax.ShapeDtypeStruct((fronts, parts, half, rows_y), BF16)
    pair = jax.ShapeDtypeStruct((2, rows_x, rows_y), F32)
    turns = jax.ShapeDtypeStruct((fronts, parts, rows_x, rows_y), F32)
    screens = jax.ShapeDtypeStruct((2, fronts, parts, rows_x, rows_y), F32)
    state = jax.ShapeDtypeStruct(down_state.shape, BF16)
    dma = pltpu.SemaphoreType.DMA

    def call(kernel, in_specs, out_specs, out_shape, scratch=(), **more):
        return pl.pallas_call(
            kernel,
            in_specs=in_specs,
            out_specs=out_specs,
            out_shape=out_shape,
            scratch_shapes=list(scratch),
            compiler_params=PARAMS,
            **more,
        )

    def kept_in_hbm(*arrays):
        return [pltpu.with_memory_space_constraint(array, pltpu.HBM) for array in arrays]

    def buffers(count, shape=plane):
        return [pltpu.VMEM(shape.shape, shape.dtype)] * count

    def work(slots):
        return pltpu.VMEM((slots, *plane.shape[1:]), BF16)

    out_outer, in_inner = call(edges_kernel, [HBM] * 2, [VMEM] * 2, [plane] * 2, [dma((2,))])(
        *kept_in_hbm(down_state, up_state)
    )
    arrived_0 = to_beyond(out_outer)
    partner_0 = to_partner(in_inner)
    q_out_inner_0, q_in_outer_0, screen, phase, refl = call(
        setup_kernel,
        [HBM] * 4 + [SMEM] * 2 + [VMEM] * 2,
        [VMEM] * 5,
        [plane] * 2 + [screens, turns, pair],
        [
            pltpu.VMEM((2, *plane.shape), BF16),
            pltpu.VMEM((2, rows_x, rows_y), jnp.int32),
            work(2 * fronts),
            dma((6,)),
        ],
    )(*kept_in_hbm(down_state, up_state, reflect, screen_class), screen_values, freq_index, hx, hy)
    fixed = (screen, refl, phase, hx, hy)
    in_inner_1, q_out_inner_1 = call(ahead_kernel, [VMEM] * 7, [VMEM] * 2, [plane] * 2, buffers(2) + [work(fronts)])(
        partner_0, q_in_outer_0, *fixed
    )
    partner_1 = to_partner(in_inner_1)
    out_outer_1, q_arrived = call(edge_kernel, [VMEM] * 8, [VMEM] * 2, [plane] * 2, [work(fronts)])(
        arrived_0, source, q_out_inner_0, *fixed
    )
    arrived_1 = to_beyond(out_outer_1)
    in_inner_2, out_inner_2 = call(
        inner_kernel, [VMEM] * 8, [VMEM] * 2, [plane] * 2, buffers(3) + [work(2 * fronts)]
    )(q_arrived, q_out_inner_0, partner_1, *fixed)
    partner_2 = to_partner(in_inner_2)
    q_out_inner_2 = call(spread_kernel, [VMEM] * 4, VMEM, plane, [work(fronts)])(out_inner_2, phase, hx, hy)
    q_arrived_1, last_far, last_near = call(
        last_edge_kernel,
        [VMEM] * 8 + [pl.BlockSpec(memory_space=pl.ANY)],
        [VMEM] * 3,
        [plane] + [half_plane] * 2,
        buffers(1) + [work(fronts)],
    )(arrived_1, source, q_out_inner_1, *fixed, q_out_inner_2)
    last_far = to_beyond(last_far)
    last_near = to_beyond(last_near)
    inner_in, inner_out, inner_terms = call(
        last_inner_kernel,
        [VMEM] * 8,
        [VMEM] * 3,
        [plane] * 2 + [jax.ShapeDtypeStruct((rows_x, rows_y), F32)],
        buffers(3) + [work(2 * fronts)],
    )(q_arrived_1, q_out_inner_1, partner_2, *fixed)
    far_in, far_out, terms = call(
        far_rows_kernel,
        [VMEM] * 6,
        [VMEM] * 3,
        [half_plane] * 2 + [jax.ShapeDtypeStruct((2, half, rows_y), BF16)],
    )(last_far, q_arrived, q_out_inner_2, screen, refl, inner_terms)
    other = across(terms) if shots == 2 else jnp.zeros_like(terms)
    down, up, gradient = call(
        functools.partial(near_rows_kernel, scale),
        [VMEM] * 11,
        [HBM] * 3,
        [state, state, jax.ShapeDtypeStruct((2, half, rows_y), F32)],
        buffers(2, half_plane) + [pltpu.VMEM((2, half, rows_y), F32), dma((4, 2))],
    )(last_near, q_arrived, q_out_inner_2, screen, refl, inner_in, inner_out, far_in, far_out, inner_terms, other)
    if shots != 2:
        terms = scale * terms.astype(F32)
        far = jnp.where(odd_place() == 0, terms, terms[::-1])
        top = lax.rem(lax.axis_index("shot"), 2) == 0
        whole = jnp.concatenate([jnp.where(top, gradient, far), jnp.where(top, far, gradient)], axis=1)
        gradient = lax.psum_scatter(whole.astype(BF16), "shot", scatter_dimension=1, tiled=True).astype(F32)
    return (down, up, gradient)


def solution(mesh):
    return jax.shard_map(
        per_device,
        mesh=mesh,
        in_specs=(
            P("depth", "shot", None, None, None),
            P("depth", "shot", None, None, None),
            P("shot", None, None, None),
            P("depth", None, None),
            P("depth", None, None),
            P(),
            P("shot"),
        ),
        out_specs=(
            P("depth", "shot", None, None, None),
            P("depth", "shot", None, None, None),
            P("depth", "shot", None),
        ),
        check_vma=False,
    )
```

```python
import functools
import math

import jax
import jax.numpy as jnp
import numpy as np
from jax import lax
from jax.experimental import pallas as pl
from jax.experimental.pallas import tpu as pltpu
from jax.sharding import PartitionSpec as P

HOPS = 3
NCLASS = 16
NFREQ = 128
F32 = jnp.float32
BF16 = jnp.bfloat16
VMEM = pl.BlockSpec(memory_space=pltpu.VMEM)
HBM = pl.BlockSpec(memory_space=pltpu.HBM)
SMEM = pl.BlockSpec(memory_space=pltpu.SMEM)
PARAMS = pltpu.CompilerParams(vmem_limit_bytes=28 * 2**20)


def passed_along(block, axis, distance):
    devices = range(lax.axis_size(axis))
    route = [(i - distance, i) for i in devices if i - distance in devices]
    return lax.ppermute(block, axis, route)


def dft_tables(length):
    counter = jnp.arange(length, dtype=jnp.int32)
    product = counter[:, None] * counter[None, :] % length
    angles = 2.0 * math.pi / length * product.astype(jnp.float32)
    return (jnp.cos(angles).astype(jnp.bfloat16), jnp.sin(angles).astype(jnp.bfloat16))


def wavenumbers(length):
    counter = jnp.arange(length, dtype=jnp.int32)
    wrapped = jnp.where(counter >= length // 2, counter - length, counter)
    return 2.0 * math.pi / length * wrapped.astype(jnp.float32)


def propagate(planes, phase_re, phase_im, tables):
    fwd_left, fwd_right, inv_left, inv_right = tables
    first = jnp.einsum(
        "cdjk,...dkl->...cjl", fwd_left, planes, preferred_element_type=jnp.float32
    ).astype(jnp.bfloat16)
    second = jnp.einsum("...djl,dclm->...cjm", first, fwd_right, preferred_element_type=jnp.float32)
    real_part = second[..., 0, :, :]
    imag_part = second[..., 1, :, :]
    turned = jnp.stack(
        [real_part * phase_re - imag_part * phase_im, real_part * phase_im + imag_part * phase_re],
        axis=-3,
    ).astype(jnp.bfloat16)
    third = jnp.einsum(
        "cdjk,...dkl->...cjl", inv_left, turned, preferred_element_type=jnp.float32
    ).astype(jnp.bfloat16)
    return jnp.einsum(
        "...djl,dclm->...cjm", third, inv_right, preferred_element_type=jnp.float32
    ).astype(jnp.bfloat16)


def trade(down_edge, up_edge):
    got_down = passed_along(down_edge, "depth", 1)
    got_up = passed_along(up_edge, "depth", -1)
    return (got_down, got_up)


def per_device_plain(down_state, up_state, source, reflect, screen_class, screen_values, freq_index):
    levels = down_state.shape[0]
    rows_x = down_state.shape[3]
    rows_y = down_state.shape[4]
    front_count = down_state.shape[1]
    depth_rank = lax.axis_index("depth")
    scale = 1.0 / math.sqrt(front_count * lax.axis_size("shot"))
    cos_x, sin_x = dft_tables(rows_x)
    cos_y, sin_y = dft_tables(rows_y)
    tables = (
        jnp.stack([jnp.stack([cos_x, sin_x]), jnp.stack([-sin_x, cos_x])]),
        jnp.stack([jnp.stack([cos_y, -sin_y]), jnp.stack([sin_y, cos_y])]),
        jnp.stack([jnp.stack([cos_x, -sin_x]), jnp.stack([sin_x, cos_x])]),
        jnp.stack([jnp.stack([cos_y, sin_y]), jnp.stack([-sin_y, cos_y])]),
    )
    kwave = 0.95 * math.pi * (freq_index.astype(jnp.float32) + 1.0) / NFREQ
    kx_wave = wavenumbers(rows_x)
    ky_wave = wavenumbers(rows_y)
    vertical = kwave[:, None, None] ** 2 - kx_wave[None, :, None] ** 2 - ky_wave[None, None, :] ** 2
    propag = jnp.sqrt(jnp.maximum(vertical, 0.0))
    damping = jnp.exp(-jnp.sqrt(jnp.maximum(-vertical, 0.0))) / (rows_x * rows_y)
    phase_re = damping * jnp.cos(propag)
    phase_im = damping * jnp.sin(propag)
    classes = jnp.arange(NCLASS, dtype=jnp.int32)
    onehot = (screen_class[None] == classes[:, None, None, None]).astype(jnp.float32)
    slowness = jnp.einsum("c,clxy->lxy", screen_values, onehot, precision=lax.Precision.HIGHEST)
    angle = kwave[None, :, None, None] * slowness[:, None]
    screen_re = jnp.cos(angle)
    screen_im = jnp.sin(angle)
    refl = reflect[:, None]
    top_slab = depth_rank == 0
    down = down_state
    up = up_state
    a_re = a_im = b_re = b_im = None
    for repeat in range(HOPS):
        down_edge = down[levels - 1]
        up_edge = up[0]
        got_down, got_up = trade(down_edge, up_edge)
        got_down = jnp.where(top_slab, source, got_down)
        moved = propagate(
            jnp.concatenate([got_down[None], down[: levels - 1], up[1:], got_up[None]], axis=0),
            phase_re,
            phase_im,
            tables,
        )
        from_above = moved[:levels]
        from_below = moved[levels:]
        qa_re = from_above[:, :, 0].astype(jnp.float32)
        qa_im = from_above[:, :, 1].astype(jnp.float32)
        qb_re = from_below[:, :, 0].astype(jnp.float32)
        qb_im = from_below[:, :, 1].astype(jnp.float32)
        a_re = screen_re * qa_re - screen_im * qa_im
        a_im = screen_re * qa_im + screen_im * qa_re
        b_re = screen_re * qb_re - screen_im * qb_im
        b_im = screen_re * qb_im + screen_im * qb_re
        down = jnp.stack(
            [(1.0 + refl) * a_re - refl * b_re, (1.0 + refl) * a_im - refl * b_im], axis=2
        ).astype(jnp.bfloat16)
        up = jnp.stack(
            [(1.0 - refl) * b_re + refl * a_re, (1.0 - refl) * b_im + refl * a_im], axis=2
        ).astype(jnp.bfloat16)
    terms = scale * jnp.sum(a_re * b_re + a_im * b_im, axis=1)
    gradient = lax.psum_scatter(
        terms.astype(jnp.bfloat16), "shot", scatter_dimension=1, tiled=True
    ).astype(jnp.float32)
    return (down, up, gradient)


def hartley(length):
    counter = np.arange(length)
    angles = 2.0 * np.pi / length * (counter[:, None] * counter[None, :] % length)
    cosine = np.cos(angles).astype(BF16).astype(np.float32)
    sine = np.sin(angles).astype(BF16).astype(np.float32)
    return (cosine + sine).astype(BF16)


def odd_place():
    return lax.rem(lax.axis_index("depth"), 2)


def mm(left, right):
    return jnp.dot(left, right, preferred_element_type=F32)


def spread(jobs, work, hx, hy, phase):
    jobs = list(enumerate(jobs))
    for slot, (plane, _, _) in jobs:
        for part in range(2):
            work[slot, part] = mm(plane(part) if callable(plane) else plane[part], hy[...]).astype(BF16)
    for slot, (_, front, _) in jobs:
        turn_re, turn_im = phase[front, 0], phase[front, 1]
        part_re = mm(hx[...], work[slot, 0])
        part_im = mm(hx[...], work[slot, 1])
        work[slot, 0] = (part_re * turn_re - part_im * turn_im).astype(BF16)
        work[slot, 1] = (part_re * turn_im + part_im * turn_re).astype(BF16)
    for slot, _ in jobs:
        for part in range(2):
            work[slot, part] = mm(hx[...], work[slot, part]).astype(BF16)
    for slot, (_, _, target) in jobs:
        for part in range(2):
            if isinstance(target, list):
                for rows, piece in target:
                    piece[part] = mm(work[slot, part, rows, :], hy[...]).astype(BF16)
            else:
                target[part] = mm(work[slot, part], hy[...]).astype(BF16)


def screened(real_part, imag_part, screen_re, screen_im):
    return (
        screen_re * real_part - screen_im * imag_part,
        screen_re * imag_part + screen_im * real_part,
    )


def mixed(a_re, a_im, b_re, b_im, refl, screen_re, screen_im, waves="both"):
    a_re, a_im, b_re, b_im = (part.astype(F32) for part in (a_re, a_im, b_re, b_im))
    step_re = refl * (a_re - b_re)
    step_im = refl * (a_im - b_im)
    fields = ()
    if waves != "outward":
        fields += screened(a_re + step_re, a_im + step_im, screen_re, screen_im)
    if waves != "inward":
        fields += screened(b_re + step_re, b_im + step_im, screen_re, screen_im)
    return fields


def put(target, real_part, imag_part):
    target[0] = real_part.astype(BF16)
    target[1] = imag_part.astype(BF16)


def half_rows(of, half):
    shot = lax.rem(lax.axis_index("shot"), 2)
    return pl.ds(pl.multiple_of((shot if of == 0 else 1 - shot) * half, half), half)


def edges_kernel(down, up, outward_outer, inward_inner, sems):
    levels = down.shape[0]
    odd = odd_place()

    def fetch(first, second):
        pltpu.make_async_copy(first, outward_outer, sems.at[0]).start()
        pltpu.make_async_copy(second, inward_inner, sems.at[1]).start()

    @pl.when(odd == 0)
    def _():
        fetch(up.at[0], down.at[levels - 1])

    @pl.when(odd == 1)
    def _():
        fetch(down.at[levels - 1], up.at[0])

    pltpu.make_async_copy(up.at[0], outward_outer, sems.at[0]).wait()
    pltpu.make_async_copy(up.at[0], inward_inner, sems.at[1]).wait()


def class_rows(slowness, kwave, shape):
    lanes = lax.broadcasted_iota(jnp.int32, shape, 1)
    table = jnp.zeros(shape, F32)
    for entry in range(NCLASS):
        table = jnp.where(lanes == entry, slowness[entry], table)
    angle = kwave * table
    return jnp.cos(angle), jnp.sin(angle)


def look_up(table, classes):
    width = 128
    rows = classes.shape[0]
    wide = jnp.broadcast_to(table[:1], (rows, width))
    pieces = [
        jnp.take_along_axis(wide, classes[:, start : start + width], axis=1, mode="promise_in_bounds")
        for start in range(0, classes.shape[1], width)
    ]
    return jnp.concatenate(pieces, axis=1)


def front_wave(freq, front):
    return 0.95 * math.pi * (freq[front].astype(F32) + 1.0) / NFREQ


def series(square, shift):
    total = jnp.full_like(square, 1.0 / math.factorial(18 + shift))
    for order in range(16, -1, -2):
        total = 1.0 / math.factorial(order + shift) - square * total
    return total


def setup_kernel(
    down, up, reflect, classes_in, slowness, freq, hx, hy,
    q_out_inner, q_in_outer, screen, phase, refl, outward_outer,
    fields, klass, work, sems,
):
    fronts = q_out_inner.shape[0]
    rows_x, rows_y = refl.shape[1:]
    odd = odd_place()
    fixed = [
        pltpu.make_async_copy(reflect.at[odd], refl.at[0], sems.at[2]),
        pltpu.make_async_copy(reflect.at[1 - odd], refl.at[1], sems.at[3]),
        pltpu.make_async_copy(classes_in.at[odd], klass.at[0], sems.at[4]),
        pltpu.make_async_copy(classes_in.at[1 - odd], klass.at[1], sems.at[5]),
    ]
    for copy in fixed:
        copy.start()

    @pl.when(odd == 0)
    def _():
        pltpu.make_async_copy(down.at[0], fields.at[0], sems.at[0]).start()
        pltpu.make_async_copy(up.at[1], fields.at[1], sems.at[1]).start()
        pltpu.make_async_copy(up.at[0], outward_outer, sems.at[6]).start()

    @pl.when(odd == 1)
    def _():
        pltpu.make_async_copy(up.at[1], fields.at[0], sems.at[0]).start()
        pltpu.make_async_copy(down.at[0], fields.at[1], sems.at[1]).start()
        pltpu.make_async_copy(down.at[1], outward_outer, sems.at[6]).start()

    def squares(length, axis):
        counter = lax.broadcasted_iota(jnp.int32, (rows_x, rows_y), axis)
        wrapped = jnp.where(counter >= length // 2, counter - length, counter)
        wave = 2.0 * math.pi / length * wrapped.astype(F32)
        return wave * wave

    lateral = squares(rows_x, 0) + squares(rows_y, 1)
    level_out = 1.0 / (rows_x * rows_y)
    for front in range(fronts):
        kwave = front_wave(freq, front)
        vertical = kwave * kwave - lateral
        travels = vertical > 0.0
        square = jnp.maximum(vertical, 0.0)
        root = jnp.sqrt(jnp.abs(vertical))
        phase[front, 0] = jnp.where(travels, series(square, 0), jnp.exp(-root)) * level_out
        phase[front, 1] = jnp.where(travels, root * series(square, 1), 0.0) * level_out
    for copy in fixed:
        copy.wait()
    sign = jnp.where(odd == 0, 1.0, -1.0).astype(F32)
    for level in range(2):
        refl[level] = sign * refl[level]
    for front in range(fronts):
        cos_row, sin_row = class_rows(slowness, front_wave(freq, front), (8, 128))
        for level in range(2):
            screen[level, front, 0] = look_up(cos_row, klass[level])
            screen[level, front, 1] = look_up(sin_row, klass[level])
    pltpu.make_async_copy(down.at[0], fields.at[0], sems.at[0]).wait()
    pltpu.make_async_copy(down.at[0], fields.at[1], sems.at[1]).wait()
    pltpu.make_async_copy(down.at[0], outward_outer, sems.at[6]).wait()
    jobs = [(fields.at[1, front], front, q_out_inner.at[front]) for front in range(fronts)]
    jobs += [(fields.at[0, front], front, q_in_outer.at[front]) for front in range(fronts)]
    spread(jobs, work, hx, hy, phase)


def ahead_kernel(
    partner, q_in_outer, screen, refl, phase, hx, hy,
    inward_inner, q_out_inner,
    q_field, field, work,
):
    everyone = range(partner.shape[0])
    spread([(partner.at[front], front, q_field.at[front]) for front in everyone], work, hx, hy, phase)
    for front in everyone:
        in_re, in_im, out_re, out_im = mixed(
            q_in_outer[front, 0], q_in_outer[front, 1], q_field[front, 0], q_field[front, 1],
            refl[1], screen[1, front, 0], screen[1, front, 1],
        )
        put(inward_inner.at[front], in_re, in_im)
        put(field.at[front], out_re, out_im)
    spread([(field.at[front], front, q_out_inner.at[front]) for front in everyone], work, hx, hy, phase)


def entering(arrived, source, front):
    first = lax.axis_index("depth") == 0
    return lambda part: jnp.where(first, source[front, part], arrived(front, part))


def outer_step(q_arrived, q_out_inner, screen, refl, waves, field):
    for front in range(field.shape[0]):
        put(
            field.at[front],
            *mixed(
                q_arrived[front, 0], q_arrived[front, 1], q_out_inner[front, 0], q_out_inner[front, 1],
                refl[0], screen[0, front, 0], screen[0, front, 1], waves,
            ),
        )


def late_pair():
    return lax.rem(lax.div(lax.axis_index("depth") + 1, 2), 2) == 1


def edge_kernel(early, late, source, q_out_inner, screen, refl, phase, hx, hy, outward, q_arrived, work):
    everyone = range(early.shape[0])
    is_late = late_pair()

    def arrived(front, part):
        return jnp.where(is_late, late[front, part], early[front, part])

    spread([(entering(arrived, source, front), front, q_arrived.at[front]) for front in everyone], work, hx, hy, phase)
    outer_step(q_arrived, q_out_inner, screen, refl, "outward", outward)


def last_edge_kernel(
    arrived, source, q_out_inner, screen, refl, phase, hx, hy, after,
    q_arrived, last_far, last_near,
    outward, work,
):
    del after
    everyone = range(arrived.shape[0])
    half = arrived.shape[2] // 2

    def received(front, part):
        return arrived[front, part]

    spread([(entering(received, source, front), front, q_arrived.at[front]) for front in everyone], work, hx, hy, phase)
    outer_step(q_arrived, q_out_inner, screen, refl, "outward", outward)
    jobs = [
        (outward.at[front], front, [(half_rows(1, half), last_far.at[front]), (half_rows(0, half), last_near.at[front])])
        for front in everyone
    ]
    spread(jobs, work, hx, hy, phase)


def inner_kernel(
    q_arrived, q_out_inner, partner, screen, refl, phase, hx, hy,
    inward, outward,
    field, q_inward, q_partner, work,
):
    everyone = range(partner.shape[0])
    outer_step(q_arrived, q_out_inner, screen, refl, "inward", field)
    jobs = [(partner.at[front], front, q_partner.at[front]) for front in everyone]
    jobs += [(field.at[front], front, q_inward.at[front]) for front in everyone]
    spread(jobs, work, hx, hy, phase)
    for front in everyone:
        in_re, in_im, out_re, out_im = mixed(
            q_inward[front, 0], q_inward[front, 1], q_partner[front, 0], q_partner[front, 1],
            refl[1], screen[1, front, 0], screen[1, front, 1],
        )
        put(inward.at[front], in_re, in_im)
        put(outward.at[front], out_re, out_im)


def spread_kernel(fields, phase, hx, hy, q_fields, work):
    everyone = range(fields.shape[0])
    spread([(fields.at[front], front, q_fields.at[front]) for front in everyone], work, hx, hy, phase)


def last_inner_kernel(
    q_arrived, q_out_inner, partner, screen, refl, phase, hx, hy,
    inward, outward, terms, far_terms,
    field, q_inward, q_partner, work,
):
    everyone = range(partner.shape[0])
    outer_step(q_arrived, q_out_inner, screen, refl, "inward", field)
    jobs = [(partner.at[front], front, q_partner.at[front]) for front in everyone]
    jobs += [(field.at[front], front, q_inward.at[front]) for front in everyone]
    spread(jobs, work, hx, hy, phase)
    total = None
    for front in everyone:
        a_re, a_im = (q_inward[front, part].astype(F32) for part in range(2))
        b_re, b_im = (q_partner[front, part].astype(F32) for part in range(2))
        in_re, in_im, out_re, out_im = mixed(
            a_re, a_im, b_re, b_im, refl[1], screen[1, front, 0], screen[1, front, 1]
        )
        put(inward.at[front], in_re, in_im)
        put(outward.at[front], out_re, out_im)
        term = a_re * b_re + a_im * b_im
        total = term if total is None else total + term
    terms[...] = total
    far_terms[...] = terms[half_rows(1, far_terms.shape[0]), :].astype(BF16)


def far_rows_kernel(last, q_arrived, q_out_inner, screen, refl, after, inward, outward, terms):
    del after
    _, total = outer_rows(1, last, q_arrived, q_out_inner, screen, refl, inward, outward)
    terms[...] = total.astype(BF16)


def outer_rows(of, last, q_arrived, q_out_inner, screen, refl, inward, outward):
    fronts, _, half, _ = last.shape
    first = lax.axis_index("depth") == 0
    rows = half_rows(of, half)
    total = None
    for front in range(fronts):
        a_re, a_im = (
            jnp.where(first, q_arrived[front, part, rows, :], last[front, part]).astype(F32)
            for part in range(2)
        )
        b_re, b_im = (q_out_inner[front, part, rows, :].astype(F32) for part in range(2))
        in_re, in_im, out_re, out_im = mixed(
            a_re, a_im, b_re, b_im, refl[0, rows, :], screen[0, front, 0, rows, :], screen[0, front, 1, rows, :]
        )
        put(inward.at[front], in_re, in_im)
        put(outward.at[front], out_re, out_im)
        term = a_re * b_re + a_im * b_im
        total = term if total is None else total + term
    return rows, total


def send_home(level, rows, inward, outward, down_out, up_out, sems):
    odd = odd_place()

    def copies(place, inward_out, outward_out):
        return [
            pltpu.make_async_copy(inward, inward_out.at[place, :, :, rows, :], sems.at[0]),
            pltpu.make_async_copy(outward, outward_out.at[place, :, :, rows, :], sems.at[1]),
        ]

    @pl.when(odd == 0)
    def _():
        for copy in copies(level, down_out, up_out):
            copy.start()

    @pl.when(odd == 1)
    def _():
        for copy in copies(1 - level, up_out, down_out):
            copy.start()

    return copies(0, down_out, up_out)


def near_rows_kernel(
    last, q_arrived, q_out_inner, screen, refl, inner_in, inner_out, far_in, far_out,
    down_out, up_out, terms,
    inward, outward, sems,
):
    rows_x, half = inner_in.shape[2], far_in.shape[2]
    waits = send_home(1, pl.ds(0, rows_x), inner_in, inner_out, down_out, up_out, sems.at[0])
    waits += send_home(0, half_rows(1, half), far_in, far_out, down_out, up_out, sems.at[1])
    rows, total = outer_rows(0, last, q_arrived, q_out_inner, screen, refl, inward, outward)
    waits += send_home(0, rows, inward, outward, down_out, up_out, sems.at[2])
    terms[...] = total
    for copy in waits:
        copy.wait()


def gradient_kernel(scale, outer_terms, inner_terms, outer_other, inner_other, gradient, sums, sems):
    odd = odd_place()
    sums[odd] = scale * (outer_terms[...] + outer_other[...].astype(F32))
    sums[1 - odd] = scale * (inner_terms[half_rows(0, sums.shape[1]), :] + inner_other[...].astype(F32))
    done = pltpu.make_async_copy(sums, gradient, sems.at[0])
    done.start()
    done.wait()


def per_device(down_state, up_state, source, reflect, screen_class, screen_values, freq_index):
    depth = lax.axis_size("depth")
    shots = lax.axis_size("shot")
    levels, fronts, parts, rows_x, rows_y = down_state.shape
    if levels != 2 or depth % 2 or shots % 2 or HOPS != 3:
        return per_device_plain(down_state, up_state, source, reflect, screen_class, screen_values, freq_index)
    scale = 1.0 / math.sqrt(fronts * shots)
    half = rows_x // 2
    hx = jnp.asarray(hartley(rows_x))
    hy = jnp.asarray(hartley(rows_y))
    partners = [(i, i ^ 1) for i in range(depth)]
    early_pairs, late_pairs = (
        [(i, i + 1) for i in range(start, depth - 1, 4)] + [(i + 1, i) for i in range(start, depth - 1, 4)]
        for start in (3, 1)
    )
    beyond = early_pairs + late_pairs
    to_partner = functools.partial(lax.ppermute, axis_name="depth", perm=partners)
    to_beyond = functools.partial(lax.ppermute, axis_name="depth", perm=beyond)
    across = functools.partial(lax.ppermute, axis_name="shot", perm=[(i, i ^ 1) for i in range(shots)])
    plane = jax.ShapeDtypeStruct((fronts, parts, rows_x, rows_y), BF16)
    half_plane = jax.ShapeDtypeStruct((fronts, parts, half, rows_y), BF16)
    pair = jax.ShapeDtypeStruct((2, rows_x, rows_y), F32)
    turns = jax.ShapeDtypeStruct((fronts, parts, rows_x, rows_y), F32)
    screens = jax.ShapeDtypeStruct((2, fronts, parts, rows_x, rows_y), F32)
    state = jax.ShapeDtypeStruct(down_state.shape, BF16)
    dma = pltpu.SemaphoreType.DMA

    def call(kernel, in_specs, out_specs, out_shape, scratch=(), **more):
        return pl.pallas_call(
            kernel,
            in_specs=in_specs,
            out_specs=out_specs,
            out_shape=out_shape,
            scratch_shapes=list(scratch),
            compiler_params=PARAMS,
            **more,
        )

    def kept_in_hbm(*arrays):
        return [pltpu.with_memory_space_constraint(array, pltpu.HBM) for array in arrays]

    def buffers(count, shape=plane):
        return [pltpu.VMEM(shape.shape, shape.dtype)] * count

    def work(slots):
        return pltpu.VMEM((slots, *plane.shape[1:]), BF16)

    out_outer, in_inner = call(edges_kernel, [HBM] * 2, [VMEM] * 2, [plane] * 2, [dma((2,))])(
        *kept_in_hbm(down_state, up_state)
    )
    arrived_early = to_beyond(out_outer, perm=early_pairs)
    partner_0 = to_partner(in_inner)
    q_out_inner_0, q_in_outer_0, screen, phase, refl, out_outer_again = call(
        setup_kernel,
        [HBM] * 4 + [SMEM] * 2 + [VMEM] * 2,
        [VMEM] * 6,
        [plane] * 2 + [screens, turns, pair, plane],
        [
            pltpu.VMEM((2, *plane.shape), BF16),
            pltpu.VMEM((2, rows_x, rows_y), jnp.int32),
            work(2 * fronts),
            dma((7,)),
        ],
    )(*kept_in_hbm(down_state, up_state, reflect, screen_class), screen_values, freq_index, hx, hy)
    arrived_late = to_beyond(out_outer_again, perm=late_pairs)
    fixed = (screen, refl, phase, hx, hy)
    in_inner_1, q_out_inner_1 = call(ahead_kernel, [VMEM] * 7, [VMEM] * 2, [plane] * 2, buffers(2) + [work(fronts)])(
        partner_0, q_in_outer_0, *fixed
    )
    partner_1 = to_partner(in_inner_1)
    out_outer_1, q_arrived = call(edge_kernel, [VMEM] * 9, [VMEM] * 2, [plane] * 2, [work(fronts)])(
        arrived_early, arrived_late, source, q_out_inner_0, *fixed
    )
    arrived_1 = to_beyond(out_outer_1)
    in_inner_2, out_inner_2 = call(
        inner_kernel, [VMEM] * 8, [VMEM] * 2, [plane] * 2, buffers(3) + [work(2 * fronts)]
    )(q_arrived, q_out_inner_0, partner_1, *fixed)
    partner_2 = to_partner(in_inner_2)
    q_out_inner_2 = call(spread_kernel, [VMEM] * 4, VMEM, plane, [work(fronts)])(out_inner_2, phase, hx, hy)
    q_arrived_1, last_far, last_near = call(
        last_edge_kernel,
        [VMEM] * 8 + [pl.BlockSpec(memory_space=pl.ANY)],
        [VMEM] * 3,
        [plane] + [half_plane] * 2,
        buffers(1) + [work(fronts)],
    )(arrived_1, source, q_out_inner_1, *fixed, q_out_inner_2)
    last_far = to_beyond(last_far)
    last_near = to_beyond(last_near)
    half_sum = jax.ShapeDtypeStruct((half, rows_y), BF16)
    inner_in, inner_out, inner_terms, inner_far = call(
        last_inner_kernel,
        [VMEM] * 8,
        [VMEM] * 4,
        [plane] * 2 + [jax.ShapeDtypeStruct((rows_x, rows_y), F32), half_sum],
        buffers(3) + [work(2 * fronts)],
    )(q_arrived_1, q_out_inner_1, partner_2, *fixed)
    inner_other = across(inner_far) if shots == 2 else jnp.zeros_like(inner_far)
    far_in, far_out, outer_far = call(
        far_rows_kernel,
        [VMEM] * 5 + [pl.BlockSpec(memory_space=pl.ANY)],
        [VMEM] * 3,
        [half_plane] * 2 + [half_sum],
    )(last_far, q_arrived, q_out_inner_2, screen, refl, inner_terms)
    outer_other = across(outer_far) if shots == 2 else jnp.zeros_like(outer_far)
    down, up, outer_near = call(
        near_rows_kernel,
        [VMEM] * 9,
        [HBM] * 2 + [VMEM],
        [state, state, jax.ShapeDtypeStruct((half, rows_y), F32)],
        buffers(2, half_plane) + [dma((3, 2))],
    )(last_near, q_arrived, q_out_inner_2, screen, refl, inner_in, inner_out, far_in, far_out)
    gradient = call(
        functools.partial(gradient_kernel, scale),
        [VMEM] * 4,
        HBM,
        jax.ShapeDtypeStruct((2, half, rows_y), F32),
        [pltpu.VMEM((2, half, rows_y), F32), dma((1,))],
    )(outer_near, inner_terms, outer_other, inner_other)
    if shots != 2:
        terms = scale * jnp.stack([outer_far, inner_far]).astype(F32)
        far = jnp.where(odd_place() == 0, terms, terms[::-1])
        top = lax.rem(lax.axis_index("shot"), 2) == 0
        whole = jnp.concatenate([jnp.where(top, gradient, far), jnp.where(top, far, gradient)], axis=1)
        gradient = lax.psum_scatter(whole.astype(BF16), "shot", scatter_dimension=1, tiled=True).astype(F32)
    return (down, up, gradient)


def solution(mesh):
    return jax.shard_map(
        per_device,
        mesh=mesh,
        in_specs=(
            P("depth", "shot", None, None, None),
            P("depth", "shot", None, None, None),
            P("shot", None, None, None),
            P("depth", None, None),
            P("depth", None, None),
            P(),
            P("shot"),
        ),
        out_specs=(
            P("depth", "shot", None, None, None),
            P("depth", "shot", None, None, None),
            P("depth", "shot", None),
        ),
        check_vma=False,
    )
```

```python
import functools
import math

import jax
import jax.numpy as jnp
import numpy as np
from jax import lax
from jax.experimental import pallas as pl
from jax.experimental.pallas import tpu as pltpu
from jax.sharding import PartitionSpec as P

HOPS = 3
NCLASS = 16
NFREQ = 128
F32 = jnp.float32
BF16 = jnp.bfloat16
VMEM = pl.BlockSpec(memory_space=pltpu.VMEM)
HBM = pl.BlockSpec(memory_space=pltpu.HBM)
SMEM = pl.BlockSpec(memory_space=pltpu.SMEM)
PARAMS = pltpu.CompilerParams(vmem_limit_bytes=28 * 2**20)


def passed_along(block, axis, distance):
    devices = range(lax.axis_size(axis))
    route = [(i - distance, i) for i in devices if i - distance in devices]
    return lax.ppermute(block, axis, route)


def dft_tables(length):
    counter = jnp.arange(length, dtype=jnp.int32)
    product = counter[:, None] * counter[None, :] % length
    angles = 2.0 * math.pi / length * product.astype(jnp.float32)
    return (jnp.cos(angles).astype(jnp.bfloat16), jnp.sin(angles).astype(jnp.bfloat16))


def wavenumbers(length):
    counter = jnp.arange(length, dtype=jnp.int32)
    wrapped = jnp.where(counter >= length // 2, counter - length, counter)
    return 2.0 * math.pi / length * wrapped.astype(jnp.float32)


def propagate(planes, phase_re, phase_im, tables):
    fwd_left, fwd_right, inv_left, inv_right = tables
    first = jnp.einsum(
        "cdjk,...dkl->...cjl", fwd_left, planes, preferred_element_type=jnp.float32
    ).astype(jnp.bfloat16)
    second = jnp.einsum("...djl,dclm->...cjm", first, fwd_right, preferred_element_type=jnp.float32)
    real_part = second[..., 0, :, :]
    imag_part = second[..., 1, :, :]
    turned = jnp.stack(
        [real_part * phase_re - imag_part * phase_im, real_part * phase_im + imag_part * phase_re],
        axis=-3,
    ).astype(jnp.bfloat16)
    third = jnp.einsum(
        "cdjk,...dkl->...cjl", inv_left, turned, preferred_element_type=jnp.float32
    ).astype(jnp.bfloat16)
    return jnp.einsum(
        "...djl,dclm->...cjm", third, inv_right, preferred_element_type=jnp.float32
    ).astype(jnp.bfloat16)


def trade(down_edge, up_edge):
    got_down = passed_along(down_edge, "depth", 1)
    got_up = passed_along(up_edge, "depth", -1)
    return (got_down, got_up)


def per_device_plain(down_state, up_state, source, reflect, screen_class, screen_values, freq_index):
    levels = down_state.shape[0]
    rows_x = down_state.shape[3]
    rows_y = down_state.shape[4]
    front_count = down_state.shape[1]
    depth_rank = lax.axis_index("depth")
    scale = 1.0 / math.sqrt(front_count * lax.axis_size("shot"))
    cos_x, sin_x = dft_tables(rows_x)
    cos_y, sin_y = dft_tables(rows_y)
    tables = (
        jnp.stack([jnp.stack([cos_x, sin_x]), jnp.stack([-sin_x, cos_x])]),
        jnp.stack([jnp.stack([cos_y, -sin_y]), jnp.stack([sin_y, cos_y])]),
        jnp.stack([jnp.stack([cos_x, -sin_x]), jnp.stack([sin_x, cos_x])]),
        jnp.stack([jnp.stack([cos_y, sin_y]), jnp.stack([-sin_y, cos_y])]),
    )
    kwave = 0.95 * math.pi * (freq_index.astype(jnp.float32) + 1.0) / NFREQ
    kx_wave = wavenumbers(rows_x)
    ky_wave = wavenumbers(rows_y)
    vertical = kwave[:, None, None] ** 2 - kx_wave[None, :, None] ** 2 - ky_wave[None, None, :] ** 2
    propag = jnp.sqrt(jnp.maximum(vertical, 0.0))
    damping = jnp.exp(-jnp.sqrt(jnp.maximum(-vertical, 0.0))) / (rows_x * rows_y)
    phase_re = damping * jnp.cos(propag)
    phase_im = damping * jnp.sin(propag)
    classes = jnp.arange(NCLASS, dtype=jnp.int32)
    onehot = (screen_class[None] == classes[:, None, None, None]).astype(jnp.float32)
    slowness = jnp.einsum("c,clxy->lxy", screen_values, onehot, precision=lax.Precision.HIGHEST)
    angle = kwave[None, :, None, None] * slowness[:, None]
    screen_re = jnp.cos(angle)
    screen_im = jnp.sin(angle)
    refl = reflect[:, None]
    top_slab = depth_rank == 0
    down = down_state
    up = up_state
    a_re = a_im = b_re = b_im = None
    for repeat in range(HOPS):
        down_edge = down[levels - 1]
        up_edge = up[0]
        got_down, got_up = trade(down_edge, up_edge)
        got_down = jnp.where(top_slab, source, got_down)
        moved = propagate(
            jnp.concatenate([got_down[None], down[: levels - 1], up[1:], got_up[None]], axis=0),
            phase_re,
            phase_im,
            tables,
        )
        from_above = moved[:levels]
        from_below = moved[levels:]
        qa_re = from_above[:, :, 0].astype(jnp.float32)
        qa_im = from_above[:, :, 1].astype(jnp.float32)
        qb_re = from_below[:, :, 0].astype(jnp.float32)
        qb_im = from_below[:, :, 1].astype(jnp.float32)
        a_re = screen_re * qa_re - screen_im * qa_im
        a_im = screen_re * qa_im + screen_im * qa_re
        b_re = screen_re * qb_re - screen_im * qb_im
        b_im = screen_re * qb_im + screen_im * qb_re
        down = jnp.stack(
            [(1.0 + refl) * a_re - refl * b_re, (1.0 + refl) * a_im - refl * b_im], axis=2
        ).astype(jnp.bfloat16)
        up = jnp.stack(
            [(1.0 - refl) * b_re + refl * a_re, (1.0 - refl) * b_im + refl * a_im], axis=2
        ).astype(jnp.bfloat16)
    terms = scale * jnp.sum(a_re * b_re + a_im * b_im, axis=1)
    gradient = lax.psum_scatter(
        terms.astype(jnp.bfloat16), "shot", scatter_dimension=1, tiled=True
    ).astype(jnp.float32)
    return (down, up, gradient)


def hartley(length):
    counter = np.arange(length)
    angles = 2.0 * np.pi / length * (counter[:, None] * counter[None, :] % length)
    cosine = np.cos(angles).astype(BF16).astype(np.float32)
    sine = np.sin(angles).astype(BF16).astype(np.float32)
    return (cosine + sine).astype(BF16)


def odd_place():
    return lax.rem(lax.axis_index("depth"), 2)


def mm(left, right):
    return jnp.dot(left, right, preferred_element_type=F32)


def spread(jobs, work, hx, hy, phase):
    jobs = list(enumerate(jobs))
    for slot, (plane, _, _) in jobs:
        for part in range(2):
            work[slot, part] = mm(plane(part) if callable(plane) else plane[part], hy[...]).astype(BF16)
    for slot, (_, front, _) in jobs:
        turn_re, turn_im = phase[front, 0], phase[front, 1]
        part_re = mm(hx[...], work[slot, 0])
        part_im = mm(hx[...], work[slot, 1])
        work[slot, 0] = (part_re * turn_re - part_im * turn_im).astype(BF16)
        work[slot, 1] = (part_re * turn_im + part_im * turn_re).astype(BF16)
    for slot, _ in jobs:
        for part in range(2):
            work[slot, part] = mm(hx[...], work[slot, part]).astype(BF16)
    for slot, (_, _, target) in jobs:
        for part in range(2):
            if isinstance(target, list):
                for rows, piece in target:
                    piece[part] = mm(work[slot, part, rows, :], hy[...]).astype(BF16)
            else:
                target[part] = mm(work[slot, part], hy[...]).astype(BF16)


def screened(real_part, imag_part, screen_re, screen_im):
    return (
        screen_re * real_part - screen_im * imag_part,
        screen_re * imag_part + screen_im * real_part,
    )


def mixed(a_re, a_im, b_re, b_im, refl, screen_re, screen_im, waves="both"):
    a_re, a_im, b_re, b_im = (part.astype(F32) for part in (a_re, a_im, b_re, b_im))
    step_re = refl * (a_re - b_re)
    step_im = refl * (a_im - b_im)
    fields = ()
    if waves != "outward":
        fields += screened(a_re + step_re, a_im + step_im, screen_re, screen_im)
    if waves != "inward":
        fields += screened(b_re + step_re, b_im + step_im, screen_re, screen_im)
    return fields


def put(target, real_part, imag_part):
    target[0] = real_part.astype(BF16)
    target[1] = imag_part.astype(BF16)


def half_rows(of, half):
    shot = lax.rem(lax.axis_index("shot"), 2)
    return pl.ds(pl.multiple_of((shot if of == 0 else 1 - shot) * half, half), half)


def edges_kernel(down, up, outward_outer, inward_inner, sems):
    levels = down.shape[0]
    odd = odd_place()

    def fetch(first, second):
        pltpu.make_async_copy(first, outward_outer, sems.at[0]).start()
        pltpu.make_async_copy(second, inward_inner, sems.at[1]).start()

    @pl.when(odd == 0)
    def _():
        fetch(up.at[0], down.at[levels - 1])

    @pl.when(odd == 1)
    def _():
        fetch(down.at[levels - 1], up.at[0])

    pltpu.make_async_copy(up.at[0], outward_outer, sems.at[0]).wait()
    pltpu.make_async_copy(up.at[0], inward_inner, sems.at[1]).wait()


def class_rows(slowness, kwave, shape):
    lanes = lax.broadcasted_iota(jnp.int32, shape, 1)
    table = jnp.zeros(shape, F32)
    for entry in range(NCLASS):
        table = jnp.where(lanes == entry, slowness[entry], table)
    angle = kwave * table
    return jnp.cos(angle), jnp.sin(angle)


def look_up(table, classes):
    width = 128
    rows = classes.shape[0]
    wide = jnp.broadcast_to(table[:1], (rows, width))
    pieces = [
        jnp.take_along_axis(wide, classes[:, start : start + width], axis=1, mode="promise_in_bounds")
        for start in range(0, classes.shape[1], width)
    ]
    return jnp.concatenate(pieces, axis=1)


def front_wave(freq, front):
    return 0.95 * math.pi * (freq[front].astype(F32) + 1.0) / NFREQ


def series(square, shift):
    total = jnp.full_like(square, 1.0 / math.factorial(18 + shift))
    for order in range(16, -1, -2):
        total = 1.0 / math.factorial(order + shift) - square * total
    return total


def setup_kernel(
    down, up, reflect, classes_in, slowness, freq, hx, hy,
    q_out_inner, q_in_outer, screen, phase, refl,
    fields, klass, work, sems,
):
    fronts = q_out_inner.shape[0]
    rows_x, rows_y = refl.shape[1:]
    odd = odd_place()
    fixed = [
        pltpu.make_async_copy(reflect.at[odd], refl.at[0], sems.at[2]),
        pltpu.make_async_copy(reflect.at[1 - odd], refl.at[1], sems.at[3]),
        pltpu.make_async_copy(classes_in.at[odd], klass.at[0], sems.at[4]),
        pltpu.make_async_copy(classes_in.at[1 - odd], klass.at[1], sems.at[5]),
    ]
    for copy in fixed:
        copy.start()

    @pl.when(odd == 0)
    def _():
        pltpu.make_async_copy(down.at[0], fields.at[0], sems.at[0]).start()
        pltpu.make_async_copy(up.at[1], fields.at[1], sems.at[1]).start()

    @pl.when(odd == 1)
    def _():
        pltpu.make_async_copy(up.at[1], fields.at[0], sems.at[0]).start()
        pltpu.make_async_copy(down.at[0], fields.at[1], sems.at[1]).start()

    def squares(length, axis):
        counter = lax.broadcasted_iota(jnp.int32, (rows_x, rows_y), axis)
        wrapped = jnp.where(counter >= length // 2, counter - length, counter)
        wave = 2.0 * math.pi / length * wrapped.astype(F32)
        return wave * wave

    lateral = squares(rows_x, 0) + squares(rows_y, 1)
    level_out = 1.0 / (rows_x * rows_y)
    for front in range(fronts):
        kwave = front_wave(freq, front)
        vertical = kwave * kwave - lateral
        travels = vertical > 0.0
        square = jnp.maximum(vertical, 0.0)
        root = jnp.sqrt(jnp.abs(vertical))
        phase[front, 0] = jnp.where(travels, series(square, 0), jnp.exp(-root)) * level_out
        phase[front, 1] = jnp.where(travels, root * series(square, 1), 0.0) * level_out
    for copy in fixed:
        copy.wait()
    sign = jnp.where(odd == 0, 1.0, -1.0).astype(F32)
    for level in range(2):
        refl[level] = sign * refl[level]
    for front in range(fronts):
        cos_row, sin_row = class_rows(slowness, front_wave(freq, front), (8, 128))
        for level in range(2):
            screen[level, front, 0] = look_up(cos_row, klass[level])
            screen[level, front, 1] = look_up(sin_row, klass[level])
    pltpu.make_async_copy(down.at[0], fields.at[0], sems.at[0]).wait()
    pltpu.make_async_copy(down.at[0], fields.at[1], sems.at[1]).wait()
    jobs = [(fields.at[1, front], front, q_out_inner.at[front]) for front in range(fronts)]
    jobs += [(fields.at[0, front], front, q_in_outer.at[front]) for front in range(fronts)]
    spread(jobs, work, hx, hy, phase)


def ahead_kernel(
    partner, q_in_outer, screen, refl, phase, hx, hy,
    inward_inner, q_out_inner,
    q_field, field, work,
):
    everyone = range(partner.shape[0])
    spread([(partner.at[front], front, q_field.at[front]) for front in everyone], work, hx, hy, phase)
    for front in everyone:
        in_re, in_im, out_re, out_im = mixed(
            q_in_outer[front, 0], q_in_outer[front, 1], q_field[front, 0], q_field[front, 1],
            refl[1], screen[1, front, 0], screen[1, front, 1],
        )
        put(inward_inner.at[front], in_re, in_im)
        put(field.at[front], out_re, out_im)
    spread([(field.at[front], front, q_out_inner.at[front]) for front in everyone], work, hx, hy, phase)


def entering(arrived, source, front):
    first = lax.axis_index("depth") == 0
    return lambda part: jnp.where(first, source[front, part], arrived[front, part])


def outer_step(q_arrived, q_out_inner, screen, refl, waves, field):
    for front in range(field.shape[0]):
        put(
            field.at[front],
            *mixed(
                q_arrived[front, 0], q_arrived[front, 1], q_out_inner[front, 0], q_out_inner[front, 1],
                refl[0], screen[0, front, 0], screen[0, front, 1], waves,
            ),
        )


def edge_kernel(arrived, source, q_out_inner, screen, refl, phase, hx, hy, outward, q_arrived, work):
    everyone = range(arrived.shape[0])
    spread([(entering(arrived, source, front), front, q_arrived.at[front]) for front in everyone], work, hx, hy, phase)
    outer_step(q_arrived, q_out_inner, screen, refl, "outward", outward)


def last_edge_kernel(
    arrived, source, q_out_inner, screen, refl, phase, hx, hy, after,
    q_arrived, last_far, last_near,
    outward, work,
):
    del after
    everyone = range(arrived.shape[0])
    half = arrived.shape[2] // 2
    spread([(entering(arrived, source, front), front, q_arrived.at[front]) for front in everyone], work, hx, hy, phase)
    outer_step(q_arrived, q_out_inner, screen, refl, "outward", outward)
    jobs = [
        (outward.at[front], front, [(half_rows(1, half), last_far.at[front]), (half_rows(0, half), last_near.at[front])])
        for front in everyone
    ]
    spread(jobs, work, hx, hy, phase)


def inner_kernel(
    q_arrived, q_out_inner, partner, screen, refl, phase, hx, hy,
    inward, outward,
    field, q_inward, q_partner, work,
):
    everyone = range(partner.shape[0])
    outer_step(q_arrived, q_out_inner, screen, refl, "inward", field)
    jobs = [(partner.at[front], front, q_partner.at[front]) for front in everyone]
    jobs += [(field.at[front], front, q_inward.at[front]) for front in everyone]
    spread(jobs, work, hx, hy, phase)
    for front in everyone:
        in_re, in_im, out_re, out_im = mixed(
            q_inward[front, 0], q_inward[front, 1], q_partner[front, 0], q_partner[front, 1],
            refl[1], screen[1, front, 0], screen[1, front, 1],
        )
        put(inward.at[front], in_re, in_im)
        put(outward.at[front], out_re, out_im)


def spread_kernel(fields, phase, hx, hy, q_fields, work):
    everyone = range(fields.shape[0])
    spread([(fields.at[front], front, q_fields.at[front]) for front in everyone], work, hx, hy, phase)


def last_inner_kernel(
    q_arrived, q_out_inner, partner, screen, refl, phase, hx, hy,
    inward, outward, terms, far_terms,
    field, q_inward, q_partner, work,
):
    everyone = range(partner.shape[0])
    outer_step(q_arrived, q_out_inner, screen, refl, "inward", field)
    jobs = [(partner.at[front], front, q_partner.at[front]) for front in everyone]
    jobs += [(field.at[front], front, q_inward.at[front]) for front in everyone]
    spread(jobs, work, hx, hy, phase)
    total = None
    for front in everyone:
        a_re, a_im = (q_inward[front, part].astype(F32) for part in range(2))
        b_re, b_im = (q_partner[front, part].astype(F32) for part in range(2))
        in_re, in_im, out_re, out_im = mixed(
            a_re, a_im, b_re, b_im, refl[1], screen[1, front, 0], screen[1, front, 1]
        )
        put(inward.at[front], in_re, in_im)
        put(outward.at[front], out_re, out_im)
        term = a_re * b_re + a_im * b_im
        total = term if total is None else total + term
    terms[...] = total
    far_terms[...] = terms[half_rows(1, far_terms.shape[0]), :].astype(BF16)


def far_rows_kernel(last, q_arrived, q_out_inner, screen, refl, after, inward, outward, terms):
    del after
    _, total = outer_rows(1, last, q_arrived, q_out_inner, screen, refl, inward, outward)
    terms[...] = total.astype(BF16)


def outer_rows(of, last, q_arrived, q_out_inner, screen, refl, inward, outward):
    fronts, _, half, _ = last.shape
    first = lax.axis_index("depth") == 0
    rows = half_rows(of, half)
    total = None
    for front in range(fronts):
        a_re, a_im = (
            jnp.where(first, q_arrived[front, part, rows, :], last[front, part]).astype(F32)
            for part in range(2)
        )
        b_re, b_im = (q_out_inner[front, part, rows, :].astype(F32) for part in range(2))
        in_re, in_im, out_re, out_im = mixed(
            a_re, a_im, b_re, b_im, refl[0, rows, :], screen[0, front, 0, rows, :], screen[0, front, 1, rows, :]
        )
        put(inward.at[front], in_re, in_im)
        put(outward.at[front], out_re, out_im)
        term = a_re * b_re + a_im * b_im
        total = term if total is None else total + term
    return rows, total


def send_home(level, rows, inward, outward, down_out, up_out, sems):
    odd = odd_place()

    def copies(place, inward_out, outward_out):
        return [
            pltpu.make_async_copy(inward, inward_out.at[place, :, :, rows, :], sems.at[0]),
            pltpu.make_async_copy(outward, outward_out.at[place, :, :, rows, :], sems.at[1]),
        ]

    @pl.when(odd == 0)
    def _():
        for copy in copies(level, down_out, up_out):
            copy.start()

    @pl.when(odd == 1)
    def _():
        for copy in copies(1 - level, up_out, down_out):
            copy.start()

    return copies(0, down_out, up_out)


def near_rows_kernel(
    last, q_arrived, q_out_inner, screen, refl, inner_in, inner_out, far_in, far_out,
    down_out, up_out, terms,
    inward, outward, sems,
):
    rows_x, half = inner_in.shape[2], far_in.shape[2]
    waits = send_home(1, pl.ds(0, rows_x), inner_in, inner_out, down_out, up_out, sems.at[0])
    waits += send_home(0, half_rows(1, half), far_in, far_out, down_out, up_out, sems.at[1])
    rows, total = outer_rows(0, last, q_arrived, q_out_inner, screen, refl, inward, outward)
    waits += send_home(0, rows, inward, outward, down_out, up_out, sems.at[2])
    terms[...] = total
    for copy in waits:
        copy.wait()


def gradient_kernel(scale, outer_terms, inner_terms, outer_other, inner_other, gradient, sums, sems):
    odd = odd_place()
    sums[odd] = scale * (outer_terms[...] + outer_other[...].astype(F32))
    sums[1 - odd] = scale * (inner_terms[half_rows(0, sums.shape[1]), :] + inner_other[...].astype(F32))
    done = pltpu.make_async_copy(sums, gradient, sems.at[0])
    done.start()
    done.wait()


def per_device(down_state, up_state, source, reflect, screen_class, screen_values, freq_index):
    depth = lax.axis_size("depth")
    shots = lax.axis_size("shot")
    levels, fronts, parts, rows_x, rows_y = down_state.shape
    if levels != 2 or depth % 2 or shots % 2 or HOPS != 3:
        return per_device_plain(down_state, up_state, source, reflect, screen_class, screen_values, freq_index)
    scale = 1.0 / math.sqrt(fronts * shots)
    half = rows_x // 2
    hx = jnp.asarray(hartley(rows_x))
    hy = jnp.asarray(hartley(rows_y))
    partners = [(i, i ^ 1) for i in range(depth)]
    beyond = [(i, i + 1) for i in range(1, depth - 1, 2)] + [(i + 1, i) for i in range(1, depth - 1, 2)]
    to_partner = functools.partial(lax.ppermute, axis_name="depth", perm=partners)
    to_beyond = functools.partial(lax.ppermute, axis_name="depth", perm=beyond)
    across = functools.partial(lax.ppermute, axis_name="shot", perm=[(i, i ^ 1) for i in range(shots)])
    plane = jax.ShapeDtypeStruct((fronts, parts, rows_x, rows_y), BF16)
    half_plane = jax.ShapeDtypeStruct((fronts, parts, half, rows_y), BF16)
    pair = jax.ShapeDtypeStruct((2, rows_x, rows_y), F32)
    turns = jax.ShapeDtypeStruct((fronts, parts, rows_x, rows_y), F32)
    screens = jax.ShapeDtypeStruct((2, fronts, parts, rows_x, rows_y), F32)
    state = jax.ShapeDtypeStruct(down_state.shape, BF16)
    dma = pltpu.SemaphoreType.DMA

    def call(kernel, in_specs, out_specs, out_shape, scratch=(), **more):
        return pl.pallas_call(
            kernel,
            in_specs=in_specs,
            out_specs=out_specs,
            out_shape=out_shape,
            scratch_shapes=list(scratch),
            compiler_params=PARAMS,
            **more,
        )

    def kept_in_hbm(*arrays):
        return [pltpu.with_memory_space_constraint(array, pltpu.HBM) for array in arrays]

    def buffers(count, shape=plane):
        return [pltpu.VMEM(shape.shape, shape.dtype)] * count

    def work(slots):
        return pltpu.VMEM((slots, *plane.shape[1:]), BF16)

    out_outer, in_inner = call(edges_kernel, [HBM] * 2, [VMEM] * 2, [plane] * 2, [dma((2,))])(
        *kept_in_hbm(down_state, up_state)
    )
    arrived_0 = to_beyond(out_outer)
    partner_0 = to_partner(in_inner)
    q_out_inner_0, q_in_outer_0, screen, phase, refl = call(
        setup_kernel,
        [HBM] * 4 + [SMEM] * 2 + [VMEM] * 2,
        [VMEM] * 5,
        [plane] * 2 + [screens, turns, pair],
        [
            pltpu.VMEM((2, *plane.shape), BF16),
            pltpu.VMEM((2, rows_x, rows_y), jnp.int32),
            work(2 * fronts),
            dma((6,)),
        ],
    )(*kept_in_hbm(down_state, up_state, reflect, screen_class), screen_values, freq_index, hx, hy)
    fixed = (screen, refl, phase, hx, hy)
    in_inner_1, q_out_inner_1 = call(ahead_kernel, [VMEM] * 7, [VMEM] * 2, [plane] * 2, buffers(2) + [work(fronts)])(
        partner_0, q_in_outer_0, *fixed
    )
    partner_1 = to_partner(in_inner_1)
    out_outer_1, q_arrived = call(edge_kernel, [VMEM] * 8, [VMEM] * 2, [plane] * 2, [work(fronts)])(
        arrived_0, source, q_out_inner_0, *fixed
    )
    arrived_1 = to_beyond(out_outer_1)
    in_inner_2, out_inner_2 = call(
        inner_kernel, [VMEM] * 8, [VMEM] * 2, [plane] * 2, buffers(3) + [work(2 * fronts)]
    )(q_arrived, q_out_inner_0, partner_1, *fixed)
    partner_2 = to_partner(in_inner_2)
    q_out_inner_2 = call(spread_kernel, [VMEM] * 4, VMEM, plane, [work(fronts)])(out_inner_2, phase, hx, hy)
    q_arrived_1, last_far, last_near = call(
        last_edge_kernel,
        [VMEM] * 8 + [pl.BlockSpec(memory_space=pl.ANY)],
        [VMEM] * 3,
        [plane] + [half_plane] * 2,
        buffers(1) + [work(fronts)],
    )(arrived_1, source, q_out_inner_1, *fixed, q_out_inner_2)
    last_far = to_beyond(last_far)
    last_near = to_beyond(last_near)
    half_sum = jax.ShapeDtypeStruct((half, rows_y), BF16)
    inner_in, inner_out, inner_terms, inner_far = call(
        last_inner_kernel,
        [VMEM] * 8,
        [VMEM] * 4,
        [plane] * 2 + [jax.ShapeDtypeStruct((rows_x, rows_y), F32), half_sum],
        buffers(3) + [work(2 * fronts)],
    )(q_arrived_1, q_out_inner_1, partner_2, *fixed)
    inner_other = across(inner_far) if shots == 2 else jnp.zeros_like(inner_far)
    far_in, far_out, outer_far = call(
        far_rows_kernel,
        [VMEM] * 5 + [pl.BlockSpec(memory_space=pl.ANY)],
        [VMEM] * 3,
        [half_plane] * 2 + [half_sum],
    )(last_far, q_arrived, q_out_inner_2, screen, refl, inner_terms)
    outer_other = across(outer_far) if shots == 2 else jnp.zeros_like(outer_far)
    down, up, outer_near = call(
        near_rows_kernel,
        [VMEM] * 9,
        [HBM] * 2 + [VMEM],
        [state, state, jax.ShapeDtypeStruct((half, rows_y), F32)],
        buffers(2, half_plane) + [dma((3, 2))],
    )(last_near, q_arrived, q_out_inner_2, screen, refl, inner_in, inner_out, far_in, far_out)
    gradient = call(
        functools.partial(gradient_kernel, scale),
        [VMEM] * 4,
        HBM,
        jax.ShapeDtypeStruct((2, half, rows_y), F32),
        [pltpu.VMEM((2, half, rows_y), F32), dma((1,))],
    )(outer_near, inner_terms, outer_other, inner_other)
    if shots != 2:
        terms = scale * jnp.stack([outer_far, inner_far]).astype(F32)
        far = jnp.where(odd_place() == 0, terms, terms[::-1])
        top = lax.rem(lax.axis_index("shot"), 2) == 0
        whole = jnp.concatenate([jnp.where(top, gradient, far), jnp.where(top, far, gradient)], axis=1)
        gradient = lax.psum_scatter(whole.astype(BF16), "shot", scatter_dimension=1, tiled=True).astype(F32)
    return (down, up, gradient)


def solution(mesh):
    return jax.shard_map(
        per_device,
        mesh=mesh,
        in_specs=(
            P("depth", "shot", None, None, None),
            P("depth", "shot", None, None, None),
            P("shot", None, None, None),
            P("depth", None, None),
            P("depth", None, None),
            P(),
            P("shot"),
        ),
        out_specs=(
            P("depth", "shot", None, None, None),
            P("depth", "shot", None, None, None),
            P("depth", "shot", None),
        ),
        check_vma=False,
    )
```

```python
import functools
import math

import jax
import jax.numpy as jnp
import numpy as np
from jax import lax
from jax.experimental import pallas as pl
from jax.experimental.pallas import tpu as pltpu
from jax.sharding import PartitionSpec as P

HOPS = 3
NCLASS = 16
NFREQ = 128
F32 = jnp.float32
BF16 = jnp.bfloat16
VMEM = pl.BlockSpec(memory_space=pltpu.VMEM)
HBM = pl.BlockSpec(memory_space=pltpu.HBM)
SMEM = pl.BlockSpec(memory_space=pltpu.SMEM)
PARAMS = pltpu.CompilerParams(vmem_limit_bytes=28 * 2**20)


def passed_along(block, axis, distance):
    devices = range(lax.axis_size(axis))
    route = [(i - distance, i) for i in devices if i - distance in devices]
    return lax.ppermute(block, axis, route)


def dft_tables(length):
    counter = jnp.arange(length, dtype=jnp.int32)
    product = counter[:, None] * counter[None, :] % length
    angles = 2.0 * math.pi / length * product.astype(jnp.float32)
    return (jnp.cos(angles).astype(jnp.bfloat16), jnp.sin(angles).astype(jnp.bfloat16))


def wavenumbers(length):
    counter = jnp.arange(length, dtype=jnp.int32)
    wrapped = jnp.where(counter >= length // 2, counter - length, counter)
    return 2.0 * math.pi / length * wrapped.astype(jnp.float32)


def propagate(planes, phase_re, phase_im, tables):
    fwd_left, fwd_right, inv_left, inv_right = tables
    first = jnp.einsum(
        "cdjk,...dkl->...cjl", fwd_left, planes, preferred_element_type=jnp.float32
    ).astype(jnp.bfloat16)
    second = jnp.einsum("...djl,dclm->...cjm", first, fwd_right, preferred_element_type=jnp.float32)
    real_part = second[..., 0, :, :]
    imag_part = second[..., 1, :, :]
    turned = jnp.stack(
        [real_part * phase_re - imag_part * phase_im, real_part * phase_im + imag_part * phase_re],
        axis=-3,
    ).astype(jnp.bfloat16)
    third = jnp.einsum(
        "cdjk,...dkl->...cjl", inv_left, turned, preferred_element_type=jnp.float32
    ).astype(jnp.bfloat16)
    return jnp.einsum(
        "...djl,dclm->...cjm", third, inv_right, preferred_element_type=jnp.float32
    ).astype(jnp.bfloat16)


def trade(down_edge, up_edge):
    got_down = passed_along(down_edge, "depth", 1)
    got_up = passed_along(up_edge, "depth", -1)
    return (got_down, got_up)


def per_device_plain(down_state, up_state, source, reflect, screen_class, screen_values, freq_index):
    levels = down_state.shape[0]
    rows_x = down_state.shape[3]
    rows_y = down_state.shape[4]
    front_count = down_state.shape[1]
    depth_rank = lax.axis_index("depth")
    scale = 1.0 / math.sqrt(front_count * lax.axis_size("shot"))
    cos_x, sin_x = dft_tables(rows_x)
    cos_y, sin_y = dft_tables(rows_y)
    tables = (
        jnp.stack([jnp.stack([cos_x, sin_x]), jnp.stack([-sin_x, cos_x])]),
        jnp.stack([jnp.stack([cos_y, -sin_y]), jnp.stack([sin_y, cos_y])]),
        jnp.stack([jnp.stack([cos_x, -sin_x]), jnp.stack([sin_x, cos_x])]),
        jnp.stack([jnp.stack([cos_y, sin_y]), jnp.stack([-sin_y, cos_y])]),
    )
    kwave = 0.95 * math.pi * (freq_index.astype(jnp.float32) + 1.0) / NFREQ
    kx_wave = wavenumbers(rows_x)
    ky_wave = wavenumbers(rows_y)
    vertical = kwave[:, None, None] ** 2 - kx_wave[None, :, None] ** 2 - ky_wave[None, None, :] ** 2
    propag = jnp.sqrt(jnp.maximum(vertical, 0.0))
    damping = jnp.exp(-jnp.sqrt(jnp.maximum(-vertical, 0.0))) / (rows_x * rows_y)
    phase_re = damping * jnp.cos(propag)
    phase_im = damping * jnp.sin(propag)
    classes = jnp.arange(NCLASS, dtype=jnp.int32)
    onehot = (screen_class[None] == classes[:, None, None, None]).astype(jnp.float32)
    slowness = jnp.einsum("c,clxy->lxy", screen_values, onehot, precision=lax.Precision.HIGHEST)
    angle = kwave[None, :, None, None] * slowness[:, None]
    screen_re = jnp.cos(angle)
    screen_im = jnp.sin(angle)
    refl = reflect[:, None]
    top_slab = depth_rank == 0
    down = down_state
    up = up_state
    a_re = a_im = b_re = b_im = None
    for repeat in range(HOPS):
        down_edge = down[levels - 1]
        up_edge = up[0]
        got_down, got_up = trade(down_edge, up_edge)
        got_down = jnp.where(top_slab, source, got_down)
        moved = propagate(
            jnp.concatenate([got_down[None], down[: levels - 1], up[1:], got_up[None]], axis=0),
            phase_re,
            phase_im,
            tables,
        )
        from_above = moved[:levels]
        from_below = moved[levels:]
        qa_re = from_above[:, :, 0].astype(jnp.float32)
        qa_im = from_above[:, :, 1].astype(jnp.float32)
        qb_re = from_below[:, :, 0].astype(jnp.float32)
        qb_im = from_below[:, :, 1].astype(jnp.float32)
        a_re = screen_re * qa_re - screen_im * qa_im
        a_im = screen_re * qa_im + screen_im * qa_re
        b_re = screen_re * qb_re - screen_im * qb_im
        b_im = screen_re * qb_im + screen_im * qb_re
        down = jnp.stack(
            [(1.0 + refl) * a_re - refl * b_re, (1.0 + refl) * a_im - refl * b_im], axis=2
        ).astype(jnp.bfloat16)
        up = jnp.stack(
            [(1.0 - refl) * b_re + refl * a_re, (1.0 - refl) * b_im + refl * a_im], axis=2
        ).astype(jnp.bfloat16)
    terms = scale * jnp.sum(a_re * b_re + a_im * b_im, axis=1)
    gradient = lax.psum_scatter(
        terms.astype(jnp.bfloat16), "shot", scatter_dimension=1, tiled=True
    ).astype(jnp.float32)
    return (down, up, gradient)


def hartley(length):
    counter = np.arange(length)
    angles = 2.0 * np.pi / length * (counter[:, None] * counter[None, :] % length)
    cosine = np.cos(angles).astype(BF16).astype(np.float32)
    sine = np.sin(angles).astype(BF16).astype(np.float32)
    return (cosine + sine).astype(BF16)


def odd_place():
    return lax.rem(lax.axis_index("depth"), 2)


def mm(left, right):
    return jnp.dot(left, right, preferred_element_type=F32)


def spread(jobs, work, hx, hy, phase):
    jobs = list(enumerate(jobs))
    for slot, (plane, _, _) in jobs:
        for part in range(2):
            work[slot, part] = mm(plane(part) if callable(plane) else plane[part], hy[...]).astype(BF16)
    for slot, (_, front, _) in jobs:
        turn_re, turn_im = phase[front, 0], phase[front, 1]
        part_re = mm(hx[...], work[slot, 0])
        part_im = mm(hx[...], work[slot, 1])
        work[slot, 0] = (part_re * turn_re - part_im * turn_im).astype(BF16)
        work[slot, 1] = (part_re * turn_im + part_im * turn_re).astype(BF16)
    for slot, _ in jobs:
        for part in range(2):
            work[slot, part] = mm(hx[...], work[slot, part]).astype(BF16)
    for slot, (_, _, target) in jobs:
        for part in range(2):
            if isinstance(target, list):
                for rows, piece in target:
                    piece[part] = mm(work[slot, part, rows, :], hy[...]).astype(BF16)
            else:
                target[part] = mm(work[slot, part], hy[...]).astype(BF16)


def screened(real_part, imag_part, screen_re, screen_im):
    return (
        screen_re * real_part - screen_im * imag_part,
        screen_re * imag_part + screen_im * real_part,
    )


def mixed(a_re, a_im, b_re, b_im, refl, screen_re, screen_im, waves="both"):
    a_re, a_im, b_re, b_im = (part.astype(F32) for part in (a_re, a_im, b_re, b_im))
    step_re = refl * (a_re - b_re)
    step_im = refl * (a_im - b_im)
    fields = ()
    if waves != "outward":
        fields += screened(a_re + step_re, a_im + step_im, screen_re, screen_im)
    if waves != "inward":
        fields += screened(b_re + step_re, b_im + step_im, screen_re, screen_im)
    return fields


def put(target, real_part, imag_part):
    target[0] = real_part.astype(BF16)
    target[1] = imag_part.astype(BF16)


def half_rows(of, half):
    shot = lax.rem(lax.axis_index("shot"), 2)
    return pl.ds(pl.multiple_of((shot if of == 0 else 1 - shot) * half, half), half)


def edges_kernel(down, up, outward_outer, inward_inner, sems):
    levels = down.shape[0]
    odd = odd_place()

    def fetch(first, second):
        pltpu.make_async_copy(first, outward_outer, sems.at[0]).start()
        pltpu.make_async_copy(second, inward_inner, sems.at[1]).start()

    @pl.when(odd == 0)
    def _():
        fetch(up.at[0], down.at[levels - 1])

    @pl.when(odd == 1)
    def _():
        fetch(down.at[levels - 1], up.at[0])

    pltpu.make_async_copy(up.at[0], outward_outer, sems.at[0]).wait()
    pltpu.make_async_copy(up.at[0], inward_inner, sems.at[1]).wait()


def class_rows(slowness, kwave, shape):
    lanes = lax.broadcasted_iota(jnp.int32, shape, 1)
    table = jnp.zeros(shape, F32)
    for entry in range(NCLASS):
        table = jnp.where(lanes == entry, slowness[entry], table)
    angle = kwave * table
    return jnp.cos(angle), jnp.sin(angle)


def look_up(table, classes):
    width = 128
    rows = classes.shape[0]
    wide = jnp.broadcast_to(table[:1], (rows, width))
    pieces = [
        jnp.take_along_axis(wide, classes[:, start : start + width], axis=1, mode="promise_in_bounds")
        for start in range(0, classes.shape[1], width)
    ]
    return jnp.concatenate(pieces, axis=1)


def front_wave(freq, front):
    return 0.95 * math.pi * (freq[front].astype(F32) + 1.0) / NFREQ


def series(square, shift):
    total = jnp.full_like(square, 1.0 / math.factorial(18 + shift))
    for order in range(16, -1, -2):
        total = 1.0 / math.factorial(order + shift) - square * total
    return total


def setup_kernel(
    down, up, reflect, classes_in, slowness, freq, hx, hy,
    q_out_inner, q_in_outer, screen, phase, refl,
    fields, klass, work, sems,
):
    fronts = q_out_inner.shape[0]
    rows_x, rows_y = refl.shape[1:]
    odd = odd_place()
    fixed = [
        pltpu.make_async_copy(reflect.at[odd], refl.at[0], sems.at[2]),
        pltpu.make_async_copy(reflect.at[1 - odd], refl.at[1], sems.at[3]),
        pltpu.make_async_copy(classes_in.at[odd], klass.at[0], sems.at[4]),
        pltpu.make_async_copy(classes_in.at[1 - odd], klass.at[1], sems.at[5]),
    ]
    for copy in fixed:
        copy.start()

    @pl.when(odd == 0)
    def _():
        pltpu.make_async_copy(down.at[0], fields.at[0], sems.at[0]).start()
        pltpu.make_async_copy(up.at[1], fields.at[1], sems.at[1]).start()

    @pl.when(odd == 1)
    def _():
        pltpu.make_async_copy(up.at[1], fields.at[0], sems.at[0]).start()
        pltpu.make_async_copy(down.at[0], fields.at[1], sems.at[1]).start()

    def squares(length, axis):
        counter = lax.broadcasted_iota(jnp.int32, (rows_x, rows_y), axis)
        wrapped = jnp.where(counter >= length // 2, counter - length, counter)
        wave = 2.0 * math.pi / length * wrapped.astype(F32)
        return wave * wave

    lateral = squares(rows_x, 0) + squares(rows_y, 1)
    level_out = 1.0 / (rows_x * rows_y)
    for front in range(fronts):
        kwave = front_wave(freq, front)
        vertical = kwave * kwave - lateral
        travels = vertical > 0.0
        square = jnp.maximum(vertical, 0.0)
        root = jnp.sqrt(jnp.abs(vertical))
        phase[front, 0] = jnp.where(travels, series(square, 0), jnp.exp(-root)) * level_out
        phase[front, 1] = jnp.where(travels, root * series(square, 1), 0.0) * level_out
    for copy in fixed:
        copy.wait()
    sign = jnp.where(odd == 0, 1.0, -1.0).astype(F32)
    for level in range(2):
        refl[level] = sign * refl[level]
    for front in range(fronts):
        cos_row, sin_row = class_rows(slowness, front_wave(freq, front), (8, 128))
        for level in range(2):
            screen[level, front, 0] = look_up(cos_row, klass[level])
            screen[level, front, 1] = look_up(sin_row, klass[level])
    pltpu.make_async_copy(down.at[0], fields.at[0], sems.at[0]).wait()
    pltpu.make_async_copy(down.at[0], fields.at[1], sems.at[1]).wait()
    jobs = [(fields.at[1, front], front, q_out_inner.at[front]) for front in range(fronts)]
    jobs += [(fields.at[0, front], front, q_in_outer.at[front]) for front in range(fronts)]
    spread(jobs, work, hx, hy, phase)


def ahead_kernel(
    partner, q_in_outer, screen, refl, phase, hx, hy,
    inward_inner, q_out_inner,
    q_field, field, work,
):
    everyone = range(partner.shape[0])
    spread([(partner.at[front], front, q_field.at[front]) for front in everyone], work, hx, hy, phase)
    for front in everyone:
        in_re, in_im, out_re, out_im = mixed(
            q_in_outer[front, 0], q_in_outer[front, 1], q_field[front, 0], q_field[front, 1],
            refl[1], screen[1, front, 0], screen[1, front, 1],
        )
        put(inward_inner.at[front], in_re, in_im)
        put(field.at[front], out_re, out_im)
    spread([(field.at[front], front, q_out_inner.at[front]) for front in everyone], work, hx, hy, phase)


def entering(arrived, source, front):
    first = lax.axis_index("depth") == 0
    return lambda part: jnp.where(first, source[front, part], arrived[front, part])


def outer_step(q_arrived, q_out_inner, screen, refl, waves, field):
    for front in range(field.shape[0]):
        put(
            field.at[front],
            *mixed(
                q_arrived[front, 0], q_arrived[front, 1], q_out_inner[front, 0], q_out_inner[front, 1],
                refl[0], screen[0, front, 0], screen[0, front, 1], waves,
            ),
        )


def edge_kernel(arrived, source, q_out_inner, screen, refl, phase, hx, hy, outward, q_arrived, work):
    everyone = range(arrived.shape[0])
    spread([(entering(arrived, source, front), front, q_arrived.at[front]) for front in everyone], work, hx, hy, phase)
    outer_step(q_arrived, q_out_inner, screen, refl, "outward", outward)


def last_edge_kernel(
    arrived, source, q_out_inner, screen, refl, phase, hx, hy, after,
    q_arrived, last_far, last_near,
    outward, work,
):
    del after
    everyone = range(arrived.shape[0])
    half = arrived.shape[2] // 2
    spread([(entering(arrived, source, front), front, q_arrived.at[front]) for front in everyone], work, hx, hy, phase)
    outer_step(q_arrived, q_out_inner, screen, refl, "outward", outward)
    jobs = [
        (outward.at[front], front, [(half_rows(1, half), last_far.at[front]), (half_rows(0, half), last_near.at[front])])
        for front in everyone
    ]
    spread(jobs, work, hx, hy, phase)


def inner_kernel(
    q_arrived, q_out_inner, partner, screen, refl, phase, hx, hy,
    inward, outward,
    field, q_inward, q_partner, work,
):
    everyone = range(partner.shape[0])
    outer_step(q_arrived, q_out_inner, screen, refl, "inward", field)
    jobs = [(partner.at[front], front, q_partner.at[front]) for front in everyone]
    jobs += [(field.at[front], front, q_inward.at[front]) for front in everyone]
    spread(jobs, work, hx, hy, phase)
    for front in everyone:
        in_re, in_im, out_re, out_im = mixed(
            q_inward[front, 0], q_inward[front, 1], q_partner[front, 0], q_partner[front, 1],
            refl[1], screen[1, front, 0], screen[1, front, 1],
        )
        put(inward.at[front], in_re, in_im)
        put(outward.at[front], out_re, out_im)


def spread_kernel(fields, phase, hx, hy, q_fields, work):
    everyone = range(fields.shape[0])
    spread([(fields.at[front], front, q_fields.at[front]) for front in everyone], work, hx, hy, phase)


def last_inner_kernel(
    q_arrived, q_out_inner, partner, screen, refl, phase, hx, hy,
    inward, outward, terms, far_terms,
    field, q_inward, q_partner, work,
):
    everyone = range(partner.shape[0])
    outer_step(q_arrived, q_out_inner, screen, refl, "inward", field)
    jobs = [(partner.at[front], front, q_partner.at[front]) for front in everyone]
    jobs += [(field.at[front], front, q_inward.at[front]) for front in everyone]
    spread(jobs, work, hx, hy, phase)
    total = None
    for front in everyone:
        a_re, a_im = (q_inward[front, part].astype(F32) for part in range(2))
        b_re, b_im = (q_partner[front, part].astype(F32) for part in range(2))
        in_re, in_im, out_re, out_im = mixed(
            a_re, a_im, b_re, b_im, refl[1], screen[1, front, 0], screen[1, front, 1]
        )
        put(inward.at[front], in_re, in_im)
        put(outward.at[front], out_re, out_im)
        term = a_re * b_re + a_im * b_im
        total = term if total is None else total + term
    terms[...] = total
    far_terms[...] = terms[half_rows(1, far_terms.shape[0]), :].astype(BF16)


def incoming(last, q_arrived, front, rows):
    first = lax.axis_index("depth") == 0
    return [jnp.where(first, q_arrived[front, part, rows, :], last[front, part]).astype(F32) for part in range(2)]


def row_terms(of, last, q_arrived, q_out_inner):
    total = None
    rows = half_rows(of, last.shape[2])
    for front in range(last.shape[0]):
        a_re, a_im = incoming(last, q_arrived, front, rows)
        b_re, b_im = (q_out_inner[front, part, rows, :].astype(F32) for part in range(2))
        term = a_re * b_re + a_im * b_im
        total = term if total is None else total + term
    return total


def row_fields(of, last, q_arrived, q_out_inner, screen, refl, inward, outward):
    rows = half_rows(of, last.shape[2])
    for front in range(last.shape[0]):
        a_re, a_im = incoming(last, q_arrived, front, rows)
        b_re, b_im = (q_out_inner[front, part, rows, :].astype(F32) for part in range(2))
        in_re, in_im, out_re, out_im = mixed(
            a_re, a_im, b_re, b_im, refl[0, rows, :], screen[0, front, 0, rows, :], screen[0, front, 1, rows, :]
        )
        put(inward.at[front], in_re, in_im)
        put(outward.at[front], out_re, out_im)
    return rows


def far_terms_kernel(last, q_arrived, q_out_inner, after, terms):
    del after
    terms[...] = row_terms(1, last, q_arrived, q_out_inner).astype(BF16)


def send_home(level, rows, inward, outward, down_out, up_out, sems):
    odd = odd_place()

    def copies(place, inward_out, outward_out):
        return [
            pltpu.make_async_copy(inward, inward_out.at[place, :, :, rows, :], sems.at[0]),
            pltpu.make_async_copy(outward, outward_out.at[place, :, :, rows, :], sems.at[1]),
        ]

    @pl.when(odd == 0)
    def _():
        for copy in copies(level, down_out, up_out):
            copy.start()

    @pl.when(odd == 1)
    def _():
        for copy in copies(1 - level, up_out, down_out):
            copy.start()

    return copies(0, down_out, up_out)


def outer_fields_kernel(
    scale, near, far, q_arrived, q_out_inner, screen, refl, inner_in, inner_out, inner_terms, inner_other,
    down_out, up_out, gradient, terms,
    near_in, near_out, far_in, far_out, inner_sum, sems,
):
    rows_x = inner_in.shape[2]
    waits = send_home(1, pl.ds(0, rows_x), inner_in, inner_out, down_out, up_out, sems.at[0])
    rows = row_fields(1, far, q_arrived, q_out_inner, screen, refl, far_in, far_out)
    waits += send_home(0, rows, far_in, far_out, down_out, up_out, sems.at[1])
    rows = row_fields(0, near, q_arrived, q_out_inner, screen, refl, near_in, near_out)
    waits += send_home(0, rows, near_in, near_out, down_out, up_out, sems.at[2])
    inner_sum[...] = scale * (inner_terms[rows, :] + inner_other[...].astype(F32))
    waits.append(pltpu.make_async_copy(inner_sum, gradient.at[1 - odd_place()], sems.at[3, 0]))
    waits[-1].start()
    terms[...] = row_terms(0, near, q_arrived, q_out_inner)
    for copy in waits:
        copy.wait()


def outer_gradient_kernel(scale, terms, other, gradient_in, gradient, outer_sum, sems):
    del gradient_in
    outer_sum[...] = scale * (terms[...] + other[...].astype(F32))
    done = pltpu.make_async_copy(outer_sum, gradient.at[odd_place()], sems.at[0])
    done.start()
    done.wait()


def per_device(down_state, up_state, source, reflect, screen_class, screen_values, freq_index):
    depth = lax.axis_size("depth")
    shots = lax.axis_size("shot")
    levels, fronts, parts, rows_x, rows_y = down_state.shape
    if levels != 2 or depth % 2 or shots % 2 or HOPS != 3:
        return per_device_plain(down_state, up_state, source, reflect, screen_class, screen_values, freq_index)
    scale = 1.0 / math.sqrt(fronts * shots)
    half = rows_x // 2
    hx = jnp.asarray(hartley(rows_x))
    hy = jnp.asarray(hartley(rows_y))
    partners = [(i, i ^ 1) for i in range(depth)]
    beyond = [(i, i + 1) for i in range(1, depth - 1, 2)] + [(i + 1, i) for i in range(1, depth - 1, 2)]
    to_partner = functools.partial(lax.ppermute, axis_name="depth", perm=partners)
    to_beyond = functools.partial(lax.ppermute, axis_name="depth", perm=beyond)
    across = functools.partial(lax.ppermute, axis_name="shot", perm=[(i, i ^ 1) for i in range(shots)])
    plane = jax.ShapeDtypeStruct((fronts, parts, rows_x, rows_y), BF16)
    half_plane = jax.ShapeDtypeStruct((fronts, parts, half, rows_y), BF16)
    pair = jax.ShapeDtypeStruct((2, rows_x, rows_y), F32)
    turns = jax.ShapeDtypeStruct((fronts, parts, rows_x, rows_y), F32)
    screens = jax.ShapeDtypeStruct((2, fronts, parts, rows_x, rows_y), F32)
    state = jax.ShapeDtypeStruct(down_state.shape, BF16)
    dma = pltpu.SemaphoreType.DMA

    def call(kernel, in_specs, out_specs, out_shape, scratch=(), **more):
        return pl.pallas_call(
            kernel,
            in_specs=in_specs,
            out_specs=out_specs,
            out_shape=out_shape,
            scratch_shapes=list(scratch),
            compiler_params=PARAMS,
            **more,
        )

    def kept_in_hbm(*arrays):
        return [pltpu.with_memory_space_constraint(array, pltpu.HBM) for array in arrays]

    def buffers(count, shape=plane):
        return [pltpu.VMEM(shape.shape, shape.dtype)] * count

    def work(slots):
        return pltpu.VMEM((slots, *plane.shape[1:]), BF16)

    out_outer, in_inner = call(edges_kernel, [HBM] * 2, [VMEM] * 2, [plane] * 2, [dma((2,))])(
        *kept_in_hbm(down_state, up_state)
    )
    arrived_0 = to_beyond(out_outer)
    partner_0 = to_partner(in_inner)
    q_out_inner_0, q_in_outer_0, screen, phase, refl = call(
        setup_kernel,
        [HBM] * 4 + [SMEM] * 2 + [VMEM] * 2,
        [VMEM] * 5,
        [plane] * 2 + [screens, turns, pair],
        [
            pltpu.VMEM((2, *plane.shape), BF16),
            pltpu.VMEM((2, rows_x, rows_y), jnp.int32),
            work(2 * fronts),
            dma((6,)),
        ],
    )(*kept_in_hbm(down_state, up_state, reflect, screen_class), screen_values, freq_index, hx, hy)
    fixed = (screen, refl, phase, hx, hy)
    in_inner_1, q_out_inner_1 = call(ahead_kernel, [VMEM] * 7, [VMEM] * 2, [plane] * 2, buffers(2) + [work(fronts)])(
        partner_0, q_in_outer_0, *fixed
    )
    partner_1 = to_partner(in_inner_1)
    out_outer_1, q_arrived = call(edge_kernel, [VMEM] * 8, [VMEM] * 2, [plane] * 2, [work(fronts)])(
        arrived_0, source, q_out_inner_0, *fixed
    )
    arrived_1 = to_beyond(out_outer_1)
    in_inner_2, out_inner_2 = call(
        inner_kernel, [VMEM] * 8, [VMEM] * 2, [plane] * 2, buffers(3) + [work(2 * fronts)]
    )(q_arrived, q_out_inner_0, partner_1, *fixed)
    partner_2 = to_partner(in_inner_2)
    q_out_inner_2 = call(spread_kernel, [VMEM] * 4, VMEM, plane, [work(fronts)])(out_inner_2, phase, hx, hy)
    q_arrived_1, last_far, last_near = call(
        last_edge_kernel,
        [VMEM] * 8 + [pl.BlockSpec(memory_space=pl.ANY)],
        [VMEM] * 3,
        [plane] + [half_plane] * 2,
        buffers(1) + [work(fronts)],
    )(arrived_1, source, q_out_inner_1, *fixed, q_out_inner_2)
    last_far = to_beyond(last_far)
    last_near = to_beyond(last_near)
    half_sum = jax.ShapeDtypeStruct((half, rows_y), BF16)
    inner_in, inner_out, inner_terms, inner_far = call(
        last_inner_kernel,
        [VMEM] * 8,
        [VMEM] * 4,
        [plane] * 2 + [jax.ShapeDtypeStruct((rows_x, rows_y), F32), half_sum],
        buffers(3) + [work(2 * fronts)],
    )(q_arrived_1, q_out_inner_1, partner_2, *fixed)
    inner_other = across(inner_far) if shots == 2 else jnp.zeros_like(inner_far)
    outer_far = call(far_terms_kernel, [VMEM] * 3 + [pl.BlockSpec(memory_space=pl.ANY)], VMEM, half_sum)(
        last_far, q_arrived, q_out_inner_2, inner_terms
    )
    outer_other = across(outer_far) if shots == 2 else jnp.zeros_like(outer_far)
    half_total = jax.ShapeDtypeStruct((half, rows_y), F32)
    share = jax.ShapeDtypeStruct((2, half, rows_y), F32)
    down, up, gradient, outer_near = call(
        functools.partial(outer_fields_kernel, scale),
        [VMEM] * 10,
        [HBM] * 3 + [VMEM],
        [state, state, share, half_total],
        buffers(4, half_plane) + buffers(1, half_total) + [dma((4, 2))],
    )(
        last_near, last_far, q_arrived, q_out_inner_2, screen, refl, inner_in, inner_out, inner_terms, inner_other
    )
    gradient = call(
        functools.partial(outer_gradient_kernel, scale),
        [VMEM] * 2 + [HBM],
        HBM,
        share,
        buffers(1, half_total) + [dma((1,))],
        input_output_aliases={2: 0},
    )(outer_near, outer_other, gradient)
    if shots != 2:
        terms = scale * jnp.stack([outer_far, inner_far]).astype(F32)
        far = jnp.where(odd_place() == 0, terms, terms[::-1])
        top = lax.rem(lax.axis_index("shot"), 2) == 0
        whole = jnp.concatenate([jnp.where(top, gradient, far), jnp.where(top, far, gradient)], axis=1)
        gradient = lax.psum_scatter(whole.astype(BF16), "shot", scatter_dimension=1, tiled=True).astype(F32)
    return (down, up, gradient)


def solution(mesh):
    return jax.shard_map(
        per_device,
        mesh=mesh,
        in_specs=(
            P("depth", "shot", None, None, None),
            P("depth", "shot", None, None, None),
            P("shot", None, None, None),
            P("depth", None, None),
            P("depth", None, None),
            P(),
            P("shot"),
        ),
        out_specs=(
            P("depth", "shot", None, None, None),
            P("depth", "shot", None, None, None),
            P("depth", "shot", None),
        ),
        check_vma=False,
    )
```

```python
import functools
import math

import jax
import jax.numpy as jnp
import numpy as np
from jax import lax
from jax.experimental import pallas as pl
from jax.experimental.pallas import tpu as pltpu
from jax.sharding import PartitionSpec as P

HOPS = 3
NCLASS = 16
NFREQ = 128
F32 = jnp.float32
BF16 = jnp.bfloat16
VMEM = pl.BlockSpec(memory_space=pltpu.VMEM)
HBM = pl.BlockSpec(memory_space=pltpu.HBM)
SMEM = pl.BlockSpec(memory_space=pltpu.SMEM)
PARAMS = pltpu.CompilerParams(vmem_limit_bytes=28 * 2**20)


def passed_along(block, axis, distance):
    devices = range(lax.axis_size(axis))
    route = [(i - distance, i) for i in devices if i - distance in devices]
    return lax.ppermute(block, axis, route)


def dft_tables(length):
    counter = jnp.arange(length, dtype=jnp.int32)
    product = counter[:, None] * counter[None, :] % length
    angles = 2.0 * math.pi / length * product.astype(jnp.float32)
    return (jnp.cos(angles).astype(jnp.bfloat16), jnp.sin(angles).astype(jnp.bfloat16))


def wavenumbers(length):
    counter = jnp.arange(length, dtype=jnp.int32)
    wrapped = jnp.where(counter >= length // 2, counter - length, counter)
    return 2.0 * math.pi / length * wrapped.astype(jnp.float32)


def propagate(planes, phase_re, phase_im, tables):
    fwd_left, fwd_right, inv_left, inv_right = tables
    first = jnp.einsum(
        "cdjk,...dkl->...cjl", fwd_left, planes, preferred_element_type=jnp.float32
    ).astype(jnp.bfloat16)
    second = jnp.einsum("...djl,dclm->...cjm", first, fwd_right, preferred_element_type=jnp.float32)
    real_part = second[..., 0, :, :]
    imag_part = second[..., 1, :, :]
    turned = jnp.stack(
        [real_part * phase_re - imag_part * phase_im, real_part * phase_im + imag_part * phase_re],
        axis=-3,
    ).astype(jnp.bfloat16)
    third = jnp.einsum(
        "cdjk,...dkl->...cjl", inv_left, turned, preferred_element_type=jnp.float32
    ).astype(jnp.bfloat16)
    return jnp.einsum(
        "...djl,dclm->...cjm", third, inv_right, preferred_element_type=jnp.float32
    ).astype(jnp.bfloat16)


def trade(down_edge, up_edge):
    got_down = passed_along(down_edge, "depth", 1)
    got_up = passed_along(up_edge, "depth", -1)
    return (got_down, got_up)


def per_device_plain(down_state, up_state, source, reflect, screen_class, screen_values, freq_index):
    levels = down_state.shape[0]
    rows_x = down_state.shape[3]
    rows_y = down_state.shape[4]
    front_count = down_state.shape[1]
    depth_rank = lax.axis_index("depth")
    scale = 1.0 / math.sqrt(front_count * lax.axis_size("shot"))
    cos_x, sin_x = dft_tables(rows_x)
    cos_y, sin_y = dft_tables(rows_y)
    tables = (
        jnp.stack([jnp.stack([cos_x, sin_x]), jnp.stack([-sin_x, cos_x])]),
        jnp.stack([jnp.stack([cos_y, -sin_y]), jnp.stack([sin_y, cos_y])]),
        jnp.stack([jnp.stack([cos_x, -sin_x]), jnp.stack([sin_x, cos_x])]),
        jnp.stack([jnp.stack([cos_y, sin_y]), jnp.stack([-sin_y, cos_y])]),
    )
    kwave = 0.95 * math.pi * (freq_index.astype(jnp.float32) + 1.0) / NFREQ
    kx_wave = wavenumbers(rows_x)
    ky_wave = wavenumbers(rows_y)
    vertical = kwave[:, None, None] ** 2 - kx_wave[None, :, None] ** 2 - ky_wave[None, None, :] ** 2
    propag = jnp.sqrt(jnp.maximum(vertical, 0.0))
    damping = jnp.exp(-jnp.sqrt(jnp.maximum(-vertical, 0.0))) / (rows_x * rows_y)
    phase_re = damping * jnp.cos(propag)
    phase_im = damping * jnp.sin(propag)
    classes = jnp.arange(NCLASS, dtype=jnp.int32)
    onehot = (screen_class[None] == classes[:, None, None, None]).astype(jnp.float32)
    slowness = jnp.einsum("c,clxy->lxy", screen_values, onehot, precision=lax.Precision.HIGHEST)
    angle = kwave[None, :, None, None] * slowness[:, None]
    screen_re = jnp.cos(angle)
    screen_im = jnp.sin(angle)
    refl = reflect[:, None]
    top_slab = depth_rank == 0
    down = down_state
    up = up_state
    a_re = a_im = b_re = b_im = None
    for repeat in range(HOPS):
        down_edge = down[levels - 1]
        up_edge = up[0]
        got_down, got_up = trade(down_edge, up_edge)
        got_down = jnp.where(top_slab, source, got_down)
        moved = propagate(
            jnp.concatenate([got_down[None], down[: levels - 1], up[1:], got_up[None]], axis=0),
            phase_re,
            phase_im,
            tables,
        )
        from_above = moved[:levels]
        from_below = moved[levels:]
        qa_re = from_above[:, :, 0].astype(jnp.float32)
        qa_im = from_above[:, :, 1].astype(jnp.float32)
        qb_re = from_below[:, :, 0].astype(jnp.float32)
        qb_im = from_below[:, :, 1].astype(jnp.float32)
        a_re = screen_re * qa_re - screen_im * qa_im
        a_im = screen_re * qa_im + screen_im * qa_re
        b_re = screen_re * qb_re - screen_im * qb_im
        b_im = screen_re * qb_im + screen_im * qb_re
        down = jnp.stack(
            [(1.0 + refl) * a_re - refl * b_re, (1.0 + refl) * a_im - refl * b_im], axis=2
        ).astype(jnp.bfloat16)
        up = jnp.stack(
            [(1.0 - refl) * b_re + refl * a_re, (1.0 - refl) * b_im + refl * a_im], axis=2
        ).astype(jnp.bfloat16)
    terms = scale * jnp.sum(a_re * b_re + a_im * b_im, axis=1)
    gradient = lax.psum_scatter(
        terms.astype(jnp.bfloat16), "shot", scatter_dimension=1, tiled=True
    ).astype(jnp.float32)
    return (down, up, gradient)


def hartley(length):
    counter = np.arange(length)
    angles = 2.0 * np.pi / length * (counter[:, None] * counter[None, :] % length)
    cosine = np.cos(angles).astype(BF16).astype(np.float32)
    sine = np.sin(angles).astype(BF16).astype(np.float32)
    return (cosine + sine).astype(BF16)


def odd_place():
    return lax.rem(lax.axis_index("depth"), 2)


def mm(left, right):
    return jnp.dot(left, right, preferred_element_type=F32)


def spread(jobs, work, hx, hy, phase):
    jobs = list(enumerate(jobs))
    for slot, (plane, _, _) in jobs:
        for part in range(2):
            work[slot, part] = mm(plane(part) if callable(plane) else plane[part], hy[...]).astype(BF16)
    for slot, (_, front, _) in jobs:
        turn_re, turn_im = phase[front, 0], phase[front, 1]
        part_re = mm(hx[...], work[slot, 0])
        part_im = mm(hx[...], work[slot, 1])
        work[slot, 0] = (part_re * turn_re - part_im * turn_im).astype(BF16)
        work[slot, 1] = (part_re * turn_im + part_im * turn_re).astype(BF16)
    for slot, _ in jobs:
        for part in range(2):
            work[slot, part] = mm(hx[...], work[slot, part]).astype(BF16)
    for slot, (_, _, target) in jobs:
        for part in range(2):
            if isinstance(target, list):
                for rows, piece in target:
                    piece[part] = mm(work[slot, part, rows, :], hy[...]).astype(BF16)
            else:
                target[part] = mm(work[slot, part], hy[...]).astype(BF16)


def screened(real_part, imag_part, screen_re, screen_im):
    return (
        screen_re * real_part - screen_im * imag_part,
        screen_re * imag_part + screen_im * real_part,
    )


def mixed(a_re, a_im, b_re, b_im, refl, screen_re, screen_im, waves="both"):
    a_re, a_im, b_re, b_im = (part.astype(F32) for part in (a_re, a_im, b_re, b_im))
    step_re = refl * (a_re - b_re)
    step_im = refl * (a_im - b_im)
    fields = ()
    if waves != "outward":
        fields += screened(a_re + step_re, a_im + step_im, screen_re, screen_im)
    if waves != "inward":
        fields += screened(b_re + step_re, b_im + step_im, screen_re, screen_im)
    return fields


def put(target, real_part, imag_part):
    target[0] = real_part.astype(BF16)
    target[1] = imag_part.astype(BF16)


def half_rows(of, half):
    shot = lax.rem(lax.axis_index("shot"), 2)
    return pl.ds(pl.multiple_of((shot if of == 0 else 1 - shot) * half, half), half)


def late_pair():
    return lax.rem(lax.div(lax.axis_index("depth") + 1, 2), 2) == 1


def by_turn(early, late):
    is_late = late_pair()
    pl.when(jnp.logical_not(is_late))(early)
    pl.when(is_late)(late)


def edges_kernel(down, up, outward_outer, inward_inner, sems):
    levels = down.shape[0]
    odd = odd_place()

    def fetch(first, second):
        pltpu.make_async_copy(first, outward_outer, sems.at[0]).start()
        pltpu.make_async_copy(second, inward_inner, sems.at[1]).start()

    @pl.when(odd == 0)
    def _():
        fetch(up.at[0], down.at[levels - 1])

    @pl.when(odd == 1)
    def _():
        fetch(down.at[levels - 1], up.at[0])

    pltpu.make_async_copy(up.at[0], outward_outer, sems.at[0]).wait()
    pltpu.make_async_copy(up.at[0], inward_inner, sems.at[1]).wait()


def class_rows(slowness, kwave, shape):
    lanes = lax.broadcasted_iota(jnp.int32, shape, 1)
    table = jnp.zeros(shape, F32)
    for entry in range(NCLASS):
        table = jnp.where(lanes == entry, slowness[entry], table)
    angle = kwave * table
    return jnp.cos(angle), jnp.sin(angle)


def look_up(table, classes):
    width = 128
    rows = classes.shape[0]
    wide = jnp.broadcast_to(table[:1], (rows, width))
    pieces = [
        jnp.take_along_axis(wide, classes[:, start : start + width], axis=1, mode="promise_in_bounds")
        for start in range(0, classes.shape[1], width)
    ]
    return jnp.concatenate(pieces, axis=1)


def front_wave(freq, front):
    return 0.95 * math.pi * (freq[front].astype(F32) + 1.0) / NFREQ


def series(square, shift):
    total = jnp.full_like(square, 1.0 / math.factorial(18 + shift))
    for order in range(16, -1, -2):
        total = 1.0 / math.factorial(order + shift) - square * total
    return total


def setup_kernel(
    down, up, reflect, classes_in, slowness, freq, hx, hy,
    q_out_inner, q_in_outer, screen, phase, refl,
    fields, klass, work, sems,
):
    fronts = q_out_inner.shape[0]
    rows_x, rows_y = refl.shape[1:]
    odd = odd_place()
    fixed = [
        pltpu.make_async_copy(reflect.at[odd], refl.at[0], sems.at[2]),
        pltpu.make_async_copy(reflect.at[1 - odd], refl.at[1], sems.at[3]),
        pltpu.make_async_copy(classes_in.at[odd], klass.at[0], sems.at[4]),
        pltpu.make_async_copy(classes_in.at[1 - odd], klass.at[1], sems.at[5]),
    ]
    for copy in fixed:
        copy.start()

    @pl.when(odd == 0)
    def _():
        pltpu.make_async_copy(down.at[0], fields.at[0], sems.at[0]).start()
        pltpu.make_async_copy(up.at[1], fields.at[1], sems.at[1]).start()

    @pl.when(odd == 1)
    def _():
        pltpu.make_async_copy(up.at[1], fields.at[0], sems.at[0]).start()
        pltpu.make_async_copy(down.at[0], fields.at[1], sems.at[1]).start()

    def squares(length, axis):
        counter = lax.broadcasted_iota(jnp.int32, (rows_x, rows_y), axis)
        wrapped = jnp.where(counter >= length // 2, counter - length, counter)
        wave = 2.0 * math.pi / length * wrapped.astype(F32)
        return wave * wave

    lateral = squares(rows_x, 0) + squares(rows_y, 1)
    level_out = 1.0 / (rows_x * rows_y)
    for front in range(fronts):
        kwave = front_wave(freq, front)
        vertical = kwave * kwave - lateral
        travels = vertical > 0.0
        square = jnp.maximum(vertical, 0.0)
        root = jnp.sqrt(jnp.abs(vertical))
        phase[front, 0] = jnp.where(travels, series(square, 0), jnp.exp(-root)) * level_out
        phase[front, 1] = jnp.where(travels, root * series(square, 1), 0.0) * level_out
    for copy in fixed:
        copy.wait()
    sign = jnp.where(odd == 0, 1.0, -1.0).astype(F32)
    for level in range(2):
        refl[level] = sign * refl[level]
    for front in range(fronts):
        cos_row, sin_row = class_rows(slowness, front_wave(freq, front), (8, 128))
        for level in range(2):
            screen[level, front, 0] = look_up(cos_row, klass[level])
            screen[level, front, 1] = look_up(sin_row, klass[level])
    pltpu.make_async_copy(down.at[0], fields.at[0], sems.at[0]).wait()
    pltpu.make_async_copy(down.at[0], fields.at[1], sems.at[1]).wait()
    jobs = [(fields.at[1, front], front, q_out_inner.at[front]) for front in range(fronts)]
    jobs += [(fields.at[0, front], front, q_in_outer.at[front]) for front in range(fronts)]
    spread(jobs, work, hx, hy, phase)


def ahead_kernel(
    partner, q_in_outer, screen, refl, phase, hx, hy,
    inward_inner, q_out_inner,
    q_field, field, work,
):
    everyone = range(partner.shape[0])
    spread([(partner.at[front], front, q_field.at[front]) for front in everyone], work, hx, hy, phase)
    for front in everyone:
        in_re, in_im, out_re, out_im = mixed(
            q_in_outer[front, 0], q_in_outer[front, 1], q_field[front, 0], q_field[front, 1],
            refl[1], screen[1, front, 0], screen[1, front, 1],
        )
        put(inward_inner.at[front], in_re, in_im)
        put(field.at[front], out_re, out_im)
    spread([(field.at[front], front, q_out_inner.at[front]) for front in everyone], work, hx, hy, phase)


def entering(arrived, source, front):
    first = lax.axis_index("depth") == 0
    return lambda part: jnp.where(first, source[front, part], arrived[front, part])


def outer_step(q_arrived, q_out_inner, screen, refl, waves, field):
    for front in range(field.shape[0]):
        put(
            field.at[front],
            *mixed(
                q_arrived[front, 0], q_arrived[front, 1], q_out_inner[front, 0], q_out_inner[front, 1],
                refl[0], screen[0, front, 0], screen[0, front, 1], waves,
            ),
        )


def edge_kernel(arrived, source, q_out_inner, screen, refl, phase, hx, hy, sent, q_arrived, field, work):
    everyone = range(arrived.shape[0])
    spread([(entering(arrived, source, front), front, q_arrived.at[front]) for front in everyone], work, hx, hy, phase)

    def early():
        outer_step(q_arrived, q_out_inner, screen, refl, "outward", sent)

    def late():
        outer_step(q_arrived, q_out_inner, screen, refl, "outward", field)
        spread([(field.at[front], front, sent.at[front]) for front in everyone], work, hx, hy, phase)

    by_turn(early, late)


def last_edge_kernel(
    arrived, source, q_out_inner, screen, refl, phase, hx, hy, after,
    q_arrived, last_far, last_near,
    outward, work,
):
    del after
    everyone = range(arrived.shape[0])
    half = arrived.shape[2] // 2

    def early():
        jobs = [(entering(arrived, source, front), front, q_arrived.at[front]) for front in everyone]
        spread(jobs, work, hx, hy, phase)

    def late():
        q_arrived[...] = arrived[...]

    by_turn(early, late)
    outer_step(q_arrived, q_out_inner, screen, refl, "outward", outward)
    jobs = [
        (outward.at[front], front, [(half_rows(1, half), last_far.at[front]), (half_rows(0, half), last_near.at[front])])
        for front in everyone
    ]
    spread(jobs, work, hx, hy, phase)


def inner_kernel(
    q_arrived, q_out_inner, partner, screen, refl, phase, hx, hy,
    inward, outward,
    field, q_inward, q_partner, work,
):
    everyone = range(partner.shape[0])
    outer_step(q_arrived, q_out_inner, screen, refl, "inward", field)
    jobs = [(partner.at[front], front, q_partner.at[front]) for front in everyone]
    jobs += [(field.at[front], front, q_inward.at[front]) for front in everyone]
    spread(jobs, work, hx, hy, phase)
    for front in everyone:
        in_re, in_im, out_re, out_im = mixed(
            q_inward[front, 0], q_inward[front, 1], q_partner[front, 0], q_partner[front, 1],
            refl[1], screen[1, front, 0], screen[1, front, 1],
        )
        put(inward.at[front], in_re, in_im)
        put(outward.at[front], out_re, out_im)


def spread_kernel(fields, phase, hx, hy, q_fields, work):
    everyone = range(fields.shape[0])
    spread([(fields.at[front], front, q_fields.at[front]) for front in everyone], work, hx, hy, phase)


def last_inner_kernel(
    q_arrived, q_out_inner, partner, screen, refl, phase, hx, hy,
    inward, outward, terms, far_terms,
    field, q_inward, q_partner, work,
):
    everyone = range(partner.shape[0])
    outer_step(q_arrived, q_out_inner, screen, refl, "inward", field)
    jobs = [(partner.at[front], front, q_partner.at[front]) for front in everyone]
    jobs += [(field.at[front], front, q_inward.at[front]) for front in everyone]
    spread(jobs, work, hx, hy, phase)
    total = None
    for front in everyone:
        a_re, a_im = (q_inward[front, part].astype(F32) for part in range(2))
        b_re, b_im = (q_partner[front, part].astype(F32) for part in range(2))
        in_re, in_im, out_re, out_im = mixed(
            a_re, a_im, b_re, b_im, refl[1], screen[1, front, 0], screen[1, front, 1]
        )
        put(inward.at[front], in_re, in_im)
        put(outward.at[front], out_re, out_im)
        term = a_re * b_re + a_im * b_im
        total = term if total is None else total + term
    terms[...] = total
    far_terms[...] = terms[half_rows(1, far_terms.shape[0]), :].astype(BF16)


def incoming(last, q_arrived, front, rows):
    first = lax.axis_index("depth") == 0
    return [jnp.where(first, q_arrived[front, part, rows, :], last[front, part]).astype(F32) for part in range(2)]


def row_terms(of, last, q_arrived, q_out_inner):
    total = None
    rows = half_rows(of, last.shape[2])
    for front in range(last.shape[0]):
        a_re, a_im = incoming(last, q_arrived, front, rows)
        b_re, b_im = (q_out_inner[front, part, rows, :].astype(F32) for part in range(2))
        term = a_re * b_re + a_im * b_im
        total = term if total is None else total + term
    return total


def row_fields(of, last, q_arrived, q_out_inner, screen, refl, inward, outward):
    rows = half_rows(of, last.shape[2])
    for front in range(last.shape[0]):
        a_re, a_im = incoming(last, q_arrived, front, rows)
        b_re, b_im = (q_out_inner[front, part, rows, :].astype(F32) for part in range(2))
        in_re, in_im, out_re, out_im = mixed(
            a_re, a_im, b_re, b_im, refl[0, rows, :], screen[0, front, 0, rows, :], screen[0, front, 1, rows, :]
        )
        put(inward.at[front], in_re, in_im)
        put(outward.at[front], out_re, out_im)
    return rows


def far_terms_kernel(last, q_arrived, q_out_inner, after, terms):
    del after
    terms[...] = row_terms(1, last, q_arrived, q_out_inner).astype(BF16)


def send_home(level, rows, inward, outward, down_out, up_out, sems):
    odd = odd_place()

    def copies(place, inward_out, outward_out):
        return [
            pltpu.make_async_copy(inward, inward_out.at[place, :, :, rows, :], sems.at[0]),
            pltpu.make_async_copy(outward, outward_out.at[place, :, :, rows, :], sems.at[1]),
        ]

    @pl.when(odd == 0)
    def _():
        for copy in copies(level, down_out, up_out):
            copy.start()

    @pl.when(odd == 1)
    def _():
        for copy in copies(1 - level, up_out, down_out):
            copy.start()

    return copies(0, down_out, up_out)


def outer_fields_kernel(
    scale, near, far, q_arrived, q_out_inner, screen, refl, inner_in, inner_out, inner_terms, inner_other,
    down_out, up_out, gradient, terms,
    near_in, near_out, far_in, far_out, inner_sum, sems,
):
    rows_x = inner_in.shape[2]
    waits = send_home(1, pl.ds(0, rows_x), inner_in, inner_out, down_out, up_out, sems.at[0])
    rows = row_fields(1, far, q_arrived, q_out_inner, screen, refl, far_in, far_out)
    waits += send_home(0, rows, far_in, far_out, down_out, up_out, sems.at[1])
    rows = row_fields(0, near, q_arrived, q_out_inner, screen, refl, near_in, near_out)
    waits += send_home(0, rows, near_in, near_out, down_out, up_out, sems.at[2])
    inner_sum[...] = scale * (inner_terms[rows, :] + inner_other[...].astype(F32))
    waits.append(pltpu.make_async_copy(inner_sum, gradient.at[1 - odd_place()], sems.at[3, 0]))
    waits[-1].start()
    terms[...] = row_terms(0, near, q_arrived, q_out_inner)
    for copy in waits:
        copy.wait()


def outer_gradient_kernel(scale, terms, other, gradient_in, gradient, outer_sum, sems):
    del gradient_in
    outer_sum[...] = scale * (terms[...] + other[...].astype(F32))
    done = pltpu.make_async_copy(outer_sum, gradient.at[odd_place()], sems.at[0])
    done.start()
    done.wait()


def per_device(down_state, up_state, source, reflect, screen_class, screen_values, freq_index):
    depth = lax.axis_size("depth")
    shots = lax.axis_size("shot")
    levels, fronts, parts, rows_x, rows_y = down_state.shape
    if levels != 2 or depth % 2 or shots % 2 or HOPS != 3:
        return per_device_plain(down_state, up_state, source, reflect, screen_class, screen_values, freq_index)
    scale = 1.0 / math.sqrt(fronts * shots)
    half = rows_x // 2
    hx = jnp.asarray(hartley(rows_x))
    hy = jnp.asarray(hartley(rows_y))
    partners = [(i, i ^ 1) for i in range(depth)]
    beyond = [(i, i + 1) for i in range(1, depth - 1, 2)] + [(i + 1, i) for i in range(1, depth - 1, 2)]
    to_partner = functools.partial(lax.ppermute, axis_name="depth", perm=partners)
    to_beyond = functools.partial(lax.ppermute, axis_name="depth", perm=beyond)
    across = functools.partial(lax.ppermute, axis_name="shot", perm=[(i, i ^ 1) for i in range(shots)])
    plane = jax.ShapeDtypeStruct((fronts, parts, rows_x, rows_y), BF16)
    half_plane = jax.ShapeDtypeStruct((fronts, parts, half, rows_y), BF16)
    pair = jax.ShapeDtypeStruct((2, rows_x, rows_y), F32)
    turns = jax.ShapeDtypeStruct((fronts, parts, rows_x, rows_y), F32)
    screens = jax.ShapeDtypeStruct((2, fronts, parts, rows_x, rows_y), F32)
    state = jax.ShapeDtypeStruct(down_state.shape, BF16)
    dma = pltpu.SemaphoreType.DMA

    def call(kernel, in_specs, out_specs, out_shape, scratch=(), **more):
        return pl.pallas_call(
            kernel,
            in_specs=in_specs,
            out_specs=out_specs,
            out_shape=out_shape,
            scratch_shapes=list(scratch),
            compiler_params=PARAMS,
            **more,
        )

    def kept_in_hbm(*arrays):
        return [pltpu.with_memory_space_constraint(array, pltpu.HBM) for array in arrays]

    def buffers(count, shape=plane):
        return [pltpu.VMEM(shape.shape, shape.dtype)] * count

    def work(slots):
        return pltpu.VMEM((slots, *plane.shape[1:]), BF16)

    out_outer, in_inner = call(edges_kernel, [HBM] * 2, [VMEM] * 2, [plane] * 2, [dma((2,))])(
        *kept_in_hbm(down_state, up_state)
    )
    arrived_0 = to_beyond(out_outer)
    partner_0 = to_partner(in_inner)
    q_out_inner_0, q_in_outer_0, screen, phase, refl = call(
        setup_kernel,
        [HBM] * 4 + [SMEM] * 2 + [VMEM] * 2,
        [VMEM] * 5,
        [plane] * 2 + [screens, turns, pair],
        [
            pltpu.VMEM((2, *plane.shape), BF16),
            pltpu.VMEM((2, rows_x, rows_y), jnp.int32),
            work(2 * fronts),
            dma((6,)),
        ],
    )(*kept_in_hbm(down_state, up_state, reflect, screen_class), screen_values, freq_index, hx, hy)
    fixed = (screen, refl, phase, hx, hy)
    in_inner_1, q_out_inner_1 = call(ahead_kernel, [VMEM] * 7, [VMEM] * 2, [plane] * 2, buffers(2) + [work(fronts)])(
        partner_0, q_in_outer_0, *fixed
    )
    partner_1 = to_partner(in_inner_1)
    out_outer_1, q_arrived = call(edge_kernel, [VMEM] * 8, [VMEM] * 2, [plane] * 2, buffers(1) + [work(fronts)])(
        arrived_0, source, q_out_inner_0, *fixed
    )
    arrived_1 = to_beyond(out_outer_1)
    in_inner_2, out_inner_2 = call(
        inner_kernel, [VMEM] * 8, [VMEM] * 2, [plane] * 2, buffers(3) + [work(2 * fronts)]
    )(q_arrived, q_out_inner_0, partner_1, *fixed)
    partner_2 = to_partner(in_inner_2)
    q_out_inner_2 = call(spread_kernel, [VMEM] * 4, VMEM, plane, [work(fronts)])(out_inner_2, phase, hx, hy)
    q_arrived_1, last_far, last_near = call(
        last_edge_kernel,
        [VMEM] * 8 + [pl.BlockSpec(memory_space=pl.ANY)],
        [VMEM] * 3,
        [plane] + [half_plane] * 2,
        buffers(1) + [work(fronts)],
    )(arrived_1, source, q_out_inner_1, *fixed, q_out_inner_2)
    last_far = to_beyond(last_far)
    last_near = to_beyond(last_near)
    half_sum = jax.ShapeDtypeStruct((half, rows_y), BF16)
    inner_in, inner_out, inner_terms, inner_far = call(
        last_inner_kernel,
        [VMEM] * 8,
        [VMEM] * 4,
        [plane] * 2 + [jax.ShapeDtypeStruct((rows_x, rows_y), F32), half_sum],
        buffers(3) + [work(2 * fronts)],
    )(q_arrived_1, q_out_inner_1, partner_2, *fixed)
    inner_other = across(inner_far) if shots == 2 else jnp.zeros_like(inner_far)
    outer_far = call(far_terms_kernel, [VMEM] * 3 + [pl.BlockSpec(memory_space=pl.ANY)], VMEM, half_sum)(
        last_far, q_arrived, q_out_inner_2, inner_terms
    )
    outer_other = across(outer_far) if shots == 2 else jnp.zeros_like(outer_far)
    half_total = jax.ShapeDtypeStruct((half, rows_y), F32)
    share = jax.ShapeDtypeStruct((2, half, rows_y), F32)
    down, up, gradient, outer_near = call(
        functools.partial(outer_fields_kernel, scale),
        [VMEM] * 10,
        [HBM] * 3 + [VMEM],
        [state, state, share, half_total],
        buffers(4, half_plane) + buffers(1, half_total) + [dma((4, 2))],
    )(
        last_near, last_far, q_arrived, q_out_inner_2, screen, refl, inner_in, inner_out, inner_terms, inner_other
    )
    gradient = call(
        functools.partial(outer_gradient_kernel, scale),
        [VMEM] * 2 + [HBM],
        HBM,
        share,
        buffers(1, half_total) + [dma((1,))],
        input_output_aliases={2: 0},
    )(outer_near, outer_other, gradient)
    if shots != 2:
        terms = scale * jnp.stack([outer_far, inner_far]).astype(F32)
        far = jnp.where(odd_place() == 0, terms, terms[::-1])
        top = lax.rem(lax.axis_index("shot"), 2) == 0
        whole = jnp.concatenate([jnp.where(top, gradient, far), jnp.where(top, far, gradient)], axis=1)
        gradient = lax.psum_scatter(whole.astype(BF16), "shot", scatter_dimension=1, tiled=True).astype(F32)
    return (down, up, gradient)


def solution(mesh):
    return jax.shard_map(
        per_device,
        mesh=mesh,
        in_specs=(
            P("depth", "shot", None, None, None),
            P("depth", "shot", None, None, None),
            P("shot", None, None, None),
            P("depth", None, None),
            P("depth", None, None),
            P(),
            P("shot"),
        ),
        out_specs=(
            P("depth", "shot", None, None, None),
            P("depth", "shot", None, None, None),
            P("depth", "shot", None),
        ),
        check_vma=False,
    )
```

```python
import functools
import math

import jax
import jax.numpy as jnp
import numpy as np
from jax import lax
from jax.experimental import pallas as pl
from jax.experimental.pallas import tpu as pltpu
from jax.sharding import PartitionSpec as P

HOPS = 3
NCLASS = 16
NFREQ = 128
F32 = jnp.float32
BF16 = jnp.bfloat16
VMEM = pl.BlockSpec(memory_space=pltpu.VMEM)
HBM = pl.BlockSpec(memory_space=pltpu.HBM)
SMEM = pl.BlockSpec(memory_space=pltpu.SMEM)
PARAMS = pltpu.CompilerParams(vmem_limit_bytes=28 * 2**20)


def passed_along(block, axis, distance):
    devices = range(lax.axis_size(axis))
    route = [(i - distance, i) for i in devices if i - distance in devices]
    return lax.ppermute(block, axis, route)


def dft_tables(length):
    counter = jnp.arange(length, dtype=jnp.int32)
    product = counter[:, None] * counter[None, :] % length
    angles = 2.0 * math.pi / length * product.astype(jnp.float32)
    return (jnp.cos(angles).astype(jnp.bfloat16), jnp.sin(angles).astype(jnp.bfloat16))


def wavenumbers(length):
    counter = jnp.arange(length, dtype=jnp.int32)
    wrapped = jnp.where(counter >= length // 2, counter - length, counter)
    return 2.0 * math.pi / length * wrapped.astype(jnp.float32)


def propagate(planes, phase_re, phase_im, tables):
    fwd_left, fwd_right, inv_left, inv_right = tables
    first = jnp.einsum(
        "cdjk,...dkl->...cjl", fwd_left, planes, preferred_element_type=jnp.float32
    ).astype(jnp.bfloat16)
    second = jnp.einsum("...djl,dclm->...cjm", first, fwd_right, preferred_element_type=jnp.float32)
    real_part = second[..., 0, :, :]
    imag_part = second[..., 1, :, :]
    turned = jnp.stack(
        [real_part * phase_re - imag_part * phase_im, real_part * phase_im + imag_part * phase_re],
        axis=-3,
    ).astype(jnp.bfloat16)
    third = jnp.einsum(
        "cdjk,...dkl->...cjl", inv_left, turned, preferred_element_type=jnp.float32
    ).astype(jnp.bfloat16)
    return jnp.einsum(
        "...djl,dclm->...cjm", third, inv_right, preferred_element_type=jnp.float32
    ).astype(jnp.bfloat16)


def trade(down_edge, up_edge):
    got_down = passed_along(down_edge, "depth", 1)
    got_up = passed_along(up_edge, "depth", -1)
    return (got_down, got_up)


def per_device_plain(down_state, up_state, source, reflect, screen_class, screen_values, freq_index):
    levels = down_state.shape[0]
    rows_x = down_state.shape[3]
    rows_y = down_state.shape[4]
    front_count = down_state.shape[1]
    depth_rank = lax.axis_index("depth")
    scale = 1.0 / math.sqrt(front_count * lax.axis_size("shot"))
    cos_x, sin_x = dft_tables(rows_x)
    cos_y, sin_y = dft_tables(rows_y)
    tables = (
        jnp.stack([jnp.stack([cos_x, sin_x]), jnp.stack([-sin_x, cos_x])]),
        jnp.stack([jnp.stack([cos_y, -sin_y]), jnp.stack([sin_y, cos_y])]),
        jnp.stack([jnp.stack([cos_x, -sin_x]), jnp.stack([sin_x, cos_x])]),
        jnp.stack([jnp.stack([cos_y, sin_y]), jnp.stack([-sin_y, cos_y])]),
    )
    kwave = 0.95 * math.pi * (freq_index.astype(jnp.float32) + 1.0) / NFREQ
    kx_wave = wavenumbers(rows_x)
    ky_wave = wavenumbers(rows_y)
    vertical = kwave[:, None, None] ** 2 - kx_wave[None, :, None] ** 2 - ky_wave[None, None, :] ** 2
    propag = jnp.sqrt(jnp.maximum(vertical, 0.0))
    damping = jnp.exp(-jnp.sqrt(jnp.maximum(-vertical, 0.0))) / (rows_x * rows_y)
    phase_re = damping * jnp.cos(propag)
    phase_im = damping * jnp.sin(propag)
    classes = jnp.arange(NCLASS, dtype=jnp.int32)
    onehot = (screen_class[None] == classes[:, None, None, None]).astype(jnp.float32)
    slowness = jnp.einsum("c,clxy->lxy", screen_values, onehot, precision=lax.Precision.HIGHEST)
    angle = kwave[None, :, None, None] * slowness[:, None]
    screen_re = jnp.cos(angle)
    screen_im = jnp.sin(angle)
    refl = reflect[:, None]
    top_slab = depth_rank == 0
    down = down_state
    up = up_state
    a_re = a_im = b_re = b_im = None
    for repeat in range(HOPS):
        down_edge = down[levels - 1]
        up_edge = up[0]
        got_down, got_up = trade(down_edge, up_edge)
        got_down = jnp.where(top_slab, source, got_down)
        moved = propagate(
            jnp.concatenate([got_down[None], down[: levels - 1], up[1:], got_up[None]], axis=0),
            phase_re,
            phase_im,
            tables,
        )
        from_above = moved[:levels]
        from_below = moved[levels:]
        qa_re = from_above[:, :, 0].astype(jnp.float32)
        qa_im = from_above[:, :, 1].astype(jnp.float32)
        qb_re = from_below[:, :, 0].astype(jnp.float32)
        qb_im = from_below[:, :, 1].astype(jnp.float32)
        a_re = screen_re * qa_re - screen_im * qa_im
        a_im = screen_re * qa_im + screen_im * qa_re
        b_re = screen_re * qb_re - screen_im * qb_im
        b_im = screen_re * qb_im + screen_im * qb_re
        down = jnp.stack(
            [(1.0 + refl) * a_re - refl * b_re, (1.0 + refl) * a_im - refl * b_im], axis=2
        ).astype(jnp.bfloat16)
        up = jnp.stack(
            [(1.0 - refl) * b_re + refl * a_re, (1.0 - refl) * b_im + refl * a_im], axis=2
        ).astype(jnp.bfloat16)
    terms = scale * jnp.sum(a_re * b_re + a_im * b_im, axis=1)
    gradient = lax.psum_scatter(
        terms.astype(jnp.bfloat16), "shot", scatter_dimension=1, tiled=True
    ).astype(jnp.float32)
    return (down, up, gradient)


def hartley(length):
    counter = np.arange(length)
    angles = 2.0 * np.pi / length * (counter[:, None] * counter[None, :] % length)
    cosine = np.cos(angles).astype(BF16).astype(np.float32)
    sine = np.sin(angles).astype(BF16).astype(np.float32)
    return (cosine + sine).astype(BF16)


def odd_place():
    return lax.rem(lax.axis_index("depth"), 2)


def mm(left, right):
    return jnp.dot(left, right, preferred_element_type=F32)


def spread(jobs, work, hx, hy, phase):
    jobs = list(enumerate(jobs))
    for slot, (plane, _, _) in jobs:
        for part in range(2):
            work[slot, part] = mm(plane(part) if callable(plane) else plane[part], hy[...]).astype(BF16)
    for slot, (_, front, _) in jobs:
        turn_re, turn_im = phase[front, 0], phase[front, 1]
        part_re = mm(hx[...], work[slot, 0])
        part_im = mm(hx[...], work[slot, 1])
        work[slot, 0] = (part_re * turn_re - part_im * turn_im).astype(BF16)
        work[slot, 1] = (part_re * turn_im + part_im * turn_re).astype(BF16)
    for slot, _ in jobs:
        for part in range(2):
            work[slot, part] = mm(hx[...], work[slot, part]).astype(BF16)
    for slot, (_, _, target) in jobs:
        for part in range(2):
            if isinstance(target, list):
                for rows, piece in target:
                    piece[part] = mm(work[slot, part, rows, :], hy[...]).astype(BF16)
            else:
                target[part] = mm(work[slot, part], hy[...]).astype(BF16)


def screened(real_part, imag_part, screen_re, screen_im):
    return (
        screen_re * real_part - screen_im * imag_part,
        screen_re * imag_part + screen_im * real_part,
    )


def mixed(a_re, a_im, b_re, b_im, refl, screen_re, screen_im, waves="both"):
    a_re, a_im, b_re, b_im = (part.astype(F32) for part in (a_re, a_im, b_re, b_im))
    step_re = refl * (a_re - b_re)
    step_im = refl * (a_im - b_im)
    fields = ()
    if waves != "outward":
        fields += screened(a_re + step_re, a_im + step_im, screen_re, screen_im)
    if waves != "inward":
        fields += screened(b_re + step_re, b_im + step_im, screen_re, screen_im)
    return fields


def put(target, real_part, imag_part):
    target[0] = real_part.astype(BF16)
    target[1] = imag_part.astype(BF16)


def half_rows(of, half):
    shot = lax.rem(lax.axis_index("shot"), 2)
    return pl.ds(pl.multiple_of((shot if of == 0 else 1 - shot) * half, half), half)


def late_pair():
    return lax.rem(lax.div(lax.axis_index("depth") + 1, 2), 2) == 1


def by_turn(early, late):
    is_late = late_pair()
    pl.when(jnp.logical_not(is_late))(early)
    pl.when(is_late)(late)


def edges_kernel(down, up, outward_outer, inward_inner, sems):
    levels = down.shape[0]
    odd = odd_place()

    def fetch(first, second):
        pltpu.make_async_copy(first, outward_outer, sems.at[0]).start()
        pltpu.make_async_copy(second, inward_inner, sems.at[1]).start()

    @pl.when(odd == 0)
    def _():
        fetch(up.at[0], down.at[levels - 1])

    @pl.when(odd == 1)
    def _():
        fetch(down.at[levels - 1], up.at[0])

    pltpu.make_async_copy(up.at[0], outward_outer, sems.at[0]).wait()
    pltpu.make_async_copy(up.at[0], inward_inner, sems.at[1]).wait()


def class_rows(slowness, kwave, shape):
    lanes = lax.broadcasted_iota(jnp.int32, shape, 1)
    table = jnp.zeros(shape, F32)
    for entry in range(NCLASS):
        table = jnp.where(lanes == entry, slowness[entry], table)
    angle = kwave * table
    return jnp.cos(angle), jnp.sin(angle)


def look_up(table, classes):
    width = 128
    rows = classes.shape[0]
    wide = jnp.broadcast_to(table[:1], (rows, width))
    pieces = [
        jnp.take_along_axis(wide, classes[:, start : start + width], axis=1, mode="promise_in_bounds")
        for start in range(0, classes.shape[1], width)
    ]
    return jnp.concatenate(pieces, axis=1)


def front_wave(freq, front):
    return 0.95 * math.pi * (freq[front].astype(F32) + 1.0) / NFREQ


def series(square, shift):
    total = jnp.full_like(square, 1.0 / math.factorial(18 + shift))
    for order in range(16, -1, -2):
        total = 1.0 / math.factorial(order + shift) - square * total
    return total


def setup_kernel(
    down, up, reflect, classes_in, slowness, freq, hx, hy,
    q_out_inner, q_in_outer, screen, phase, refl,
    fields, klass, work, sems,
):
    fronts = q_out_inner.shape[0]
    rows_x, rows_y = refl.shape[1:]
    odd = odd_place()
    fixed = [
        pltpu.make_async_copy(reflect.at[odd], refl.at[0], sems.at[2]),
        pltpu.make_async_copy(reflect.at[1 - odd], refl.at[1], sems.at[3]),
        pltpu.make_async_copy(classes_in.at[odd], klass.at[0], sems.at[4]),
        pltpu.make_async_copy(classes_in.at[1 - odd], klass.at[1], sems.at[5]),
    ]
    for copy in fixed:
        copy.start()

    @pl.when(odd == 0)
    def _():
        pltpu.make_async_copy(down.at[0], fields.at[0], sems.at[0]).start()
        pltpu.make_async_copy(up.at[1], fields.at[1], sems.at[1]).start()

    @pl.when(odd == 1)
    def _():
        pltpu.make_async_copy(up.at[1], fields.at[0], sems.at[0]).start()
        pltpu.make_async_copy(down.at[0], fields.at[1], sems.at[1]).start()

    def squares(length, axis):
        counter = lax.broadcasted_iota(jnp.int32, (rows_x, rows_y), axis)
        wrapped = jnp.where(counter >= length // 2, counter - length, counter)
        wave = 2.0 * math.pi / length * wrapped.astype(F32)
        return wave * wave

    lateral = squares(rows_x, 0) + squares(rows_y, 1)
    level_out = 1.0 / (rows_x * rows_y)
    for front in range(fronts):
        kwave = front_wave(freq, front)
        vertical = kwave * kwave - lateral
        travels = vertical > 0.0
        square = jnp.maximum(vertical, 0.0)
        root = jnp.sqrt(jnp.abs(vertical))
        phase[front, 0] = jnp.where(travels, series(square, 0), jnp.exp(-root)) * level_out
        phase[front, 1] = jnp.where(travels, root * series(square, 1), 0.0) * level_out
    for copy in fixed:
        copy.wait()
    sign = jnp.where(odd == 0, 1.0, -1.0).astype(F32)
    for level in range(2):
        refl[level] = sign * refl[level]
    for front in range(fronts):
        cos_row, sin_row = class_rows(slowness, front_wave(freq, front), (8, 128))
        for level in range(2):
            screen[level, front, 0] = look_up(cos_row, klass[level])
            screen[level, front, 1] = look_up(sin_row, klass[level])
    pltpu.make_async_copy(down.at[0], fields.at[0], sems.at[0]).wait()
    pltpu.make_async_copy(down.at[0], fields.at[1], sems.at[1]).wait()
    jobs = [(fields.at[1, front], front, q_out_inner.at[front]) for front in range(fronts)]
    jobs += [(fields.at[0, front], front, q_in_outer.at[front]) for front in range(fronts)]
    spread(jobs, work, hx, hy, phase)


def ahead_kernel(
    partner, q_in_outer, screen, refl, phase, hx, hy,
    inward_inner, q_out_inner,
    q_field, field, work,
):
    everyone = range(partner.shape[0])
    spread([(partner.at[front], front, q_field.at[front]) for front in everyone], work, hx, hy, phase)
    for front in everyone:
        in_re, in_im, out_re, out_im = mixed(
            q_in_outer[front, 0], q_in_outer[front, 1], q_field[front, 0], q_field[front, 1],
            refl[1], screen[1, front, 0], screen[1, front, 1],
        )
        put(inward_inner.at[front], in_re, in_im)
        put(field.at[front], out_re, out_im)
    spread([(field.at[front], front, q_out_inner.at[front]) for front in everyone], work, hx, hy, phase)


def entering(arrived, source, front):
    first = lax.axis_index("depth") == 0
    return lambda part: jnp.where(first, source[front, part], arrived[front, part])


def outer_step(q_arrived, q_out_inner, screen, refl, waves, field):
    for front in range(field.shape[0]):
        put(
            field.at[front],
            *mixed(
                q_arrived[front, 0], q_arrived[front, 1], q_out_inner[front, 0], q_out_inner[front, 1],
                refl[0], screen[0, front, 0], screen[0, front, 1], waves,
            ),
        )


def edge_kernel(arrived, source, q_out_inner, screen, refl, phase, hx, hy, sent, q_arrived, field, work):
    everyone = range(arrived.shape[0])

    def step(target):
        jobs = [(entering(arrived, source, front), front, q_arrived.at[front]) for front in everyone]
        spread(jobs, work, hx, hy, phase)
        outer_step(q_arrived, q_out_inner, screen, refl, "outward", target)

    def early():
        step(sent)

    def late():
        step(field)
        spread([(field.at[front], front, sent.at[front]) for front in everyone], work, hx, hy, phase)

    by_turn(early, late)


def last_edge_kernel(
    arrived, source, q_out_inner, screen, refl, phase, hx, hy, after,
    q_arrived, last_far, last_near,
    outward, work,
):
    del after
    everyone = range(arrived.shape[0])
    half = arrived.shape[2] // 2

    def step():
        outer_step(q_arrived, q_out_inner, screen, refl, "outward", outward)
        jobs = [
            (outward.at[front], front, [(half_rows(1, half), last_far.at[front]), (half_rows(0, half), last_near.at[front])])
            for front in everyone
        ]
        spread(jobs, work, hx, hy, phase)

    def early():
        jobs = [(entering(arrived, source, front), front, q_arrived.at[front]) for front in everyone]
        spread(jobs, work, hx, hy, phase)
        step()

    def late():
        q_arrived[...] = arrived[...]
        step()

    by_turn(early, late)


def inner_kernel(
    q_arrived, q_out_inner, partner, screen, refl, phase, hx, hy,
    inward, outward,
    field, q_inward, q_partner, work,
):
    everyone = range(partner.shape[0])
    outer_step(q_arrived, q_out_inner, screen, refl, "inward", field)
    jobs = [(partner.at[front], front, q_partner.at[front]) for front in everyone]
    jobs += [(field.at[front], front, q_inward.at[front]) for front in everyone]
    spread(jobs, work, hx, hy, phase)
    for front in everyone:
        in_re, in_im, out_re, out_im = mixed(
            q_inward[front, 0], q_inward[front, 1], q_partner[front, 0], q_partner[front, 1],
            refl[1], screen[1, front, 0], screen[1, front, 1],
        )
        put(inward.at[front], in_re, in_im)
        put(outward.at[front], out_re, out_im)


def spread_kernel(fields, phase, hx, hy, q_fields, work):
    @pl.when(late_pair())
    def _():
        everyone = range(fields.shape[0])
        spread([(fields.at[front], front, q_fields.at[front]) for front in everyone], work, hx, hy, phase)


def last_inner_kernel(
    q_arrived, q_out_inner, partner, screen, refl, phase, hx, hy, out_inner, q_next_in,
    inward, outward, terms, far_terms, q_next,
    field, q_inward, q_partner, work,
):
    del q_next_in
    everyone = range(partner.shape[0])

    @pl.when(jnp.logical_not(late_pair()))
    def _():
        spread([(out_inner.at[front], front, q_next.at[front]) for front in everyone], work, hx, hy, phase)

    outer_step(q_arrived, q_out_inner, screen, refl, "inward", field)
    jobs = [(partner.at[front], front, q_partner.at[front]) for front in everyone]
    jobs += [(field.at[front], front, q_inward.at[front]) for front in everyone]
    spread(jobs, work, hx, hy, phase)
    total = None
    for front in everyone:
        a_re, a_im = (q_inward[front, part].astype(F32) for part in range(2))
        b_re, b_im = (q_partner[front, part].astype(F32) for part in range(2))
        in_re, in_im, out_re, out_im = mixed(
            a_re, a_im, b_re, b_im, refl[1], screen[1, front, 0], screen[1, front, 1]
        )
        put(inward.at[front], in_re, in_im)
        put(outward.at[front], out_re, out_im)
        term = a_re * b_re + a_im * b_im
        total = term if total is None else total + term
    terms[...] = total
    far_terms[...] = terms[half_rows(1, far_terms.shape[0]), :].astype(BF16)


def incoming(last, q_arrived, front, rows):
    first = lax.axis_index("depth") == 0
    return [jnp.where(first, q_arrived[front, part, rows, :], last[front, part]).astype(F32) for part in range(2)]


def row_terms(of, last, q_arrived, q_out_inner):
    total = None
    rows = half_rows(of, last.shape[2])
    for front in range(last.shape[0]):
        a_re, a_im = incoming(last, q_arrived, front, rows)
        b_re, b_im = (q_out_inner[front, part, rows, :].astype(F32) for part in range(2))
        term = a_re * b_re + a_im * b_im
        total = term if total is None else total + term
    return total


def row_fields(of, last, q_arrived, q_out_inner, screen, refl, inward, outward):
    rows = half_rows(of, last.shape[2])
    for front in range(last.shape[0]):
        a_re, a_im = incoming(last, q_arrived, front, rows)
        b_re, b_im = (q_out_inner[front, part, rows, :].astype(F32) for part in range(2))
        in_re, in_im, out_re, out_im = mixed(
            a_re, a_im, b_re, b_im, refl[0, rows, :], screen[0, front, 0, rows, :], screen[0, front, 1, rows, :]
        )
        put(inward.at[front], in_re, in_im)
        put(outward.at[front], out_re, out_im)
    return rows


def far_terms_kernel(last, q_arrived, q_out_inner, after, terms):
    del after
    terms[...] = row_terms(1, last, q_arrived, q_out_inner).astype(BF16)


def send_home(level, rows, inward, outward, down_out, up_out, sems):
    odd = odd_place()

    def copies(place, inward_out, outward_out):
        return [
            pltpu.make_async_copy(inward, inward_out.at[place, :, :, rows, :], sems.at[0]),
            pltpu.make_async_copy(outward, outward_out.at[place, :, :, rows, :], sems.at[1]),
        ]

    @pl.when(odd == 0)
    def _():
        for copy in copies(level, down_out, up_out):
            copy.start()

    @pl.when(odd == 1)
    def _():
        for copy in copies(1 - level, up_out, down_out):
            copy.start()

    return copies(0, down_out, up_out)


def outer_fields_kernel(
    scale, near, far, q_arrived, q_out_inner, screen, refl, inner_in, inner_out, inner_terms, inner_other,
    down_out, up_out, gradient, terms,
    near_in, near_out, far_in, far_out, inner_sum, sems,
):
    rows_x = inner_in.shape[2]
    waits = send_home(1, pl.ds(0, rows_x), inner_in, inner_out, down_out, up_out, sems.at[0])
    rows = row_fields(1, far, q_arrived, q_out_inner, screen, refl, far_in, far_out)
    waits += send_home(0, rows, far_in, far_out, down_out, up_out, sems.at[1])
    rows = row_fields(0, near, q_arrived, q_out_inner, screen, refl, near_in, near_out)
    waits += send_home(0, rows, near_in, near_out, down_out, up_out, sems.at[2])
    inner_sum[...] = scale * (inner_terms[rows, :] + inner_other[...].astype(F32))
    waits.append(pltpu.make_async_copy(inner_sum, gradient.at[1 - odd_place()], sems.at[3, 0]))
    waits[-1].start()
    terms[...] = row_terms(0, near, q_arrived, q_out_inner)
    for copy in waits:
        copy.wait()


def outer_gradient_kernel(scale, terms, other, gradient_in, gradient, outer_sum, sems):
    del gradient_in
    outer_sum[...] = scale * (terms[...] + other[...].astype(F32))
    done = pltpu.make_async_copy(outer_sum, gradient.at[odd_place()], sems.at[0])
    done.start()
    done.wait()


def per_device(down_state, up_state, source, reflect, screen_class, screen_values, freq_index):
    depth = lax.axis_size("depth")
    shots = lax.axis_size("shot")
    levels, fronts, parts, rows_x, rows_y = down_state.shape
    if levels != 2 or depth % 2 or shots % 2 or HOPS != 3:
        return per_device_plain(down_state, up_state, source, reflect, screen_class, screen_values, freq_index)
    scale = 1.0 / math.sqrt(fronts * shots)
    half = rows_x // 2
    hx = jnp.asarray(hartley(rows_x))
    hy = jnp.asarray(hartley(rows_y))
    partners = [(i, i ^ 1) for i in range(depth)]
    beyond = [(i, i + 1) for i in range(1, depth - 1, 2)] + [(i + 1, i) for i in range(1, depth - 1, 2)]
    to_partner = functools.partial(lax.ppermute, axis_name="depth", perm=partners)
    to_beyond = functools.partial(lax.ppermute, axis_name="depth", perm=beyond)
    across = functools.partial(lax.ppermute, axis_name="shot", perm=[(i, i ^ 1) for i in range(shots)])
    plane = jax.ShapeDtypeStruct((fronts, parts, rows_x, rows_y), BF16)
    half_plane = jax.ShapeDtypeStruct((fronts, parts, half, rows_y), BF16)
    pair = jax.ShapeDtypeStruct((2, rows_x, rows_y), F32)
    turns = jax.ShapeDtypeStruct((fronts, parts, rows_x, rows_y), F32)
    screens = jax.ShapeDtypeStruct((2, fronts, parts, rows_x, rows_y), F32)
    state = jax.ShapeDtypeStruct(down_state.shape, BF16)
    dma = pltpu.SemaphoreType.DMA

    def call(kernel, in_specs, out_specs, out_shape, scratch=(), **more):
        return pl.pallas_call(
            kernel,
            in_specs=in_specs,
            out_specs=out_specs,
            out_shape=out_shape,
            scratch_shapes=list(scratch),
            compiler_params=PARAMS,
            **more,
        )

    def kept_in_hbm(*arrays):
        return [pltpu.with_memory_space_constraint(array, pltpu.HBM) for array in arrays]

    def buffers(count, shape=plane):
        return [pltpu.VMEM(shape.shape, shape.dtype)] * count

    def work(slots):
        return pltpu.VMEM((slots, *plane.shape[1:]), BF16)

    out_outer, in_inner = call(edges_kernel, [HBM] * 2, [VMEM] * 2, [plane] * 2, [dma((2,))])(
        *kept_in_hbm(down_state, up_state)
    )
    arrived_0 = to_beyond(out_outer)
    partner_0 = to_partner(in_inner)
    q_out_inner_0, q_in_outer_0, screen, phase, refl = call(
        setup_kernel,
        [HBM] * 4 + [SMEM] * 2 + [VMEM] * 2,
        [VMEM] * 5,
        [plane] * 2 + [screens, turns, pair],
        [
            pltpu.VMEM((2, *plane.shape), BF16),
            pltpu.VMEM((2, rows_x, rows_y), jnp.int32),
            work(2 * fronts),
            dma((6,)),
        ],
    )(*kept_in_hbm(down_state, up_state, reflect, screen_class), screen_values, freq_index, hx, hy)
    fixed = (screen, refl, phase, hx, hy)
    in_inner_1, q_out_inner_1 = call(ahead_kernel, [VMEM] * 7, [VMEM] * 2, [plane] * 2, buffers(2) + [work(fronts)])(
        partner_0, q_in_outer_0, *fixed
    )
    partner_1 = to_partner(in_inner_1)
    out_outer_1, q_arrived = call(edge_kernel, [VMEM] * 8, [VMEM] * 2, [plane] * 2, buffers(1) + [work(fronts)])(
        arrived_0, source, q_out_inner_0, *fixed
    )
    arrived_1 = to_beyond(out_outer_1)
    in_inner_2, out_inner_2 = call(
        inner_kernel, [VMEM] * 8, [VMEM] * 2, [plane] * 2, buffers(3) + [work(2 * fronts)]
    )(q_arrived, q_out_inner_0, partner_1, *fixed)
    partner_2 = to_partner(in_inner_2)
    q_out_inner_2 = call(spread_kernel, [VMEM] * 4, VMEM, plane, [work(fronts)])(out_inner_2, phase, hx, hy)
    q_arrived_1, last_far, last_near = call(
        last_edge_kernel,
        [VMEM] * 8 + [pl.BlockSpec(memory_space=pl.ANY)],
        [VMEM] * 3,
        [plane] + [half_plane] * 2,
        buffers(1) + [work(fronts)],
    )(arrived_1, source, q_out_inner_1, *fixed, q_out_inner_2)
    last_far = to_beyond(last_far)
    last_near = to_beyond(last_near)
    half_sum = jax.ShapeDtypeStruct((half, rows_y), BF16)
    inner_in, inner_out, inner_terms, inner_far, q_out_inner_2 = call(
        last_inner_kernel,
        [VMEM] * 10,
        [VMEM] * 5,
        [plane] * 2 + [jax.ShapeDtypeStruct((rows_x, rows_y), F32), half_sum, plane],
        buffers(3) + [work(2 * fronts)],
        input_output_aliases={9: 4},
    )(q_arrived_1, q_out_inner_1, partner_2, *fixed, out_inner_2, q_out_inner_2)
    inner_other = across(inner_far) if shots == 2 else jnp.zeros_like(inner_far)
    outer_far = call(far_terms_kernel, [VMEM] * 3 + [pl.BlockSpec(memory_space=pl.ANY)], VMEM, half_sum)(
        last_far, q_arrived, q_out_inner_2, inner_terms
    )
    outer_other = across(outer_far) if shots == 2 else jnp.zeros_like(outer_far)
    half_total = jax.ShapeDtypeStruct((half, rows_y), F32)
    share = jax.ShapeDtypeStruct((2, half, rows_y), F32)
    down, up, gradient, outer_near = call(
        functools.partial(outer_fields_kernel, scale),
        [VMEM] * 10,
        [HBM] * 3 + [VMEM],
        [state, state, share, half_total],
        buffers(4, half_plane) + buffers(1, half_total) + [dma((4, 2))],
    )(
        last_near, last_far, q_arrived, q_out_inner_2, screen, refl, inner_in, inner_out, inner_terms, inner_other
    )
    gradient = call(
        functools.partial(outer_gradient_kernel, scale),
        [VMEM] * 2 + [HBM],
        HBM,
        share,
        buffers(1, half_total) + [dma((1,))],
        input_output_aliases={2: 0},
    )(outer_near, outer_other, gradient)
    if shots != 2:
        terms = scale * jnp.stack([outer_far, inner_far]).astype(F32)
        far = jnp.where(odd_place() == 0, terms, terms[::-1])
        top = lax.rem(lax.axis_index("shot"), 2) == 0
        whole = jnp.concatenate([jnp.where(top, gradient, far), jnp.where(top, far, gradient)], axis=1)
        gradient = lax.psum_scatter(whole.astype(BF16), "shot", scatter_dimension=1, tiled=True).astype(F32)
    return (down, up, gradient)


def solution(mesh):
    return jax.shard_map(
        per_device,
        mesh=mesh,
        in_specs=(
            P("depth", "shot", None, None, None),
            P("depth", "shot", None, None, None),
            P("shot", None, None, None),
            P("depth", None, None),
            P("depth", None, None),
            P(),
            P("shot"),
        ),
        out_specs=(
            P("depth", "shot", None, None, None),
            P("depth", "shot", None, None, None),
            P("depth", "shot", None),
        ),
        check_vma=False,
    )
```

```python
import functools
import math

import jax
import jax.numpy as jnp
import numpy as np
from jax import lax
from jax.experimental import pallas as pl
from jax.experimental.pallas import tpu as pltpu
from jax.sharding import PartitionSpec as P

HOPS = 3
NCLASS = 16
NFREQ = 128
F32 = jnp.float32
BF16 = jnp.bfloat16
VMEM = pl.BlockSpec(memory_space=pltpu.VMEM)
HBM = pl.BlockSpec(memory_space=pltpu.HBM)
SMEM = pl.BlockSpec(memory_space=pltpu.SMEM)
PARAMS = pltpu.CompilerParams(vmem_limit_bytes=28 * 2**20)


def passed_along(block, axis, distance):
    devices = range(lax.axis_size(axis))
    route = [(i - distance, i) for i in devices if i - distance in devices]
    return lax.ppermute(block, axis, route)


def dft_tables(length):
    counter = jnp.arange(length, dtype=jnp.int32)
    product = counter[:, None] * counter[None, :] % length
    angles = 2.0 * math.pi / length * product.astype(jnp.float32)
    return (jnp.cos(angles).astype(jnp.bfloat16), jnp.sin(angles).astype(jnp.bfloat16))


def wavenumbers(length):
    counter = jnp.arange(length, dtype=jnp.int32)
    wrapped = jnp.where(counter >= length // 2, counter - length, counter)
    return 2.0 * math.pi / length * wrapped.astype(jnp.float32)


def propagate(planes, phase_re, phase_im, tables):
    fwd_left, fwd_right, inv_left, inv_right = tables
    first = jnp.einsum(
        "cdjk,...dkl->...cjl", fwd_left, planes, preferred_element_type=jnp.float32
    ).astype(jnp.bfloat16)
    second = jnp.einsum("...djl,dclm->...cjm", first, fwd_right, preferred_element_type=jnp.float32)
    real_part = second[..., 0, :, :]
    imag_part = second[..., 1, :, :]
    turned = jnp.stack(
        [real_part * phase_re - imag_part * phase_im, real_part * phase_im + imag_part * phase_re],
        axis=-3,
    ).astype(jnp.bfloat16)
    third = jnp.einsum(
        "cdjk,...dkl->...cjl", inv_left, turned, preferred_element_type=jnp.float32
    ).astype(jnp.bfloat16)
    return jnp.einsum(
        "...djl,dclm->...cjm", third, inv_right, preferred_element_type=jnp.float32
    ).astype(jnp.bfloat16)


def trade(down_edge, up_edge):
    got_down = passed_along(down_edge, "depth", 1)
    got_up = passed_along(up_edge, "depth", -1)
    return (got_down, got_up)


def per_device_plain(down_state, up_state, source, reflect, screen_class, screen_values, freq_index):
    levels = down_state.shape[0]
    rows_x = down_state.shape[3]
    rows_y = down_state.shape[4]
    front_count = down_state.shape[1]
    depth_rank = lax.axis_index("depth")
    scale = 1.0 / math.sqrt(front_count * lax.axis_size("shot"))
    cos_x, sin_x = dft_tables(rows_x)
    cos_y, sin_y = dft_tables(rows_y)
    tables = (
        jnp.stack([jnp.stack([cos_x, sin_x]), jnp.stack([-sin_x, cos_x])]),
        jnp.stack([jnp.stack([cos_y, -sin_y]), jnp.stack([sin_y, cos_y])]),
        jnp.stack([jnp.stack([cos_x, -sin_x]), jnp.stack([sin_x, cos_x])]),
        jnp.stack([jnp.stack([cos_y, sin_y]), jnp.stack([-sin_y, cos_y])]),
    )
    kwave = 0.95 * math.pi * (freq_index.astype(jnp.float32) + 1.0) / NFREQ
    kx_wave = wavenumbers(rows_x)
    ky_wave = wavenumbers(rows_y)
    vertical = kwave[:, None, None] ** 2 - kx_wave[None, :, None] ** 2 - ky_wave[None, None, :] ** 2
    propag = jnp.sqrt(jnp.maximum(vertical, 0.0))
    damping = jnp.exp(-jnp.sqrt(jnp.maximum(-vertical, 0.0))) / (rows_x * rows_y)
    phase_re = damping * jnp.cos(propag)
    phase_im = damping * jnp.sin(propag)
    classes = jnp.arange(NCLASS, dtype=jnp.int32)
    onehot = (screen_class[None] == classes[:, None, None, None]).astype(jnp.float32)
    slowness = jnp.einsum("c,clxy->lxy", screen_values, onehot, precision=lax.Precision.HIGHEST)
    angle = kwave[None, :, None, None] * slowness[:, None]
    screen_re = jnp.cos(angle)
    screen_im = jnp.sin(angle)
    refl = reflect[:, None]
    top_slab = depth_rank == 0
    down = down_state
    up = up_state
    a_re = a_im = b_re = b_im = None
    for repeat in range(HOPS):
        down_edge = down[levels - 1]
        up_edge = up[0]
        got_down, got_up = trade(down_edge, up_edge)
        got_down = jnp.where(top_slab, source, got_down)
        moved = propagate(
            jnp.concatenate([got_down[None], down[: levels - 1], up[1:], got_up[None]], axis=0),
            phase_re,
            phase_im,
            tables,
        )
        from_above = moved[:levels]
        from_below = moved[levels:]
        qa_re = from_above[:, :, 0].astype(jnp.float32)
        qa_im = from_above[:, :, 1].astype(jnp.float32)
        qb_re = from_below[:, :, 0].astype(jnp.float32)
        qb_im = from_below[:, :, 1].astype(jnp.float32)
        a_re = screen_re * qa_re - screen_im * qa_im
        a_im = screen_re * qa_im + screen_im * qa_re
        b_re = screen_re * qb_re - screen_im * qb_im
        b_im = screen_re * qb_im + screen_im * qb_re
        down = jnp.stack(
            [(1.0 + refl) * a_re - refl * b_re, (1.0 + refl) * a_im - refl * b_im], axis=2
        ).astype(jnp.bfloat16)
        up = jnp.stack(
            [(1.0 - refl) * b_re + refl * a_re, (1.0 - refl) * b_im + refl * a_im], axis=2
        ).astype(jnp.bfloat16)
    terms = scale * jnp.sum(a_re * b_re + a_im * b_im, axis=1)
    gradient = lax.psum_scatter(
        terms.astype(jnp.bfloat16), "shot", scatter_dimension=1, tiled=True
    ).astype(jnp.float32)
    return (down, up, gradient)


def hartley(length):
    counter = np.arange(length)
    angles = 2.0 * np.pi / length * (counter[:, None] * counter[None, :] % length)
    cosine = np.cos(angles).astype(BF16).astype(np.float32)
    sine = np.sin(angles).astype(BF16).astype(np.float32)
    return (cosine + sine).astype(BF16)


def odd_place():
    return lax.rem(lax.axis_index("depth"), 2)


def mm(left, right):
    return jnp.dot(left, right, preferred_element_type=F32)


def spread(jobs, work, hx, hy, phase):
    jobs = list(enumerate(jobs))
    for slot, (plane, _, _) in jobs:
        for part in range(2):
            work[slot, part] = mm(hx[...], plane(part) if callable(plane) else plane[part]).astype(BF16)
    for slot, (_, front, _) in jobs:
        turn_re, turn_im = phase[front, 0], phase[front, 1]
        part_re = mm(work[slot, 0], hy[...])
        part_im = mm(work[slot, 1], hy[...])
        work[slot, 0] = (part_re * turn_re - part_im * turn_im).astype(BF16)
        work[slot, 1] = (part_re * turn_im + part_im * turn_re).astype(BF16)
    for slot, _ in jobs:
        for part in range(2):
            work[slot, part] = mm(work[slot, part], hy[...]).astype(BF16)
    for slot, (_, _, target) in jobs:
        for part in range(2):
            if isinstance(target, list):
                for rows, piece in target:
                    piece[part] = mm(hx[rows, :], work[slot, part]).astype(BF16)
            else:
                target[part] = mm(hx[...], work[slot, part]).astype(BF16)


def screened(real_part, imag_part, screen_re, screen_im):
    return (
        screen_re * real_part - screen_im * imag_part,
        screen_re * imag_part + screen_im * real_part,
    )


def mixed(a_re, a_im, b_re, b_im, refl, screen_re, screen_im, waves="both"):
    a_re, a_im, b_re, b_im = (part.astype(F32) for part in (a_re, a_im, b_re, b_im))
    step_re = refl * (a_re - b_re)
    step_im = refl * (a_im - b_im)
    fields = ()
    if waves != "outward":
        fields += screened(a_re + step_re, a_im + step_im, screen_re, screen_im)
    if waves != "inward":
        fields += screened(b_re + step_re, b_im + step_im, screen_re, screen_im)
    return fields


def put(target, real_part, imag_part):
    target[0] = real_part.astype(BF16)
    target[1] = imag_part.astype(BF16)


def half_rows(of, half):
    shot = lax.rem(lax.axis_index("shot"), 2)
    return pl.ds(pl.multiple_of((shot if of == 0 else 1 - shot) * half, half), half)


def late_pair():
    return lax.rem(lax.div(lax.axis_index("depth") + 1, 2), 2) == 1


def by_turn(early, late):
    is_late = late_pair()
    pl.when(jnp.logical_not(is_late))(early)
    pl.when(is_late)(late)


def edges_kernel(down, up, outward_outer, inward_inner, sems):
    levels = down.shape[0]
    odd = odd_place()

    def fetch(first, second):
        pltpu.make_async_copy(first, outward_outer, sems.at[0]).start()
        pltpu.make_async_copy(second, inward_inner, sems.at[1]).start()

    @pl.when(odd == 0)
    def _():
        fetch(up.at[0], down.at[levels - 1])

    @pl.when(odd == 1)
    def _():
        fetch(down.at[levels - 1], up.at[0])

    pltpu.make_async_copy(up.at[0], outward_outer, sems.at[0]).wait()
    pltpu.make_async_copy(up.at[0], inward_inner, sems.at[1]).wait()


def class_rows(slowness, kwave, shape):
    lanes = lax.broadcasted_iota(jnp.int32, shape, 1)
    table = jnp.zeros(shape, F32)
    for entry in range(NCLASS):
        table = jnp.where(lanes == entry, slowness[entry], table)
    angle = kwave * table
    return jnp.cos(angle), jnp.sin(angle)


def look_up(table, classes):
    width = 128
    rows = classes.shape[0]
    wide = jnp.broadcast_to(table[:1], (rows, width))
    pieces = [
        jnp.take_along_axis(wide, classes[:, start : start + width], axis=1, mode="promise_in_bounds")
        for start in range(0, classes.shape[1], width)
    ]
    return jnp.concatenate(pieces, axis=1)


def front_wave(freq, front):
    return 0.95 * math.pi * (freq[front].astype(F32) + 1.0) / NFREQ


def series(square, shift):
    total = jnp.full_like(square, 1.0 / math.factorial(18 + shift))
    for order in range(16, -1, -2):
        total = 1.0 / math.factorial(order + shift) - square * total
    return total


def setup_kernel(
    down, up, reflect, classes_in, slowness, freq, hx, hy,
    q_out_inner, q_in_outer, screen, phase, refl,
    fields, klass, work, sems,
):
    fronts = q_out_inner.shape[0]
    rows_x, rows_y = refl.shape[1:]
    odd = odd_place()
    fixed = [
        pltpu.make_async_copy(reflect.at[odd], refl.at[0], sems.at[2]),
        pltpu.make_async_copy(reflect.at[1 - odd], refl.at[1], sems.at[3]),
        pltpu.make_async_copy(classes_in.at[odd], klass.at[0], sems.at[4]),
        pltpu.make_async_copy(classes_in.at[1 - odd], klass.at[1], sems.at[5]),
    ]
    for copy in fixed:
        copy.start()

    @pl.when(odd == 0)
    def _():
        pltpu.make_async_copy(down.at[0], fields.at[0], sems.at[0]).start()
        pltpu.make_async_copy(up.at[1], fields.at[1], sems.at[1]).start()

    @pl.when(odd == 1)
    def _():
        pltpu.make_async_copy(up.at[1], fields.at[0], sems.at[0]).start()
        pltpu.make_async_copy(down.at[0], fields.at[1], sems.at[1]).start()

    def squares(length, axis):
        counter = lax.broadcasted_iota(jnp.int32, (rows_x, rows_y), axis)
        wrapped = jnp.where(counter >= length // 2, counter - length, counter)
        wave = 2.0 * math.pi / length * wrapped.astype(F32)
        return wave * wave

    lateral = squares(rows_x, 0) + squares(rows_y, 1)
    level_out = 1.0 / (rows_x * rows_y)
    for front in range(fronts):
        kwave = front_wave(freq, front)
        vertical = kwave * kwave - lateral
        travels = vertical > 0.0
        square = jnp.maximum(vertical, 0.0)
        root = jnp.sqrt(jnp.abs(vertical))
        phase[front, 0] = jnp.where(travels, series(square, 0), jnp.exp(-root)) * level_out
        phase[front, 1] = jnp.where(travels, root * series(square, 1), 0.0) * level_out
    for copy in fixed:
        copy.wait()
    sign = jnp.where(odd == 0, 1.0, -1.0).astype(F32)
    for level in range(2):
        refl[level] = sign * refl[level]
    for front in range(fronts):
        cos_row, sin_row = class_rows(slowness, front_wave(freq, front), (8, 128))
        for level in range(2):
            screen[level, front, 0] = look_up(cos_row, klass[level])
            screen[level, front, 1] = look_up(sin_row, klass[level])
    pltpu.make_async_copy(down.at[0], fields.at[0], sems.at[0]).wait()
    pltpu.make_async_copy(down.at[0], fields.at[1], sems.at[1]).wait()
    jobs = [(fields.at[1, front], front, q_out_inner.at[front]) for front in range(fronts)]
    jobs += [(fields.at[0, front], front, q_in_outer.at[front]) for front in range(fronts)]
    spread(jobs, work, hx, hy, phase)


def ahead_kernel(
    partner, q_in_outer, screen, refl, phase, hx, hy,
    inward_inner, q_out_inner,
    q_field, field, work,
):
    everyone = range(partner.shape[0])
    spread([(partner.at[front], front, q_field.at[front]) for front in everyone], work, hx, hy, phase)
    for front in everyone:
        in_re, in_im, out_re, out_im = mixed(
            q_in_outer[front, 0], q_in_outer[front, 1], q_field[front, 0], q_field[front, 1],
            refl[1], screen[1, front, 0], screen[1, front, 1],
        )
        put(inward_inner.at[front], in_re, in_im)
        put(field.at[front], out_re, out_im)
    spread([(field.at[front], front, q_out_inner.at[front]) for front in everyone], work, hx, hy, phase)


def entering(arrived, source, front):
    first = lax.axis_index("depth") == 0
    return lambda part: jnp.where(first, source[front, part], arrived[front, part])


def outer_step(q_arrived, q_out_inner, screen, refl, waves, field):
    for front in range(field.shape[0]):
        put(
            field.at[front],
            *mixed(
                q_arrived[front, 0], q_arrived[front, 1], q_out_inner[front, 0], q_out_inner[front, 1],
                refl[0], screen[0, front, 0], screen[0, front, 1], waves,
            ),
        )


def edge_kernel(arrived, source, q_out_inner, screen, refl, phase, hx, hy, sent, q_arrived, field, work):
    everyone = range(arrived.shape[0])

    def step(target):
        jobs = [(entering(arrived, source, front), front, q_arrived.at[front]) for front in everyone]
        spread(jobs, work, hx, hy, phase)
        outer_step(q_arrived, q_out_inner, screen, refl, "outward", target)

    def early():
        step(sent)

    def late():
        step(field)
        spread([(field.at[front], front, sent.at[front]) for front in everyone], work, hx, hy, phase)

    by_turn(early, late)


def last_edge_kernel(
    arrived, source, q_out_inner, screen, refl, phase, hx, hy, after,
    q_arrived, last_far, last_near,
    outward, work,
):
    del after
    everyone = range(arrived.shape[0])
    half = arrived.shape[2] // 2

    def step():
        outer_step(q_arrived, q_out_inner, screen, refl, "outward", outward)
        jobs = [
            (outward.at[front], front, [(half_rows(1, half), last_far.at[front]), (half_rows(0, half), last_near.at[front])])
            for front in everyone
        ]
        spread(jobs, work, hx, hy, phase)

    def early():
        jobs = [(entering(arrived, source, front), front, q_arrived.at[front]) for front in everyone]
        spread(jobs, work, hx, hy, phase)
        step()

    def late():
        q_arrived[...] = arrived[...]
        step()

    by_turn(early, late)


def inner_kernel(
    q_arrived, q_out_inner, partner, screen, refl, phase, hx, hy,
    inward, outward,
    field, q_inward, q_partner, work,
):
    everyone = range(partner.shape[0])
    outer_step(q_arrived, q_out_inner, screen, refl, "inward", field)
    jobs = [(partner.at[front], front, q_partner.at[front]) for front in everyone]
    jobs += [(field.at[front], front, q_inward.at[front]) for front in everyone]
    spread(jobs, work, hx, hy, phase)
    for front in everyone:
        in_re, in_im, out_re, out_im = mixed(
            q_inward[front, 0], q_inward[front, 1], q_partner[front, 0], q_partner[front, 1],
            refl[1], screen[1, front, 0], screen[1, front, 1],
        )
        put(inward.at[front], in_re, in_im)
        put(outward.at[front], out_re, out_im)


def spread_kernel(fields, phase, hx, hy, q_fields, work):
    @pl.when(late_pair())
    def _():
        everyone = range(fields.shape[0])
        spread([(fields.at[front], front, q_fields.at[front]) for front in everyone], work, hx, hy, phase)


def last_inner_kernel(
    q_arrived, q_out_inner, partner, screen, refl, phase, hx, hy, out_inner, q_next_in,
    inward, outward, terms, far_terms, q_next,
    field, q_inward, q_partner, work,
):
    del q_next_in
    everyone = range(partner.shape[0])

    @pl.when(jnp.logical_not(late_pair()))
    def _():
        spread([(out_inner.at[front], front, q_next.at[front]) for front in everyone], work, hx, hy, phase)

    outer_step(q_arrived, q_out_inner, screen, refl, "inward", field)
    jobs = [(partner.at[front], front, q_partner.at[front]) for front in everyone]
    jobs += [(field.at[front], front, q_inward.at[front]) for front in everyone]
    spread(jobs, work, hx, hy, phase)
    total = None
    for front in everyone:
        a_re, a_im = (q_inward[front, part].astype(F32) for part in range(2))
        b_re, b_im = (q_partner[front, part].astype(F32) for part in range(2))
        in_re, in_im, out_re, out_im = mixed(
            a_re, a_im, b_re, b_im, refl[1], screen[1, front, 0], screen[1, front, 1]
        )
        put(inward.at[front], in_re, in_im)
        put(outward.at[front], out_re, out_im)
        term = a_re * b_re + a_im * b_im
        total = term if total is None else total + term
    terms[...] = total
    far_terms[...] = terms[half_rows(1, far_terms.shape[0]), :].astype(BF16)


def incoming(last, q_arrived, front, rows):
    first = lax.axis_index("depth") == 0
    return [jnp.where(first, q_arrived[front, part, rows, :], last[front, part]).astype(F32) for part in range(2)]


def row_terms(of, last, q_arrived, q_out_inner):
    total = None
    rows = half_rows(of, last.shape[2])
    for front in range(last.shape[0]):
        a_re, a_im = incoming(last, q_arrived, front, rows)
        b_re, b_im = (q_out_inner[front, part, rows, :].astype(F32) for part in range(2))
        term = a_re * b_re + a_im * b_im
        total = term if total is None else total + term
    return total


def row_fields(of, last, q_arrived, q_out_inner, screen, refl, inward, outward):
    rows = half_rows(of, last.shape[2])
    for front in range(last.shape[0]):
        a_re, a_im = incoming(last, q_arrived, front, rows)
        b_re, b_im = (q_out_inner[front, part, rows, :].astype(F32) for part in range(2))
        in_re, in_im, out_re, out_im = mixed(
            a_re, a_im, b_re, b_im, refl[0, rows, :], screen[0, front, 0, rows, :], screen[0, front, 1, rows, :]
        )
        put(inward.at[front], in_re, in_im)
        put(outward.at[front], out_re, out_im)
    return rows


def far_terms_kernel(last, q_arrived, q_out_inner, after, terms):
    del after
    terms[...] = row_terms(1, last, q_arrived, q_out_inner).astype(BF16)


def send_home(level, rows, inward, outward, down_out, up_out, sems):
    odd = odd_place()

    def copies(place, inward_out, outward_out):
        return [
            pltpu.make_async_copy(inward, inward_out.at[place, :, :, rows, :], sems.at[0]),
            pltpu.make_async_copy(outward, outward_out.at[place, :, :, rows, :], sems.at[1]),
        ]

    @pl.when(odd == 0)
    def _():
        for copy in copies(level, down_out, up_out):
            copy.start()

    @pl.when(odd == 1)
    def _():
        for copy in copies(1 - level, up_out, down_out):
            copy.start()

    return copies(0, down_out, up_out)


def outer_fields_kernel(
    scale, near, far, q_arrived, q_out_inner, screen, refl, inner_in, inner_out, inner_terms, inner_other,
    down_out, up_out, gradient, terms,
    near_in, near_out, far_in, far_out, inner_sum, sems,
):
    rows_x = inner_in.shape[2]
    waits = send_home(1, pl.ds(0, rows_x), inner_in, inner_out, down_out, up_out, sems.at[0])
    rows = row_fields(1, far, q_arrived, q_out_inner, screen, refl, far_in, far_out)
    waits += send_home(0, rows, far_in, far_out, down_out, up_out, sems.at[1])
    rows = row_fields(0, near, q_arrived, q_out_inner, screen, refl, near_in, near_out)
    waits += send_home(0, rows, near_in, near_out, down_out, up_out, sems.at[2])
    inner_sum[...] = scale * (inner_terms[rows, :] + inner_other[...].astype(F32))
    waits.append(pltpu.make_async_copy(inner_sum, gradient.at[1 - odd_place()], sems.at[3, 0]))
    waits[-1].start()
    terms[...] = row_terms(0, near, q_arrived, q_out_inner)
    for copy in waits:
        copy.wait()


def outer_gradient_kernel(scale, terms, other, gradient_in, gradient, outer_sum, sems):
    del gradient_in
    outer_sum[...] = scale * (terms[...] + other[...].astype(F32))
    done = pltpu.make_async_copy(outer_sum, gradient.at[odd_place()], sems.at[0])
    done.start()
    done.wait()


def per_device(down_state, up_state, source, reflect, screen_class, screen_values, freq_index):
    depth = lax.axis_size("depth")
    shots = lax.axis_size("shot")
    levels, fronts, parts, rows_x, rows_y = down_state.shape
    if levels != 2 or depth % 2 or shots % 2 or HOPS != 3:
        return per_device_plain(down_state, up_state, source, reflect, screen_class, screen_values, freq_index)
    scale = 1.0 / math.sqrt(fronts * shots)
    half = rows_x // 2
    hx = jnp.asarray(hartley(rows_x))
    hy = jnp.asarray(hartley(rows_y))
    partners = [(i, i ^ 1) for i in range(depth)]
    beyond = [(i, i + 1) for i in range(1, depth - 1, 2)] + [(i + 1, i) for i in range(1, depth - 1, 2)]
    to_partner = functools.partial(lax.ppermute, axis_name="depth", perm=partners)
    to_beyond = functools.partial(lax.ppermute, axis_name="depth", perm=beyond)
    across = functools.partial(lax.ppermute, axis_name="shot", perm=[(i, i ^ 1) for i in range(shots)])
    plane = jax.ShapeDtypeStruct((fronts, parts, rows_x, rows_y), BF16)
    half_plane = jax.ShapeDtypeStruct((fronts, parts, half, rows_y), BF16)
    pair = jax.ShapeDtypeStruct((2, rows_x, rows_y), F32)
    turns = jax.ShapeDtypeStruct((fronts, parts, rows_x, rows_y), F32)
    screens = jax.ShapeDtypeStruct((2, fronts, parts, rows_x, rows_y), F32)
    state = jax.ShapeDtypeStruct(down_state.shape, BF16)
    dma = pltpu.SemaphoreType.DMA

    def call(kernel, in_specs, out_specs, out_shape, scratch=(), **more):
        return pl.pallas_call(
            kernel,
            in_specs=in_specs,
            out_specs=out_specs,
            out_shape=out_shape,
            scratch_shapes=list(scratch),
            compiler_params=PARAMS,
            **more,
        )

    def kept_in_hbm(*arrays):
        return [pltpu.with_memory_space_constraint(array, pltpu.HBM) for array in arrays]

    def buffers(count, shape=plane):
        return [pltpu.VMEM(shape.shape, shape.dtype)] * count

    def work(slots):
        return pltpu.VMEM((slots, *plane.shape[1:]), BF16)

    out_outer, in_inner = call(edges_kernel, [HBM] * 2, [VMEM] * 2, [plane] * 2, [dma((2,))])(
        *kept_in_hbm(down_state, up_state)
    )
    arrived_0 = to_beyond(out_outer)
    partner_0 = to_partner(in_inner)
    q_out_inner_0, q_in_outer_0, screen, phase, refl = call(
        setup_kernel,
        [HBM] * 4 + [SMEM] * 2 + [VMEM] * 2,
        [VMEM] * 5,
        [plane] * 2 + [screens, turns, pair],
        [
            pltpu.VMEM((2, *plane.shape), BF16),
            pltpu.VMEM((2, rows_x, rows_y), jnp.int32),
            work(2 * fronts),
            dma((6,)),
        ],
    )(*kept_in_hbm(down_state, up_state, reflect, screen_class), screen_values, freq_index, hx, hy)
    fixed = (screen, refl, phase, hx, hy)
    in_inner_1, q_out_inner_1 = call(ahead_kernel, [VMEM] * 7, [VMEM] * 2, [plane] * 2, buffers(2) + [work(fronts)])(
        partner_0, q_in_outer_0, *fixed
    )
    partner_1 = to_partner(in_inner_1)
    out_outer_1, q_arrived = call(edge_kernel, [VMEM] * 8, [VMEM] * 2, [plane] * 2, buffers(1) + [work(fronts)])(
        arrived_0, source, q_out_inner_0, *fixed
    )
    arrived_1 = to_beyond(out_outer_1)
    in_inner_2, out_inner_2 = call(
        inner_kernel, [VMEM] * 8, [VMEM] * 2, [plane] * 2, buffers(3) + [work(2 * fronts)]
    )(q_arrived, q_out_inner_0, partner_1, *fixed)
    partner_2 = to_partner(in_inner_2)
    q_out_inner_2 = call(spread_kernel, [VMEM] * 4, VMEM, plane, [work(fronts)])(out_inner_2, phase, hx, hy)
    q_arrived_1, last_far, last_near = call(
        last_edge_kernel,
        [VMEM] * 8 + [pl.BlockSpec(memory_space=pl.ANY)],
        [VMEM] * 3,
        [plane] + [half_plane] * 2,
        buffers(1) + [work(fronts)],
    )(arrived_1, source, q_out_inner_1, *fixed, q_out_inner_2)
    last_far = to_beyond(last_far)
    last_near = to_beyond(last_near)
    half_sum = jax.ShapeDtypeStruct((half, rows_y), BF16)
    inner_in, inner_out, inner_terms, inner_far, q_out_inner_2 = call(
        last_inner_kernel,
        [VMEM] * 10,
        [VMEM] * 5,
        [plane] * 2 + [jax.ShapeDtypeStruct((rows_x, rows_y), F32), half_sum, plane],
        buffers(3) + [work(2 * fronts)],
        input_output_aliases={9: 4},
    )(q_arrived_1, q_out_inner_1, partner_2, *fixed, out_inner_2, q_out_inner_2)
    inner_other = across(inner_far) if shots == 2 else jnp.zeros_like(inner_far)
    outer_far = call(far_terms_kernel, [VMEM] * 3 + [pl.BlockSpec(memory_space=pl.ANY)], VMEM, half_sum)(
        last_far, q_arrived, q_out_inner_2, inner_terms
    )
    outer_other = across(outer_far) if shots == 2 else jnp.zeros_like(outer_far)
    half_total = jax.ShapeDtypeStruct((half, rows_y), F32)
    share = jax.ShapeDtypeStruct((2, half, rows_y), F32)
    down, up, gradient, outer_near = call(
        functools.partial(outer_fields_kernel, scale),
        [VMEM] * 10,
        [HBM] * 3 + [VMEM],
        [state, state, share, half_total],
        buffers(4, half_plane) + buffers(1, half_total) + [dma((4, 2))],
    )(
        last_near, last_far, q_arrived, q_out_inner_2, screen, refl, inner_in, inner_out, inner_terms, inner_other
    )
    gradient = call(
        functools.partial(outer_gradient_kernel, scale),
        [VMEM] * 2 + [HBM],
        HBM,
        share,
        buffers(1, half_total) + [dma((1,))],
        input_output_aliases={2: 0},
    )(outer_near, outer_other, gradient)
    if shots != 2:
        terms = scale * jnp.stack([outer_far, inner_far]).astype(F32)
        far = jnp.where(odd_place() == 0, terms, terms[::-1])
        top = lax.rem(lax.axis_index("shot"), 2) == 0
        whole = jnp.concatenate([jnp.where(top, gradient, far), jnp.where(top, far, gradient)], axis=1)
        gradient = lax.psum_scatter(whole.astype(BF16), "shot", scatter_dimension=1, tiled=True).astype(F32)
    return (down, up, gradient)


def solution(mesh):
    return jax.shard_map(
        per_device,
        mesh=mesh,
        in_specs=(
            P("depth", "shot", None, None, None),
            P("depth", "shot", None, None, None),
            P("shot", None, None, None),
            P("depth", None, None),
            P("depth", None, None),
            P(),
            P("shot"),
        ),
        out_specs=(
            P("depth", "shot", None, None, None),
            P("depth", "shot", None, None, None),
            P("depth", "shot", None),
        ),
        check_vma=False,
    )
```

```python
import functools
import math

import jax
import jax.numpy as jnp
import numpy as np
from jax import lax
from jax.experimental import pallas as pl
from jax.experimental.pallas import tpu as pltpu
from jax.sharding import PartitionSpec as P

HOPS = 3
NCLASS = 16
NFREQ = 128
F32 = jnp.float32
BF16 = jnp.bfloat16
VMEM = pl.BlockSpec(memory_space=pltpu.VMEM)
HBM = pl.BlockSpec(memory_space=pltpu.HBM)
SMEM = pl.BlockSpec(memory_space=pltpu.SMEM)
PARAMS = pltpu.CompilerParams(vmem_limit_bytes=28 * 2**20)


def passed_along(block, axis, distance):
    devices = range(lax.axis_size(axis))
    route = [(i - distance, i) for i in devices if i - distance in devices]
    return lax.ppermute(block, axis, route)


def dft_tables(length):
    counter = jnp.arange(length, dtype=jnp.int32)
    product = counter[:, None] * counter[None, :] % length
    angles = 2.0 * math.pi / length * product.astype(jnp.float32)
    return (jnp.cos(angles).astype(jnp.bfloat16), jnp.sin(angles).astype(jnp.bfloat16))


def wavenumbers(length):
    counter = jnp.arange(length, dtype=jnp.int32)
    wrapped = jnp.where(counter >= length // 2, counter - length, counter)
    return 2.0 * math.pi / length * wrapped.astype(jnp.float32)


def propagate(planes, phase_re, phase_im, tables):
    fwd_left, fwd_right, inv_left, inv_right = tables
    first = jnp.einsum(
        "cdjk,...dkl->...cjl", fwd_left, planes, preferred_element_type=jnp.float32
    ).astype(jnp.bfloat16)
    second = jnp.einsum("...djl,dclm->...cjm", first, fwd_right, preferred_element_type=jnp.float32)
    real_part = second[..., 0, :, :]
    imag_part = second[..., 1, :, :]
    turned = jnp.stack(
        [real_part * phase_re - imag_part * phase_im, real_part * phase_im + imag_part * phase_re],
        axis=-3,
    ).astype(jnp.bfloat16)
    third = jnp.einsum(
        "cdjk,...dkl->...cjl", inv_left, turned, preferred_element_type=jnp.float32
    ).astype(jnp.bfloat16)
    return jnp.einsum(
        "...djl,dclm->...cjm", third, inv_right, preferred_element_type=jnp.float32
    ).astype(jnp.bfloat16)


def trade(down_edge, up_edge):
    got_down = passed_along(down_edge, "depth", 1)
    got_up = passed_along(up_edge, "depth", -1)
    return (got_down, got_up)


def per_device_plain(down_state, up_state, source, reflect, screen_class, screen_values, freq_index):
    levels = down_state.shape[0]
    rows_x = down_state.shape[3]
    rows_y = down_state.shape[4]
    front_count = down_state.shape[1]
    depth_rank = lax.axis_index("depth")
    scale = 1.0 / math.sqrt(front_count * lax.axis_size("shot"))
    cos_x, sin_x = dft_tables(rows_x)
    cos_y, sin_y = dft_tables(rows_y)
    tables = (
        jnp.stack([jnp.stack([cos_x, sin_x]), jnp.stack([-sin_x, cos_x])]),
        jnp.stack([jnp.stack([cos_y, -sin_y]), jnp.stack([sin_y, cos_y])]),
        jnp.stack([jnp.stack([cos_x, -sin_x]), jnp.stack([sin_x, cos_x])]),
        jnp.stack([jnp.stack([cos_y, sin_y]), jnp.stack([-sin_y, cos_y])]),
    )
    kwave = 0.95 * math.pi * (freq_index.astype(jnp.float32) + 1.0) / NFREQ
    kx_wave = wavenumbers(rows_x)
    ky_wave = wavenumbers(rows_y)
    vertical = kwave[:, None, None] ** 2 - kx_wave[None, :, None] ** 2 - ky_wave[None, None, :] ** 2
    propag = jnp.sqrt(jnp.maximum(vertical, 0.0))
    damping = jnp.exp(-jnp.sqrt(jnp.maximum(-vertical, 0.0))) / (rows_x * rows_y)
    phase_re = damping * jnp.cos(propag)
    phase_im = damping * jnp.sin(propag)
    classes = jnp.arange(NCLASS, dtype=jnp.int32)
    onehot = (screen_class[None] == classes[:, None, None, None]).astype(jnp.float32)
    slowness = jnp.einsum("c,clxy->lxy", screen_values, onehot, precision=lax.Precision.HIGHEST)
    angle = kwave[None, :, None, None] * slowness[:, None]
    screen_re = jnp.cos(angle)
    screen_im = jnp.sin(angle)
    refl = reflect[:, None]
    top_slab = depth_rank == 0
    down = down_state
    up = up_state
    a_re = a_im = b_re = b_im = None
    for repeat in range(HOPS):
        down_edge = down[levels - 1]
        up_edge = up[0]
        got_down, got_up = trade(down_edge, up_edge)
        got_down = jnp.where(top_slab, source, got_down)
        moved = propagate(
            jnp.concatenate([got_down[None], down[: levels - 1], up[1:], got_up[None]], axis=0),
            phase_re,
            phase_im,
            tables,
        )
        from_above = moved[:levels]
        from_below = moved[levels:]
        qa_re = from_above[:, :, 0].astype(jnp.float32)
        qa_im = from_above[:, :, 1].astype(jnp.float32)
        qb_re = from_below[:, :, 0].astype(jnp.float32)
        qb_im = from_below[:, :, 1].astype(jnp.float32)
        a_re = screen_re * qa_re - screen_im * qa_im
        a_im = screen_re * qa_im + screen_im * qa_re
        b_re = screen_re * qb_re - screen_im * qb_im
        b_im = screen_re * qb_im + screen_im * qb_re
        down = jnp.stack(
            [(1.0 + refl) * a_re - refl * b_re, (1.0 + refl) * a_im - refl * b_im], axis=2
        ).astype(jnp.bfloat16)
        up = jnp.stack(
            [(1.0 - refl) * b_re + refl * a_re, (1.0 - refl) * b_im + refl * a_im], axis=2
        ).astype(jnp.bfloat16)
    terms = scale * jnp.sum(a_re * b_re + a_im * b_im, axis=1)
    gradient = lax.psum_scatter(
        terms.astype(jnp.bfloat16), "shot", scatter_dimension=1, tiled=True
    ).astype(jnp.float32)
    return (down, up, gradient)


def hartley(length):
    counter = np.arange(length)
    angles = 2.0 * np.pi / length * (counter[:, None] * counter[None, :] % length)
    cosine = np.cos(angles).astype(BF16).astype(np.float32)
    sine = np.sin(angles).astype(BF16).astype(np.float32)
    return (cosine + sine).astype(BF16)


def odd_place():
    return lax.rem(lax.axis_index("depth"), 2)


def mm(left, right):
    return jnp.dot(left, right, preferred_element_type=F32)


def spread(jobs, work, hx, hy, phase):
    jobs = list(enumerate(jobs))
    for slot, (plane, _, _) in jobs:
        for part in range(2):
            work[slot, part] = mm(hx[...], plane(part) if callable(plane) else plane[part]).astype(BF16)
    for slot, (_, front, _) in jobs:
        turn_re, turn_im = phase[front, 0], phase[front, 1]
        part_re = mm(work[slot, 0], hy[...])
        part_im = mm(work[slot, 1], hy[...])
        work[slot, 0] = (part_re * turn_re - part_im * turn_im).astype(BF16)
        work[slot, 1] = (part_re * turn_im + part_im * turn_re).astype(BF16)
    for slot, _ in jobs:
        for part in range(2):
            work[slot, part] = mm(work[slot, part], hy[...]).astype(BF16)
    for slot, (_, _, target) in jobs:
        for part in range(2):
            if isinstance(target, list):
                rows = jnp.concatenate([hx[rows, :] for rows, _ in target], axis=0)
                ends = np.cumsum([piece.shape[1] for _, piece in target])
                done = mm(rows, work[slot, part]).astype(BF16)
                for (_, piece), end in zip(target, ends, strict=True):
                    piece[part] = done[end - piece.shape[1] : end]
            else:
                target[part] = mm(hx[...], work[slot, part]).astype(BF16)


def screened(real_part, imag_part, screen_re, screen_im):
    return (
        screen_re * real_part - screen_im * imag_part,
        screen_re * imag_part + screen_im * real_part,
    )


def mixed(a_re, a_im, b_re, b_im, refl, screen_re, screen_im, waves="both"):
    a_re, a_im, b_re, b_im = (part.astype(F32) for part in (a_re, a_im, b_re, b_im))
    step_re = refl * (a_re - b_re)
    step_im = refl * (a_im - b_im)
    fields = ()
    if waves != "outward":
        fields += screened(a_re + step_re, a_im + step_im, screen_re, screen_im)
    if waves != "inward":
        fields += screened(b_re + step_re, b_im + step_im, screen_re, screen_im)
    return fields


def put(target, real_part, imag_part):
    target[0] = real_part.astype(BF16)
    target[1] = imag_part.astype(BF16)


def half_rows(of, half):
    shot = lax.rem(lax.axis_index("shot"), 2)
    return pl.ds(pl.multiple_of((shot if of == 0 else 1 - shot) * half, half), half)


def late_pair():
    return lax.rem(lax.div(lax.axis_index("depth") + 1, 2), 2) == 1


def by_turn(early, late):
    is_late = late_pair()
    pl.when(jnp.logical_not(is_late))(early)
    pl.when(is_late)(late)


def edges_kernel(down, up, outward_outer, inward_inner, sems):
    levels = down.shape[0]
    odd = odd_place()

    def fetch(first, second):
        pltpu.make_async_copy(first, outward_outer, sems.at[0]).start()
        pltpu.make_async_copy(second, inward_inner, sems.at[1]).start()

    @pl.when(odd == 0)
    def _():
        fetch(up.at[0], down.at[levels - 1])

    @pl.when(odd == 1)
    def _():
        fetch(down.at[levels - 1], up.at[0])

    pltpu.make_async_copy(up.at[0], outward_outer, sems.at[0]).wait()
    pltpu.make_async_copy(up.at[0], inward_inner, sems.at[1]).wait()


def class_rows(slowness, kwave, shape):
    lanes = lax.broadcasted_iota(jnp.int32, shape, 1)
    table = jnp.zeros(shape, F32)
    for entry in range(NCLASS):
        table = jnp.where(lanes == entry, slowness[entry], table)
    angle = kwave * table
    return jnp.cos(angle), jnp.sin(angle)


def look_up(table, classes):
    width = 128
    rows = classes.shape[0]
    wide = jnp.broadcast_to(table[:1], (rows, width))
    pieces = [
        jnp.take_along_axis(wide, classes[:, start : start + width], axis=1, mode="promise_in_bounds")
        for start in range(0, classes.shape[1], width)
    ]
    return jnp.concatenate(pieces, axis=1)


def front_wave(freq, front):
    return 0.95 * math.pi * (freq[front].astype(F32) + 1.0) / NFREQ


def series(square, shift):
    total = jnp.full_like(square, 1.0 / math.factorial(18 + shift))
    for order in range(16, -1, -2):
        total = 1.0 / math.factorial(order + shift) - square * total
    return total


def setup_kernel(
    down, up, reflect, classes_in, slowness, freq, hx, hy,
    q_out_inner, q_in_outer, screen, phase, refl,
    fields, klass, work, sems,
):
    fronts = q_out_inner.shape[0]
    rows_x, rows_y = refl.shape[1:]
    odd = odd_place()
    fixed = [
        pltpu.make_async_copy(reflect.at[odd], refl.at[0], sems.at[2]),
        pltpu.make_async_copy(reflect.at[1 - odd], refl.at[1], sems.at[3]),
        pltpu.make_async_copy(classes_in.at[odd], klass.at[0], sems.at[4]),
        pltpu.make_async_copy(classes_in.at[1 - odd], klass.at[1], sems.at[5]),
    ]
    for copy in fixed:
        copy.start()

    @pl.when(odd == 0)
    def _():
        pltpu.make_async_copy(down.at[0], fields.at[0], sems.at[0]).start()
        pltpu.make_async_copy(up.at[1], fields.at[1], sems.at[1]).start()

    @pl.when(odd == 1)
    def _():
        pltpu.make_async_copy(up.at[1], fields.at[0], sems.at[0]).start()
        pltpu.make_async_copy(down.at[0], fields.at[1], sems.at[1]).start()

    def squares(length, axis):
        counter = lax.broadcasted_iota(jnp.int32, (rows_x, rows_y), axis)
        wrapped = jnp.where(counter >= length // 2, counter - length, counter)
        wave = 2.0 * math.pi / length * wrapped.astype(F32)
        return wave * wave

    lateral = squares(rows_x, 0) + squares(rows_y, 1)
    level_out = 1.0 / (rows_x * rows_y)
    for front in range(fronts):
        kwave = front_wave(freq, front)
        vertical = kwave * kwave - lateral
        travels = vertical > 0.0
        square = jnp.maximum(vertical, 0.0)
        root = jnp.sqrt(jnp.abs(vertical))
        phase[front, 0] = jnp.where(travels, series(square, 0), jnp.exp(-root)) * level_out
        phase[front, 1] = jnp.where(travels, root * series(square, 1), 0.0) * level_out
    for copy in fixed:
        copy.wait()
    sign = jnp.where(odd == 0, 1.0, -1.0).astype(F32)
    for level in range(2):
        refl[level] = sign * refl[level]
    for front in range(fronts):
        cos_row, sin_row = class_rows(slowness, front_wave(freq, front), (8, 128))
        for level in range(2):
            screen[level, front, 0] = look_up(cos_row, klass[level])
            screen[level, front, 1] = look_up(sin_row, klass[level])
    pltpu.make_async_copy(down.at[0], fields.at[0], sems.at[0]).wait()
    pltpu.make_async_copy(down.at[0], fields.at[1], sems.at[1]).wait()
    jobs = [(fields.at[1, front], front, q_out_inner.at[front]) for front in range(fronts)]
    jobs += [(fields.at[0, front], front, q_in_outer.at[front]) for front in range(fronts)]
    spread(jobs, work, hx, hy, phase)


def ahead_kernel(
    partner, q_in_outer, screen, refl, phase, hx, hy,
    inward_inner, q_out_inner,
    q_field, field, work,
):
    everyone = range(partner.shape[0])
    spread([(partner.at[front], front, q_field.at[front]) for front in everyone], work, hx, hy, phase)
    for front in everyone:
        in_re, in_im, out_re, out_im = mixed(
            q_in_outer[front, 0], q_in_outer[front, 1], q_field[front, 0], q_field[front, 1],
            refl[1], screen[1, front, 0], screen[1, front, 1],
        )
        put(inward_inner.at[front], in_re, in_im)
        put(field.at[front], out_re, out_im)
    spread([(field.at[front], front, q_out_inner.at[front]) for front in everyone], work, hx, hy, phase)


def entering(arrived, source, front):
    first = lax.axis_index("depth") == 0
    return lambda part: jnp.where(first, source[front, part], arrived[front, part])


def outer_step(q_arrived, q_out_inner, screen, refl, waves, field):
    for front in range(field.shape[0]):
        put(
            field.at[front],
            *mixed(
                q_arrived[front, 0], q_arrived[front, 1], q_out_inner[front, 0], q_out_inner[front, 1],
                refl[0], screen[0, front, 0], screen[0, front, 1], waves,
            ),
        )


def edge_kernel(arrived, source, q_out_inner, screen, refl, phase, hx, hy, sent, q_arrived, field, work):
    everyone = range(arrived.shape[0])

    def step(target):
        jobs = [(entering(arrived, source, front), front, q_arrived.at[front]) for front in everyone]
        spread(jobs, work, hx, hy, phase)
        outer_step(q_arrived, q_out_inner, screen, refl, "outward", target)

    def early():
        step(sent)

    def late():
        step(field)
        spread([(field.at[front], front, sent.at[front]) for front in everyone], work, hx, hy, phase)

    by_turn(early, late)


def last_edge_kernel(
    arrived, source, q_out_inner, screen, refl, phase, hx, hy, after,
    q_arrived, last_far, last_near,
    outward, work,
):
    del after
    everyone = range(arrived.shape[0])
    half = arrived.shape[2] // 2

    def step():
        outer_step(q_arrived, q_out_inner, screen, refl, "outward", outward)
        jobs = [
            (outward.at[front], front, [(half_rows(1, half), last_far.at[front]), (half_rows(0, half), last_near.at[front])])
            for front in everyone
        ]
        spread(jobs, work, hx, hy, phase)

    def early():
        jobs = [(entering(arrived, source, front), front, q_arrived.at[front]) for front in everyone]
        spread(jobs, work, hx, hy, phase)
        step()

    def late():
        q_arrived[...] = arrived[...]
        step()

    by_turn(early, late)


def inner_kernel(
    q_arrived, q_out_inner, partner, screen, refl, phase, hx, hy,
    inward, outward,
    field, q_inward, q_partner, work,
):
    everyone = range(partner.shape[0])
    outer_step(q_arrived, q_out_inner, screen, refl, "inward", field)
    jobs = [(partner.at[front], front, q_partner.at[front]) for front in everyone]
    jobs += [(field.at[front], front, q_inward.at[front]) for front in everyone]
    spread(jobs, work, hx, hy, phase)
    for front in everyone:
        in_re, in_im, out_re, out_im = mixed(
            q_inward[front, 0], q_inward[front, 1], q_partner[front, 0], q_partner[front, 1],
            refl[1], screen[1, front, 0], screen[1, front, 1],
        )
        put(inward.at[front], in_re, in_im)
        put(outward.at[front], out_re, out_im)


def spread_kernel(fields, phase, hx, hy, q_fields, work):
    @pl.when(late_pair())
    def _():
        everyone = range(fields.shape[0])
        spread([(fields.at[front], front, q_fields.at[front]) for front in everyone], work, hx, hy, phase)


def last_inner_kernel(
    q_arrived, q_out_inner, partner, screen, refl, phase, hx, hy, out_inner, q_next_in,
    inward, outward, terms, far_terms, q_next,
    field, q_inward, q_partner, work,
):
    del q_next_in
    everyone = range(partner.shape[0])

    @pl.when(jnp.logical_not(late_pair()))
    def _():
        spread([(out_inner.at[front], front, q_next.at[front]) for front in everyone], work, hx, hy, phase)

    outer_step(q_arrived, q_out_inner, screen, refl, "inward", field)
    jobs = [(partner.at[front], front, q_partner.at[front]) for front in everyone]
    jobs += [(field.at[front], front, q_inward.at[front]) for front in everyone]
    spread(jobs, work, hx, hy, phase)
    total = None
    for front in everyone:
        a_re, a_im = (q_inward[front, part].astype(F32) for part in range(2))
        b_re, b_im = (q_partner[front, part].astype(F32) for part in range(2))
        in_re, in_im, out_re, out_im = mixed(
            a_re, a_im, b_re, b_im, refl[1], screen[1, front, 0], screen[1, front, 1]
        )
        put(inward.at[front], in_re, in_im)
        put(outward.at[front], out_re, out_im)
        term = a_re * b_re + a_im * b_im
        total = term if total is None else total + term
    terms[...] = total
    far_terms[...] = terms[half_rows(1, far_terms.shape[0]), :].astype(BF16)


def incoming(last, q_arrived, front, rows):
    first = lax.axis_index("depth") == 0
    return [jnp.where(first, q_arrived[front, part, rows, :], last[front, part]).astype(F32) for part in range(2)]


def row_terms(of, last, q_arrived, q_out_inner):
    total = None
    rows = half_rows(of, last.shape[2])
    for front in range(last.shape[0]):
        a_re, a_im = incoming(last, q_arrived, front, rows)
        b_re, b_im = (q_out_inner[front, part, rows, :].astype(F32) for part in range(2))
        term = a_re * b_re + a_im * b_im
        total = term if total is None else total + term
    return total


def row_fields(of, last, q_arrived, q_out_inner, screen, refl, inward, outward):
    rows = half_rows(of, last.shape[2])
    for front in range(last.shape[0]):
        a_re, a_im = incoming(last, q_arrived, front, rows)
        b_re, b_im = (q_out_inner[front, part, rows, :].astype(F32) for part in range(2))
        in_re, in_im, out_re, out_im = mixed(
            a_re, a_im, b_re, b_im, refl[0, rows, :], screen[0, front, 0, rows, :], screen[0, front, 1, rows, :]
        )
        put(inward.at[front], in_re, in_im)
        put(outward.at[front], out_re, out_im)
    return rows


def far_terms_kernel(last, q_arrived, q_out_inner, after, terms):
    del after
    terms[...] = row_terms(1, last, q_arrived, q_out_inner).astype(BF16)


def send_home(level, rows, inward, outward, down_out, up_out, sems):
    odd = odd_place()

    def copies(place, inward_out, outward_out):
        return [
            pltpu.make_async_copy(inward, inward_out.at[place, :, :, rows, :], sems.at[0]),
            pltpu.make_async_copy(outward, outward_out.at[place, :, :, rows, :], sems.at[1]),
        ]

    @pl.when(odd == 0)
    def _():
        for copy in copies(level, down_out, up_out):
            copy.start()

    @pl.when(odd == 1)
    def _():
        for copy in copies(1 - level, up_out, down_out):
            copy.start()

    return copies(0, down_out, up_out)


def home_kernel(
    far, q_arrived, q_out_inner, screen, refl, inner_in, inner_out, down_out, up_out, far_in, far_out, sems
):
    waits = send_home(1, pl.ds(0, inner_in.shape[2]), inner_in, inner_out, down_out, up_out, sems.at[0])
    rows = row_fields(1, far, q_arrived, q_out_inner, screen, refl, far_in, far_out)
    waits += send_home(0, rows, far_in, far_out, down_out, up_out, sems.at[1])
    for copy in waits:
        copy.wait()


def near_kernel(
    scale, near, q_arrived, q_out_inner, screen, refl, inner_terms, inner_other, down_in, up_in,
    down_out, up_out, gradient, terms,
    near_in, near_out, inner_sum, sems,
):
    del down_in, up_in
    rows = row_fields(0, near, q_arrived, q_out_inner, screen, refl, near_in, near_out)
    waits = send_home(0, rows, near_in, near_out, down_out, up_out, sems.at[0])
    inner_sum[...] = scale * (inner_terms[rows, :] + inner_other[...].astype(F32))
    waits.append(pltpu.make_async_copy(inner_sum, gradient.at[1 - odd_place()], sems.at[1, 0]))
    waits[-1].start()
    terms[...] = row_terms(0, near, q_arrived, q_out_inner)
    for copy in waits:
        copy.wait()


def outer_gradient_kernel(scale, terms, other, gradient_in, gradient, outer_sum, sems):
    del gradient_in
    outer_sum[...] = scale * (terms[...] + other[...].astype(F32))
    done = pltpu.make_async_copy(outer_sum, gradient.at[odd_place()], sems.at[0])
    done.start()
    done.wait()


def per_device(down_state, up_state, source, reflect, screen_class, screen_values, freq_index):
    depth = lax.axis_size("depth")
    shots = lax.axis_size("shot")
    levels, fronts, parts, rows_x, rows_y = down_state.shape
    if levels != 2 or depth % 2 or shots % 2 or HOPS != 3:
        return per_device_plain(down_state, up_state, source, reflect, screen_class, screen_values, freq_index)
    scale = 1.0 / math.sqrt(fronts * shots)
    half = rows_x // 2
    hx = jnp.asarray(hartley(rows_x))
    hy = jnp.asarray(hartley(rows_y))
    partners = [(i, i ^ 1) for i in range(depth)]
    beyond = [(i, i + 1) for i in range(1, depth - 1, 2)] + [(i + 1, i) for i in range(1, depth - 1, 2)]
    to_partner = functools.partial(lax.ppermute, axis_name="depth", perm=partners)
    to_beyond = functools.partial(lax.ppermute, axis_name="depth", perm=beyond)
    across = functools.partial(lax.ppermute, axis_name="shot", perm=[(i, i ^ 1) for i in range(shots)])
    plane = jax.ShapeDtypeStruct((fronts, parts, rows_x, rows_y), BF16)
    half_plane = jax.ShapeDtypeStruct((fronts, parts, half, rows_y), BF16)
    pair = jax.ShapeDtypeStruct((2, rows_x, rows_y), F32)
    turns = jax.ShapeDtypeStruct((fronts, parts, rows_x, rows_y), F32)
    screens = jax.ShapeDtypeStruct((2, fronts, parts, rows_x, rows_y), F32)
    state = jax.ShapeDtypeStruct(down_state.shape, BF16)
    dma = pltpu.SemaphoreType.DMA

    def call(kernel, in_specs, out_specs, out_shape, scratch=(), **more):
        return pl.pallas_call(
            kernel,
            in_specs=in_specs,
            out_specs=out_specs,
            out_shape=out_shape,
            scratch_shapes=list(scratch),
            compiler_params=PARAMS,
            **more,
        )

    def kept_in_hbm(*arrays):
        return [pltpu.with_memory_space_constraint(array, pltpu.HBM) for array in arrays]

    def buffers(count, shape=plane):
        return [pltpu.VMEM(shape.shape, shape.dtype)] * count

    def work(slots):
        return pltpu.VMEM((slots, *plane.shape[1:]), BF16)

    out_outer, in_inner = call(edges_kernel, [HBM] * 2, [VMEM] * 2, [plane] * 2, [dma((2,))])(
        *kept_in_hbm(down_state, up_state)
    )
    arrived_0 = to_beyond(out_outer)
    partner_0 = to_partner(in_inner)
    q_out_inner_0, q_in_outer_0, screen, phase, refl = call(
        setup_kernel,
        [HBM] * 4 + [SMEM] * 2 + [VMEM] * 2,
        [VMEM] * 5,
        [plane] * 2 + [screens, turns, pair],
        [
            pltpu.VMEM((2, *plane.shape), BF16),
            pltpu.VMEM((2, rows_x, rows_y), jnp.int32),
            work(2 * fronts),
            dma((6,)),
        ],
    )(*kept_in_hbm(down_state, up_state, reflect, screen_class), screen_values, freq_index, hx, hy)
    fixed = (screen, refl, phase, hx, hy)
    in_inner_1, q_out_inner_1 = call(ahead_kernel, [VMEM] * 7, [VMEM] * 2, [plane] * 2, buffers(2) + [work(fronts)])(
        partner_0, q_in_outer_0, *fixed
    )
    partner_1 = to_partner(in_inner_1)
    out_outer_1, q_arrived = call(edge_kernel, [VMEM] * 8, [VMEM] * 2, [plane] * 2, buffers(1) + [work(fronts)])(
        arrived_0, source, q_out_inner_0, *fixed
    )
    arrived_1 = to_beyond(out_outer_1)
    in_inner_2, out_inner_2 = call(
        inner_kernel, [VMEM] * 8, [VMEM] * 2, [plane] * 2, buffers(3) + [work(2 * fronts)]
    )(q_arrived, q_out_inner_0, partner_1, *fixed)
    partner_2 = to_partner(in_inner_2)
    q_out_inner_2 = call(spread_kernel, [VMEM] * 4, VMEM, plane, [work(fronts)])(out_inner_2, phase, hx, hy)
    q_arrived_1, last_far, last_near = call(
        last_edge_kernel,
        [VMEM] * 8 + [pl.BlockSpec(memory_space=pl.ANY)],
        [VMEM] * 3,
        [plane] + [half_plane] * 2,
        buffers(1) + [work(fronts)],
    )(arrived_1, source, q_out_inner_1, *fixed, q_out_inner_2)
    last_far = to_beyond(last_far)
    last_near = to_beyond(last_near)
    half_sum = jax.ShapeDtypeStruct((half, rows_y), BF16)
    inner_in, inner_out, inner_terms, inner_far, q_out_inner_2 = call(
        last_inner_kernel,
        [VMEM] * 10,
        [VMEM] * 5,
        [plane] * 2 + [jax.ShapeDtypeStruct((rows_x, rows_y), F32), half_sum, plane],
        buffers(3) + [work(2 * fronts)],
        input_output_aliases={9: 4},
    )(q_arrived_1, q_out_inner_1, partner_2, *fixed, out_inner_2, q_out_inner_2)
    inner_other = across(inner_far) if shots == 2 else jnp.zeros_like(inner_far)
    outer_far = call(far_terms_kernel, [VMEM] * 3 + [pl.BlockSpec(memory_space=pl.ANY)], VMEM, half_sum)(
        last_far, q_arrived, q_out_inner_2, inner_terms
    )
    outer_other = across(outer_far) if shots == 2 else jnp.zeros_like(outer_far)
    half_total = jax.ShapeDtypeStruct((half, rows_y), F32)
    share = jax.ShapeDtypeStruct((2, half, rows_y), F32)
    down, up = call(
        home_kernel, [VMEM] * 7, [HBM] * 2, [state] * 2, buffers(2, half_plane) + [dma((2, 2))]
    )(last_far, q_arrived, q_out_inner_2, screen, refl, inner_in, inner_out)
    down, up, gradient, outer_near = call(
        functools.partial(near_kernel, scale),
        [VMEM] * 7 + [HBM] * 2,
        [HBM] * 3 + [VMEM],
        [state, state, share, half_total],
        buffers(2, half_plane) + buffers(1, half_total) + [dma((2, 2))],
        input_output_aliases={7: 0, 8: 1},
    )(last_near, q_arrived, q_out_inner_2, screen, refl, inner_terms, inner_other, down, up)
    gradient = call(
        functools.partial(outer_gradient_kernel, scale),
        [VMEM] * 2 + [HBM],
        HBM,
        share,
        buffers(1, half_total) + [dma((1,))],
        input_output_aliases={2: 0},
    )(outer_near, outer_other, gradient)
    if shots != 2:
        terms = scale * jnp.stack([outer_far, inner_far]).astype(F32)
        far = jnp.where(odd_place() == 0, terms, terms[::-1])
        top = lax.rem(lax.axis_index("shot"), 2) == 0
        whole = jnp.concatenate([jnp.where(top, gradient, far), jnp.where(top, far, gradient)], axis=1)
        gradient = lax.psum_scatter(whole.astype(BF16), "shot", scatter_dimension=1, tiled=True).astype(F32)
    return (down, up, gradient)


def solution(mesh):
    return jax.shard_map(
        per_device,
        mesh=mesh,
        in_specs=(
            P("depth", "shot", None, None, None),
            P("depth", "shot", None, None, None),
            P("shot", None, None, None),
            P("depth", None, None),
            P("depth", None, None),
            P(),
            P("shot"),
        ),
        out_specs=(
            P("depth", "shot", None, None, None),
            P("depth", "shot", None, None, None),
            P("depth", "shot", None),
        ),
        check_vma=False,
    )
```

```python
import functools
import math

import jax
import jax.numpy as jnp
import numpy as np
from jax import lax
from jax.experimental import pallas as pl
from jax.experimental.pallas import tpu as pltpu
from jax.sharding import PartitionSpec as P

HOPS = 3
NCLASS = 16
NFREQ = 128
F32 = jnp.float32
BF16 = jnp.bfloat16
VMEM = pl.BlockSpec(memory_space=pltpu.VMEM)
HBM = pl.BlockSpec(memory_space=pltpu.HBM)
SMEM = pl.BlockSpec(memory_space=pltpu.SMEM)
PARAMS = pltpu.CompilerParams(vmem_limit_bytes=28 * 2**20)


def passed_along(block, axis, distance):
    devices = range(lax.axis_size(axis))
    route = [(i - distance, i) for i in devices if i - distance in devices]
    return lax.ppermute(block, axis, route)


def dft_tables(length):
    counter = jnp.arange(length, dtype=jnp.int32)
    product = counter[:, None] * counter[None, :] % length
    angles = 2.0 * math.pi / length * product.astype(jnp.float32)
    return (jnp.cos(angles).astype(jnp.bfloat16), jnp.sin(angles).astype(jnp.bfloat16))


def wavenumbers(length):
    counter = jnp.arange(length, dtype=jnp.int32)
    wrapped = jnp.where(counter >= length // 2, counter - length, counter)
    return 2.0 * math.pi / length * wrapped.astype(jnp.float32)


def propagate(planes, phase_re, phase_im, tables):
    fwd_left, fwd_right, inv_left, inv_right = tables
    first = jnp.einsum(
        "cdjk,...dkl->...cjl", fwd_left, planes, preferred_element_type=jnp.float32
    ).astype(jnp.bfloat16)
    second = jnp.einsum("...djl,dclm->...cjm", first, fwd_right, preferred_element_type=jnp.float32)
    real_part = second[..., 0, :, :]
    imag_part = second[..., 1, :, :]
    turned = jnp.stack(
        [real_part * phase_re - imag_part * phase_im, real_part * phase_im + imag_part * phase_re],
        axis=-3,
    ).astype(jnp.bfloat16)
    third = jnp.einsum(
        "cdjk,...dkl->...cjl", inv_left, turned, preferred_element_type=jnp.float32
    ).astype(jnp.bfloat16)
    return jnp.einsum(
        "...djl,dclm->...cjm", third, inv_right, preferred_element_type=jnp.float32
    ).astype(jnp.bfloat16)


def trade(down_edge, up_edge):
    got_down = passed_along(down_edge, "depth", 1)
    got_up = passed_along(up_edge, "depth", -1)
    return (got_down, got_up)


def per_device_plain(down_state, up_state, source, reflect, screen_class, screen_values, freq_index):
    levels = down_state.shape[0]
    rows_x = down_state.shape[3]
    rows_y = down_state.shape[4]
    front_count = down_state.shape[1]
    depth_rank = lax.axis_index("depth")
    scale = 1.0 / math.sqrt(front_count * lax.axis_size("shot"))
    cos_x, sin_x = dft_tables(rows_x)
    cos_y, sin_y = dft_tables(rows_y)
    tables = (
        jnp.stack([jnp.stack([cos_x, sin_x]), jnp.stack([-sin_x, cos_x])]),
        jnp.stack([jnp.stack([cos_y, -sin_y]), jnp.stack([sin_y, cos_y])]),
        jnp.stack([jnp.stack([cos_x, -sin_x]), jnp.stack([sin_x, cos_x])]),
        jnp.stack([jnp.stack([cos_y, sin_y]), jnp.stack([-sin_y, cos_y])]),
    )
    kwave = 0.95 * math.pi * (freq_index.astype(jnp.float32) + 1.0) / NFREQ
    kx_wave = wavenumbers(rows_x)
    ky_wave = wavenumbers(rows_y)
    vertical = kwave[:, None, None] ** 2 - kx_wave[None, :, None] ** 2 - ky_wave[None, None, :] ** 2
    propag = jnp.sqrt(jnp.maximum(vertical, 0.0))
    damping = jnp.exp(-jnp.sqrt(jnp.maximum(-vertical, 0.0))) / (rows_x * rows_y)
    phase_re = damping * jnp.cos(propag)
    phase_im = damping * jnp.sin(propag)
    classes = jnp.arange(NCLASS, dtype=jnp.int32)
    onehot = (screen_class[None] == classes[:, None, None, None]).astype(jnp.float32)
    slowness = jnp.einsum("c,clxy->lxy", screen_values, onehot, precision=lax.Precision.HIGHEST)
    angle = kwave[None, :, None, None] * slowness[:, None]
    screen_re = jnp.cos(angle)
    screen_im = jnp.sin(angle)
    refl = reflect[:, None]
    top_slab = depth_rank == 0
    down = down_state
    up = up_state
    a_re = a_im = b_re = b_im = None
    for repeat in range(HOPS):
        down_edge = down[levels - 1]
        up_edge = up[0]
        got_down, got_up = trade(down_edge, up_edge)
        got_down = jnp.where(top_slab, source, got_down)
        moved = propagate(
            jnp.concatenate([got_down[None], down[: levels - 1], up[1:], got_up[None]], axis=0),
            phase_re,
            phase_im,
            tables,
        )
        from_above = moved[:levels]
        from_below = moved[levels:]
        qa_re = from_above[:, :, 0].astype(jnp.float32)
        qa_im = from_above[:, :, 1].astype(jnp.float32)
        qb_re = from_below[:, :, 0].astype(jnp.float32)
        qb_im = from_below[:, :, 1].astype(jnp.float32)
        a_re = screen_re * qa_re - screen_im * qa_im
        a_im = screen_re * qa_im + screen_im * qa_re
        b_re = screen_re * qb_re - screen_im * qb_im
        b_im = screen_re * qb_im + screen_im * qb_re
        down = jnp.stack(
            [(1.0 + refl) * a_re - refl * b_re, (1.0 + refl) * a_im - refl * b_im], axis=2
        ).astype(jnp.bfloat16)
        up = jnp.stack(
            [(1.0 - refl) * b_re + refl * a_re, (1.0 - refl) * b_im + refl * a_im], axis=2
        ).astype(jnp.bfloat16)
    terms = scale * jnp.sum(a_re * b_re + a_im * b_im, axis=1)
    gradient = lax.psum_scatter(
        terms.astype(jnp.bfloat16), "shot", scatter_dimension=1, tiled=True
    ).astype(jnp.float32)
    return (down, up, gradient)


def hartley(length):
    counter = np.arange(length)
    angles = 2.0 * np.pi / length * (counter[:, None] * counter[None, :] % length)
    cosine = np.cos(angles).astype(BF16).astype(np.float32)
    sine = np.sin(angles).astype(BF16).astype(np.float32)
    return (cosine + sine).astype(BF16)


def odd_place():
    return lax.rem(lax.axis_index("depth"), 2)


def mm(left, right):
    return jnp.dot(left, right, preferred_element_type=F32)


def spread(jobs, work, hx, hy, phase):
    jobs = list(enumerate(jobs))
    for slot, (plane, _, _) in jobs:
        for part in range(2):
            work[slot, part] = mm(hx[...], plane(part) if callable(plane) else plane[part]).astype(BF16)
    for slot, (_, front, _) in jobs:
        turn_re, turn_im = phase[front, 0], phase[front, 1]
        part_re = mm(work[slot, 0], hy[...])
        part_im = mm(work[slot, 1], hy[...])
        work[slot, 0] = (part_re * turn_re - part_im * turn_im).astype(BF16)
        work[slot, 1] = (part_re * turn_im + part_im * turn_re).astype(BF16)
    for slot, _ in jobs:
        for part in range(2):
            work[slot, part] = mm(work[slot, part], hy[...]).astype(BF16)
    for slot, (_, _, target) in jobs:
        for part in range(2):
            if isinstance(target, list):
                rows = jnp.concatenate([hx[rows, :] for rows, _ in target], axis=0)
                ends = np.cumsum([piece.shape[1] for _, piece in target])
                done = mm(rows, work[slot, part]).astype(BF16)
                for (_, piece), end in zip(target, ends, strict=True):
                    piece[part] = done[end - piece.shape[1] : end]
            else:
                target[part] = mm(hx[...], work[slot, part]).astype(BF16)


def screened(real_part, imag_part, screen_re, screen_im):
    return (
        screen_re * real_part - screen_im * imag_part,
        screen_re * imag_part + screen_im * real_part,
    )


def mixed(a_re, a_im, b_re, b_im, refl, screen_re, screen_im, waves="both"):
    a_re, a_im, b_re, b_im = (part.astype(F32) for part in (a_re, a_im, b_re, b_im))
    step_re = refl * (a_re - b_re)
    step_im = refl * (a_im - b_im)
    fields = ()
    if waves != "outward":
        fields += screened(a_re + step_re, a_im + step_im, screen_re, screen_im)
    if waves != "inward":
        fields += screened(b_re + step_re, b_im + step_im, screen_re, screen_im)
    return fields


def put(target, real_part, imag_part):
    target[0] = real_part.astype(BF16)
    target[1] = imag_part.astype(BF16)


def half_rows(of, half):
    shot = lax.rem(lax.axis_index("shot"), 2)
    return pl.ds(pl.multiple_of((shot if of == 0 else 1 - shot) * half, half), half)


def late_pair():
    return lax.rem(lax.div(lax.axis_index("depth") + 1, 2), 2) == 1


def by_turn(early, late):
    is_late = late_pair()
    pl.when(jnp.logical_not(is_late))(early)
    pl.when(is_late)(late)


def edges_kernel(down, up, outward_outer, inward_inner, sems):
    levels = down.shape[0]
    odd = odd_place()

    def fetch(first, second):
        pltpu.make_async_copy(first, outward_outer, sems.at[0]).start()
        pltpu.make_async_copy(second, inward_inner, sems.at[1]).start()

    @pl.when(odd == 0)
    def _():
        fetch(up.at[0], down.at[levels - 1])

    @pl.when(odd == 1)
    def _():
        fetch(down.at[levels - 1], up.at[0])

    pltpu.make_async_copy(up.at[0], outward_outer, sems.at[0]).wait()
    pltpu.make_async_copy(up.at[0], inward_inner, sems.at[1]).wait()


def class_rows(slowness, kwave, shape):
    lanes = lax.broadcasted_iota(jnp.int32, shape, 1)
    table = jnp.zeros(shape, F32)
    for entry in range(NCLASS):
        table = jnp.where(lanes == entry, slowness[entry], table)
    angle = kwave * table
    return jnp.cos(angle), jnp.sin(angle)


def look_up(table, classes):
    width = 128
    rows = classes.shape[0]
    wide = jnp.broadcast_to(table[:1], (rows, width))
    pieces = [
        jnp.take_along_axis(wide, classes[:, start : start + width], axis=1, mode="promise_in_bounds")
        for start in range(0, classes.shape[1], width)
    ]
    return jnp.concatenate(pieces, axis=1)


def front_wave(freq, front):
    return 0.95 * math.pi * (freq[front].astype(F32) + 1.0) / NFREQ


def series(square, shift):
    total = jnp.full_like(square, 1.0 / math.factorial(18 + shift))
    for order in range(16, -1, -2):
        total = 1.0 / math.factorial(order + shift) - square * total
    return total


def setup_kernel(
    down, up, reflect, classes_in, slowness, freq, hx, hy,
    q_out_inner, q_in_outer, screen, phase, refl,
    fields, klass, work, sems,
):
    fronts = q_out_inner.shape[0]
    rows_x, rows_y = refl.shape[1:]
    odd = odd_place()
    fixed = [
        pltpu.make_async_copy(reflect.at[odd], refl.at[0], sems.at[2]),
        pltpu.make_async_copy(reflect.at[1 - odd], refl.at[1], sems.at[3]),
        pltpu.make_async_copy(classes_in.at[odd], klass.at[0], sems.at[4]),
        pltpu.make_async_copy(classes_in.at[1 - odd], klass.at[1], sems.at[5]),
    ]
    for copy in fixed:
        copy.start()

    @pl.when(odd == 0)
    def _():
        pltpu.make_async_copy(down.at[0], fields.at[0], sems.at[0]).start()
        pltpu.make_async_copy(up.at[1], fields.at[1], sems.at[1]).start()

    @pl.when(odd == 1)
    def _():
        pltpu.make_async_copy(up.at[1], fields.at[0], sems.at[0]).start()
        pltpu.make_async_copy(down.at[0], fields.at[1], sems.at[1]).start()

    def squares(length, axis):
        counter = lax.broadcasted_iota(jnp.int32, (rows_x, rows_y), axis)
        wrapped = jnp.where(counter >= length // 2, counter - length, counter)
        wave = 2.0 * math.pi / length * wrapped.astype(F32)
        return wave * wave

    lateral = squares(rows_x, 0) + squares(rows_y, 1)
    level_out = 1.0 / (rows_x * rows_y)
    for front in range(fronts):
        kwave = front_wave(freq, front)
        vertical = kwave * kwave - lateral
        travels = vertical > 0.0
        square = jnp.maximum(vertical, 0.0)
        root = jnp.sqrt(jnp.abs(vertical))
        phase[front, 0] = jnp.where(travels, series(square, 0), jnp.exp(-root)) * level_out
        phase[front, 1] = jnp.where(travels, root * series(square, 1), 0.0) * level_out
    for copy in fixed:
        copy.wait()
    sign = jnp.where(odd == 0, 1.0, -1.0).astype(F32)
    for level in range(2):
        refl[level] = sign * refl[level]
    for front in range(fronts):
        cos_row, sin_row = class_rows(slowness, front_wave(freq, front), (8, 128))
        for level in range(2):
            screen[level, front, 0] = look_up(cos_row, klass[level])
            screen[level, front, 1] = look_up(sin_row, klass[level])
    pltpu.make_async_copy(down.at[0], fields.at[0], sems.at[0]).wait()
    pltpu.make_async_copy(down.at[0], fields.at[1], sems.at[1]).wait()
    jobs = [(fields.at[1, front], front, q_out_inner.at[front]) for front in range(fronts)]
    jobs += [(fields.at[0, front], front, q_in_outer.at[front]) for front in range(fronts)]
    spread(jobs, work, hx, hy, phase)


def ahead_kernel(
    partner, q_in_outer, screen, refl, phase, hx, hy,
    inward_inner, q_out_inner,
    q_field, field, work,
):
    everyone = range(partner.shape[0])
    spread([(partner.at[front], front, q_field.at[front]) for front in everyone], work, hx, hy, phase)
    for front in everyone:
        in_re, in_im, out_re, out_im = mixed(
            q_in_outer[front, 0], q_in_outer[front, 1], q_field[front, 0], q_field[front, 1],
            refl[1], screen[1, front, 0], screen[1, front, 1],
        )
        put(inward_inner.at[front], in_re, in_im)
        put(field.at[front], out_re, out_im)
    spread([(field.at[front], front, q_out_inner.at[front]) for front in everyone], work, hx, hy, phase)


def entering(arrived, source, front):
    first = lax.axis_index("depth") == 0
    return lambda part: jnp.where(first, source[front, part], arrived[front, part])


def outer_step(q_arrived, q_out_inner, screen, refl, waves, field):
    for front in range(field.shape[0]):
        put(
            field.at[front],
            *mixed(
                q_arrived[front, 0], q_arrived[front, 1], q_out_inner[front, 0], q_out_inner[front, 1],
                refl[0], screen[0, front, 0], screen[0, front, 1], waves,
            ),
        )


def edge_kernel(arrived, source, q_out_inner, screen, refl, phase, hx, hy, sent, q_arrived, field, work):
    everyone = range(arrived.shape[0])

    def step(target):
        jobs = [(entering(arrived, source, front), front, q_arrived.at[front]) for front in everyone]
        spread(jobs, work, hx, hy, phase)
        outer_step(q_arrived, q_out_inner, screen, refl, "outward", target)

    def early():
        step(sent)

    def late():
        step(field)
        spread([(field.at[front], front, sent.at[front]) for front in everyone], work, hx, hy, phase)

    by_turn(early, late)


def last_edge_kernel(
    arrived, source, q_out_inner, screen, refl, phase, hx, hy, after,
    q_arrived, last_far, last_near,
    outward, work,
):
    del after
    everyone = range(arrived.shape[0])
    half = arrived.shape[2] // 2

    def step():
        outer_step(q_arrived, q_out_inner, screen, refl, "outward", outward)
        jobs = [
            (outward.at[front], front, [(half_rows(1, half), last_far.at[front]), (half_rows(0, half), last_near.at[front])])
            for front in everyone
        ]
        spread(jobs, work, hx, hy, phase)

    def early():
        jobs = [(entering(arrived, source, front), front, q_arrived.at[front]) for front in everyone]
        spread(jobs, work, hx, hy, phase)
        step()

    def late():
        q_arrived[...] = arrived[...]
        step()

    by_turn(early, late)


def inner_kernel(
    q_arrived, q_out_inner, partner, screen, refl, phase, hx, hy,
    inward, outward,
    field, q_inward, q_partner, work,
):
    everyone = range(partner.shape[0])
    outer_step(q_arrived, q_out_inner, screen, refl, "inward", field)
    jobs = [(partner.at[front], front, q_partner.at[front]) for front in everyone]
    jobs += [(field.at[front], front, q_inward.at[front]) for front in everyone]
    spread(jobs, work, hx, hy, phase)
    for front in everyone:
        in_re, in_im, out_re, out_im = mixed(
            q_inward[front, 0], q_inward[front, 1], q_partner[front, 0], q_partner[front, 1],
            refl[1], screen[1, front, 0], screen[1, front, 1],
        )
        put(inward.at[front], in_re, in_im)
        put(outward.at[front], out_re, out_im)


def spread_kernel(fields, phase, hx, hy, q_fields, work):
    @pl.when(late_pair())
    def _():
        everyone = range(fields.shape[0])
        spread([(fields.at[front], front, q_fields.at[front]) for front in everyone], work, hx, hy, phase)


def last_inner_step(
    extra, q_arrived, q_out_inner, partner, screen, refl, phase, hx, hy,
    inward, outward, terms, far_terms, field, q_inward, q_partner, work,
):
    everyone = range(partner.shape[0])
    outer_step(q_arrived, q_out_inner, screen, refl, "inward", field)
    jobs = [(partner.at[front], front, q_partner.at[front]) for front in everyone]
    jobs += [(field.at[front], front, q_inward.at[front]) for front in everyone]
    spread(jobs + extra, work, hx, hy, phase)
    total = None
    for front in everyone:
        a_re, a_im = (q_inward[front, part].astype(F32) for part in range(2))
        b_re, b_im = (q_partner[front, part].astype(F32) for part in range(2))
        in_re, in_im, out_re, out_im = mixed(
            a_re, a_im, b_re, b_im, refl[1], screen[1, front, 0], screen[1, front, 1]
        )
        put(inward.at[front], in_re, in_im)
        put(outward.at[front], out_re, out_im)
        term = a_re * b_re + a_im * b_im
        total = term if total is None else total + term
    terms[...] = total
    far_terms[...] = terms[half_rows(1, far_terms.shape[0]), :].astype(BF16)


def late_inner_kernel(
    q_arrived, q_out_inner, partner, screen, refl, phase, hx, hy, held_in,
    inward, outward, terms, far_terms, held_out,
    field, q_inward, q_partner, work,
):
    del held_in, held_out

    @pl.when(late_pair())
    def _():
        last_inner_step(
            [], q_arrived, q_out_inner, partner, screen, refl, phase, hx, hy,
            inward, outward, terms, far_terms, field, q_inward, q_partner, work,
        )


def early_inner_kernel(
    q_arrived, q_out_inner, partner, screen, refl, phase, hx, hy, out_inner, inward_in, outward_in, terms_in,
    far_terms_in, q_next_in,
    inward, outward, terms, far_terms, q_next,
    field, q_inward, q_partner, work,
):
    del inward_in, outward_in, terms_in, far_terms_in, q_next_in

    @pl.when(jnp.logical_not(late_pair()))
    def _():
        extra = [(out_inner.at[front], front, q_next.at[front]) for front in range(partner.shape[0])]
        last_inner_step(
            extra, q_arrived, q_out_inner, partner, screen, refl, phase, hx, hy,
            inward, outward, terms, far_terms, field, q_inward, q_partner, work,
        )


def incoming(last, q_arrived, front, rows):
    first = lax.axis_index("depth") == 0
    return [jnp.where(first, q_arrived[front, part, rows, :], last[front, part]).astype(F32) for part in range(2)]


def row_terms(of, last, q_arrived, q_out_inner):
    total = None
    rows = half_rows(of, last.shape[2])
    for front in range(last.shape[0]):
        a_re, a_im = incoming(last, q_arrived, front, rows)
        b_re, b_im = (q_out_inner[front, part, rows, :].astype(F32) for part in range(2))
        term = a_re * b_re + a_im * b_im
        total = term if total is None else total + term
    return total


def row_fields(of, last, q_arrived, q_out_inner, screen, refl, inward, outward):
    rows = half_rows(of, last.shape[2])
    for front in range(last.shape[0]):
        a_re, a_im = incoming(last, q_arrived, front, rows)
        b_re, b_im = (q_out_inner[front, part, rows, :].astype(F32) for part in range(2))
        in_re, in_im, out_re, out_im = mixed(
            a_re, a_im, b_re, b_im, refl[0, rows, :], screen[0, front, 0, rows, :], screen[0, front, 1, rows, :]
        )
        put(inward.at[front], in_re, in_im)
        put(outward.at[front], out_re, out_im)
    return rows


def far_terms_kernel(last, q_arrived, q_out_inner, after, terms):
    del after
    terms[...] = row_terms(1, last, q_arrived, q_out_inner).astype(BF16)


def send_home(level, rows, inward, outward, down_out, up_out, sems):
    odd = odd_place()

    def copies(place, inward_out, outward_out):
        return [
            pltpu.make_async_copy(inward, inward_out.at[place, :, :, rows, :], sems.at[0]),
            pltpu.make_async_copy(outward, outward_out.at[place, :, :, rows, :], sems.at[1]),
        ]

    @pl.when(odd == 0)
    def _():
        for copy in copies(level, down_out, up_out):
            copy.start()

    @pl.when(odd == 1)
    def _():
        for copy in copies(1 - level, up_out, down_out):
            copy.start()

    return copies(0, down_out, up_out)


def home_kernel(
    far, q_arrived, q_out_inner, screen, refl, inner_in, inner_out, down_out, up_out, far_in, far_out, sems
):
    waits = send_home(1, pl.ds(0, inner_in.shape[2]), inner_in, inner_out, down_out, up_out, sems.at[0])
    rows = row_fields(1, far, q_arrived, q_out_inner, screen, refl, far_in, far_out)
    waits += send_home(0, rows, far_in, far_out, down_out, up_out, sems.at[1])
    for copy in waits:
        copy.wait()


def near_kernel(
    scale, near, q_arrived, q_out_inner, screen, refl, inner_terms, inner_other, down_in, up_in,
    down_out, up_out, gradient, terms,
    near_in, near_out, inner_sum, sems,
):
    del down_in, up_in
    rows = row_fields(0, near, q_arrived, q_out_inner, screen, refl, near_in, near_out)
    waits = send_home(0, rows, near_in, near_out, down_out, up_out, sems.at[0])
    inner_sum[...] = scale * (inner_terms[rows, :] + inner_other[...].astype(F32))
    waits.append(pltpu.make_async_copy(inner_sum, gradient.at[1 - odd_place()], sems.at[1, 0]))
    waits[-1].start()
    terms[...] = row_terms(0, near, q_arrived, q_out_inner)
    for copy in waits:
        copy.wait()


def outer_gradient_kernel(scale, terms, other, gradient_in, gradient, outer_sum, sems):
    del gradient_in
    outer_sum[...] = scale * (terms[...] + other[...].astype(F32))
    done = pltpu.make_async_copy(outer_sum, gradient.at[odd_place()], sems.at[0])
    done.start()
    done.wait()


def per_device(down_state, up_state, source, reflect, screen_class, screen_values, freq_index):
    depth = lax.axis_size("depth")
    shots = lax.axis_size("shot")
    levels, fronts, parts, rows_x, rows_y = down_state.shape
    if levels != 2 or depth % 2 or shots % 2 or HOPS != 3:
        return per_device_plain(down_state, up_state, source, reflect, screen_class, screen_values, freq_index)
    scale = 1.0 / math.sqrt(fronts * shots)
    half = rows_x // 2
    hx = jnp.asarray(hartley(rows_x))
    hy = jnp.asarray(hartley(rows_y))
    partners = [(i, i ^ 1) for i in range(depth)]
    beyond = [(i, i + 1) for i in range(1, depth - 1, 2)] + [(i + 1, i) for i in range(1, depth - 1, 2)]
    to_partner = functools.partial(lax.ppermute, axis_name="depth", perm=partners)
    to_beyond = functools.partial(lax.ppermute, axis_name="depth", perm=beyond)
    across = functools.partial(lax.ppermute, axis_name="shot", perm=[(i, i ^ 1) for i in range(shots)])
    plane = jax.ShapeDtypeStruct((fronts, parts, rows_x, rows_y), BF16)
    half_plane = jax.ShapeDtypeStruct((fronts, parts, half, rows_y), BF16)
    pair = jax.ShapeDtypeStruct((2, rows_x, rows_y), F32)
    turns = jax.ShapeDtypeStruct((fronts, parts, rows_x, rows_y), F32)
    screens = jax.ShapeDtypeStruct((2, fronts, parts, rows_x, rows_y), F32)
    state = jax.ShapeDtypeStruct(down_state.shape, BF16)
    dma = pltpu.SemaphoreType.DMA

    def call(kernel, in_specs, out_specs, out_shape, scratch=(), **more):
        return pl.pallas_call(
            kernel,
            in_specs=in_specs,
            out_specs=out_specs,
            out_shape=out_shape,
            scratch_shapes=list(scratch),
            compiler_params=PARAMS,
            **more,
        )

    def kept_in_hbm(*arrays):
        return [pltpu.with_memory_space_constraint(array, pltpu.HBM) for array in arrays]

    def buffers(count, shape=plane):
        return [pltpu.VMEM(shape.shape, shape.dtype)] * count

    def work(slots):
        return pltpu.VMEM((slots, *plane.shape[1:]), BF16)

    out_outer, in_inner = call(edges_kernel, [HBM] * 2, [VMEM] * 2, [plane] * 2, [dma((2,))])(
        *kept_in_hbm(down_state, up_state)
    )
    arrived_0 = to_beyond(out_outer)
    partner_0 = to_partner(in_inner)
    q_out_inner_0, q_in_outer_0, screen, phase, refl = call(
        setup_kernel,
        [HBM] * 4 + [SMEM] * 2 + [VMEM] * 2,
        [VMEM] * 5,
        [plane] * 2 + [screens, turns, pair],
        [
            pltpu.VMEM((2, *plane.shape), BF16),
            pltpu.VMEM((2, rows_x, rows_y), jnp.int32),
            work(2 * fronts),
            dma((6,)),
        ],
    )(*kept_in_hbm(down_state, up_state, reflect, screen_class), screen_values, freq_index, hx, hy)
    fixed = (screen, refl, phase, hx, hy)
    in_inner_1, q_out_inner_1 = call(ahead_kernel, [VMEM] * 7, [VMEM] * 2, [plane] * 2, buffers(2) + [work(fronts)])(
        partner_0, q_in_outer_0, *fixed
    )
    partner_1 = to_partner(in_inner_1)
    out_outer_1, q_arrived = call(edge_kernel, [VMEM] * 8, [VMEM] * 2, [plane] * 2, buffers(1) + [work(fronts)])(
        arrived_0, source, q_out_inner_0, *fixed
    )
    arrived_1 = to_beyond(out_outer_1)
    in_inner_2, out_inner_2 = call(
        inner_kernel, [VMEM] * 8, [VMEM] * 2, [plane] * 2, buffers(3) + [work(2 * fronts)]
    )(q_arrived, q_out_inner_0, partner_1, *fixed)
    partner_2 = to_partner(in_inner_2)
    q_out_inner_2 = call(spread_kernel, [VMEM] * 4, VMEM, plane, [work(fronts)])(out_inner_2, phase, hx, hy)
    q_arrived_1, last_far, last_near = call(
        last_edge_kernel,
        [VMEM] * 8 + [pl.BlockSpec(memory_space=pl.ANY)],
        [VMEM] * 3,
        [plane] + [half_plane] * 2,
        buffers(1) + [work(fronts)],
    )(arrived_1, source, q_out_inner_1, *fixed, q_out_inner_2)
    last_far = to_beyond(last_far)
    half_sum = jax.ShapeDtypeStruct((half, rows_y), BF16)
    inner_parts = [plane] * 2 + [jax.ShapeDtypeStruct((rows_x, rows_y), F32), half_sum]
    *inner, last_near = call(
        late_inner_kernel,
        [VMEM] * 9,
        [VMEM] * 5,
        inner_parts + [half_plane],
        buffers(3) + [work(2 * fronts)],
        input_output_aliases={8: 4},
    )(q_arrived_1, q_out_inner_1, partner_2, *fixed, last_near)
    last_near = to_beyond(last_near)
    inner_in, inner_out, inner_terms, inner_far, q_out_inner_2 = call(
        early_inner_kernel,
        [VMEM] * 14,
        [VMEM] * 5,
        inner_parts + [plane],
        buffers(3) + [work(3 * fronts)],
        input_output_aliases={9 + index: index for index in range(5)},
    )(q_arrived_1, q_out_inner_1, partner_2, *fixed, out_inner_2, *inner, q_out_inner_2)
    inner_other = across(inner_far) if shots == 2 else jnp.zeros_like(inner_far)
    outer_far = call(far_terms_kernel, [VMEM] * 3 + [pl.BlockSpec(memory_space=pl.ANY)], VMEM, half_sum)(
        last_far, q_arrived, q_out_inner_2, inner_terms
    )
    outer_other = across(outer_far) if shots == 2 else jnp.zeros_like(outer_far)
    half_total = jax.ShapeDtypeStruct((half, rows_y), F32)
    share = jax.ShapeDtypeStruct((2, half, rows_y), F32)
    down, up = call(
        home_kernel, [VMEM] * 7, [HBM] * 2, [state] * 2, buffers(2, half_plane) + [dma((2, 2))]
    )(last_far, q_arrived, q_out_inner_2, screen, refl, inner_in, inner_out)
    down, up, gradient, outer_near = call(
        functools.partial(near_kernel, scale),
        [VMEM] * 7 + [HBM] * 2,
        [HBM] * 3 + [VMEM],
        [state, state, share, half_total],
        buffers(2, half_plane) + buffers(1, half_total) + [dma((2, 2))],
        input_output_aliases={7: 0, 8: 1},
    )(last_near, q_arrived, q_out_inner_2, screen, refl, inner_terms, inner_other, down, up)
    gradient = call(
        functools.partial(outer_gradient_kernel, scale),
        [VMEM] * 2 + [HBM],
        HBM,
        share,
        buffers(1, half_total) + [dma((1,))],
        input_output_aliases={2: 0},
    )(outer_near, outer_other, gradient)
    if shots != 2:
        terms = scale * jnp.stack([outer_far, inner_far]).astype(F32)
        far = jnp.where(odd_place() == 0, terms, terms[::-1])
        top = lax.rem(lax.axis_index("shot"), 2) == 0
        whole = jnp.concatenate([jnp.where(top, gradient, far), jnp.where(top, far, gradient)], axis=1)
        gradient = lax.psum_scatter(whole.astype(BF16), "shot", scatter_dimension=1, tiled=True).astype(F32)
    return (down, up, gradient)


def solution(mesh):
    return jax.shard_map(
        per_device,
        mesh=mesh,
        in_specs=(
            P("depth", "shot", None, None, None),
            P("depth", "shot", None, None, None),
            P("shot", None, None, None),
            P("depth", None, None),
            P("depth", None, None),
            P(),
            P("shot"),
        ),
        out_specs=(
            P("depth", "shot", None, None, None),
            P("depth", "shot", None, None, None),
            P("depth", "shot", None),
        ),
        check_vma=False,
    )
```

```python
import functools
import math

import jax
import jax.numpy as jnp
import numpy as np
from jax import lax
from jax.experimental import pallas as pl
from jax.experimental.pallas import tpu as pltpu
from jax.sharding import PartitionSpec as P

HOPS = 3
NCLASS = 16
NFREQ = 128
F32 = jnp.float32
BF16 = jnp.bfloat16
VMEM = pl.BlockSpec(memory_space=pltpu.VMEM)
HBM = pl.BlockSpec(memory_space=pltpu.HBM)
SMEM = pl.BlockSpec(memory_space=pltpu.SMEM)
PARAMS = pltpu.CompilerParams(vmem_limit_bytes=28 * 2**20)


def passed_along(block, axis, distance):
    devices = range(lax.axis_size(axis))
    route = [(i - distance, i) for i in devices if i - distance in devices]
    return lax.ppermute(block, axis, route)


def dft_tables(length):
    counter = jnp.arange(length, dtype=jnp.int32)
    product = counter[:, None] * counter[None, :] % length
    angles = 2.0 * math.pi / length * product.astype(jnp.float32)
    return (jnp.cos(angles).astype(jnp.bfloat16), jnp.sin(angles).astype(jnp.bfloat16))


def wavenumbers(length):
    counter = jnp.arange(length, dtype=jnp.int32)
    wrapped = jnp.where(counter >= length // 2, counter - length, counter)
    return 2.0 * math.pi / length * wrapped.astype(jnp.float32)


def propagate(planes, phase_re, phase_im, tables):
    fwd_left, fwd_right, inv_left, inv_right = tables
    first = jnp.einsum(
        "cdjk,...dkl->...cjl", fwd_left, planes, preferred_element_type=jnp.float32
    ).astype(jnp.bfloat16)
    second = jnp.einsum("...djl,dclm->...cjm", first, fwd_right, preferred_element_type=jnp.float32)
    real_part = second[..., 0, :, :]
    imag_part = second[..., 1, :, :]
    turned = jnp.stack(
        [real_part * phase_re - imag_part * phase_im, real_part * phase_im + imag_part * phase_re],
        axis=-3,
    ).astype(jnp.bfloat16)
    third = jnp.einsum(
        "cdjk,...dkl->...cjl", inv_left, turned, preferred_element_type=jnp.float32
    ).astype(jnp.bfloat16)
    return jnp.einsum(
        "...djl,dclm->...cjm", third, inv_right, preferred_element_type=jnp.float32
    ).astype(jnp.bfloat16)


def trade(down_edge, up_edge):
    got_down = passed_along(down_edge, "depth", 1)
    got_up = passed_along(up_edge, "depth", -1)
    return (got_down, got_up)


def per_device_plain(down_state, up_state, source, reflect, screen_class, screen_values, freq_index):
    levels = down_state.shape[0]
    rows_x = down_state.shape[3]
    rows_y = down_state.shape[4]
    front_count = down_state.shape[1]
    depth_rank = lax.axis_index("depth")
    scale = 1.0 / math.sqrt(front_count * lax.axis_size("shot"))
    cos_x, sin_x = dft_tables(rows_x)
    cos_y, sin_y = dft_tables(rows_y)
    tables = (
        jnp.stack([jnp.stack([cos_x, sin_x]), jnp.stack([-sin_x, cos_x])]),
        jnp.stack([jnp.stack([cos_y, -sin_y]), jnp.stack([sin_y, cos_y])]),
        jnp.stack([jnp.stack([cos_x, -sin_x]), jnp.stack([sin_x, cos_x])]),
        jnp.stack([jnp.stack([cos_y, sin_y]), jnp.stack([-sin_y, cos_y])]),
    )
    kwave = 0.95 * math.pi * (freq_index.astype(jnp.float32) + 1.0) / NFREQ
    kx_wave = wavenumbers(rows_x)
    ky_wave = wavenumbers(rows_y)
    vertical = kwave[:, None, None] ** 2 - kx_wave[None, :, None] ** 2 - ky_wave[None, None, :] ** 2
    propag = jnp.sqrt(jnp.maximum(vertical, 0.0))
    damping = jnp.exp(-jnp.sqrt(jnp.maximum(-vertical, 0.0))) / (rows_x * rows_y)
    phase_re = damping * jnp.cos(propag)
    phase_im = damping * jnp.sin(propag)
    classes = jnp.arange(NCLASS, dtype=jnp.int32)
    onehot = (screen_class[None] == classes[:, None, None, None]).astype(jnp.float32)
    slowness = jnp.einsum("c,clxy->lxy", screen_values, onehot, precision=lax.Precision.HIGHEST)
    angle = kwave[None, :, None, None] * slowness[:, None]
    screen_re = jnp.cos(angle)
    screen_im = jnp.sin(angle)
    refl = reflect[:, None]
    top_slab = depth_rank == 0
    down = down_state
    up = up_state
    a_re = a_im = b_re = b_im = None
    for repeat in range(HOPS):
        down_edge = down[levels - 1]
        up_edge = up[0]
        got_down, got_up = trade(down_edge, up_edge)
        got_down = jnp.where(top_slab, source, got_down)
        moved = propagate(
            jnp.concatenate([got_down[None], down[: levels - 1], up[1:], got_up[None]], axis=0),
            phase_re,
            phase_im,
            tables,
        )
        from_above = moved[:levels]
        from_below = moved[levels:]
        qa_re = from_above[:, :, 0].astype(jnp.float32)
        qa_im = from_above[:, :, 1].astype(jnp.float32)
        qb_re = from_below[:, :, 0].astype(jnp.float32)
        qb_im = from_below[:, :, 1].astype(jnp.float32)
        a_re = screen_re * qa_re - screen_im * qa_im
        a_im = screen_re * qa_im + screen_im * qa_re
        b_re = screen_re * qb_re - screen_im * qb_im
        b_im = screen_re * qb_im + screen_im * qb_re
        down = jnp.stack(
            [(1.0 + refl) * a_re - refl * b_re, (1.0 + refl) * a_im - refl * b_im], axis=2
        ).astype(jnp.bfloat16)
        up = jnp.stack(
            [(1.0 - refl) * b_re + refl * a_re, (1.0 - refl) * b_im + refl * a_im], axis=2
        ).astype(jnp.bfloat16)
    terms = scale * jnp.sum(a_re * b_re + a_im * b_im, axis=1)
    gradient = lax.psum_scatter(
        terms.astype(jnp.bfloat16), "shot", scatter_dimension=1, tiled=True
    ).astype(jnp.float32)
    return (down, up, gradient)


def hartley(length):
    counter = np.arange(length)
    angles = 2.0 * np.pi / length * (counter[:, None] * counter[None, :] % length)
    cosine = np.cos(angles).astype(BF16).astype(np.float32)
    sine = np.sin(angles).astype(BF16).astype(np.float32)
    return (cosine + sine).astype(BF16)


def odd_place():
    return lax.rem(lax.axis_index("depth"), 2)


def mm(left, right):
    return jnp.dot(left, right, preferred_element_type=F32)


def spread(jobs, work, hx, hy, phase):
    jobs = list(enumerate(jobs))
    for slot, (plane, _, _) in jobs:
        for part in range(2):
            work[slot, part] = mm(hx[...], plane(part) if callable(plane) else plane[part]).astype(BF16)
    for slot, (_, front, _) in jobs:
        turn_re, turn_im = phase[front, 0], phase[front, 1]
        part_re = mm(work[slot, 0], hy[...])
        part_im = mm(work[slot, 1], hy[...])
        work[slot, 0] = (part_re * turn_re - part_im * turn_im).astype(BF16)
        work[slot, 1] = (part_re * turn_im + part_im * turn_re).astype(BF16)
    for slot, _ in jobs:
        for part in range(2):
            work[slot, part] = mm(work[slot, part], hy[...]).astype(BF16)
    for slot, (_, _, target) in jobs:
        for part in range(2):
            if isinstance(target, list):
                rows = jnp.concatenate([hx[rows, :] for rows, _ in target], axis=0)
                ends = np.cumsum([piece.shape[1] for _, piece in target])
                done = mm(rows, work[slot, part]).astype(BF16)
                for (_, piece), end in zip(target, ends, strict=True):
                    piece[part] = done[end - piece.shape[1] : end]
            else:
                target[part] = mm(hx[...], work[slot, part]).astype(BF16)


def screened(real_part, imag_part, screen_re, screen_im):
    return (
        screen_re * real_part - screen_im * imag_part,
        screen_re * imag_part + screen_im * real_part,
    )


def mixed(a_re, a_im, b_re, b_im, refl, screen_re, screen_im, waves="both"):
    a_re, a_im, b_re, b_im = (part.astype(F32) for part in (a_re, a_im, b_re, b_im))
    step_re = refl * (a_re - b_re)
    step_im = refl * (a_im - b_im)
    fields = ()
    if waves != "outward":
        fields += screened(a_re + step_re, a_im + step_im, screen_re, screen_im)
    if waves != "inward":
        fields += screened(b_re + step_re, b_im + step_im, screen_re, screen_im)
    return fields


def put(target, real_part, imag_part):
    target[0] = real_part.astype(BF16)
    target[1] = imag_part.astype(BF16)


def half_rows(of, half):
    shot = lax.rem(lax.axis_index("shot"), 2)
    return pl.ds(pl.multiple_of((shot if of == 0 else 1 - shot) * half, half), half)


def late_pair():
    return lax.rem(lax.div(lax.axis_index("depth") + 1, 2), 2) == 1


def by_turn(early, late):
    is_late = late_pair()
    pl.when(jnp.logical_not(is_late))(early)
    pl.when(is_late)(late)


def edges_kernel(down, up, outward_outer, inward_inner, sems):
    levels = down.shape[0]
    odd = odd_place()

    def fetch(first, second):
        pltpu.make_async_copy(first, outward_outer, sems.at[0]).start()
        pltpu.make_async_copy(second, inward_inner, sems.at[1]).start()

    @pl.when(odd == 0)
    def _():
        fetch(up.at[0], down.at[levels - 1])

    @pl.when(odd == 1)
    def _():
        fetch(down.at[levels - 1], up.at[0])

    pltpu.make_async_copy(up.at[0], outward_outer, sems.at[0]).wait()
    pltpu.make_async_copy(up.at[0], inward_inner, sems.at[1]).wait()


def class_rows(slowness, kwave, shape):
    lanes = lax.broadcasted_iota(jnp.int32, shape, 1)
    table = jnp.zeros(shape, F32)
    for entry in range(NCLASS):
        table = jnp.where(lanes == entry, slowness[entry], table)
    angle = kwave * table
    return jnp.cos(angle), jnp.sin(angle)


def look_up(table, classes):
    width = 128
    rows = classes.shape[0]
    wide = jnp.broadcast_to(table[:1], (rows, width))
    pieces = [
        jnp.take_along_axis(wide, classes[:, start : start + width], axis=1, mode="promise_in_bounds")
        for start in range(0, classes.shape[1], width)
    ]
    return jnp.concatenate(pieces, axis=1)


def front_wave(freq, front):
    return 0.95 * math.pi * (freq[front].astype(F32) + 1.0) / NFREQ


def series(square, shift):
    total = jnp.full_like(square, 1.0 / math.factorial(18 + shift))
    for order in range(16, -1, -2):
        total = 1.0 / math.factorial(order + shift) - square * total
    return total


def setup_kernel(
    down, up, reflect, classes_in, slowness, freq, hx, hy,
    q_out_inner, q_in_outer, screen, phase, refl, back, base,
    fields, klass, work, sems,
):
    fronts = q_out_inner.shape[0]
    rows_x, rows_y = refl.shape[1:]
    odd = odd_place()
    fixed = [
        pltpu.make_async_copy(reflect.at[odd], refl.at[0], sems.at[2]),
        pltpu.make_async_copy(reflect.at[1 - odd], refl.at[1], sems.at[3]),
        pltpu.make_async_copy(classes_in.at[odd], klass.at[0], sems.at[4]),
        pltpu.make_async_copy(classes_in.at[1 - odd], klass.at[1], sems.at[5]),
    ]
    for copy in fixed:
        copy.start()

    @pl.when(odd == 0)
    def _():
        pltpu.make_async_copy(down.at[0], fields.at[0], sems.at[0]).start()
        pltpu.make_async_copy(up.at[1], fields.at[1], sems.at[1]).start()

    @pl.when(odd == 1)
    def _():
        pltpu.make_async_copy(up.at[1], fields.at[0], sems.at[0]).start()
        pltpu.make_async_copy(down.at[0], fields.at[1], sems.at[1]).start()

    def squares(length, axis):
        counter = lax.broadcasted_iota(jnp.int32, (rows_x, rows_y), axis)
        wrapped = jnp.where(counter >= length // 2, counter - length, counter)
        wave = 2.0 * math.pi / length * wrapped.astype(F32)
        return wave * wave

    lateral = squares(rows_x, 0) + squares(rows_y, 1)
    level_out = 1.0 / (rows_x * rows_y)
    for front in range(fronts):
        kwave = front_wave(freq, front)
        vertical = kwave * kwave - lateral
        travels = vertical > 0.0
        square = jnp.maximum(vertical, 0.0)
        root = jnp.sqrt(jnp.abs(vertical))
        phase[front, 0] = jnp.where(travels, series(square, 0), jnp.exp(-root)) * level_out
        phase[front, 1] = jnp.where(travels, root * series(square, 1), 0.0) * level_out
    for copy in fixed:
        copy.wait()
    sign = jnp.where(odd == 0, 1.0, -1.0).astype(F32)
    for level in range(2):
        refl[level] = sign * refl[level]
    for front in range(fronts):
        cos_row, sin_row = class_rows(slowness, front_wave(freq, front), (8, 128))
        for level in range(2):
            screen[level, front, 0] = look_up(cos_row, klass[level])
            screen[level, front, 1] = look_up(sin_row, klass[level])
    pltpu.make_async_copy(down.at[0], fields.at[0], sems.at[0]).wait()
    pltpu.make_async_copy(down.at[0], fields.at[1], sems.at[1]).wait()
    jobs = [(fields.at[1, front], front, q_out_inner.at[front]) for front in range(fronts)]
    jobs += [(fields.at[0, front], front, q_in_outer.at[front]) for front in range(fronts)]
    spread(jobs, work, hx, hy, phase)
    for front in range(fronts):
        for part in range(2):
            back[front, part] = refl[0] * screen[0, front, part]
    outward_base(q_out_inner, screen, refl, base)


def outward_base(q_out_inner, screen, refl, base):
    kept = 1.0 - refl[0]
    for front in range(base.shape[0]):
        b_re, b_im = (q_out_inner[front, part].astype(F32) for part in range(2))
        b_re, b_im = screened(b_re, b_im, screen[0, front, 0], screen[0, front, 1])
        base[front, 0] = kept * b_re
        base[front, 1] = kept * b_im


def outward_step(q_arrived, back, base, field):
    for front in range(field.shape[0]):
        a_re, a_im = (q_arrived[front, part].astype(F32) for part in range(2))
        back_re, back_im = back[front, 0], back[front, 1]
        put(
            field.at[front],
            base[front, 0] + (back_re * a_re - back_im * a_im),
            base[front, 1] + (back_re * a_im + back_im * a_re),
        )


def ahead_kernel(
    partner, q_in_outer, screen, refl, phase, hx, hy,
    inward_inner, q_out_inner, base,
    q_field, field, work,
):
    everyone = range(partner.shape[0])
    spread([(partner.at[front], front, q_field.at[front]) for front in everyone], work, hx, hy, phase)
    for front in everyone:
        in_re, in_im, out_re, out_im = mixed(
            q_in_outer[front, 0], q_in_outer[front, 1], q_field[front, 0], q_field[front, 1],
            refl[1], screen[1, front, 0], screen[1, front, 1],
        )
        put(inward_inner.at[front], in_re, in_im)
        put(field.at[front], out_re, out_im)
    spread([(field.at[front], front, q_out_inner.at[front]) for front in everyone], work, hx, hy, phase)
    outward_base(q_out_inner, screen, refl, base)


def entering(arrived, source, front):
    first = lax.axis_index("depth") == 0
    return lambda part: jnp.where(first, source[front, part], arrived[front, part])


def outer_step(q_arrived, q_out_inner, screen, refl, waves, field):
    for front in range(field.shape[0]):
        put(
            field.at[front],
            *mixed(
                q_arrived[front, 0], q_arrived[front, 1], q_out_inner[front, 0], q_out_inner[front, 1],
                refl[0], screen[0, front, 0], screen[0, front, 1], waves,
            ),
        )


def edge_kernel(arrived, source, back, base, phase, hx, hy, sent, q_arrived, field, work):
    everyone = range(arrived.shape[0])

    def step(target):
        jobs = [(entering(arrived, source, front), front, q_arrived.at[front]) for front in everyone]
        spread(jobs, work, hx, hy, phase)
        outward_step(q_arrived, back, base, target)

    def early():
        step(sent)

    def late():
        step(field)
        spread([(field.at[front], front, sent.at[front]) for front in everyone], work, hx, hy, phase)

    by_turn(early, late)


def last_edge_kernel(
    arrived, source, back, base, phase, hx, hy, after,
    q_arrived, last_far, last_near,
    outward, work,
):
    del after
    everyone = range(arrived.shape[0])
    half = arrived.shape[2] // 2

    def step(q_entered):
        outward_step(q_entered, back, base, outward)
        jobs = [
            (outward.at[front], front, [(half_rows(1, half), last_far.at[front]), (half_rows(0, half), last_near.at[front])])
            for front in everyone
        ]
        spread(jobs, work, hx, hy, phase)

    def early():
        jobs = [(entering(arrived, source, front), front, q_arrived.at[front]) for front in everyone]
        spread(jobs, work, hx, hy, phase)
        step(q_arrived)

    def late():
        step(arrived)

    by_turn(early, late)


def inner_kernel(
    q_arrived, q_out_inner, partner, screen, refl, phase, hx, hy,
    inward, outward,
    field, q_inward, q_partner, work,
):
    everyone = range(partner.shape[0])
    outer_step(q_arrived, q_out_inner, screen, refl, "inward", field)
    jobs = [(partner.at[front], front, q_partner.at[front]) for front in everyone]
    jobs += [(field.at[front], front, q_inward.at[front]) for front in everyone]
    spread(jobs, work, hx, hy, phase)
    for front in everyone:
        in_re, in_im, out_re, out_im = mixed(
            q_inward[front, 0], q_inward[front, 1], q_partner[front, 0], q_partner[front, 1],
            refl[1], screen[1, front, 0], screen[1, front, 1],
        )
        put(inward.at[front], in_re, in_im)
        put(outward.at[front], out_re, out_im)


def spread_kernel(fields, phase, hx, hy, q_fields, work):
    @pl.when(late_pair())
    def _():
        everyone = range(fields.shape[0])
        spread([(fields.at[front], front, q_fields.at[front]) for front in everyone], work, hx, hy, phase)


def last_inner_kernel(
    q_arrived, arrived, q_out_inner, partner, screen, refl, phase, hx, hy, out_inner, q_next_in,
    inward, outward, terms, far_terms, q_next,
    field, q_inward, q_partner, work,
):
    del q_next_in
    everyone = range(partner.shape[0])

    def early():
        outer_step(q_arrived, q_out_inner, screen, refl, "inward", field)
        spread([(out_inner.at[front], front, q_next.at[front]) for front in everyone], work, hx, hy, phase)

    def late():
        outer_step(arrived, q_out_inner, screen, refl, "inward", field)

    by_turn(early, late)
    jobs = [(partner.at[front], front, q_partner.at[front]) for front in everyone]
    jobs += [(field.at[front], front, q_inward.at[front]) for front in everyone]
    spread(jobs, work, hx, hy, phase)
    total = None
    for front in everyone:
        a_re, a_im = (q_inward[front, part].astype(F32) for part in range(2))
        b_re, b_im = (q_partner[front, part].astype(F32) for part in range(2))
        in_re, in_im, out_re, out_im = mixed(
            a_re, a_im, b_re, b_im, refl[1], screen[1, front, 0], screen[1, front, 1]
        )
        put(inward.at[front], in_re, in_im)
        put(outward.at[front], out_re, out_im)
        term = a_re * b_re + a_im * b_im
        total = term if total is None else total + term
    terms[...] = total
    far_terms[...] = terms[half_rows(1, far_terms.shape[0]), :].astype(BF16)


def incoming(last, q_arrived, front, rows):
    first = lax.axis_index("depth") == 0
    return [jnp.where(first, q_arrived[front, part, rows, :], last[front, part]).astype(F32) for part in range(2)]


def row_terms(of, last, q_arrived, q_out_inner):
    total = None
    rows = half_rows(of, last.shape[2])
    for front in range(last.shape[0]):
        a_re, a_im = incoming(last, q_arrived, front, rows)
        b_re, b_im = (q_out_inner[front, part, rows, :].astype(F32) for part in range(2))
        term = a_re * b_re + a_im * b_im
        total = term if total is None else total + term
    return total


def row_fields(of, last, q_arrived, q_out_inner, screen, refl, inward, outward):
    rows = half_rows(of, last.shape[2])
    for front in range(last.shape[0]):
        a_re, a_im = incoming(last, q_arrived, front, rows)
        b_re, b_im = (q_out_inner[front, part, rows, :].astype(F32) for part in range(2))
        in_re, in_im, out_re, out_im = mixed(
            a_re, a_im, b_re, b_im, refl[0, rows, :], screen[0, front, 0, rows, :], screen[0, front, 1, rows, :]
        )
        put(inward.at[front], in_re, in_im)
        put(outward.at[front], out_re, out_im)
    return rows


def far_terms_kernel(last, q_arrived, q_out_inner, after, terms):
    del after
    terms[...] = row_terms(1, last, q_arrived, q_out_inner).astype(BF16)


def send_home(level, rows, inward, outward, down_out, up_out, sems):
    odd = odd_place()

    def copies(place, inward_out, outward_out):
        return [
            pltpu.make_async_copy(inward, inward_out.at[place, :, :, rows, :], sems.at[0]),
            pltpu.make_async_copy(outward, outward_out.at[place, :, :, rows, :], sems.at[1]),
        ]

    @pl.when(odd == 0)
    def _():
        for copy in copies(level, down_out, up_out):
            copy.start()

    @pl.when(odd == 1)
    def _():
        for copy in copies(1 - level, up_out, down_out):
            copy.start()

    return copies(0, down_out, up_out)


def home_kernel(
    far, q_arrived, q_out_inner, screen, refl, inner_in, inner_out, down_out, up_out, far_in, far_out, sems
):
    waits = send_home(1, pl.ds(0, inner_in.shape[2]), inner_in, inner_out, down_out, up_out, sems.at[0])
    rows = row_fields(1, far, q_arrived, q_out_inner, screen, refl, far_in, far_out)
    waits += send_home(0, rows, far_in, far_out, down_out, up_out, sems.at[1])
    for copy in waits:
        copy.wait()


def near_kernel(
    scale, near, q_arrived, q_out_inner, screen, refl, inner_terms, inner_other, down_in, up_in,
    down_out, up_out, gradient, terms,
    near_in, near_out, inner_sum, sems,
):
    del down_in, up_in
    rows = row_fields(0, near, q_arrived, q_out_inner, screen, refl, near_in, near_out)
    waits = send_home(0, rows, near_in, near_out, down_out, up_out, sems.at[0])
    inner_sum[...] = scale * (inner_terms[rows, :] + inner_other[...].astype(F32))
    waits.append(pltpu.make_async_copy(inner_sum, gradient.at[1 - odd_place()], sems.at[1, 0]))
    waits[-1].start()
    terms[...] = row_terms(0, near, q_arrived, q_out_inner)
    for copy in waits:
        copy.wait()


def outer_gradient_kernel(scale, terms, other, gradient_in, gradient, outer_sum, sems):
    del gradient_in
    outer_sum[...] = scale * (terms[...] + other[...].astype(F32))
    done = pltpu.make_async_copy(outer_sum, gradient.at[odd_place()], sems.at[0])
    done.start()
    done.wait()


def per_device(down_state, up_state, source, reflect, screen_class, screen_values, freq_index):
    depth = lax.axis_size("depth")
    shots = lax.axis_size("shot")
    levels, fronts, parts, rows_x, rows_y = down_state.shape
    if levels != 2 or depth % 2 or shots % 2 or HOPS != 3:
        return per_device_plain(down_state, up_state, source, reflect, screen_class, screen_values, freq_index)
    scale = 1.0 / math.sqrt(fronts * shots)
    half = rows_x // 2
    hx = jnp.asarray(hartley(rows_x))
    hy = jnp.asarray(hartley(rows_y))
    partners = [(i, i ^ 1) for i in range(depth)]
    beyond = [(i, i + 1) for i in range(1, depth - 1, 2)] + [(i + 1, i) for i in range(1, depth - 1, 2)]
    to_partner = functools.partial(lax.ppermute, axis_name="depth", perm=partners)
    to_beyond = functools.partial(lax.ppermute, axis_name="depth", perm=beyond)
    across = functools.partial(lax.ppermute, axis_name="shot", perm=[(i, i ^ 1) for i in range(shots)])
    plane = jax.ShapeDtypeStruct((fronts, parts, rows_x, rows_y), BF16)
    half_plane = jax.ShapeDtypeStruct((fronts, parts, half, rows_y), BF16)
    pair = jax.ShapeDtypeStruct((2, rows_x, rows_y), F32)
    turns = jax.ShapeDtypeStruct((fronts, parts, rows_x, rows_y), F32)
    screens = jax.ShapeDtypeStruct((2, fronts, parts, rows_x, rows_y), F32)
    state = jax.ShapeDtypeStruct(down_state.shape, BF16)
    dma = pltpu.SemaphoreType.DMA

    def call(kernel, in_specs, out_specs, out_shape, scratch=(), **more):
        return pl.pallas_call(
            kernel,
            in_specs=in_specs,
            out_specs=out_specs,
            out_shape=out_shape,
            scratch_shapes=list(scratch),
            compiler_params=PARAMS,
            **more,
        )

    def kept_in_hbm(*arrays):
        return [pltpu.with_memory_space_constraint(array, pltpu.HBM) for array in arrays]

    def buffers(count, shape=plane):
        return [pltpu.VMEM(shape.shape, shape.dtype)] * count

    def work(slots):
        return pltpu.VMEM((slots, *plane.shape[1:]), BF16)

    out_outer, in_inner = call(edges_kernel, [HBM] * 2, [VMEM] * 2, [plane] * 2, [dma((2,))])(
        *kept_in_hbm(down_state, up_state)
    )
    arrived_0 = to_beyond(out_outer)
    partner_0 = to_partner(in_inner)
    q_out_inner_0, q_in_outer_0, screen, phase, refl, back, base_0 = call(
        setup_kernel,
        [HBM] * 4 + [SMEM] * 2 + [VMEM] * 2,
        [VMEM] * 7,
        [plane] * 2 + [screens, turns, pair, turns, turns],
        [
            pltpu.VMEM((2, *plane.shape), BF16),
            pltpu.VMEM((2, rows_x, rows_y), jnp.int32),
            work(2 * fronts),
            dma((6,)),
        ],
    )(*kept_in_hbm(down_state, up_state, reflect, screen_class), screen_values, freq_index, hx, hy)
    fixed = (screen, refl, phase, hx, hy)
    in_inner_1, q_out_inner_1, base_1 = call(
        ahead_kernel, [VMEM] * 7, [VMEM] * 3, [plane] * 2 + [turns], buffers(2) + [work(fronts)]
    )(
        partner_0, q_in_outer_0, *fixed
    )
    partner_1 = to_partner(in_inner_1)
    out_outer_1, q_arrived = call(edge_kernel, [VMEM] * 7, [VMEM] * 2, [plane] * 2, buffers(1) + [work(fronts)])(
        arrived_0, source, back, base_0, phase, hx, hy
    )
    arrived_1 = to_beyond(out_outer_1)
    in_inner_2, out_inner_2 = call(
        inner_kernel, [VMEM] * 8, [VMEM] * 2, [plane] * 2, buffers(3) + [work(2 * fronts)]
    )(q_arrived, q_out_inner_0, partner_1, *fixed)
    partner_2 = to_partner(in_inner_2)
    q_out_inner_2 = call(spread_kernel, [VMEM] * 4, VMEM, plane, [work(fronts)])(out_inner_2, phase, hx, hy)
    q_arrived_1, last_far, last_near = call(
        last_edge_kernel,
        [VMEM] * 7 + [pl.BlockSpec(memory_space=pl.ANY)],
        [VMEM] * 3,
        [plane] + [half_plane] * 2,
        buffers(1) + [work(fronts)],
    )(arrived_1, source, back, base_1, phase, hx, hy, q_out_inner_2)
    last_far = to_beyond(last_far)
    last_near = to_beyond(last_near)
    half_sum = jax.ShapeDtypeStruct((half, rows_y), BF16)
    inner_in, inner_out, inner_terms, inner_far, q_out_inner_2 = call(
        last_inner_kernel,
        [VMEM] * 11,
        [VMEM] * 5,
        [plane] * 2 + [jax.ShapeDtypeStruct((rows_x, rows_y), F32), half_sum, plane],
        buffers(3) + [work(2 * fronts)],
        input_output_aliases={10: 4},
    )(q_arrived_1, arrived_1, q_out_inner_1, partner_2, *fixed, out_inner_2, q_out_inner_2)
    inner_other = across(inner_far) if shots == 2 else jnp.zeros_like(inner_far)
    outer_far = call(far_terms_kernel, [VMEM] * 3 + [pl.BlockSpec(memory_space=pl.ANY)], VMEM, half_sum)(
        last_far, q_arrived, q_out_inner_2, inner_terms
    )
    outer_other = across(outer_far) if shots == 2 else jnp.zeros_like(outer_far)
    half_total = jax.ShapeDtypeStruct((half, rows_y), F32)
    share = jax.ShapeDtypeStruct((2, half, rows_y), F32)
    down, up = call(
        home_kernel, [VMEM] * 7, [HBM] * 2, [state] * 2, buffers(2, half_plane) + [dma((2, 2))]
    )(last_far, q_arrived, q_out_inner_2, screen, refl, inner_in, inner_out)
    down, up, gradient, outer_near = call(
        functools.partial(near_kernel, scale),
        [VMEM] * 7 + [HBM] * 2,
        [HBM] * 3 + [VMEM],
        [state, state, share, half_total],
        buffers(2, half_plane) + buffers(1, half_total) + [dma((2, 2))],
        input_output_aliases={7: 0, 8: 1},
    )(last_near, q_arrived, q_out_inner_2, screen, refl, inner_terms, inner_other, down, up)
    gradient = call(
        functools.partial(outer_gradient_kernel, scale),
        [VMEM] * 2 + [HBM],
        HBM,
        share,
        buffers(1, half_total) + [dma((1,))],
        input_output_aliases={2: 0},
    )(outer_near, outer_other, gradient)
    if shots != 2:
        terms = scale * jnp.stack([outer_far, inner_far]).astype(F32)
        far = jnp.where(odd_place() == 0, terms, terms[::-1])
        top = lax.rem(lax.axis_index("shot"), 2) == 0
        whole = jnp.concatenate([jnp.where(top, gradient, far), jnp.where(top, far, gradient)], axis=1)
        gradient = lax.psum_scatter(whole.astype(BF16), "shot", scatter_dimension=1, tiled=True).astype(F32)
    return (down, up, gradient)


def solution(mesh):
    return jax.shard_map(
        per_device,
        mesh=mesh,
        in_specs=(
            P("depth", "shot", None, None, None),
            P("depth", "shot", None, None, None),
            P("shot", None, None, None),
            P("depth", None, None),
            P("depth", None, None),
            P(),
            P("shot"),
        ),
        out_specs=(
            P("depth", "shot", None, None, None),
            P("depth", "shot", None, None, None),
            P("depth", "shot", None),
        ),
        check_vma=False,
    )
```

```python
import functools
import math

import jax
import jax.numpy as jnp
import numpy as np
from jax import lax
from jax.experimental import pallas as pl
from jax.experimental.pallas import tpu as pltpu
from jax.sharding import PartitionSpec as P

HOPS = 3
NCLASS = 16
NFREQ = 128
F32 = jnp.float32
BF16 = jnp.bfloat16
VMEM = pl.BlockSpec(memory_space=pltpu.VMEM)
HBM = pl.BlockSpec(memory_space=pltpu.HBM)
SMEM = pl.BlockSpec(memory_space=pltpu.SMEM)
PARAMS = pltpu.CompilerParams(vmem_limit_bytes=28 * 2**20)


def passed_along(block, axis, distance):
    devices = range(lax.axis_size(axis))
    route = [(i - distance, i) for i in devices if i - distance in devices]
    return lax.ppermute(block, axis, route)


def dft_tables(length):
    counter = jnp.arange(length, dtype=jnp.int32)
    product = counter[:, None] * counter[None, :] % length
    angles = 2.0 * math.pi / length * product.astype(jnp.float32)
    return (jnp.cos(angles).astype(jnp.bfloat16), jnp.sin(angles).astype(jnp.bfloat16))


def wavenumbers(length):
    counter = jnp.arange(length, dtype=jnp.int32)
    wrapped = jnp.where(counter >= length // 2, counter - length, counter)
    return 2.0 * math.pi / length * wrapped.astype(jnp.float32)


def propagate(planes, phase_re, phase_im, tables):
    fwd_left, fwd_right, inv_left, inv_right = tables
    first = jnp.einsum(
        "cdjk,...dkl->...cjl", fwd_left, planes, preferred_element_type=jnp.float32
    ).astype(jnp.bfloat16)
    second = jnp.einsum("...djl,dclm->...cjm", first, fwd_right, preferred_element_type=jnp.float32)
    real_part = second[..., 0, :, :]
    imag_part = second[..., 1, :, :]
    turned = jnp.stack(
        [real_part * phase_re - imag_part * phase_im, real_part * phase_im + imag_part * phase_re],
        axis=-3,
    ).astype(jnp.bfloat16)
    third = jnp.einsum(
        "cdjk,...dkl->...cjl", inv_left, turned, preferred_element_type=jnp.float32
    ).astype(jnp.bfloat16)
    return jnp.einsum(
        "...djl,dclm->...cjm", third, inv_right, preferred_element_type=jnp.float32
    ).astype(jnp.bfloat16)


def trade(down_edge, up_edge):
    got_down = passed_along(down_edge, "depth", 1)
    got_up = passed_along(up_edge, "depth", -1)
    return (got_down, got_up)


def per_device_plain(down_state, up_state, source, reflect, screen_class, screen_values, freq_index):
    levels = down_state.shape[0]
    rows_x = down_state.shape[3]
    rows_y = down_state.shape[4]
    front_count = down_state.shape[1]
    depth_rank = lax.axis_index("depth")
    scale = 1.0 / math.sqrt(front_count * lax.axis_size("shot"))
    cos_x, sin_x = dft_tables(rows_x)
    cos_y, sin_y = dft_tables(rows_y)
    tables = (
        jnp.stack([jnp.stack([cos_x, sin_x]), jnp.stack([-sin_x, cos_x])]),
        jnp.stack([jnp.stack([cos_y, -sin_y]), jnp.stack([sin_y, cos_y])]),
        jnp.stack([jnp.stack([cos_x, -sin_x]), jnp.stack([sin_x, cos_x])]),
        jnp.stack([jnp.stack([cos_y, sin_y]), jnp.stack([-sin_y, cos_y])]),
    )
    kwave = 0.95 * math.pi * (freq_index.astype(jnp.float32) + 1.0) / NFREQ
    kx_wave = wavenumbers(rows_x)
    ky_wave = wavenumbers(rows_y)
    vertical = kwave[:, None, None] ** 2 - kx_wave[None, :, None] ** 2 - ky_wave[None, None, :] ** 2
    propag = jnp.sqrt(jnp.maximum(vertical, 0.0))
    damping = jnp.exp(-jnp.sqrt(jnp.maximum(-vertical, 0.0))) / (rows_x * rows_y)
    phase_re = damping * jnp.cos(propag)
    phase_im = damping * jnp.sin(propag)
    classes = jnp.arange(NCLASS, dtype=jnp.int32)
    onehot = (screen_class[None] == classes[:, None, None, None]).astype(jnp.float32)
    slowness = jnp.einsum("c,clxy->lxy", screen_values, onehot, precision=lax.Precision.HIGHEST)
    angle = kwave[None, :, None, None] * slowness[:, None]
    screen_re = jnp.cos(angle)
    screen_im = jnp.sin(angle)
    refl = reflect[:, None]
    top_slab = depth_rank == 0
    down = down_state
    up = up_state
    a_re = a_im = b_re = b_im = None
    for repeat in range(HOPS):
        down_edge = down[levels - 1]
        up_edge = up[0]
        got_down, got_up = trade(down_edge, up_edge)
        got_down = jnp.where(top_slab, source, got_down)
        moved = propagate(
            jnp.concatenate([got_down[None], down[: levels - 1], up[1:], got_up[None]], axis=0),
            phase_re,
            phase_im,
            tables,
        )
        from_above = moved[:levels]
        from_below = moved[levels:]
        qa_re = from_above[:, :, 0].astype(jnp.float32)
        qa_im = from_above[:, :, 1].astype(jnp.float32)
        qb_re = from_below[:, :, 0].astype(jnp.float32)
        qb_im = from_below[:, :, 1].astype(jnp.float32)
        a_re = screen_re * qa_re - screen_im * qa_im
        a_im = screen_re * qa_im + screen_im * qa_re
        b_re = screen_re * qb_re - screen_im * qb_im
        b_im = screen_re * qb_im + screen_im * qb_re
        down = jnp.stack(
            [(1.0 + refl) * a_re - refl * b_re, (1.0 + refl) * a_im - refl * b_im], axis=2
        ).astype(jnp.bfloat16)
        up = jnp.stack(
            [(1.0 - refl) * b_re + refl * a_re, (1.0 - refl) * b_im + refl * a_im], axis=2
        ).astype(jnp.bfloat16)
    terms = scale * jnp.sum(a_re * b_re + a_im * b_im, axis=1)
    gradient = lax.psum_scatter(
        terms.astype(jnp.bfloat16), "shot", scatter_dimension=1, tiled=True
    ).astype(jnp.float32)
    return (down, up, gradient)


def hartley(length):
    counter = np.arange(length)
    angles = 2.0 * np.pi / length * (counter[:, None] * counter[None, :] % length)
    cosine = np.cos(angles).astype(BF16).astype(np.float32)
    sine = np.sin(angles).astype(BF16).astype(np.float32)
    return (cosine + sine).astype(BF16)


def odd_place():
    return lax.rem(lax.axis_index("depth"), 2)


def mm(left, right):
    return jnp.dot(left, right, preferred_element_type=F32)


def spread(jobs, work, hx, hy, phase):
    jobs = list(enumerate(jobs))
    for slot, (plane, _, _) in jobs:
        for part in range(2):
            work[slot, part] = mm(hx[...], plane(part) if callable(plane) else plane[part]).astype(BF16)
    for slot, (_, front, _) in jobs:
        turn_re, turn_im = phase[front, 0], phase[front, 1]
        part_re = mm(work[slot, 0], hy[...])
        part_im = mm(work[slot, 1], hy[...])
        work[slot, 0] = (part_re * turn_re - part_im * turn_im).astype(BF16)
        work[slot, 1] = (part_re * turn_im + part_im * turn_re).astype(BF16)
    for slot, _ in jobs:
        for part in range(2):
            work[slot, part] = mm(work[slot, part], hy[...]).astype(BF16)
    for slot, (_, _, target) in jobs:
        for part in range(2):
            if isinstance(target, list):
                rows = jnp.concatenate([hx[rows, :] for rows, _ in target], axis=0)
                ends = np.cumsum([piece.shape[1] for _, piece in target])
                done = mm(rows, work[slot, part]).astype(BF16)
                for (_, piece), end in zip(target, ends, strict=True):
                    piece[part] = done[end - piece.shape[1] : end]
            else:
                target[part] = mm(hx[...], work[slot, part]).astype(BF16)


def screened(real_part, imag_part, screen_re, screen_im):
    return (
        screen_re * real_part - screen_im * imag_part,
        screen_re * imag_part + screen_im * real_part,
    )


def mixed(a_re, a_im, b_re, b_im, refl, screen_re, screen_im, waves="both"):
    a_re, a_im, b_re, b_im = (part.astype(F32) for part in (a_re, a_im, b_re, b_im))
    step_re = refl * (a_re - b_re)
    step_im = refl * (a_im - b_im)
    fields = ()
    if waves != "outward":
        fields += screened(a_re + step_re, a_im + step_im, screen_re, screen_im)
    if waves != "inward":
        fields += screened(b_re + step_re, b_im + step_im, screen_re, screen_im)
    return fields


def put(target, real_part, imag_part):
    target[0] = real_part.astype(BF16)
    target[1] = imag_part.astype(BF16)


def half_rows(of, half):
    shot = lax.rem(lax.axis_index("shot"), 2)
    return pl.ds(pl.multiple_of((shot if of == 0 else 1 - shot) * half, half), half)


def late_pair():
    return lax.rem(lax.div(lax.axis_index("depth") + 1, 2), 2) == 1


def by_turn(early, late):
    is_late = late_pair()
    pl.when(jnp.logical_not(is_late))(early)
    pl.when(is_late)(late)


def edges_kernel(down, up, outward_outer, inward_inner, sems):
    levels = down.shape[0]
    odd = odd_place()

    def fetch(first, second):
        pltpu.make_async_copy(first, outward_outer, sems.at[0]).start()
        pltpu.make_async_copy(second, inward_inner, sems.at[1]).start()

    @pl.when(odd == 0)
    def _():
        fetch(up.at[0], down.at[levels - 1])

    @pl.when(odd == 1)
    def _():
        fetch(down.at[levels - 1], up.at[0])

    pltpu.make_async_copy(up.at[0], outward_outer, sems.at[0]).wait()
    pltpu.make_async_copy(up.at[0], inward_inner, sems.at[1]).wait()


def class_rows(slowness, kwave, shape):
    lanes = lax.broadcasted_iota(jnp.int32, shape, 1)
    table = jnp.zeros(shape, F32)
    for entry in range(NCLASS):
        table = jnp.where(lanes == entry, slowness[entry], table)
    angle = kwave * table
    return jnp.cos(angle), jnp.sin(angle)


def look_up(table, classes):
    width = 128
    rows = classes.shape[0]
    wide = jnp.broadcast_to(table[:1], (rows, width))
    pieces = [
        jnp.take_along_axis(wide, classes[:, start : start + width], axis=1, mode="promise_in_bounds")
        for start in range(0, classes.shape[1], width)
    ]
    return jnp.concatenate(pieces, axis=1)


def front_wave(freq, front):
    return 0.95 * math.pi * (freq[front].astype(F32) + 1.0) / NFREQ


def series(square, shift):
    total = jnp.full_like(square, 1.0 / math.factorial(18 + shift))
    for order in range(16, -1, -2):
        total = 1.0 / math.factorial(order + shift) - square * total
    return total


def setup_kernel(
    down, up, reflect, classes_in, slowness, freq, hx, hy,
    q_out_inner, q_in_outer, screen, phase, refl, back, base,
    fields, klass, work, sems,
):
    fronts = q_out_inner.shape[0]
    rows_x, rows_y = refl.shape[1:]
    odd = odd_place()
    fixed = [
        pltpu.make_async_copy(reflect.at[odd], refl.at[0], sems.at[2]),
        pltpu.make_async_copy(reflect.at[1 - odd], refl.at[1], sems.at[3]),
        pltpu.make_async_copy(classes_in.at[odd], klass.at[0], sems.at[4]),
        pltpu.make_async_copy(classes_in.at[1 - odd], klass.at[1], sems.at[5]),
    ]
    for copy in fixed:
        copy.start()

    @pl.when(odd == 0)
    def _():
        pltpu.make_async_copy(down.at[0], fields.at[0], sems.at[0]).start()
        pltpu.make_async_copy(up.at[1], fields.at[1], sems.at[1]).start()

    @pl.when(odd == 1)
    def _():
        pltpu.make_async_copy(up.at[1], fields.at[0], sems.at[0]).start()
        pltpu.make_async_copy(down.at[0], fields.at[1], sems.at[1]).start()

    def squares(length, axis):
        counter = lax.broadcasted_iota(jnp.int32, (rows_x, rows_y), axis)
        wrapped = jnp.where(counter >= length // 2, counter - length, counter)
        wave = 2.0 * math.pi / length * wrapped.astype(F32)
        return wave * wave

    lateral = squares(rows_x, 0) + squares(rows_y, 1)
    level_out = 1.0 / (rows_x * rows_y)
    for front in range(fronts):
        kwave = front_wave(freq, front)
        vertical = kwave * kwave - lateral
        travels = vertical > 0.0
        square = jnp.maximum(vertical, 0.0)
        root = jnp.sqrt(jnp.abs(vertical))
        phase[front, 0] = jnp.where(travels, series(square, 0), jnp.exp(-root)) * level_out
        phase[front, 1] = jnp.where(travels, root * series(square, 1), 0.0) * level_out
    for copy in fixed:
        copy.wait()
    sign = jnp.where(odd == 0, 1.0, -1.0).astype(F32)
    for level in range(2):
        refl[level] = sign * refl[level]
    for front in range(fronts):
        cos_row, sin_row = class_rows(slowness, front_wave(freq, front), (8, 128))
        for level in range(2):
            screen[level, front, 0] = look_up(cos_row, klass[level])
            screen[level, front, 1] = look_up(sin_row, klass[level])
    pltpu.make_async_copy(down.at[0], fields.at[0], sems.at[0]).wait()
    pltpu.make_async_copy(down.at[0], fields.at[1], sems.at[1]).wait()
    jobs = [(fields.at[1, front], front, q_out_inner.at[front]) for front in range(fronts)]
    jobs += [(fields.at[0, front], front, q_in_outer.at[front]) for front in range(fronts)]
    spread(jobs, work, hx, hy, phase)
    for front in range(fronts):
        for part in range(2):
            back[front, part] = refl[0] * screen[0, front, part]
    outward_base(q_out_inner, screen, refl, base)


def outward_base(q_out_inner, screen, refl, base):
    kept = 1.0 - refl[0]
    for front in range(base.shape[0]):
        b_re, b_im = (q_out_inner[front, part].astype(F32) for part in range(2))
        b_re, b_im = screened(b_re, b_im, screen[0, front, 0], screen[0, front, 1])
        base[front, 0] = kept * b_re
        base[front, 1] = kept * b_im


def outward_step(q_arrived, back, base, field):
    for front in range(field.shape[0]):
        a_re, a_im = (q_arrived[front, part].astype(F32) for part in range(2))
        back_re, back_im = back[front, 0], back[front, 1]
        put(
            field.at[front],
            base[front, 0] + (back_re * a_re - back_im * a_im),
            base[front, 1] + (back_re * a_im + back_im * a_re),
        )


def ahead_kernel(
    partner, q_in_outer, screen, refl, phase, hx, hy,
    inward_inner, q_out_inner, base,
    q_field, field, work,
):
    everyone = range(partner.shape[0])
    spread([(partner.at[front], front, q_field.at[front]) for front in everyone], work, hx, hy, phase)
    for front in everyone:
        in_re, in_im, out_re, out_im = mixed(
            q_in_outer[front, 0], q_in_outer[front, 1], q_field[front, 0], q_field[front, 1],
            refl[1], screen[1, front, 0], screen[1, front, 1],
        )
        put(inward_inner.at[front], in_re, in_im)
        put(field.at[front], out_re, out_im)
    spread([(field.at[front], front, q_out_inner.at[front]) for front in everyone], work, hx, hy, phase)
    outward_base(q_out_inner, screen, refl, base)


def entering(arrived, source, front):
    first = lax.axis_index("depth") == 0
    return lambda part: jnp.where(first, source[front, part], arrived[front, part])


def outer_step(q_arrived, q_out_inner, screen, refl, waves, field):
    for front in range(field.shape[0]):
        put(
            field.at[front],
            *mixed(
                q_arrived[front, 0], q_arrived[front, 1], q_out_inner[front, 0], q_out_inner[front, 1],
                refl[0], screen[0, front, 0], screen[0, front, 1], waves,
            ),
        )


def edge_kernel(arrived, source, back, base, phase, hx, hy, sent, q_arrived, field, work):
    everyone = range(arrived.shape[0])

    def step(target):
        jobs = [(entering(arrived, source, front), front, q_arrived.at[front]) for front in everyone]
        spread(jobs, work, hx, hy, phase)
        outward_step(q_arrived, back, base, target)

    def early():
        step(sent)

    def late():
        step(field)
        spread([(field.at[front], front, sent.at[front]) for front in everyone], work, hx, hy, phase)

    by_turn(early, late)


def last_edge_kernel(
    arrived, source, back, base, phase, hx, hy, after,
    q_arrived, last_far, last_near,
    outward, work,
):
    del after
    everyone = range(arrived.shape[0])
    half = arrived.shape[2] // 2

    def step(q_entered):
        outward_step(q_entered, back, base, outward)
        jobs = [
            (outward.at[front], front, [(half_rows(1, half), last_far.at[front]), (half_rows(0, half), last_near.at[front])])
            for front in everyone
        ]
        spread(jobs, work, hx, hy, phase)

    def early():
        jobs = [(entering(arrived, source, front), front, q_arrived.at[front]) for front in everyone]
        spread(jobs, work, hx, hy, phase)
        step(q_arrived)

    def late():
        step(arrived)

    by_turn(early, late)


def inner_kernel(
    q_arrived, q_out_inner, partner, screen, refl, phase, hx, hy,
    inward, outward,
    field, q_inward, q_partner, work,
):
    everyone = range(partner.shape[0])
    outer_step(q_arrived, q_out_inner, screen, refl, "inward", field)
    jobs = [(partner.at[front], front, q_partner.at[front]) for front in everyone]
    jobs += [(field.at[front], front, q_inward.at[front]) for front in everyone]
    spread(jobs, work, hx, hy, phase)
    for front in everyone:
        in_re, in_im, out_re, out_im = mixed(
            q_inward[front, 0], q_inward[front, 1], q_partner[front, 0], q_partner[front, 1],
            refl[1], screen[1, front, 0], screen[1, front, 1],
        )
        put(inward.at[front], in_re, in_im)
        put(outward.at[front], out_re, out_im)


def spread_kernel(fields, phase, hx, hy, q_fields, work):
    @pl.when(late_pair())
    def _():
        everyone = range(fields.shape[0])
        spread([(fields.at[front], front, q_fields.at[front]) for front in everyone], work, hx, hy, phase)


def last_inner_kernel(
    q_arrived, arrived, q_out_inner, partner, screen, refl, phase, hx, hy, out_inner, q_next_in,
    inward, outward, terms, far_terms, q_next,
    field, q_inward, q_partner, work,
):
    everyone = range(partner.shape[0])

    def early():
        outer_step(q_arrived, q_out_inner, screen, refl, "inward", field)
        spread([(out_inner.at[front], front, q_next.at[front]) for front in everyone], work, hx, hy, phase)

    def late():
        outer_step(arrived, q_out_inner, screen, refl, "inward", field)
        q_next[...] = q_next_in[...]

    by_turn(early, late)
    jobs = [(partner.at[front], front, q_partner.at[front]) for front in everyone]
    jobs += [(field.at[front], front, q_inward.at[front]) for front in everyone]
    spread(jobs, work, hx, hy, phase)
    total = None
    for front in everyone:
        a_re, a_im = (q_inward[front, part].astype(F32) for part in range(2))
        b_re, b_im = (q_partner[front, part].astype(F32) for part in range(2))
        in_re, in_im, out_re, out_im = mixed(
            a_re, a_im, b_re, b_im, refl[1], screen[1, front, 0], screen[1, front, 1]
        )
        put(inward.at[front], in_re, in_im)
        put(outward.at[front], out_re, out_im)
        term = a_re * b_re + a_im * b_im
        total = term if total is None else total + term
    terms[...] = total
    far_terms[...] = terms[half_rows(1, far_terms.shape[0]), :].astype(BF16)


def incoming(last, q_arrived, front, rows):
    first = lax.axis_index("depth") == 0
    return [jnp.where(first, q_arrived[front, part, rows, :], last[front, part]).astype(F32) for part in range(2)]


def row_terms(of, last, q_arrived, q_out_inner):
    total = None
    rows = half_rows(of, last.shape[2])
    for front in range(last.shape[0]):
        a_re, a_im = incoming(last, q_arrived, front, rows)
        b_re, b_im = (q_out_inner[front, part, rows, :].astype(F32) for part in range(2))
        term = a_re * b_re + a_im * b_im
        total = term if total is None else total + term
    return total


def row_fields(of, last, q_arrived, q_out_inner, screen, refl, inward, outward):
    rows = half_rows(of, last.shape[2])
    for front in range(last.shape[0]):
        a_re, a_im = incoming(last, q_arrived, front, rows)
        b_re, b_im = (q_out_inner[front, part, rows, :].astype(F32) for part in range(2))
        in_re, in_im, out_re, out_im = mixed(
            a_re, a_im, b_re, b_im, refl[0, rows, :], screen[0, front, 0, rows, :], screen[0, front, 1, rows, :]
        )
        put(inward.at[front], in_re, in_im)
        put(outward.at[front], out_re, out_im)
    return rows


def far_terms_kernel(last, q_arrived, q_out_inner, after, terms):
    del after
    terms[...] = row_terms(1, last, q_arrived, q_out_inner).astype(BF16)


def send_home(level, rows, inward, outward, down_out, up_out, sems):
    odd = odd_place()

    def copies(place, inward_out, outward_out):
        return [
            pltpu.make_async_copy(inward, inward_out.at[place, :, :, rows, :], sems.at[0]),
            pltpu.make_async_copy(outward, outward_out.at[place, :, :, rows, :], sems.at[1]),
        ]

    @pl.when(odd == 0)
    def _():
        for copy in copies(level, down_out, up_out):
            copy.start()

    @pl.when(odd == 1)
    def _():
        for copy in copies(1 - level, up_out, down_out):
            copy.start()

    return copies(0, down_out, up_out)


def home_kernel(
    far, q_arrived, q_out_inner, screen, refl, inner_in, inner_out, down_out, up_out, far_in, far_out, sems
):
    waits = send_home(1, pl.ds(0, inner_in.shape[2]), inner_in, inner_out, down_out, up_out, sems.at[0])
    rows = row_fields(1, far, q_arrived, q_out_inner, screen, refl, far_in, far_out)
    waits += send_home(0, rows, far_in, far_out, down_out, up_out, sems.at[1])
    for copy in waits:
        copy.wait()


def near_kernel(
    scale, near, q_arrived, q_out_inner, screen, refl, inner_terms, inner_other, down_in, up_in,
    down_out, up_out, gradient, terms,
    near_in, near_out, inner_sum, sems,
):
    del down_in, up_in
    rows = row_fields(0, near, q_arrived, q_out_inner, screen, refl, near_in, near_out)
    waits = send_home(0, rows, near_in, near_out, down_out, up_out, sems.at[0])
    inner_sum[...] = scale * (inner_terms[rows, :] + inner_other[...].astype(F32))
    waits.append(pltpu.make_async_copy(inner_sum, gradient.at[1 - odd_place()], sems.at[1, 0]))
    waits[-1].start()
    terms[...] = row_terms(0, near, q_arrived, q_out_inner)
    for copy in waits:
        copy.wait()


def outer_gradient_kernel(scale, terms, other, gradient_in, gradient, outer_sum, sems):
    del gradient_in
    outer_sum[...] = scale * (terms[...] + other[...].astype(F32))
    done = pltpu.make_async_copy(outer_sum, gradient.at[odd_place()], sems.at[0])
    done.start()
    done.wait()


def per_device(down_state, up_state, source, reflect, screen_class, screen_values, freq_index):
    depth = lax.axis_size("depth")
    shots = lax.axis_size("shot")
    levels, fronts, parts, rows_x, rows_y = down_state.shape
    if levels != 2 or depth % 2 or shots % 2 or HOPS != 3:
        return per_device_plain(down_state, up_state, source, reflect, screen_class, screen_values, freq_index)
    scale = 1.0 / math.sqrt(fronts * shots)
    half = rows_x // 2
    hx = jnp.asarray(hartley(rows_x))
    hy = jnp.asarray(hartley(rows_y))
    partners = [(i, i ^ 1) for i in range(depth)]
    beyond = [(i, i + 1) for i in range(1, depth - 1, 2)] + [(i + 1, i) for i in range(1, depth - 1, 2)]
    to_partner = functools.partial(lax.ppermute, axis_name="depth", perm=partners)
    to_beyond = functools.partial(lax.ppermute, axis_name="depth", perm=beyond)
    across = functools.partial(lax.ppermute, axis_name="shot", perm=[(i, i ^ 1) for i in range(shots)])
    plane = jax.ShapeDtypeStruct((fronts, parts, rows_x, rows_y), BF16)
    half_plane = jax.ShapeDtypeStruct((fronts, parts, half, rows_y), BF16)
    pair = jax.ShapeDtypeStruct((2, rows_x, rows_y), F32)
    turns = jax.ShapeDtypeStruct((fronts, parts, rows_x, rows_y), F32)
    screens = jax.ShapeDtypeStruct((2, fronts, parts, rows_x, rows_y), F32)
    state = jax.ShapeDtypeStruct(down_state.shape, BF16)
    dma = pltpu.SemaphoreType.DMA

    def call(kernel, in_specs, out_specs, out_shape, scratch=(), **more):
        return pl.pallas_call(
            kernel,
            in_specs=in_specs,
            out_specs=out_specs,
            out_shape=out_shape,
            scratch_shapes=list(scratch),
            compiler_params=PARAMS,
            **more,
        )

    def kept_in_hbm(*arrays):
        return [pltpu.with_memory_space_constraint(array, pltpu.HBM) for array in arrays]

    def buffers(count, shape=plane):
        return [pltpu.VMEM(shape.shape, shape.dtype)] * count

    def work(slots):
        return pltpu.VMEM((slots, *plane.shape[1:]), BF16)

    out_outer, in_inner = call(edges_kernel, [HBM] * 2, [VMEM] * 2, [plane] * 2, [dma((2,))])(
        *kept_in_hbm(down_state, up_state)
    )
    arrived_0 = to_beyond(out_outer)
    partner_0 = to_partner(in_inner)
    q_out_inner_0, q_in_outer_0, screen, phase, refl, back, base_0 = call(
        setup_kernel,
        [HBM] * 4 + [SMEM] * 2 + [VMEM] * 2,
        [VMEM] * 7,
        [plane] * 2 + [screens, turns, pair, turns, turns],
        [
            pltpu.VMEM((2, *plane.shape), BF16),
            pltpu.VMEM((2, rows_x, rows_y), jnp.int32),
            work(2 * fronts),
            dma((6,)),
        ],
    )(*kept_in_hbm(down_state, up_state, reflect, screen_class), screen_values, freq_index, hx, hy)
    fixed = (screen, refl, phase, hx, hy)
    in_inner_1, q_out_inner_1, base_1 = call(
        ahead_kernel, [VMEM] * 7, [VMEM] * 3, [plane] * 2 + [turns], buffers(2) + [work(fronts)]
    )(
        partner_0, q_in_outer_0, *fixed
    )
    partner_1 = to_partner(in_inner_1)
    out_outer_1, q_arrived = call(edge_kernel, [VMEM] * 7, [VMEM] * 2, [plane] * 2, buffers(1) + [work(fronts)])(
        arrived_0, source, back, base_0, phase, hx, hy
    )
    arrived_1 = to_beyond(out_outer_1)
    in_inner_2, out_inner_2 = call(
        inner_kernel, [VMEM] * 8, [VMEM] * 2, [plane] * 2, buffers(3) + [work(2 * fronts)]
    )(q_arrived, q_out_inner_0, partner_1, *fixed)
    partner_2 = to_partner(in_inner_2)
    q_out_inner_2 = call(spread_kernel, [VMEM] * 4, VMEM, plane, [work(fronts)])(out_inner_2, phase, hx, hy)
    q_arrived_1, last_far, last_near = call(
        last_edge_kernel,
        [VMEM] * 7 + [pl.BlockSpec(memory_space=pl.ANY)],
        [VMEM] * 3,
        [plane] + [half_plane] * 2,
        buffers(1) + [work(fronts)],
    )(arrived_1, source, back, base_1, phase, hx, hy, q_out_inner_2)
    last_far = to_beyond(last_far)
    last_near = to_beyond(last_near)
    half_sum = jax.ShapeDtypeStruct((half, rows_y), BF16)
    inner_in, inner_out, inner_terms, inner_far, q_out_inner_2 = call(
        last_inner_kernel,
        [VMEM] * 11,
        [VMEM] * 5,
        [plane] * 2 + [jax.ShapeDtypeStruct((rows_x, rows_y), F32), half_sum, plane],
        buffers(3) + [work(2 * fronts)],
        input_output_aliases={10: 4},
    )(q_arrived_1, arrived_1, q_out_inner_1, partner_2, *fixed, out_inner_2, q_out_inner_2)
    inner_other = across(inner_far) if shots == 2 else jnp.zeros_like(inner_far)
    outer_far = call(far_terms_kernel, [VMEM] * 3 + [pl.BlockSpec(memory_space=pl.ANY)], VMEM, half_sum)(
        last_far, q_arrived, q_out_inner_2, inner_terms
    )
    outer_other = across(outer_far) if shots == 2 else jnp.zeros_like(outer_far)
    half_total = jax.ShapeDtypeStruct((half, rows_y), F32)
    share = jax.ShapeDtypeStruct((2, half, rows_y), F32)
    down, up = call(
        home_kernel, [VMEM] * 7, [HBM] * 2, [state] * 2, buffers(2, half_plane) + [dma((2, 2))]
    )(last_far, q_arrived, q_out_inner_2, screen, refl, inner_in, inner_out)
    down, up, gradient, outer_near = call(
        functools.partial(near_kernel, scale),
        [VMEM] * 7 + [HBM] * 2,
        [HBM] * 3 + [VMEM],
        [state, state, share, half_total],
        buffers(2, half_plane) + buffers(1, half_total) + [dma((2, 2))],
        input_output_aliases={7: 0, 8: 1},
    )(last_near, q_arrived, q_out_inner_2, screen, refl, inner_terms, inner_other, down, up)
    gradient = call(
        functools.partial(outer_gradient_kernel, scale),
        [VMEM] * 2 + [HBM],
        HBM,
        share,
        buffers(1, half_total) + [dma((1,))],
        input_output_aliases={2: 0},
    )(outer_near, outer_other, gradient)
    if shots != 2:
        terms = scale * jnp.stack([outer_far, inner_far]).astype(F32)
        far = jnp.where(odd_place() == 0, terms, terms[::-1])
        top = lax.rem(lax.axis_index("shot"), 2) == 0
        whole = jnp.concatenate([jnp.where(top, gradient, far), jnp.where(top, far, gradient)], axis=1)
        gradient = lax.psum_scatter(whole.astype(BF16), "shot", scatter_dimension=1, tiled=True).astype(F32)
    return (down, up, gradient)


def solution(mesh):
    return jax.shard_map(
        per_device,
        mesh=mesh,
        in_specs=(
            P("depth", "shot", None, None, None),
            P("depth", "shot", None, None, None),
            P("shot", None, None, None),
            P("depth", None, None),
            P("depth", None, None),
            P(),
            P("shot"),
        ),
        out_specs=(
            P("depth", "shot", None, None, None),
            P("depth", "shot", None, None, None),
            P("depth", "shot", None),
        ),
        check_vma=False,
    )
```

```python
import functools
import math

import jax
import jax.numpy as jnp
import numpy as np
from jax import lax
from jax.experimental import pallas as pl
from jax.experimental.pallas import tpu as pltpu
from jax.sharding import PartitionSpec as P

HOPS = 3
NCLASS = 16
NFREQ = 128
F32 = jnp.float32
BF16 = jnp.bfloat16
VMEM = pl.BlockSpec(memory_space=pltpu.VMEM)
HBM = pl.BlockSpec(memory_space=pltpu.HBM)
SMEM = pl.BlockSpec(memory_space=pltpu.SMEM)
PARAMS = pltpu.CompilerParams(vmem_limit_bytes=28 * 2**20)


def passed_along(block, axis, distance):
    devices = range(lax.axis_size(axis))
    route = [(i - distance, i) for i in devices if i - distance in devices]
    return lax.ppermute(block, axis, route)


def dft_tables(length):
    counter = jnp.arange(length, dtype=jnp.int32)
    product = counter[:, None] * counter[None, :] % length
    angles = 2.0 * math.pi / length * product.astype(jnp.float32)
    return (jnp.cos(angles).astype(jnp.bfloat16), jnp.sin(angles).astype(jnp.bfloat16))


def wavenumbers(length):
    counter = jnp.arange(length, dtype=jnp.int32)
    wrapped = jnp.where(counter >= length // 2, counter - length, counter)
    return 2.0 * math.pi / length * wrapped.astype(jnp.float32)


def propagate(planes, phase_re, phase_im, tables):
    fwd_left, fwd_right, inv_left, inv_right = tables
    first = jnp.einsum(
        "cdjk,...dkl->...cjl", fwd_left, planes, preferred_element_type=jnp.float32
    ).astype(jnp.bfloat16)
    second = jnp.einsum("...djl,dclm->...cjm", first, fwd_right, preferred_element_type=jnp.float32)
    real_part = second[..., 0, :, :]
    imag_part = second[..., 1, :, :]
    turned = jnp.stack(
        [real_part * phase_re - imag_part * phase_im, real_part * phase_im + imag_part * phase_re],
        axis=-3,
    ).astype(jnp.bfloat16)
    third = jnp.einsum(
        "cdjk,...dkl->...cjl", inv_left, turned, preferred_element_type=jnp.float32
    ).astype(jnp.bfloat16)
    return jnp.einsum(
        "...djl,dclm->...cjm", third, inv_right, preferred_element_type=jnp.float32
    ).astype(jnp.bfloat16)


def trade(down_edge, up_edge):
    got_down = passed_along(down_edge, "depth", 1)
    got_up = passed_along(up_edge, "depth", -1)
    return (got_down, got_up)


def per_device_plain(down_state, up_state, source, reflect, screen_class, screen_values, freq_index):
    levels = down_state.shape[0]
    rows_x = down_state.shape[3]
    rows_y = down_state.shape[4]
    front_count = down_state.shape[1]
    depth_rank = lax.axis_index("depth")
    scale = 1.0 / math.sqrt(front_count * lax.axis_size("shot"))
    cos_x, sin_x = dft_tables(rows_x)
    cos_y, sin_y = dft_tables(rows_y)
    tables = (
        jnp.stack([jnp.stack([cos_x, sin_x]), jnp.stack([-sin_x, cos_x])]),
        jnp.stack([jnp.stack([cos_y, -sin_y]), jnp.stack([sin_y, cos_y])]),
        jnp.stack([jnp.stack([cos_x, -sin_x]), jnp.stack([sin_x, cos_x])]),
        jnp.stack([jnp.stack([cos_y, sin_y]), jnp.stack([-sin_y, cos_y])]),
    )
    kwave = 0.95 * math.pi * (freq_index.astype(jnp.float32) + 1.0) / NFREQ
    kx_wave = wavenumbers(rows_x)
    ky_wave = wavenumbers(rows_y)
    vertical = kwave[:, None, None] ** 2 - kx_wave[None, :, None] ** 2 - ky_wave[None, None, :] ** 2
    propag = jnp.sqrt(jnp.maximum(vertical, 0.0))
    damping = jnp.exp(-jnp.sqrt(jnp.maximum(-vertical, 0.0))) / (rows_x * rows_y)
    phase_re = damping * jnp.cos(propag)
    phase_im = damping * jnp.sin(propag)
    classes = jnp.arange(NCLASS, dtype=jnp.int32)
    onehot = (screen_class[None] == classes[:, None, None, None]).astype(jnp.float32)
    slowness = jnp.einsum("c,clxy->lxy", screen_values, onehot, precision=lax.Precision.HIGHEST)
    angle = kwave[None, :, None, None] * slowness[:, None]
    screen_re = jnp.cos(angle)
    screen_im = jnp.sin(angle)
    refl = reflect[:, None]
    top_slab = depth_rank == 0
    down = down_state
    up = up_state
    a_re = a_im = b_re = b_im = None
    for repeat in range(HOPS):
        down_edge = down[levels - 1]
        up_edge = up[0]
        got_down, got_up = trade(down_edge, up_edge)
        got_down = jnp.where(top_slab, source, got_down)
        moved = propagate(
            jnp.concatenate([got_down[None], down[: levels - 1], up[1:], got_up[None]], axis=0),
            phase_re,
            phase_im,
            tables,
        )
        from_above = moved[:levels]
        from_below = moved[levels:]
        qa_re = from_above[:, :, 0].astype(jnp.float32)
        qa_im = from_above[:, :, 1].astype(jnp.float32)
        qb_re = from_below[:, :, 0].astype(jnp.float32)
        qb_im = from_below[:, :, 1].astype(jnp.float32)
        a_re = screen_re * qa_re - screen_im * qa_im
        a_im = screen_re * qa_im + screen_im * qa_re
        b_re = screen_re * qb_re - screen_im * qb_im
        b_im = screen_re * qb_im + screen_im * qb_re
        down = jnp.stack(
            [(1.0 + refl) * a_re - refl * b_re, (1.0 + refl) * a_im - refl * b_im], axis=2
        ).astype(jnp.bfloat16)
        up = jnp.stack(
            [(1.0 - refl) * b_re + refl * a_re, (1.0 - refl) * b_im + refl * a_im], axis=2
        ).astype(jnp.bfloat16)
    terms = scale * jnp.sum(a_re * b_re + a_im * b_im, axis=1)
    gradient = lax.psum_scatter(
        terms.astype(jnp.bfloat16), "shot", scatter_dimension=1, tiled=True
    ).astype(jnp.float32)
    return (down, up, gradient)


def hartley(length):
    counter = np.arange(length)
    angles = 2.0 * np.pi / length * (counter[:, None] * counter[None, :] % length)
    cosine = np.cos(angles).astype(BF16).astype(np.float32)
    sine = np.sin(angles).astype(BF16).astype(np.float32)
    return (cosine + sine).astype(BF16)


def odd_place():
    return lax.rem(lax.axis_index("depth"), 2)


def mm(left, right):
    return jnp.dot(left, right, preferred_element_type=F32)


def spread(jobs, work, hx, hy, phase):
    jobs = list(enumerate(jobs))
    for slot, (plane, _, _) in jobs:
        parts = [plane(part) if callable(plane) else plane[part] for part in range(2)]
        width = parts[0].shape[1]
        both = mm(hx[...], jnp.concatenate(parts, axis=1)).astype(BF16)
        work[slot, 0] = both[:, :width]
        work[slot, 1] = both[:, width:]
    for slot, (_, front, _) in jobs:
        turn_re, turn_im = phase[front, 0], phase[front, 1]
        part_re = mm(work[slot, 0], hy[...])
        part_im = mm(work[slot, 1], hy[...])
        work[slot, 0] = (part_re * turn_re - part_im * turn_im).astype(BF16)
        work[slot, 1] = (part_re * turn_im + part_im * turn_re).astype(BF16)
    for slot, _ in jobs:
        for part in range(2):
            work[slot, part] = mm(work[slot, part], hy[...]).astype(BF16)
    for slot, (_, _, target) in jobs:
        for part in range(2):
            if isinstance(target, list):
                rows = jnp.concatenate([hx[rows, :] for rows, _ in target], axis=0)
                ends = np.cumsum([piece.shape[1] for _, piece in target])
                done = mm(rows, work[slot, part]).astype(BF16)
                for (_, piece), end in zip(target, ends, strict=True):
                    piece[part] = done[end - piece.shape[1] : end]
            else:
                target[part] = mm(hx[...], work[slot, part]).astype(BF16)


def screened(real_part, imag_part, screen_re, screen_im):
    return (
        screen_re * real_part - screen_im * imag_part,
        screen_re * imag_part + screen_im * real_part,
    )


def mixed(a_re, a_im, b_re, b_im, refl, screen_re, screen_im, waves="both"):
    a_re, a_im, b_re, b_im = (part.astype(F32) for part in (a_re, a_im, b_re, b_im))
    step_re = refl * (a_re - b_re)
    step_im = refl * (a_im - b_im)
    fields = ()
    if waves != "outward":
        fields += screened(a_re + step_re, a_im + step_im, screen_re, screen_im)
    if waves != "inward":
        fields += screened(b_re + step_re, b_im + step_im, screen_re, screen_im)
    return fields


def put(target, real_part, imag_part):
    target[0] = real_part.astype(BF16)
    target[1] = imag_part.astype(BF16)


def half_rows(of, half):
    shot = lax.rem(lax.axis_index("shot"), 2)
    return pl.ds(pl.multiple_of((shot if of == 0 else 1 - shot) * half, half), half)


def late_pair():
    return lax.rem(lax.div(lax.axis_index("depth") + 1, 2), 2) == 1


def by_turn(early, late):
    is_late = late_pair()
    pl.when(jnp.logical_not(is_late))(early)
    pl.when(is_late)(late)


def edges_kernel(down, up, outward_outer, inward_inner, sems):
    levels = down.shape[0]
    odd = odd_place()

    def fetch(first, second):
        pltpu.make_async_copy(first, outward_outer, sems.at[0]).start()
        pltpu.make_async_copy(second, inward_inner, sems.at[1]).start()

    @pl.when(odd == 0)
    def _():
        fetch(up.at[0], down.at[levels - 1])

    @pl.when(odd == 1)
    def _():
        fetch(down.at[levels - 1], up.at[0])

    pltpu.make_async_copy(up.at[0], outward_outer, sems.at[0]).wait()
    pltpu.make_async_copy(up.at[0], inward_inner, sems.at[1]).wait()


def class_rows(slowness, kwave, shape):
    lanes = lax.broadcasted_iota(jnp.int32, shape, 1)
    table = jnp.zeros(shape, F32)
    for entry in range(NCLASS):
        table = jnp.where(lanes == entry, slowness[entry], table)
    angle = kwave * table
    return jnp.cos(angle), jnp.sin(angle)


def look_up(table, classes):
    width = 128
    rows = classes.shape[0]
    wide = jnp.broadcast_to(table[:1], (rows, width))
    pieces = [
        jnp.take_along_axis(wide, classes[:, start : start + width], axis=1, mode="promise_in_bounds")
        for start in range(0, classes.shape[1], width)
    ]
    return jnp.concatenate(pieces, axis=1)


def front_wave(freq, front):
    return 0.95 * math.pi * (freq[front].astype(F32) + 1.0) / NFREQ


def series(square, shift):
    total = jnp.full_like(square, 1.0 / math.factorial(18 + shift))
    for order in range(16, -1, -2):
        total = 1.0 / math.factorial(order + shift) - square * total
    return total


def setup_kernel(
    down, up, reflect, classes_in, slowness, freq, hx, hy,
    q_out_inner, q_in_outer, screen, phase, refl, back, base,
    fields, klass, work, sems,
):
    fronts = q_out_inner.shape[0]
    rows_x, rows_y = refl.shape[1:]
    odd = odd_place()
    fixed = [
        pltpu.make_async_copy(reflect.at[odd], refl.at[0], sems.at[2]),
        pltpu.make_async_copy(reflect.at[1 - odd], refl.at[1], sems.at[3]),
        pltpu.make_async_copy(classes_in.at[odd], klass.at[0], sems.at[4]),
        pltpu.make_async_copy(classes_in.at[1 - odd], klass.at[1], sems.at[5]),
    ]
    for copy in fixed:
        copy.start()

    @pl.when(odd == 0)
    def _():
        pltpu.make_async_copy(down.at[0], fields.at[0], sems.at[0]).start()
        pltpu.make_async_copy(up.at[1], fields.at[1], sems.at[1]).start()

    @pl.when(odd == 1)
    def _():
        pltpu.make_async_copy(up.at[1], fields.at[0], sems.at[0]).start()
        pltpu.make_async_copy(down.at[0], fields.at[1], sems.at[1]).start()

    def squares(length, axis):
        counter = lax.broadcasted_iota(jnp.int32, (rows_x, rows_y), axis)
        wrapped = jnp.where(counter >= length // 2, counter - length, counter)
        wave = 2.0 * math.pi / length * wrapped.astype(F32)
        return wave * wave

    lateral = squares(rows_x, 0) + squares(rows_y, 1)
    level_out = 1.0 / (rows_x * rows_y)
    for front in range(fronts):
        kwave = front_wave(freq, front)
        vertical = kwave * kwave - lateral
        travels = vertical > 0.0
        square = jnp.maximum(vertical, 0.0)
        root = jnp.sqrt(jnp.abs(vertical))
        phase[front, 0] = jnp.where(travels, series(square, 0), jnp.exp(-root)) * level_out
        phase[front, 1] = jnp.where(travels, root * series(square, 1), 0.0) * level_out
    for copy in fixed:
        copy.wait()
    sign = jnp.where(odd == 0, 1.0, -1.0).astype(F32)
    for level in range(2):
        refl[level] = sign * refl[level]
    for front in range(fronts):
        cos_row, sin_row = class_rows(slowness, front_wave(freq, front), (8, 128))
        for level in range(2):
            screen[level, front, 0] = look_up(cos_row, klass[level])
            screen[level, front, 1] = look_up(sin_row, klass[level])
    pltpu.make_async_copy(down.at[0], fields.at[0], sems.at[0]).wait()
    pltpu.make_async_copy(down.at[0], fields.at[1], sems.at[1]).wait()
    jobs = [(fields.at[1, front], front, q_out_inner.at[front]) for front in range(fronts)]
    jobs += [(fields.at[0, front], front, q_in_outer.at[front]) for front in range(fronts)]
    spread(jobs, work, hx, hy, phase)
    for front in range(fronts):
        for part in range(2):
            back[front, part] = refl[0] * screen[0, front, part]
    outward_base(q_out_inner, screen, refl, base)


def outward_base(q_out_inner, screen, refl, base):
    kept = 1.0 - refl[0]
    for front in range(base.shape[0]):
        b_re, b_im = (q_out_inner[front, part].astype(F32) for part in range(2))
        b_re, b_im = screened(b_re, b_im, screen[0, front, 0], screen[0, front, 1])
        base[front, 0] = kept * b_re
        base[front, 1] = kept * b_im


def outward_step(q_arrived, back, base, field):
    for front in range(field.shape[0]):
        a_re, a_im = (q_arrived[front, part].astype(F32) for part in range(2))
        back_re, back_im = back[front, 0], back[front, 1]
        put(
            field.at[front],
            base[front, 0] + (back_re * a_re - back_im * a_im),
            base[front, 1] + (back_re * a_im + back_im * a_re),
        )


def ahead_kernel(
    partner, q_in_outer, screen, refl, phase, hx, hy,
    inward_inner, q_out_inner, base,
    q_field, field, work,
):
    everyone = range(partner.shape[0])
    spread([(partner.at[front], front, q_field.at[front]) for front in everyone], work, hx, hy, phase)
    for front in everyone:
        in_re, in_im, out_re, out_im = mixed(
            q_in_outer[front, 0], q_in_outer[front, 1], q_field[front, 0], q_field[front, 1],
            refl[1], screen[1, front, 0], screen[1, front, 1],
        )
        put(inward_inner.at[front], in_re, in_im)
        put(field.at[front], out_re, out_im)
    spread([(field.at[front], front, q_out_inner.at[front]) for front in everyone], work, hx, hy, phase)
    outward_base(q_out_inner, screen, refl, base)


def entering(arrived, source, front):
    first = lax.axis_index("depth") == 0
    return lambda part: jnp.where(first, source[front, part], arrived[front, part])


def outer_step(q_arrived, q_out_inner, screen, refl, waves, field):
    for front in range(field.shape[0]):
        put(
            field.at[front],
            *mixed(
                q_arrived[front, 0], q_arrived[front, 1], q_out_inner[front, 0], q_out_inner[front, 1],
                refl[0], screen[0, front, 0], screen[0, front, 1], waves,
            ),
        )


def edge_kernel(arrived, source, back, base, phase, hx, hy, sent, q_arrived, field, work):
    everyone = range(arrived.shape[0])

    def step(target):
        jobs = [(entering(arrived, source, front), front, q_arrived.at[front]) for front in everyone]
        spread(jobs, work, hx, hy, phase)
        outward_step(q_arrived, back, base, target)

    def early():
        step(sent)

    def late():
        step(field)
        spread([(field.at[front], front, sent.at[front]) for front in everyone], work, hx, hy, phase)

    by_turn(early, late)


def last_edge_kernel(
    arrived, source, back, base, phase, hx, hy, after,
    q_arrived, last_far, last_near,
    outward, work,
):
    del after
    everyone = range(arrived.shape[0])
    half = arrived.shape[2] // 2

    def step(q_entered):
        outward_step(q_entered, back, base, outward)
        jobs = [
            (outward.at[front], front, [(half_rows(1, half), last_far.at[front]), (half_rows(0, half), last_near.at[front])])
            for front in everyone
        ]
        spread(jobs, work, hx, hy, phase)

    def early():
        jobs = [(entering(arrived, source, front), front, q_arrived.at[front]) for front in everyone]
        spread(jobs, work, hx, hy, phase)
        step(q_arrived)

    def late():
        step(arrived)

    by_turn(early, late)


def inner_kernel(
    q_arrived, q_out_inner, partner, screen, refl, phase, hx, hy,
    inward, outward,
    field, q_inward, q_partner, work,
):
    everyone = range(partner.shape[0])
    outer_step(q_arrived, q_out_inner, screen, refl, "inward", field)
    jobs = [(partner.at[front], front, q_partner.at[front]) for front in everyone]
    jobs += [(field.at[front], front, q_inward.at[front]) for front in everyone]
    spread(jobs, work, hx, hy, phase)
    for front in everyone:
        in_re, in_im, out_re, out_im = mixed(
            q_inward[front, 0], q_inward[front, 1], q_partner[front, 0], q_partner[front, 1],
            refl[1], screen[1, front, 0], screen[1, front, 1],
        )
        put(inward.at[front], in_re, in_im)
        put(outward.at[front], out_re, out_im)


def spread_kernel(fields, phase, hx, hy, q_fields, work):
    @pl.when(late_pair())
    def _():
        everyone = range(fields.shape[0])
        spread([(fields.at[front], front, q_fields.at[front]) for front in everyone], work, hx, hy, phase)


def last_inner_kernel(
    q_arrived, arrived, q_out_inner, partner, screen, refl, phase, hx, hy, out_inner, q_next_in,
    inward, outward, terms, far_terms, q_next,
    field, q_inward, q_partner, work,
):
    everyone = range(partner.shape[0])

    def early():
        outer_step(q_arrived, q_out_inner, screen, refl, "inward", field)
        spread([(out_inner.at[front], front, q_next.at[front]) for front in everyone], work, hx, hy, phase)

    def late():
        outer_step(arrived, q_out_inner, screen, refl, "inward", field)
        q_next[...] = q_next_in[...]

    by_turn(early, late)
    jobs = [(partner.at[front], front, q_partner.at[front]) for front in everyone]
    jobs += [(field.at[front], front, q_inward.at[front]) for front in everyone]
    spread(jobs, work, hx, hy, phase)
    total = None
    for front in everyone:
        a_re, a_im = (q_inward[front, part].astype(F32) for part in range(2))
        b_re, b_im = (q_partner[front, part].astype(F32) for part in range(2))
        in_re, in_im, out_re, out_im = mixed(
            a_re, a_im, b_re, b_im, refl[1], screen[1, front, 0], screen[1, front, 1]
        )
        put(inward.at[front], in_re, in_im)
        put(outward.at[front], out_re, out_im)
        term = a_re * b_re + a_im * b_im
        total = term if total is None else total + term
    terms[...] = total
    far_terms[...] = terms[half_rows(1, far_terms.shape[0]), :].astype(BF16)


def incoming(last, q_arrived, front, rows):
    first = lax.axis_index("depth") == 0
    return [jnp.where(first, q_arrived[front, part, rows, :], last[front, part]).astype(F32) for part in range(2)]


def row_terms(of, last, q_arrived, q_out_inner):
    total = None
    rows = half_rows(of, last.shape[2])
    for front in range(last.shape[0]):
        a_re, a_im = incoming(last, q_arrived, front, rows)
        b_re, b_im = (q_out_inner[front, part, rows, :].astype(F32) for part in range(2))
        term = a_re * b_re + a_im * b_im
        total = term if total is None else total + term
    return total


def row_fields(of, last, q_arrived, q_out_inner, screen, refl, inward, outward):
    rows = half_rows(of, last.shape[2])
    for front in range(last.shape[0]):
        a_re, a_im = incoming(last, q_arrived, front, rows)
        b_re, b_im = (q_out_inner[front, part, rows, :].astype(F32) for part in range(2))
        in_re, in_im, out_re, out_im = mixed(
            a_re, a_im, b_re, b_im, refl[0, rows, :], screen[0, front, 0, rows, :], screen[0, front, 1, rows, :]
        )
        put(inward.at[front], in_re, in_im)
        put(outward.at[front], out_re, out_im)
    return rows


def far_terms_kernel(last, q_arrived, q_out_inner, after, terms):
    del after
    terms[...] = row_terms(1, last, q_arrived, q_out_inner).astype(BF16)


def send_home(level, rows, inward, outward, down_out, up_out, sems):
    odd = odd_place()

    def copies(place, inward_out, outward_out):
        return [
            pltpu.make_async_copy(inward, inward_out.at[place, :, :, rows, :], sems.at[0]),
            pltpu.make_async_copy(outward, outward_out.at[place, :, :, rows, :], sems.at[1]),
        ]

    @pl.when(odd == 0)
    def _():
        for copy in copies(level, down_out, up_out):
            copy.start()

    @pl.when(odd == 1)
    def _():
        for copy in copies(1 - level, up_out, down_out):
            copy.start()

    return copies(0, down_out, up_out)


def home_kernel(
    far, q_arrived, q_out_inner, screen, refl, inner_in, inner_out, down_out, up_out, far_in, far_out, sems
):
    waits = send_home(1, pl.ds(0, inner_in.shape[2]), inner_in, inner_out, down_out, up_out, sems.at[0])
    rows = row_fields(1, far, q_arrived, q_out_inner, screen, refl, far_in, far_out)
    waits += send_home(0, rows, far_in, far_out, down_out, up_out, sems.at[1])
    for copy in waits:
        copy.wait()


def near_kernel(
    scale, near, q_arrived, q_out_inner, screen, refl, inner_terms, inner_other, down_in, up_in,
    down_out, up_out, gradient, terms,
    near_in, near_out, inner_sum, sems,
):
    del down_in, up_in
    rows = row_fields(0, near, q_arrived, q_out_inner, screen, refl, near_in, near_out)
    waits = send_home(0, rows, near_in, near_out, down_out, up_out, sems.at[0])
    inner_sum[...] = scale * (inner_terms[rows, :] + inner_other[...].astype(F32))
    waits.append(pltpu.make_async_copy(inner_sum, gradient.at[1 - odd_place()], sems.at[1, 0]))
    waits[-1].start()
    terms[...] = row_terms(0, near, q_arrived, q_out_inner)
    for copy in waits:
        copy.wait()


def outer_gradient_kernel(scale, terms, other, gradient_in, gradient, outer_sum, sems):
    del gradient_in
    outer_sum[...] = scale * (terms[...] + other[...].astype(F32))
    done = pltpu.make_async_copy(outer_sum, gradient.at[odd_place()], sems.at[0])
    done.start()
    done.wait()


def per_device(down_state, up_state, source, reflect, screen_class, screen_values, freq_index):
    depth = lax.axis_size("depth")
    shots = lax.axis_size("shot")
    levels, fronts, parts, rows_x, rows_y = down_state.shape
    if levels != 2 or depth % 2 or shots % 2 or HOPS != 3:
        return per_device_plain(down_state, up_state, source, reflect, screen_class, screen_values, freq_index)
    scale = 1.0 / math.sqrt(fronts * shots)
    half = rows_x // 2
    hx = jnp.asarray(hartley(rows_x))
    hy = jnp.asarray(hartley(rows_y))
    partners = [(i, i ^ 1) for i in range(depth)]
    beyond = [(i, i + 1) for i in range(1, depth - 1, 2)] + [(i + 1, i) for i in range(1, depth - 1, 2)]
    to_partner = functools.partial(lax.ppermute, axis_name="depth", perm=partners)
    to_beyond = functools.partial(lax.ppermute, axis_name="depth", perm=beyond)
    across = functools.partial(lax.ppermute, axis_name="shot", perm=[(i, i ^ 1) for i in range(shots)])
    plane = jax.ShapeDtypeStruct((fronts, parts, rows_x, rows_y), BF16)
    half_plane = jax.ShapeDtypeStruct((fronts, parts, half, rows_y), BF16)
    pair = jax.ShapeDtypeStruct((2, rows_x, rows_y), F32)
    turns = jax.ShapeDtypeStruct((fronts, parts, rows_x, rows_y), F32)
    screens = jax.ShapeDtypeStruct((2, fronts, parts, rows_x, rows_y), F32)
    state = jax.ShapeDtypeStruct(down_state.shape, BF16)
    dma = pltpu.SemaphoreType.DMA

    def call(kernel, in_specs, out_specs, out_shape, scratch=(), **more):
        return pl.pallas_call(
            kernel,
            in_specs=in_specs,
            out_specs=out_specs,
            out_shape=out_shape,
            scratch_shapes=list(scratch),
            compiler_params=PARAMS,
            **more,
        )

    def kept_in_hbm(*arrays):
        return [pltpu.with_memory_space_constraint(array, pltpu.HBM) for array in arrays]

    def buffers(count, shape=plane):
        return [pltpu.VMEM(shape.shape, shape.dtype)] * count

    def work(slots):
        return pltpu.VMEM((slots, *plane.shape[1:]), BF16)

    out_outer, in_inner = call(edges_kernel, [HBM] * 2, [VMEM] * 2, [plane] * 2, [dma((2,))])(
        *kept_in_hbm(down_state, up_state)
    )
    arrived_0 = to_beyond(out_outer)
    partner_0 = to_partner(in_inner)
    q_out_inner_0, q_in_outer_0, screen, phase, refl, back, base_0 = call(
        setup_kernel,
        [HBM] * 4 + [SMEM] * 2 + [VMEM] * 2,
        [VMEM] * 7,
        [plane] * 2 + [screens, turns, pair, turns, turns],
        [
            pltpu.VMEM((2, *plane.shape), BF16),
            pltpu.VMEM((2, rows_x, rows_y), jnp.int32),
            work(2 * fronts),
            dma((6,)),
        ],
    )(*kept_in_hbm(down_state, up_state, reflect, screen_class), screen_values, freq_index, hx, hy)
    fixed = (screen, refl, phase, hx, hy)
    in_inner_1, q_out_inner_1, base_1 = call(
        ahead_kernel, [VMEM] * 7, [VMEM] * 3, [plane] * 2 + [turns], buffers(2) + [work(fronts)]
    )(
        partner_0, q_in_outer_0, *fixed
    )
    partner_1 = to_partner(in_inner_1)
    out_outer_1, q_arrived = call(edge_kernel, [VMEM] * 7, [VMEM] * 2, [plane] * 2, buffers(1) + [work(fronts)])(
        arrived_0, source, back, base_0, phase, hx, hy
    )
    arrived_1 = to_beyond(out_outer_1)
    in_inner_2, out_inner_2 = call(
        inner_kernel, [VMEM] * 8, [VMEM] * 2, [plane] * 2, buffers(3) + [work(2 * fronts)]
    )(q_arrived, q_out_inner_0, partner_1, *fixed)
    partner_2 = to_partner(in_inner_2)
    q_out_inner_2 = call(spread_kernel, [VMEM] * 4, VMEM, plane, [work(fronts)])(out_inner_2, phase, hx, hy)
    q_arrived_1, last_far, last_near = call(
        last_edge_kernel,
        [VMEM] * 7 + [pl.BlockSpec(memory_space=pl.ANY)],
        [VMEM] * 3,
        [plane] + [half_plane] * 2,
        buffers(1) + [work(fronts)],
    )(arrived_1, source, back, base_1, phase, hx, hy, q_out_inner_2)
    last_far = to_beyond(last_far)
    last_near = to_beyond(last_near)
    half_sum = jax.ShapeDtypeStruct((half, rows_y), BF16)
    inner_in, inner_out, inner_terms, inner_far, q_out_inner_2 = call(
        last_inner_kernel,
        [VMEM] * 11,
        [VMEM] * 5,
        [plane] * 2 + [jax.ShapeDtypeStruct((rows_x, rows_y), F32), half_sum, plane],
        buffers(3) + [work(2 * fronts)],
        input_output_aliases={10: 4},
    )(q_arrived_1, arrived_1, q_out_inner_1, partner_2, *fixed, out_inner_2, q_out_inner_2)
    inner_other = across(inner_far) if shots == 2 else jnp.zeros_like(inner_far)
    outer_far = call(far_terms_kernel, [VMEM] * 3 + [pl.BlockSpec(memory_space=pl.ANY)], VMEM, half_sum)(
        last_far, q_arrived, q_out_inner_2, inner_terms
    )
    outer_other = across(outer_far) if shots == 2 else jnp.zeros_like(outer_far)
    half_total = jax.ShapeDtypeStruct((half, rows_y), F32)
    share = jax.ShapeDtypeStruct((2, half, rows_y), F32)
    down, up = call(
        home_kernel, [VMEM] * 7, [HBM] * 2, [state] * 2, buffers(2, half_plane) + [dma((2, 2))]
    )(last_far, q_arrived, q_out_inner_2, screen, refl, inner_in, inner_out)
    down, up, gradient, outer_near = call(
        functools.partial(near_kernel, scale),
        [VMEM] * 7 + [HBM] * 2,
        [HBM] * 3 + [VMEM],
        [state, state, share, half_total],
        buffers(2, half_plane) + buffers(1, half_total) + [dma((2, 2))],
        input_output_aliases={7: 0, 8: 1},
    )(last_near, q_arrived, q_out_inner_2, screen, refl, inner_terms, inner_other, down, up)
    gradient = call(
        functools.partial(outer_gradient_kernel, scale),
        [VMEM] * 2 + [HBM],
        HBM,
        share,
        buffers(1, half_total) + [dma((1,))],
        input_output_aliases={2: 0},
    )(outer_near, outer_other, gradient)
    if shots != 2:
        terms = scale * jnp.stack([outer_far, inner_far]).astype(F32)
        far = jnp.where(odd_place() == 0, terms, terms[::-1])
        top = lax.rem(lax.axis_index("shot"), 2) == 0
        whole = jnp.concatenate([jnp.where(top, gradient, far), jnp.where(top, far, gradient)], axis=1)
        gradient = lax.psum_scatter(whole.astype(BF16), "shot", scatter_dimension=1, tiled=True).astype(F32)
    return (down, up, gradient)


def solution(mesh):
    return jax.shard_map(
        per_device,
        mesh=mesh,
        in_specs=(
            P("depth", "shot", None, None, None),
            P("depth", "shot", None, None, None),
            P("shot", None, None, None),
            P("depth", None, None),
            P("depth", None, None),
            P(),
            P("shot"),
        ),
        out_specs=(
            P("depth", "shot", None, None, None),
            P("depth", "shot", None, None, None),
            P("depth", "shot", None),
        ),
        check_vma=False,
    )
```
